128 devices in a mesh: seq: 16 (over y, z), head: 8 (over x, core).
Axes of the slice: x: 4, y: 4, z: 4, core: 2. Of those that a mesh axis runs over, the one named last changes fastest.
Arguments:
- block_input: bfloat16 [8192, 2048], P('seq', 'head'), may hold values from -6 to 6
- log_decay: float32 [8192, 16], P('seq', 'head'), may hold values from -2.2 to 0, as said below
- first_gain: float32 [2048], replicated, may hold values from 0.5 to 1.5
- query_weight: bfloat16 [2048, 2048], P(None, 'head'), may hold values from -0.125 to 0.125
- key_weight: bfloat16 [2048, 2048], P(None, 'head'), may hold values from -0.125 to 0.125
- value_weight: bfloat16 [2048, 4096], P(None, 'head'), may hold values from -0.125 to 0.125
- gate_weight: bfloat16 [2048, 4096], P(None, 'head'), may hold values from -0.125 to 0.125
- beta_weight: bfloat16 [2048, 16], P(None, 'head'), may hold values from -0.125 to 0.125
- query_conv: float32 [2048, 4], P('head'), may hold values from -3 to 3
- key_conv: float32 [2048, 4], P('head'), may hold values from -3 to 3
- value_conv: float32 [4096, 4], P('head'), may hold values from -3 to 3
- mixer_gain: float32 [4096], P('head'), may hold values from 0.5 to 1.5
- mixer_weight: bfloat16 [2048, 4096], P(None, 'head'), may hold values from -0.09375 to 0.09375
- second_gain: float32 [2048], replicated, may hold values from 0.5 to 1.5
- swiglu_gate: bfloat16 [2048, 5632], P(None, 'head'), may hold values from -0.125 to 0.125
- swiglu_up: bfloat16 [2048, 5632], P(None, 'head'), may hold values from -0.125 to 0.125
- swiglu_down: bfloat16 [2048, 5632], P(None, 'head'), may hold values from -0.078125 to 0.078125
- cotangent: bfloat16 [8192, 2048], P('seq', 'head'), may hold values from -6 to 6
Outputs:
- output: bfloat16 [8192, 2048], P('seq', 'head')
- grad_input: float32 [8192, 2048], P('seq', 'head')
- grad_first_gain: float32 [2048], P('seq')
- grad_query_weight: float32 [2048, 2048], P('seq', 'head')
- grad_key_weight: float32 [2048, 2048], P('seq', 'head')
- grad_value_weight: float32 [2048, 4096], P('seq', 'head')
- grad_gate_weight: float32 [2048, 4096], P('seq', 'head')
- grad_beta_weight: float32 [2048, 16], P('seq', 'head')
- grad_query_conv: float32 [2048, 4], P('head')
- grad_key_conv: float32 [2048, 4], P('head')
- grad_value_conv: float32 [4096, 4], P('head')
- grad_mixer_gain: float32 [4096], P('head')
- grad_mixer_weight: float32 [2048, 4096], P('seq', 'head')
- grad_second_gain: float32 [2048], P('seq')
- grad_swiglu_gate: float32 [2048, 5632], P('seq', 'head')
- grad_swiglu_up: float32 [2048, 5632], P('seq', 'head')
- grad_swiglu_down: float32 [2048, 5632], P('seq', 'head')
The draws below stay inside these ranges and needn't reach their ends.
Inputs may be any that keep to these rules, and one draw needn't show every extreme that they name: `log_decay`: every entry is negative.
All inputs are finite; a program needn't handle non-finite values.
Results may differ from the reference program's by a relative error of at most 0.025.
Values may be sent and summed in bfloat16 or wider, within the bound.
No kernel may reach another device: no remote copies, remote signals or barrier semaphores. Data moves between devices by JAX's collectives and lax.ppermute only.
A program may use at most 192 MiB of HBM per device.

```python
import jax
import jax.numpy as jnp
from jax import lax

D = 2048
H = 16
DK = 128
DV = 256
FF = 5632
KW = 4
CH = 64
LENGTH = 8192


def draw_log_decay(key, part):
    key = jax.random.fold_in(key, 11)
    keys_all = jax.random.split(key, 5)
    fast_cut = 5
    fast_heads = jax.random.randint(keys_all[0], (H,), 0, 10) < fast_cut
    decay_rates = jnp.where(fast_heads, 1.0 / 40.0, 0.8 / LENGTH)
    block_decay_factor = jnp.exp(jax.random.uniform(keys_all[1], (LENGTH // CH, H), jnp.float32, -0.7, 0.7))
    block_decay_factor = jnp.repeat(block_decay_factor, CH, axis=0)
    token_decay_factor = jnp.exp(jax.random.uniform(keys_all[2], (LENGTH, H), jnp.float32, -0.35, 0.35))
    token_positions = jax.random.randint(keys_all[3], (3,), 0, LENGTH)
    block_depths = jnp.log(jax.random.uniform(keys_all[4], (3, H), jnp.float32, 0.5, 0.8))
    token_position_index = jnp.arange(LENGTH)
    block_groups = jnp.sum(jnp.where(token_position_index[None, :, None] == token_positions[:, None, None], block_depths[:, None, :], 0.0), axis=0)
    return -decay_rates[None, :] * block_decay_factor * token_decay_factor + block_groups


def level_of(key, shape, cuts, least, top_value):
    def one(position, blocks):
        heights = jax.random.uniform(jax.random.fold_in(jax.random.fold_in(key, 6), position), (blocks,), jnp.float32, least / len(cuts), top_value / len(cuts))
        return jnp.repeat(jnp.exp(heights), shape[position] // blocks).reshape((-1,) + (1,) * (len(shape) - position - 1))

    factor_of = one(*cuts[0])
    for cut in cuts[1:]:
        factor_of = factor_of * one(*cut)
    return factor_of


def bell_draw(own_key, extent, scale, reach, cuts=(), kind=jnp.bfloat16):
    values = jax.random.normal(own_key, extent, jnp.float32) * scale
    if len(cuts) > 0:
        values = level_of(own_key, extent, cuts, -0.22, 0.18) * values
    return jnp.clip(values, min=-reach, max=reach).astype(kind)


def setup_inputs(seed: int = 0) -> dict:
    keys = jax.random.split(jax.random.key(seed), 19)
    return {
        "block_input": bell_draw(keys[0], (LENGTH, D), 1.0, 6.0, ((0, 16), (1, 8))),
        "log_decay": draw_log_decay(jax.random.fold_in(keys[18], 71), 0),
        "first_gain": jnp.clip(1.0 + 0.1 * jax.random.normal(keys[2], (D,), jnp.float32), 0.5, 1.5),
        "query_weight": bell_draw(keys[3], (D, H * DK), D ** -0.5, 0.125, ((1, 8),)),
        "key_weight": bell_draw(keys[4], (D, H * DK), D ** -0.5, 0.125, ((1, 8),)),
        "value_weight": bell_draw(keys[5], (D, H * DV), D ** -0.5, 0.125, ((1, 8),)),
        "gate_weight": bell_draw(keys[6], (D, H * DV), D ** -0.5, 0.125, ((1, 8),)),
        "beta_weight": bell_draw(keys[7], (D, H), D ** -0.5, 0.125, ((1, 8),)),
        "query_conv": bell_draw(keys[8], (H * DK, KW), KW ** -0.5, 3.0, ((0, 8),), jnp.float32),
        "key_conv": bell_draw(keys[9], (H * DK, KW), KW ** -0.5, 3.0, ((0, 8),), jnp.float32),
        "value_conv": bell_draw(keys[10], (H * DV, KW), KW ** -0.5, 3.0, ((0, 8),), jnp.float32),
        "mixer_gain": jnp.clip(1.0 + 0.1 * jax.random.normal(keys[11], (H * DV,), jnp.float32), 0.5, 1.5),
        "mixer_weight": bell_draw(keys[12], (D, H * DV), (H * DV) ** -0.5, 0.09375, ((1, 8),)),
        "second_gain": jnp.clip(1.0 + 0.1 * jax.random.normal(keys[13], (D,), jnp.float32), 0.5, 1.5),
        "swiglu_gate": bell_draw(keys[14], (D, FF), D ** -0.5, 0.125, ((1, 8),)),
        "swiglu_up": bell_draw(keys[15], (D, FF), D ** -0.5, 0.125, ((1, 8),)),
        "swiglu_down": bell_draw(keys[16], (D, FF), FF ** -0.5, 0.078125, ((1, 8),)),
        "cotangent": bell_draw(keys[17], (LENGTH, D), 1.0, 6.0, ((0, 16), (1, 8))),
    }


HIGH_ACCURACY = lax.Precision.HIGHEST
EPS_NORM = 1e-06
EPS_GATE = 1e-05

@jax.custom_vjp
def low(v):
    return lax.optimization_barrier(v.astype(jnp.bfloat16)).astype(jnp.float32)

@jax.custom_vjp
def low_back(v):
    return v

def low_keep(v):
    return (low(v), None)

def low_pass(kept, grad):
    return (grad,)

def back_keep(v):
    return (v, None)

def back_low(kept, grad):
    return (low(grad),)
low.defvjp(low_keep, low_pass)
low_back.defvjp(back_keep, back_low)

def rms_norm(values, gain):
    factor = lax.rsqrt(lax.optimization_barrier(jnp.mean(values * values, axis=-1, keepdims=True)) + EPS_NORM)
    return values * factor * gain

def causal_conv(inputs, taps):
    padded = jnp.concatenate([jnp.zeros((taps.shape[1] - 1, inputs.shape[1]), jnp.float32), inputs], axis=0)
    length = inputs.shape[0]
    summed = padded[0:length] * taps[:, 0]
    for offset in range(1, taps.shape[1]):
        summed = summed + padded[offset:offset + length] * taps[:, offset]
    return summed

def unit_keys(raw_keys, head_count):
    tokens = raw_keys.shape[0]
    split_heads = raw_keys.reshape(tokens, head_count, -1)
    scaled = split_heads * lax.rsqrt(lax.optimization_barrier(jnp.sum(split_heads * split_heads, axis=-1, keepdims=True)) + EPS_NORM)
    return scaled.reshape(tokens, -1)

def to_blocks(flat_rows, head_count):
    tokens = flat_rows.shape[0]
    return flat_rows.reshape(tokens // CH, CH, head_count, -1).transpose(0, 2, 1, 3)

def group_prep(query_blocks, key_blocks, value_blocks, beta_blocks, decay_blocks):
    gammas = jnp.cumsum(decay_blocks, axis=-1)
    span_len = gammas.shape[-1]
    row_index = lax.broadcasted_iota(jnp.int32, (span_len, span_len), 0)
    col_index = lax.broadcasted_iota(jnp.int32, (span_len, span_len), 1)
    below_mask = row_index > col_index
    within_mask = row_index >= col_index
    spread = gammas[..., :, None] - gammas[..., None, :]
    below_decay = jnp.where(below_mask, jnp.exp(jnp.where(below_mask, spread, 0.0)), 0.0)
    within = jnp.where(within_mask, jnp.exp(jnp.where(within_mask, spread, 0.0)), 0.0)
    key_inner = jnp.einsum('nhik,nhjk->nhij', key_blocks, key_blocks, precision=HIGH_ACCURACY)
    lower_part = beta_blocks[..., :, None] * below_decay * key_inner
    system = jnp.eye(span_len, dtype=jnp.float32) + lower_part
    right_side = jnp.concatenate([(beta_blocks * jnp.exp(gammas))[..., None] * key_blocks, beta_blocks[..., None] * value_blocks], axis=-1)
    solved = jax.scipy.linalg.solve_triangular(system, right_side, lower=True, unit_diagonal=True)
    key_size = key_blocks.shape[-1]
    attention_scores = within * jnp.einsum('nhik,nhjk->nhij', query_blocks, key_blocks, precision=HIGH_ACCURACY)
    query_decay_factor = jnp.exp(gammas)[..., None] * query_blocks
    trailing_keys = jnp.exp(gammas[..., -1:] - gammas)[..., None] * key_blocks
    final_block_decay = jnp.exp(gammas[..., -1])
    return (query_decay_factor, attention_scores, solved[..., :key_size], solved[..., key_size:], trailing_keys, final_block_decay)

def group_step(state_sequence, pieces):
    query_decay_factor, attention_scores, triangular_keys, triangular_values, trailing_keys, final_block_decay = pieces
    corrected_values = triangular_values - jnp.einsum('osr,ora->osa', triangular_keys, state_sequence, precision=HIGH_ACCURACY)
    output_rows = jnp.einsum('osr,ora->osa', query_decay_factor, state_sequence, precision=HIGH_ACCURACY) + jnp.einsum('wpg,wgt->wpt', attention_scores, corrected_values, precision=HIGH_ACCURACY)
    following_states = final_block_decay[:, None, None] * state_sequence + jnp.einsum('fnb,fnx->fbx', trailing_keys, corrected_values, precision=HIGH_ACCURACY)
    return (following_states, output_rows)

def delta_rule(queries, key_unit, values, beta_vals, decays):
    head_count = decays.shape[1]
    beta_blocks = beta_vals.reshape(-1, CH, head_count).transpose(0, 2, 1)
    decay_blocks = decays.reshape(-1, CH, head_count).transpose(0, 2, 1)
    pieces = group_prep(to_blocks(queries, head_count), to_blocks(key_unit, head_count), to_blocks(values, head_count), beta_blocks, decay_blocks)
    initial = jnp.zeros((head_count, DK, DV), jnp.float32)
    ignored, output_rows = lax.scan(jax.checkpoint(group_step), initial, pieces)
    return output_rows.transpose(0, 2, 1, 3).reshape(-1, head_count, output_rows.shape[-1])

def gate_norm(mixed_out, gate_pre, mixer_gain):
    tokens = mixed_out.shape[0]
    factor = lax.rsqrt(lax.optimization_barrier(jnp.mean(mixed_out * mixed_out, axis=-1, keepdims=True)) + EPS_GATE)
    scaled = (mixed_out * factor).reshape(tokens, -1)
    return scaled * mixer_gain * jax.nn.silu(gate_pre)

def reference(block_input, log_decay, first_gain, query_weight, key_weight, value_weight, gate_weight, beta_weight, query_conv, key_conv, value_conv, mixer_gain, mixer_weight, second_gain, swiglu_gate, swiglu_up, swiglu_down, cotangent):
    head_count = log_decay.shape[1]

    def layer(input_rows, gain_one, weight_query, weight_key, weight_value, weight_gate, weight_beta, taps_query, taps_key, taps_value, gain_mixer, weight_mixer, gain_two, weight_swgate, weight_swup, weight_swdown):
        normed = low(rms_norm(input_rows, gain_one))
        proj_query = low(low_back(jnp.dot(normed, weight_query, precision=HIGH_ACCURACY)))
        proj_key = low(low_back(jnp.dot(normed, weight_key, precision=HIGH_ACCURACY)))
        proj_value = low(low_back(jnp.dot(normed, weight_value, precision=HIGH_ACCURACY)))
        gate_pre = low_back(jnp.dot(normed, weight_gate, precision=HIGH_ACCURACY))
        beta_vals = jax.nn.sigmoid(jnp.dot(normed, weight_beta, precision=HIGH_ACCURACY))
        queries = low(jax.nn.silu(causal_conv(proj_query, taps_query)))
        key_unit = low(unit_keys(jax.nn.silu(causal_conv(proj_key, taps_key)), head_count))
        values = low(jax.nn.silu(causal_conv(proj_value, taps_value)))
        mixed_out = delta_rule(queries, key_unit, values, beta_vals, log_decay)
        gated_out = low(gate_norm(mixed_out, gate_pre, gain_mixer))
        branch = low_back(jnp.dot(gated_out, weight_mixer.T, precision=HIGH_ACCURACY))
        hidden = input_rows + branch
        normed_two = low(rms_norm(hidden, gain_two))
        gate_act = low_back(jnp.dot(normed_two, weight_swgate, precision=HIGH_ACCURACY))
        up_act = low_back(jnp.dot(normed_two, weight_swup, precision=HIGH_ACCURACY))
        product = low(jax.nn.silu(gate_act) * up_act)
        return hidden + jnp.dot(product, weight_swdown.T, precision=HIGH_ACCURACY)
    result, backward = jax.vjp(layer, block_input.astype(jnp.float32), first_gain, query_weight.astype(jnp.float32), key_weight.astype(jnp.float32), value_weight.astype(jnp.float32), gate_weight.astype(jnp.float32), beta_weight.astype(jnp.float32), query_conv, key_conv, value_conv, mixer_gain, mixer_weight.astype(jnp.float32), second_gain, swiglu_gate.astype(jnp.float32), swiglu_up.astype(jnp.float32), swiglu_down.astype(jnp.float32))
    grads = backward(cotangent.astype(jnp.float32))
    return (result.astype(jnp.bfloat16), grads[0], grads[1], grads[2], grads[3], grads[4], grads[5], grads[6], grads[7], grads[8], grads[9], grads[10], grads[11], grads[12], grads[13], grads[14], grads[15])
```

```python
from functools import partial

import jax
import jax.numpy as jnp
from jax import lax
from jax.experimental import pallas as pl
from jax.experimental.pallas import tpu as pltpu
from jax.sharding import Mesh
from jax.sharding import PartitionSpec as P

DK = 128
DV = 256
CH = 128
EPS_NORM = 1e-06
EPS_GATE = 1e-05
FLOAT = jnp.float32
HALF = jnp.bfloat16
NN = (((1,), (0,)), ((), ()))
NT = (((1,), (1,)), ((), ()))
TN = (((0,), (0,)), ((), ()))
LIMIT = 48 * 1024 * 1024


def mm(a, b, dims=NN):
    return lax.dot_general(a.astype(HALF), b.astype(HALF), dims, preferred_element_type=FLOAT)


def halves(a):
    high = a.astype(HALF)
    return high, (a - high.astype(FLOAT)).astype(HALF)


def mm2(a, b, dims=NN):
    high, low = halves(b)
    return mm(a, high, dims) + mm(a, low, dims)


def mm3(a, b, dims=NN):
    a_high, a_low = halves(a)
    b_high, b_low = halves(b)
    return mm(a_high, b_high, dims) + (mm(a_high, b_low, dims) + mm(a_low, b_high, dims))


def sigmoid(v):
    return 1.0 / (1.0 + jnp.exp(-v))


def square_masks():
    rows = lax.broadcasted_iota(jnp.int32, (CH, CH), 0)
    cols = lax.broadcasted_iota(jnp.int32, (CH, CH), 1)
    return rows, cols


def decay_matrix(gcol, grow):
    rows, cols = square_masks()
    return jnp.where(rows >= cols, jnp.exp(jnp.minimum(gcol - grow, 0.0)), 0.0)


def conv_of(wide, taps, start, count, lanes):
    total = wide[5 + start : 5 + start + count, lanes] * taps[0:1, lanes]
    for j in range(1, 4):
        total = total + wide[5 + j + start : 5 + j + start + count, lanes] * taps[j : j + 1, lanes]
    return total


def prepare_kernel(heads, chunks, proj, taps, betas, gcol, grow, q_out, k_out, v_out, t_out, n_out, b_out, w_out, u_out, p_out, pay, wide):
    rows, cols = square_masks()
    differ = rows ^ cols
    eye = jnp.where(rows == cols, 1.0, 0.0)
    wide[...] = proj[...].astype(FLOAT)
    kq = heads * DK
    work = [(h, c) for h in range(heads) for c in range(chunks)]
    low, keys, sides = {}, {}, {}
    for h, c in work:
        span = slice(c * CH, (c + 1) * CH)
        ql, kl, vl = (
            slice(h * DK, (h + 1) * DK),
            slice(kq + h * DK, kq + (h + 1) * DK),
            slice(2 * kq + h * DV, 2 * kq + (h + 1) * DV),
        )
        cq = conv_of(wide, taps, c * CH, CH, ql)
        query = (cq * sigmoid(cq)).astype(HALF)
        ck = conv_of(wide, taps, c * CH, CH, kl)
        act = ck * sigmoid(ck)
        key = (act * lax.rsqrt(jnp.sum(act * act, axis=-1, keepdims=True) + EPS_NORM)).astype(HALF)
        cv = conv_of(wide, taps, c * CH, CH, vl)
        value = (cv * sigmoid(cv)).astype(HALF)
        q_out[span, ql] = query
        k_out[span, ql] = key
        v_out[span, h * DV : (h + 1) * DV] = value
        beta = betas[span, h : h + 1]
        g = gcol[span, h : h + 1]
        spread = decay_matrix(g, grow[h * chunks + c : h * chunks + c + 1, :])
        inner = mm(key, key, NT)
        low[h, c] = jnp.where(rows > cols, beta * spread * inner, 0.0)
        p_out[h * chunks + c] = (spread * mm(query, key, NT)).astype(HALF)
        keys[h, c] = key
        sides[h, c] = jnp.concatenate([(beta * jnp.exp(g)) * key.astype(FLOAT), beta * value.astype(FLOAT)], axis=1)
    tri = {at: eye - jnp.where(differ < 2, low[at], 0.0) for at in work}
    size = 2
    while size < CH:
        part = {at: mm3(jnp.where((differ >= size) & (differ < 2 * size), low[at], 0.0), tri[at]) for at in work}
        tri = {at: tri[at] - mm3(tri[at], part[at]) for at in work}
        size *= 2
    steps = {}
    for h, c in work:
        at = h * chunks + c
        t_out[at] = tri[h, c].astype(HALF)
        solved = mm3(tri[h, c], sides[h, c])
        w_out[at] = solved[:, :DK].astype(HALF)
        u_out[at] = solved[:, DK:].astype(HALF)
        g = gcol[c * CH : (c + 1) * CH, h : h + 1]
        last = gcol[(c + 1) * CH - 1 : (c + 1) * CH, h : h + 1]
        step = mm2(keys[h, c], jnp.exp(last - g) * solved, TN)
        n_out[at] = step[:, :DK].astype(HALF)
        b_out[at] = step[:, DK:]
        steps[h, c] = (jnp.exp(last), step)
    zero = jnp.zeros((DK, DK), FLOAT)
    for h in range(heads):
        decay, step = steps[h, 0]
        total = jnp.concatenate([decay * eye - step[:, :DK], step[:, DK:]], axis=1)
        whole = decay
        for c in range(1, chunks):
            decay, step = steps[h, c]
            total = decay * total - mm3(step[:, :DK], total) + jnp.concatenate([zero, step[:, DK:]], axis=1)
            whole = whole * decay
        pack_map(pay, h, total, whole, eye)


def whole_decay(pay, j, h):
    return pay[j, h, DK : DK + 1, 0:1].astype(FLOAT) + pay[j, h, DK + 8 : DK + 9, 0:1].astype(FLOAT)


def apply_whole(pay, j, h, state, dims):
    return whole_decay(pay, j, h) * state + mm(pay[j, h, :DK, :DK], state, dims)


def pack_map(pay, h, total, whole, eye):
    pay[h, :DK, :] = jnp.concatenate([total[:, :DK] - whole * eye, total[:, DK:]], axis=1).astype(HALF)
    rest = jnp.broadcast_to(whole, (8, DK + DV))
    first = rest.astype(HALF).astype(FLOAT)
    pay[h, DK:, :] = jnp.concatenate([first, rest - first], axis=0).astype(HALF)


def group_kernel(heads, mine, near, before, group):
    me = mine[0]
    rows, cols = square_masks()
    eye = jnp.where(rows == cols, 1.0, 0.0)
    zero = jnp.zeros((DK, DK), FLOAT)
    start = jnp.concatenate([eye, jnp.zeros((DK, DV), FLOAT)], axis=1)
    totals, keeps, wholes = [start] * heads, [start] * heads, [jnp.ones((1, 1), FLOAT)] * heads
    for j in range(near.shape[0]):
        for h in range(heads):
            added = jnp.concatenate([zero, near[j, h, :DK, DK:].astype(FLOAT)], axis=1)
            if j == 0:
                moved = jnp.concatenate([whole_decay(near, j, h) * eye + near[j, h, :DK, :DK].astype(FLOAT), added[:, DK:]], axis=1)
            else:
                moved = apply_whole(near, j, h, totals[h], NN) + added
            totals[h] = moved
            wholes[h] = wholes[h] * whole_decay(near, j, h)
            keeps[h] = jnp.where(me == j + 1, moved, keeps[h])
    for h in range(heads):
        before[h] = keeps[h]
        pack_map(group, h, totals[h], wholes[h], eye)


def group_back_kernel(heads, mine, near, ends, after, group):
    me = mine[0]
    rows, cols = square_masks()
    eye = jnp.where(rows == cols, 1.0, 0.0)
    zero = jnp.zeros((DK, DK), FLOAT)
    start = jnp.concatenate([eye, jnp.zeros((DK, DV), FLOAT)], axis=1)
    totals, keeps = [start] * heads, [start] * heads
    for j in reversed(range(near.shape[0])):
        for h in range(heads):
            keeps[h] = jnp.where(me == j, totals[h], keeps[h])
            added = jnp.concatenate([zero, ends[j, h].astype(FLOAT)], axis=1)
            totals[h] = apply_whole(near, j, h, totals[h], TN) + added
    for h in range(heads):
        after[h] = keeps[h]
        group[h] = totals[h][:, DK:].astype(HALF)


def mix_kernel(heads, chunks, mine, pay, before, q, k, w, u, p, n, b, gcol, gate, gain, s_out, vn_out, o_out, gated):
    ranks = pay.shape[0]
    me = mine[0]
    states = [jnp.zeros((DK, DV), FLOAT) for h in range(heads)]
    for j in range(ranks - 1):
        passed = j < me
        for h in range(heads):
            moved = apply_whole(pay, j, h, states[h], NN) + pay[j, h, :DK, DK:].astype(FLOAT)
            states[h] = jnp.where(passed, moved, states[h])
    for h in range(heads):
        states[h] = mm3(before[h, :, :DK], states[h]) + before[h, :, DK:]
    for c in range(chunks):
        span = slice(c * CH, (c + 1) * CH)
        for h in range(heads):
            at = h * chunks + c
            state = states[h].astype(HALF)
            s_out[at] = state
            g = gcol[span, h : h + 1]
            last = gcol[(c + 1) * CH - 1 : (c + 1) * CH, h : h + 1]
            vn = (u[at].astype(FLOAT) - mm(w[at], state)).astype(HALF)
            vn_out[at] = vn
            out = jnp.exp(g) * mm(q[span, h * DK : (h + 1) * DK], state) + mm(p[at], vn)
            vl = slice(h * DV, (h + 1) * DV)
            o_out[span, vl] = out
            factor = lax.rsqrt(jnp.mean(out * out, axis=-1, keepdims=True) + EPS_GATE)
            pre = gate[span, vl]
            gated[span, vl] = (out * factor * gain[:, vl] * (pre * sigmoid(pre))).astype(HALF)
            if c + 1 < chunks:
                states[h] = jnp.exp(last) * states[h] - mm(n[at], state) + b[at]


def gate_back_kernel(heads, chunks, d_gated, out, gate, gain, q, w, p, n, gcol, do_out, dvn_out, e_out, dpre_out, dgain_out, sums_out, pay):
    dgain = [jnp.zeros((1, DV), FLOAT) for h in range(heads)]
    ends = [None] * heads
    for c in reversed(range(chunks)):
        span = slice(c * CH, (c + 1) * CH)
        for h in range(heads):
            at = h * chunks + c
            vl = slice(h * DV, (h + 1) * DV)
            dg, o, pre, gn = d_gated[span, vl], out[span, vl], gate[span, vl], gain[:, vl]
            sig = sigmoid(pre)
            factor = lax.rsqrt(jnp.mean(o * o, axis=-1, keepdims=True) + EPS_GATE)
            m = o * factor
            s = pre * sig
            dgm = dg * m
            dgain[h] = dgain[h] + jnp.sum(dgm * s, axis=0, keepdims=True)
            dpre = dgm * gn * (sig * (1.0 + pre * (1.0 - sig)))
            dpre_out[span, vl] = dpre.astype(HALF)
            row_sum = jnp.sum(dpre * pre, axis=-1, keepdims=True)
            sums_out[span, :] = row_sum if h == 0 else sums_out[span, :] + row_sum
            e = dg * gn * s
            dout = factor * (e - m * jnp.mean(e * m, axis=-1, keepdims=True))
            do_out[span, vl] = dout.astype(HALF)
            g = gcol[span, h : h + 1]
            last = gcol[(c + 1) * CH - 1 : (c + 1) * CH, h : h + 1]
            dvn = mm(p[at], dout, TN)
            dvn_out[at] = dvn
            source = mm(q[span, h * DK : (h + 1) * DK], jnp.exp(g) * dout, TN) - mm(w[at], dvn, TN)
            e_out[at] = source
            if ends[h] is None:
                ends[h] = source
            else:
                ends[h] = jnp.exp(last) * ends[h] - mm(n[at], ends[h], TN) + source
    for h in range(heads):
        pay[h] = ends[h].astype(HALF)
        dgain_out[0:1, h * DV : (h + 1) * DV] = dgain[h]


def back_kernel(heads, chunks, mine, pay, late, after, q, k, v, betas, gcol, grow, tri, states, vns, dos, dvns, es, ns, proj, taps, dproj_out, halo_out, dlogit_out, dtaps_out, rowsum_out, wide, dconv):
    ranks = pay.shape[0]
    tokens = chunks * CH
    me = mine[0]
    kq = heads * DK
    width = 2 * kq + heads * DV
    rows, cols = square_masks()
    grads = [jnp.zeros((DK, DV), FLOAT) for h in range(heads)]
    for j in reversed(range(1, ranks)):
        passed = j > me
        for h in range(heads):
            moved = apply_whole(pay, j, h, grads[h], TN) + late[j, h].astype(FLOAT)
            grads[h] = jnp.where(passed, moved, grads[h])
    for h in range(heads):
        grads[h] = mm3(after[h, :, :DK], grads[h]) + after[h, :, DK:]
    wide[...] = proj[...].astype(FLOAT)
    dconv[0:8, :] = jnp.zeros((8, width), FLOAT)
    dconv[8 + tokens :, :] = jnp.zeros((8, width), FLOAT)
    for c in reversed(range(chunks)):
        span = slice(c * CH, (c + 1) * CH)
        for h in range(heads):
            at = h * chunks + c
            ql, kl, vl, ol = (
                slice(h * DK, (h + 1) * DK),
                slice(kq + h * DK, kq + (h + 1) * DK),
                slice(2 * kq + h * DV, 2 * kq + (h + 1) * DV),
                slice(h * DV, (h + 1) * DV),
            )
            grad = grads[h].astype(HALF)
            query, key, value = q[span, ql], k[span, ql], v[span, ol]
            state, vn, dout = states[at], vns[at], dos[span, ol]
            beta = betas[span, h : h + 1]
            g = gcol[span, h : h + 1]
            last = gcol[(c + 1) * CH - 1 : (c + 1) * CH, h : h + 1]
            eg, ed = jnp.exp(g), jnp.exp(last - g)
            spread = decay_matrix(g, grow[at : at + 1, :])
            strict = jnp.where(rows > cols, spread, 0.0)
            inner = mm(key, key, NT)
            dvn = dvns[at] + ed * mm(key, grad)
            dr = mm(tri[at], dvn, TN)
            drh = dr.astype(HALF)
            ks = mm(key, state)
            dval = beta * dr
            both = mm(jnp.concatenate([dout, drh], axis=0), state, NT)
            dkeep = mm(vn, grad, NT)
            pair = mm(jnp.concatenate([dout, drh], axis=0), vn, NT)
            dqk = spread * pair[:CH]
            da = -(strict * pair[CH:])
            dkk = beta * da
            dbeta = jnp.sum(dr * (value.astype(FLOAT) - eg * ks), axis=-1, keepdims=True) + jnp.sum(
                da * inner, axis=-1, keepdims=True
            )
            dqkh = dqk.astype(HALF)
            dkkh = dkk.astype(HALF)
            dquery = eg * both[:CH] + mm(dqkh, key)
            dkey = (
                ed * dkeep
                - (beta * eg) * both[CH:]
                + mm(dqkh, query, TN)
                + mm(dkkh, key)
                + mm(dkkh, key, TN)
            )
            if c > 0:
                grads[h] = jnp.exp(last) * grads[h] - mm(ns[at], grad, TN) + es[at]
            dlogit_out[span, h : h + 1] = dbeta * beta * (1.0 - beta)
            there = slice(8 + c * CH, 8 + (c + 1) * CH)
            cq = conv_of(wide, taps, c * CH, CH, ql)
            sig = sigmoid(cq)
            dconv[there, ql] = dquery * (sig * (1.0 + cq * (1.0 - sig)))
            cv = conv_of(wide, taps, c * CH, CH, vl)
            sig = sigmoid(cv)
            dconv[there, vl] = dval * (sig * (1.0 + cv * (1.0 - sig)))
            ck = conv_of(wide, taps, c * CH, CH, kl)
            sig = sigmoid(ck)
            act = ck * sig
            unit = lax.rsqrt(jnp.sum(act * act, axis=-1, keepdims=True) + EPS_NORM)
            u = act * unit
            dact = unit * (dkey - u * jnp.sum(dkey * u, axis=-1, keepdims=True))
            dconv[there, kl] = dact * (sig * (1.0 + ck * (1.0 - sig)))
    dtaps_out[4:8, :] = jnp.zeros((4, width), FLOAT)
    rowsum_out[...] = jnp.zeros((8 + tokens, 1), FLOAT)
    for at in range(0, width, DK):
        lanes = slice(at, at + DK)
        for j in range(4):
            dtaps_out[j : j + 1, lanes] = jnp.sum(
                dconv[8 : 8 + tokens, lanes] * wide[5 + j : 5 + j + tokens, lanes], axis=0, keepdims=True
            )
        total = dconv[3 : 3 + 8 + tokens, lanes] * taps[0:1, lanes]
        for j in range(1, 4):
            total = total + dconv[3 - j : 3 - j + 8 + tokens, lanes] * taps[j : j + 1, lanes]
        halo_out[:, lanes] = total[0:8]
        small = total.astype(HALF)
        dproj_out[:, lanes] = small
        rowsum_out[...] += jnp.sum(small.astype(FLOAT) * wide[:, lanes], axis=-1, keepdims=True)


def out(shape, dtype):
    return jax.ShapeDtypeStruct(shape, dtype)


def run(kernel, shapes, args, scratch=(), scalars=0):
    vmem = pl.BlockSpec(memory_space=pltpu.VMEM)
    smem = pl.BlockSpec(memory_space=pltpu.SMEM)
    return pl.pallas_call(
        kernel,
        out_shape=shapes,
        in_specs=[smem] * scalars + [vmem] * (len(args) - scalars),
        out_specs=[vmem] * len(shapes),
        scratch_shapes=list(scratch),
        compiler_params=pltpu.CompilerParams(vmem_limit_bytes=LIMIT),
    )(*args)


def prepare_shapes(heads, chunks):
    tokens, pairs = chunks * CH, heads * chunks
    return (
        out((tokens, heads * DK), HALF),
        out((tokens, heads * DK), HALF),
        out((tokens, heads * DV), HALF),
        out((pairs, CH, CH), HALF),
        out((pairs, DK, DK), HALF),
        out((pairs, DK, DV), FLOAT),
        out((pairs, CH, DK), HALF),
        out((pairs, CH, DV), HALF),
        out((pairs, CH, CH), HALF),
        out((heads, DK + 16, DK + DV), HALF),
    )


def mix_shapes(heads, chunks):
    tokens, pairs = chunks * CH, heads * chunks
    return (
        out((pairs, DK, DV), HALF),
        out((pairs, CH, DV), HALF),
        out((tokens, heads * DV), FLOAT),
        out((tokens, heads * DV), HALF),
    )


def gate_back_shapes(heads, chunks):
    tokens, pairs = chunks * CH, heads * chunks
    return (
        out((tokens, heads * DV), HALF),
        out((pairs, CH, DV), FLOAT),
        out((pairs, DK, DV), FLOAT),
        out((tokens, heads * DV), HALF),
        out((1, heads * DV), FLOAT),
        out((tokens, 1), FLOAT),
        out((heads, DK, DV), HALF),
    )


def back_shapes(heads, chunks):
    tokens = chunks * CH
    width = heads * (2 * DK + DV)
    return (
        out((8 + tokens, width), HALF),
        out((8, width), FLOAT),
        out((tokens, heads), FLOAT),
        out((8, width), FLOAT),
        out((8 + tokens, 1), FLOAT),
    )


def back_scratch(heads, chunks):
    tokens = chunks * CH
    width = heads * (2 * DK + DV)
    return (pltpu.VMEM((8 + tokens, width), FLOAT), pltpu.VMEM((16 + tokens, width), FLOAT))


def group_shapes(heads):
    return (out((heads, DK, DK + DV), FLOAT), out((heads, DK + 16, DK + DV), HALF))


def group_back_shapes(heads):
    return (out((heads, DK, DK + DV), FLOAT), out((heads, DK, DV), HALF))


HEAD = ("x", "c")
SEQ = ("y", "z")
CONTRACT_ROWS = (((0,), (0,)), ((), ()))
CONTRACT_COLS = (((1,), (1,)), ((), ()))


def rotated(array, axis, distance):
    size = lax.axis_size(axis)
    return lax.ppermute(array, axis, [(i, (i + distance) % size) for i in range(size)])


def ring_gather(array, axis):
    mine = lax.axis_index(axis)
    size = lax.axis_size(axis)
    arrived = [(rotated(array, axis, d), -d) for d in (1, -1, 2)]
    whole = jnp.zeros((size, *array.shape), array.dtype)
    for piece, offset in [(array, 0), *arrived]:
        whole = lax.dynamic_update_index_in_dim(whole, piece, (mine + offset) % size, 0)
    return whole


def head_gather(array):
    core = lax.axis_index("c")
    whole = ring_gather(array, "x")
    other = rotated(whole, "c", 1)
    both = jnp.where(core == 0, jnp.stack([whole, other], 1), jnp.stack([other, whole], 1))
    return both.reshape(8, *array.shape)


def head_scatter(tiles):
    mine, core = lax.axis_index("x"), lax.axis_index("c")
    tiles = tiles.reshape(4, 2, *tiles.shape[1:])
    own = lax.dynamic_index_in_dim(tiles, core, 1, False)
    other = rotated(lax.dynamic_index_in_dim(tiles, 1 - core, 1, False), "c", 1)
    summed = (own.astype(FLOAT) + other.astype(FLOAT)).astype(HALF)
    total = lax.dynamic_index_in_dim(summed, mine, 0, False).astype(FLOAT)
    for d in (1, -1, 2):
        sent = lax.dynamic_index_in_dim(summed, (mine + d) % 4, 0, False)
        total = total + rotated(sent, "x", d).astype(FLOAT)
    return total


def next_block(array, distance):
    size = 16
    route = [(i, i + distance) for i in range(size) if 0 <= i + distance < size]
    return lax.ppermute(array, SEQ, route)


def dot(a, b):
    return jnp.dot(a, b, preferred_element_type=FLOAT)


def dot_nt(a, b):
    return lax.dot_general(a, b, CONTRACT_COLS, preferred_element_type=FLOAT)


def dot_tn(a, b):
    return lax.dot_general(a, b, CONTRACT_ROWS, preferred_element_type=FLOAT)


def silu_grad(v):
    s = jax.nn.sigmoid(v)
    return s * (1.0 + v * (1.0 - s))


def seq_scatter(array):
    return lax.psum_scatter(array.astype(HALF), SEQ, scatter_dimension=0, tiled=True).astype(FLOAT)


def side_by_side(blocks):
    count, rows, cols = blocks.shape
    return blocks.transpose(1, 0, 2).reshape(rows, count * cols)


def shards(
    block_input,
    log_decay,
    first_gain,
    query_weight,
    key_weight,
    value_weight,
    gate_weight,
    beta_weight,
    query_conv,
    key_conv,
    value_conv,
    mixer_gain,
    mixer_weight,
    second_gain,
    swiglu_gate,
    swiglu_up,
    swiglu_down,
    cotangent,
):
    heads = log_decay.shape[1]
    tokens, width = block_input.shape
    chunks = tokens // CH
    rows = tokens // 8
    kq = heads * DK
    rank = lax.axis_index("x") * 2 + lax.axis_index("c")
    z_rank = lax.axis_index("z").astype(jnp.int32).reshape(1)
    y_rank = lax.axis_index("y").astype(jnp.int32).reshape(1)

    in_weight = jnp.concatenate([query_weight, key_weight, value_weight], axis=1)
    taps = jnp.concatenate([query_conv, key_conv, value_conv], axis=0).T
    gcol = jnp.cumsum(log_decay.reshape(chunks, CH, heads), axis=1)
    grow = gcol.transpose(2, 0, 1).reshape(heads * chunks, CH)
    gcol = gcol.reshape(tokens, heads)
    gain_row = mixer_gain.reshape(1, -1)

    halo = next_block(block_input[tokens - 8 :], 1)
    whole = side_by_side(head_gather(block_input))
    whole = jnp.concatenate([side_by_side(head_gather(halo)), whole], axis=0).astype(FLOAT)
    first_factor = lax.rsqrt(jnp.mean(whole * whole, axis=-1, keepdims=True) + EPS_NORM)
    first_normed = (whole * first_factor * first_gain).astype(HALF)
    proj = dot(first_normed, in_weight).astype(HALF)
    logits = dot(first_normed[8:], beta_weight)
    betas = jax.nn.sigmoid(logits)
    gate_pre = dot(first_normed[8:], gate_weight)
    q, k, v, tri, n, b, w, u, p, pay = run(
        partial(prepare_kernel, heads, chunks),
        prepare_shapes(heads, chunks),
        (proj, taps, betas, gcol, grow),
        [pltpu.VMEM((8 + tokens, taps.shape[1]), FLOAT)],
    )
    near = ring_gather(pay, "z")
    before, group = run(
        partial(group_kernel, heads), group_shapes(heads), (z_rank, near), scalars=1
    )
    far = ring_gather(group, "y")
    states, vns, mixed, gated = run(
        partial(mix_kernel, heads, chunks),
        mix_shapes(heads, chunks),
        (y_rank, far, before, q, k, w, u, p, n, b, gcol, gate_pre, gain_row),
        scalars=1,
    )
    branch = head_scatter(dot_nt(gated, mixer_weight).astype(HALF).reshape(8, rows, -1))
    my_rows = lax.dynamic_slice_in_dim(whole, 8 + rank * rows, rows, 0)
    hidden = my_rows + branch
    second_factor = lax.rsqrt(jnp.mean(hidden * hidden, axis=-1, keepdims=True) + EPS_NORM)
    second_unit = hidden * second_factor
    second_normed = head_gather((second_unit * second_gain).astype(HALF)).reshape(tokens, -1)
    gate_act = dot(second_normed, swiglu_gate)
    up_act = dot(second_normed, swiglu_up)
    silu_act = jax.nn.silu(gate_act)
    product = (silu_act * up_act).astype(HALF)
    whole_cot = side_by_side(head_gather(cotangent))
    d_product = dot(whole_cot, swiglu_down)
    d_gate = (d_product * up_act * silu_grad(gate_act)).astype(HALF)
    d_up = (d_product * silu_act).astype(HALF)
    d_second = head_scatter(
        (dot_nt(d_gate, swiglu_gate) + dot_nt(d_up, swiglu_up)).astype(HALF).reshape(8, rows, -1)
    )
    grad_swiglu_down = seq_scatter(dot_tn(whole_cot, product))
    grad_swiglu_gate = seq_scatter(dot_tn(second_normed, d_gate))
    grad_swiglu_up = seq_scatter(dot_tn(second_normed, d_up))
    second_gain_part = jnp.sum(d_second * second_unit, axis=0)
    e = d_second * second_gain
    cot_rows = lax.dynamic_slice_in_dim(whole_cot, rank * rows, rows, 0).astype(FLOAT)
    d_hidden = cot_rows + second_factor * (
        e - second_unit * jnp.mean(e * second_unit, axis=-1, keepdims=True)
    )
    d_branch = head_gather(d_hidden.astype(HALF)).reshape(tokens, -1)
    d_gated = dot(d_branch, mixer_weight)
    dos, dvns, es, d_gate_pre, gain_part, gate_sums, ends = run(
        partial(gate_back_kernel, heads, chunks),
        gate_back_shapes(heads, chunks),
        (d_gated, mixed, gate_pre, gain_row, q, w, p, n, gcol),
    )
    near_ends = ring_gather(ends, "z")
    after, group_end = run(
        partial(group_back_kernel, heads), group_back_shapes(heads), (z_rank, near, near_ends), scalars=1
    )
    far_ends = ring_gather(group_end, "y")
    grad_mixer_weight = seq_scatter(dot_tn(d_branch, gated))
    grad_gate_weight = seq_scatter(dot_tn(first_normed[8:], d_gate_pre))
    d_first_part = dot_nt(d_gate_pre, gate_weight)
    dproj, halo_grad, d_logit, taps_part, sums = run(
        partial(back_kernel, heads, chunks),
        back_shapes(heads, chunks),
        (y_rank, far, far_ends, after, q, k, v, betas, gcol, grow, tri, states, vns, dos, dvns, es, n, proj, taps),
        back_scratch(heads, chunks),
        scalars=1,
    )
    grad_in_weight = seq_scatter(dot_tn(first_normed, dproj))
    grad_beta = dot_tn(first_normed[8:], d_logit.astype(HALF))
    arrived = next_block(halo_grad, -1)
    last = dproj[tokens:].astype(FLOAT) + arrived
    d_own = jnp.concatenate([dproj[8:tokens], last.astype(HALF)], axis=0)
    late_sums = jnp.sum(arrived * proj[tokens:].astype(FLOAT), axis=-1)
    row_sums = sums[8:, 0] + gate_sums[:, 0] + jnp.sum(d_logit * logits, axis=-1)
    row_sums = row_sums + jnp.concatenate([jnp.zeros((tokens - 8,), FLOAT), late_sums])
    d_first_part = d_first_part + dot_nt(d_own, in_weight)
    d_first_part = d_first_part + dot_nt(d_logit.astype(HALF), beta_weight)
    in_blocks = d_first_part.astype(HALF).reshape(tokens, 8, width).transpose(1, 0, 2)
    d_first = head_scatter(in_blocks)
    row_mean = lax.psum(row_sums, HEAD) / (8 * width)
    own_input = block_input.astype(FLOAT)
    own_factor = first_factor[8:]
    own_unit = own_input * own_factor
    own_gain = lax.dynamic_slice_in_dim(first_gain, rank * width, width, 0)
    d_branch_own = lax.dynamic_slice_in_dim(d_branch, rank * width, width, 1).astype(FLOAT)
    grad_input = d_branch_own + own_factor * (d_first * own_gain - own_unit * row_mean[:, None])
    first_gain_part = lax.dynamic_update_slice_in_dim(
        jnp.zeros((8 * width,), FLOAT), jnp.sum(d_first * own_unit, axis=0), rank * width, 0
    )
    down_part = dot_nt(product, swiglu_down)
    mine = lax.dynamic_slice_in_dim(down_part, rank * rows, rows, 0) + hidden
    down_part = lax.dynamic_update_slice_in_dim(down_part, mine, rank * rows, 0)
    output = head_scatter(down_part.astype(HALF).reshape(tokens, 8, width).transpose(1, 0, 2)).astype(HALF)
    small = [taps_part[:4], gain_part, grad_beta]
    ends_at = [0]
    for part in small:
        ends_at.append(ends_at[-1] + part.size)
    flat = lax.psum(jnp.concatenate([part.ravel() for part in small]), SEQ)
    taps_grad, grad_mixer_gain, grad_beta = (
        flat[at:to].reshape(part.shape) for part, at, to in zip(small, ends_at, ends_at[1:])
    )
    gains = lax.psum(jnp.stack([first_gain_part, second_gain_part]), SEQ + HEAD)
    seq_rank = lax.axis_index("y") * 4 + lax.axis_index("z")
    share = 8 * width // 16
    gains = lax.dynamic_slice_in_dim(gains, seq_rank * share, share, 1)
    grad_beta = lax.dynamic_slice_in_dim(grad_beta, seq_rank * share, share, 0)
    return (
        output,
        grad_input,
        gains[0],
        grad_in_weight[:, :kq],
        grad_in_weight[:, kq : 2 * kq],
        grad_in_weight[:, 2 * kq :],
        grad_gate_weight,
        grad_beta,
        taps_grad[:, :kq].T,
        taps_grad[:, kq : 2 * kq].T,
        taps_grad[:, 2 * kq :].T,
        grad_mixer_gain[0],
        grad_mixer_weight,
        gains[1],
        grad_swiglu_gate,
        grad_swiglu_up,
        grad_swiglu_down,
    )


def solution(mesh):
    torus = Mesh(mesh.devices.reshape(4, 4, 4, 2), SEQ + HEAD)
    in_specs = (
        P(SEQ, HEAD),
        P(SEQ, HEAD),
        P(),
        P(None, HEAD),
        P(None, HEAD),
        P(None, HEAD),
        P(None, HEAD),
        P(None, HEAD),
        P(HEAD, None),
        P(HEAD, None),
        P(HEAD, None),
        P(HEAD),
        P(None, HEAD),
        P(),
        P(None, HEAD),
        P(None, HEAD),
        P(None, HEAD),
        P(SEQ, HEAD),
    )
    out_specs = (
        P(SEQ, HEAD),
        P(SEQ, HEAD),
        P(SEQ),
        P(SEQ, HEAD),
        P(SEQ, HEAD),
        P(SEQ, HEAD),
        P(SEQ, HEAD),
        P(SEQ, HEAD),
        P(HEAD, None),
        P(HEAD, None),
        P(HEAD, None),
        P(HEAD),
        P(SEQ, HEAD),
        P(SEQ),
        P(SEQ, HEAD),
        P(SEQ, HEAD),
        P(SEQ, HEAD),
    )
    return jax.shard_map(
        shards, mesh=torus, in_specs=in_specs, out_specs=out_specs, check_vma=False
    )
```

```python
from functools import partial

import jax
import jax.numpy as jnp
from jax import lax
from jax.experimental import pallas as pl
from jax.experimental.pallas import tpu as pltpu
from jax.sharding import Mesh
from jax.sharding import PartitionSpec as P

DK = 128
DV = 256
CH = 128
EPS_NORM = 1e-06
EPS_GATE = 1e-05
FLOAT = jnp.float32
HALF = jnp.bfloat16
NN = (((1,), (0,)), ((), ()))
NT = (((1,), (1,)), ((), ()))
TN = (((0,), (0,)), ((), ()))


def mm(a, b, dims=NN):
    return lax.dot_general(a.astype(HALF), b.astype(HALF), dims, preferred_element_type=FLOAT)


def halves(a):
    high = a.astype(HALF)
    return high, (a - high.astype(FLOAT)).astype(HALF)


def mm2(a, b, dims=NN):
    high, low = halves(b)
    return mm(a, high, dims) + mm(a, low, dims)


def mm3(a, b, dims=NN):
    a_high, a_low = halves(a)
    b_high, b_low = halves(b)
    return mm(a_high, b_high, dims) + (mm(a_high, b_low, dims) + mm(a_low, b_high, dims))


def sigmoid(v):
    return 1.0 / (1.0 + jnp.exp(-v))


def square_masks():
    rows = lax.broadcasted_iota(jnp.int32, (CH, CH), 0)
    cols = lax.broadcasted_iota(jnp.int32, (CH, CH), 1)
    return rows, cols


def decay_matrix(gcol, grow):
    rows, cols = square_masks()
    return jnp.where(rows >= cols, jnp.exp(jnp.minimum(gcol - grow, 0.0)), 0.0)


def conv_of(wide, taps, start, count, lanes):
    total = wide[HALO - 3 + start : HALO - 3 + start + count, lanes] * taps[0:1, lanes]
    for j in range(1, 4):
        total = total + wide[HALO - 3 + j + start : HALO - 3 + j + start + count, lanes] * taps[j : j + 1, lanes]
    return total


def prepare_kernel(heads, chunks, proj, halo, taps, logits, gcol, grow, q_out, k_out, v_out, t_out, n_out, b_out, w_out, u_out, p_out, pay, wide):
    rows, cols = square_masks()
    differ = rows ^ cols
    eye = jnp.where(rows == cols, 1.0, 0.0)
    wide[:HALO, :] = halo[...].astype(FLOAT)
    wide[HALO:, :] = proj[...].astype(FLOAT)
    kq = heads * DK
    work = [(h, c) for h in range(heads) for c in range(chunks)]
    low, keys, sides = {}, {}, {}
    for h, c in work:
        span = slice(c * CH, (c + 1) * CH)
        ql, kl, vl = (
            slice(h * DK, (h + 1) * DK),
            slice(kq + h * DK, kq + (h + 1) * DK),
            slice(2 * kq + h * DV, 2 * kq + (h + 1) * DV),
        )
        cq = conv_of(wide, taps, c * CH, CH, ql)
        query = (cq * sigmoid(cq)).astype(HALF)
        ck = conv_of(wide, taps, c * CH, CH, kl)
        act = ck * sigmoid(ck)
        key = (act * lax.rsqrt(jnp.sum(act * act, axis=-1, keepdims=True) + EPS_NORM)).astype(HALF)
        cv = conv_of(wide, taps, c * CH, CH, vl)
        value = (cv * sigmoid(cv)).astype(HALF)
        q_out[span, ql] = query
        k_out[span, ql] = key
        v_out[span, h * DV : (h + 1) * DV] = value
        beta = sigmoid(logits[span, h : h + 1])
        g = gcol[span, h : h + 1]
        spread = decay_matrix(g, grow[h * chunks + c : h * chunks + c + 1, :])
        inner = mm(key, key, NT)
        low[h, c] = jnp.where(rows > cols, beta * spread * inner, 0.0)
        p_out[h * chunks + c] = (spread * mm(query, key, NT)).astype(HALF)
        keys[h, c] = key
        sides[h, c] = jnp.concatenate([(beta * jnp.exp(g)) * key.astype(FLOAT), beta * value.astype(FLOAT)], axis=1)
    tri = {at: eye - jnp.where(differ < 2, low[at], 0.0) for at in work}
    size = 2
    while size < CH:
        part = {at: mm3(jnp.where((differ >= size) & (differ < 2 * size), low[at], 0.0), tri[at]) for at in work}
        tri = {at: tri[at] - mm3(tri[at], part[at]) for at in work}
        size *= 2
    steps = {}
    for h, c in work:
        at = h * chunks + c
        t_out[at] = tri[h, c].astype(HALF)
        solved = mm3(tri[h, c], sides[h, c])
        w_out[at] = solved[:, :DK].astype(HALF)
        u_out[at] = solved[:, DK:].astype(HALF)
        g = gcol[c * CH : (c + 1) * CH, h : h + 1]
        last = gcol[(c + 1) * CH - 1 : (c + 1) * CH, h : h + 1]
        step = mm2(keys[h, c], jnp.exp(last - g) * solved, TN)
        n_out[at] = step[:, :DK].astype(HALF)
        b_out[at] = step[:, DK:]
        steps[h, c] = (jnp.exp(last), step)
    zero = jnp.zeros((DK, DK), FLOAT)
    for h in range(heads):
        decay, step = steps[h, 0]
        total = jnp.concatenate([decay * eye - step[:, :DK], step[:, DK:]], axis=1)
        whole = decay
        for c in range(1, chunks):
            decay, step = steps[h, c]
            total = decay * total - mm3(step[:, :DK], total) + jnp.concatenate([zero, step[:, DK:]], axis=1)
            whole = whole * decay
        pack_map(pay, h, total, whole, eye)


def whole_decay(pay, j, h):
    return pay[j, h, DK : DK + 1, 0:1].astype(FLOAT) + pay[j, h, DK + 8 : DK + 9, 0:1].astype(FLOAT)


def apply_whole(pay, j, h, state, dims):
    return whole_decay(pay, j, h) * state + mm(pay[j, h, :DK, :DK], state, dims)


def pack_map(pay, h, total, whole, eye):
    pay[h, :DK, :] = jnp.concatenate([total[:, :DK] - whole * eye, total[:, DK:]], axis=1).astype(HALF)
    rest = jnp.broadcast_to(whole, (8, DK + DV))
    first = rest.astype(HALF).astype(FLOAT)
    pay[h, DK:, :] = jnp.concatenate([first, rest - first], axis=0).astype(HALF)


def group_kernel(heads, mine, p0, p1, p2, p3, before, group, near):
    me = mine[3]
    for k, piece in enumerate((p0, p1, p2, p3)):
        near[ring_place(me, k)] = piece[...]
    rows, cols = square_masks()
    eye = jnp.where(rows == cols, 1.0, 0.0)
    zero = jnp.zeros((DK, DK), FLOAT)
    start = jnp.concatenate([eye, jnp.zeros((DK, DV), FLOAT)], axis=1)
    totals, keeps, wholes = [start] * heads, [start] * heads, [jnp.ones((1, 1), FLOAT)] * heads
    for j in range(near.shape[0]):
        for h in range(heads):
            added = jnp.concatenate([zero, near[j, h, :DK, DK:].astype(FLOAT)], axis=1)
            if j == 0:
                moved = jnp.concatenate([whole_decay(near, j, h) * eye + near[j, h, :DK, :DK].astype(FLOAT), added[:, DK:]], axis=1)
            else:
                moved = apply_whole(near, j, h, totals[h], NN) + added
            totals[h] = moved
            wholes[h] = wholes[h] * whole_decay(near, j, h)
            keeps[h] = jnp.where(me == j + 1, moved, keeps[h])
    for h in range(heads):
        before[h] = keeps[h]
        pack_map(group, h, totals[h], wholes[h], eye)


def group_back_kernel(heads, mine, near, p0, p1, p2, p3, after, group, ends):
    me = mine[3]
    for k, piece in enumerate((p0, p1, p2, p3)):
        ends[ring_place(me, k)] = piece[...]
    rows, cols = square_masks()
    eye = jnp.where(rows == cols, 1.0, 0.0)
    zero = jnp.zeros((DK, DK), FLOAT)
    start = jnp.concatenate([eye, jnp.zeros((DK, DV), FLOAT)], axis=1)
    totals, keeps = [start] * heads, [start] * heads
    for j in reversed(range(near.shape[0])):
        for h in range(heads):
            keeps[h] = jnp.where(me == j, totals[h], keeps[h])
            added = jnp.concatenate([zero, ends[j, h].astype(FLOAT)], axis=1)
            totals[h] = apply_whole(near, j, h, totals[h], TN) + added
    for h in range(heads):
        after[h] = keeps[h]
        group[h] = totals[h][:, DK:].astype(HALF)


def spread_rows(core, total, own, other, rows, lanes):
    for x in range(4):
        mine = pl.ds(pl.multiple_of((2 * x + core) * rows, rows), rows)
        away = pl.ds(pl.multiple_of((2 * x + 1 - core) * rows, rows), rows)
        own[x, :, lanes] = total[mine, :].astype(HALF)
        other[x, :, lanes] = total[away, :].astype(HALF)


def mix_kernel(heads, chunks, mine, p0, p1, p2, p3, before, q, k, w, u, p, n, b, gcol, gate, gain, weight, s_out, vn_out, o_out, gated, other, own, pay, total):
    ranks = pay.shape[0]
    me = mine[2]
    for at, piece in enumerate((p0, p1, p2, p3)):
        pay[ring_place(me, at)] = piece[...]
    states = [jnp.zeros((DK, DV), FLOAT) for h in range(heads)]
    for j in range(ranks - 1):
        passed = j < me
        for h in range(heads):
            moved = apply_whole(pay, j, h, states[h], NN) + pay[j, h, :DK, DK:].astype(FLOAT)
            states[h] = jnp.where(passed, moved, states[h])
    for h in range(heads):
        states[h] = mm3(before[h, :, :DK], states[h]) + before[h, :, DK:]
    for c in range(chunks):
        span = slice(c * CH, (c + 1) * CH)
        for h in range(heads):
            at = h * chunks + c
            state = states[h].astype(HALF)
            s_out[at] = state
            g = gcol[span, h : h + 1]
            last = gcol[(c + 1) * CH - 1 : (c + 1) * CH, h : h + 1]
            vn = (u[at].astype(FLOAT) - mm(w[at], state)).astype(HALF)
            vn_out[at] = vn
            out = jnp.exp(g) * mm(q[span, h * DK : (h + 1) * DK], state) + mm(p[at], vn)
            vl = slice(h * DV, (h + 1) * DV)
            o_out[span, vl] = out
            factor = lax.rsqrt(jnp.mean(out * out, axis=-1, keepdims=True) + EPS_GATE)
            pre = gate[span, vl]
            gated[span, vl] = (out * factor * gain[:, vl] * (pre * sigmoid(pre))).astype(HALF)
            if c + 1 < chunks:
                states[h] = jnp.exp(last) * states[h] - mm(n[at], state) + b[at]
    width = weight.shape[0]
    tile = total.shape[1]
    rows = own.shape[1]
    for at in range(0, width, tile):
        lanes = slice(at, at + tile)
        total[...] = mm(gated[...], weight[lanes, :], NT)
        spread_rows(mine[1], total, own, other, rows, lanes)


def gate_back_kernel(heads, chunks, d_gated, out, gate, gain, q, w, p, n, gcol, do_out, dvn_out, e_out, dpre_out, dgain_out, sums_out, pay):
    dgain = [jnp.zeros((1, DV), FLOAT) for h in range(heads)]
    ends = [None] * heads
    for c in reversed(range(chunks)):
        span = slice(c * CH, (c + 1) * CH)
        for h in range(heads):
            at = h * chunks + c
            vl = slice(h * DV, (h + 1) * DV)
            dg, o, pre, gn = d_gated[span, vl], out[span, vl], gate[span, vl], gain[:, vl]
            sig = sigmoid(pre)
            factor = lax.rsqrt(jnp.mean(o * o, axis=-1, keepdims=True) + EPS_GATE)
            m = o * factor
            s = pre * sig
            dgm = dg * m
            dgain[h] = dgain[h] + jnp.sum(dgm * s, axis=0, keepdims=True)
            dpre = dgm * gn * (sig * (1.0 + pre * (1.0 - sig)))
            dpre_out[span, vl] = dpre.astype(HALF)
            row_sum = jnp.sum(dpre * pre, axis=-1, keepdims=True)
            sums_out[span, :] = row_sum if h == 0 else sums_out[span, :] + row_sum
            e = dg * gn * s
            dout = factor * (e - m * jnp.mean(e * m, axis=-1, keepdims=True))
            do_out[span, vl] = dout.astype(HALF)
            g = gcol[span, h : h + 1]
            last = gcol[(c + 1) * CH - 1 : (c + 1) * CH, h : h + 1]
            dvn = mm(p[at], dout, TN)
            dvn_out[at] = dvn
            source = mm(q[span, h * DK : (h + 1) * DK], jnp.exp(g) * dout, TN) - mm(w[at], dvn, TN)
            e_out[at] = source
            if ends[h] is None:
                ends[h] = source
            else:
                ends[h] = jnp.exp(last) * ends[h] - mm(n[at], ends[h], TN) + source
    for h in range(heads):
        pay[h] = ends[h].astype(HALF)
        dgain_out[0:1, h * DV : (h + 1) * DV] = dgain[h]


def back_kernel(heads, chunks, mine, pay, p0, p1, p2, p3, after, q, k, v, logits, gate_sums, gcol, grow, tri, states, vns, dos, dvns, es, ns, proj, halo, taps, dproj_out, halo_out, dlogit_out, logit_rows, dtaps_out, sums_out, wide, dconv, late, rowsum):
    ranks = pay.shape[0]
    tokens = chunks * CH
    me = mine[2]
    for at, piece in enumerate((p0, p1, p2, p3)):
        late[ring_place(me, at)] = piece[...]
    kq = heads * DK
    width = 2 * kq + heads * DV
    rows, cols = square_masks()
    grads = [jnp.zeros((DK, DV), FLOAT) for h in range(heads)]
    for j in reversed(range(1, ranks)):
        passed = j > me
        for h in range(heads):
            moved = apply_whole(pay, j, h, grads[h], TN) + late[j, h].astype(FLOAT)
            grads[h] = jnp.where(passed, moved, grads[h])
    for h in range(heads):
        grads[h] = mm3(after[h, :, :DK], grads[h]) + after[h, :, DK:]
    wide[:HALO, :] = halo[...].astype(FLOAT)
    wide[HALO:, :] = proj[...].astype(FLOAT)
    logit_rows[...] = jnp.zeros(logit_rows.shape, FLOAT)
    dconv[0:HALO, :] = jnp.zeros((HALO, width), FLOAT)
    dconv[HALO + tokens :, :] = jnp.zeros((8, width), FLOAT)
    for c in reversed(range(chunks)):
        span = slice(c * CH, (c + 1) * CH)
        for h in range(heads):
            at = h * chunks + c
            ql, kl, vl, ol = (
                slice(h * DK, (h + 1) * DK),
                slice(kq + h * DK, kq + (h + 1) * DK),
                slice(2 * kq + h * DV, 2 * kq + (h + 1) * DV),
                slice(h * DV, (h + 1) * DV),
            )
            grad = grads[h].astype(HALF)
            query, key, value = q[span, ql], k[span, ql], v[span, ol]
            state, vn, dout = states[at], vns[at], dos[span, ol]
            logit = logits[span, h : h + 1]
            beta = sigmoid(logit)
            g = gcol[span, h : h + 1]
            last = gcol[(c + 1) * CH - 1 : (c + 1) * CH, h : h + 1]
            eg, ed = jnp.exp(g), jnp.exp(last - g)
            spread = decay_matrix(g, grow[at : at + 1, :])
            strict = jnp.where(rows > cols, spread, 0.0)
            inner = mm(key, key, NT)
            dvn = dvns[at] + ed * mm(key, grad)
            dr = mm(tri[at], dvn, TN)
            drh = dr.astype(HALF)
            ks = mm(key, state)
            dval = beta * dr
            both = mm(jnp.concatenate([dout, drh], axis=0), state, NT)
            dkeep = mm(vn, grad, NT)
            pair = mm(jnp.concatenate([dout, drh], axis=0), vn, NT)
            dqk = spread * pair[:CH]
            da = -(strict * pair[CH:])
            dkk = beta * da
            dbeta = jnp.sum(dr * (value.astype(FLOAT) - eg * ks), axis=-1, keepdims=True) + jnp.sum(
                da * inner, axis=-1, keepdims=True
            )
            dqkh = dqk.astype(HALF)
            dkkh = dkk.astype(HALF)
            dquery = eg * both[:CH] + mm(dqkh, key)
            dkey = (
                ed * dkeep
                - (beta * eg) * both[CH:]
                + mm(dqkh, query, TN)
                + mm(dkkh, key)
                + mm(dkkh, key, TN)
            )
            if c > 0:
                grads[h] = jnp.exp(last) * grads[h] - mm(ns[at], grad, TN) + es[at]
            dlogit = dbeta * beta * (1.0 - beta)
            dlogit_out[span, h : h + 1] = dlogit
            logit_rows[h : h + 1, HALO + c * CH : HALO + (c + 1) * CH] = jnp.broadcast_to(dlogit, (CH, DK)).T[0:1]
            extra_sum = dlogit * logit
            sums_out[span, :] = (gate_sums[span, :] if h == 0 else sums_out[span, :]) + extra_sum
            there = slice(HALO + c * CH, HALO + (c + 1) * CH)
            cq = conv_of(wide, taps, c * CH, CH, ql)
            sig = sigmoid(cq)
            dconv[there, ql] = dquery * (sig * (1.0 + cq * (1.0 - sig)))
            cv = conv_of(wide, taps, c * CH, CH, vl)
            sig = sigmoid(cv)
            dconv[there, vl] = dval * (sig * (1.0 + cv * (1.0 - sig)))
            ck = conv_of(wide, taps, c * CH, CH, kl)
            sig = sigmoid(ck)
            act = ck * sig
            unit = lax.rsqrt(jnp.sum(act * act, axis=-1, keepdims=True) + EPS_NORM)
            u = act * unit
            dact = unit * (dkey - u * jnp.sum(dkey * u, axis=-1, keepdims=True))
            dconv[there, kl] = dact * (sig * (1.0 + ck * (1.0 - sig)))
    dtaps_out[4:8, :] = jnp.zeros((4, width), FLOAT)
    rowsum[...] = jnp.zeros((HALO + tokens, 1), FLOAT)
    for at in range(0, width, DK):
        lanes = slice(at, at + DK)
        for j in range(4):
            dtaps_out[j : j + 1, lanes] = jnp.sum(
                dconv[HALO : HALO + tokens, lanes] * wide[HALO - 3 + j : HALO - 3 + j + tokens, lanes], axis=0, keepdims=True
            )
        total = dconv[3 : 3 + HALO + tokens, lanes] * taps[0:1, lanes]
        for j in range(1, 4):
            total = total + dconv[3 - j : 3 - j + HALO + tokens, lanes] * taps[j : j + 1, lanes]
        halo_out[:, lanes] = total[0:HALO]
        small = total.astype(HALF)
        dproj_out[:, lanes] = small
        rowsum[...] += jnp.sum(small.astype(FLOAT) * wide[:, lanes], axis=-1, keepdims=True)
    sums_out[...] += rowsum[HALO:, :]


def out(shape, dtype):
    return jax.ShapeDtypeStruct(shape, dtype)


def cost(micros):
    return pl.CostEstimate(flops=int(micros * 1.1e9), bytes_accessed=0, transcendentals=0)


def run(kernel, shapes, args, scratch=(), scalars=0, after=(), micros=1.0, megs=12, kept=()):
    vmem = pl.BlockSpec(memory_space=pltpu.VMEM)
    smem = pl.BlockSpec(memory_space=pltpu.SMEM)
    count = len(args)

    def body(*refs):
        kernel(*refs[:count], *refs[count + len(after) :])

    return pl.pallas_call(
        body,
        out_shape=tuple(pltpu.HBM(a.shape, a.dtype) if i in kept else a for i, a in enumerate(shapes)),
        in_specs=[smem] * scalars + [vmem] * (count - scalars) + [pl.BlockSpec(memory_space=pl.ANY)] * len(after),
        out_specs=[pl.BlockSpec() if i in kept else vmem for i in range(len(shapes))],
        scratch_shapes=list(scratch),
        compiler_params=pltpu.CompilerParams(vmem_limit_bytes=megs * 2**20),
        cost_estimate=cost(micros),
    )(*args, *after)


def prepare_shapes(heads, chunks):
    tokens, pairs = chunks * CH, heads * chunks
    return (
        out((tokens, heads * DK), HALF),
        out((tokens, heads * DK), HALF),
        out((tokens, heads * DV), HALF),
        out((pairs, CH, CH), HALF),
        out((pairs, DK, DK), HALF),
        out((pairs, DK, DV), FLOAT),
        out((pairs, CH, DK), HALF),
        out((pairs, CH, DV), HALF),
        out((pairs, CH, CH), HALF),
        out((heads, DK + 16, DK + DV), HALF),
    )


def mix_shapes(heads, chunks):
    tokens, pairs = chunks * CH, heads * chunks
    return (
        out((pairs, DK, DV), HALF),
        out((pairs, CH, DV), HALF),
        out((tokens, heads * DV), FLOAT),
        out((tokens, heads * DV), HALF),
        out((4, heads, DK + 16, DK + DV), HALF),
    )


def gate_back_shapes(heads, chunks):
    tokens, pairs = chunks * CH, heads * chunks
    return (
        out((tokens, heads * DV), HALF),
        out((pairs, CH, DV), FLOAT),
        out((pairs, DK, DV), FLOAT),
        out((tokens, heads * DV), HALF),
        out((1, heads * DV), FLOAT),
        out((tokens, 1), FLOAT),
        out((heads, DK, DV), HALF),
    )


def back_shapes(heads, chunks):
    tokens = chunks * CH
    width = heads * (2 * DK + DV)
    return (
        out((HALO + tokens, width), HALF),
        out((HALO, width), FLOAT),
        out((tokens, heads), FLOAT),
        out((HALO, HALO + tokens), FLOAT),
        out((8, width), FLOAT),
        out((tokens, 1), FLOAT),
    )


def back_scratch(heads, chunks):
    tokens = chunks * CH
    width = heads * (2 * DK + DV)
    return (pltpu.VMEM((HALO + tokens, width), FLOAT), pltpu.VMEM((HALO + tokens + 8, width), FLOAT), pltpu.VMEM((4, heads, DK, DV), HALF), pltpu.VMEM((HALO + tokens, 1), FLOAT))


def group_shapes(heads):
    pay = (heads, DK + 16, DK + DV)
    return (out((heads, DK, DK + DV), FLOAT), out(pay, HALF), out((4, *pay), HALF))


def group_back_shapes(heads):
    return (
        out((heads, DK, DK + DV), FLOAT),
        out((heads, DK, DV), HALF),
        out((4, heads, DK, DV), HALF),
    )


HEAD = ("x", "c")
SEQ = ("y", "z")
PLANE = ("y", "z", "c")
HALO = 16
EXTRA = 48
TURNS = (0, 1, -1, 2)


def rotated(array, axis, distance):
    size = lax.axis_size(axis)
    return lax.ppermute(array, axis, [(i, (i + distance) % size) for i in range(size)])


def ring_pieces(array, axis):
    return [array] + [rotated(array, axis, -d) for d in TURNS[1:]]


def join_kernel(mine, *refs):
    for k in range(4):
        refs[4][ring_place(mine[0], k)] = refs[k][...]
    refs[5][...] = jnp.zeros(refs[5].shape, FLOAT)


def head_gather(array, mine, after=(), with_token=False):
    shapes = (out((4, *array.shape), array.dtype), out((8, DK), FLOAT))
    own, token = run(join_kernel, shapes, (mine, *ring_pieces(array, "x")), scalars=1, after=after)
    tiles = (own, rotated(own, "c", 1))
    return (*tiles, token) if with_token else tiles


def head_tiles(mine, own, other):
    core = mine[1]
    return [(2 * x + which, ref, x) for which, ref in ((core, own), (1 - core, other)) for x in range(4)]


def turned(array, first, distance):
    pairs = []
    for y in range(4):
        for z in range(4):
            for core in range(2):
                along_z = (core == 0) == first
                to = (y, (z + distance) % 4) if along_z else ((y + distance) % 4, z)
                pairs.append(((y * 4 + z) * 2 + core, (to[0] * 4 + to[1]) * 2 + core))
    return lax.ppermute(array, PLANE, pairs)


def ring_place(mine, k):
    return lax.rem(mine + TURNS[k] + 4, 4)


def lane_block(at, width):
    return pl.ds(pl.multiple_of(at * width, width), width)


def setup_kernel(query, key, value, gate, decay, in_out, gate_out, gcol, grow, token):
    at = 0
    for weight in (query, key, value):
        count = weight.shape[1]
        in_out[at : at + count, :] = weight[...].T
        at += count
    gate_out[...] = gate[...].T
    rows, cols = square_masks()
    heads, tokens = decay.shape
    chunks = tokens // CH
    for h in range(heads):
        for c in range(chunks):
            span = slice(c * CH, (c + 1) * CH)
            flat = jnp.broadcast_to(decay[h : h + 1, span], (CH, CH))
            grow[h * chunks + c : h * chunks + c + 1, :] = jnp.sum(
                jnp.where(rows <= cols, flat.T, 0.0), axis=0, keepdims=True
            )
            gcol[span, h : h + 1] = jnp.sum(jnp.where(cols <= rows, flat, 0.0), axis=1, keepdims=True)
    token[...] = jnp.zeros(token.shape, FLOAT)


def first_norm_kernel(mine, gain, beta_rows, cot, own, other, normed, factor, rows_out, logits, cot_out, halo_out):
    width = own.shape[2]
    rows = rows_out.shape[0]
    own_rows = lane_block(mine[0] * 2 + mine[1], rows)
    square = 0.0
    for _, ref, x in head_tiles(mine, own, other):
        wide = ref[x].astype(FLOAT)
        square = square + jnp.sum(wide * wide, axis=-1, keepdims=True)
    scale = lax.rsqrt(square / (8 * width) + EPS_NORM)
    factor[...] = scale
    total = 0.0
    for head, ref, x in head_tiles(mine, own, other):
        lanes = lane_block(head, width)
        small = (ref[x].astype(FLOAT) * scale * gain[:, lanes]).astype(HALF)
        normed[:, lanes] = small
        total = total + mm(small, beta_rows[:, lanes], NT)
        rows_out[:, lanes] = ref[x, own_rows, :].astype(FLOAT)
    logits[...] = total
    cot_out[...] = cot[...]
    halo_out[...] = normed[normed.shape[0] - HALO :, :]


def product_grad_kernel(mine, own, other, weight, whole, rows_out, grad, token):
    width = own.shape[2]
    rows = rows_out.shape[0]
    own_rows = lane_block(mine[0] * 2 + mine[1], rows)
    for head, ref, x in head_tiles(mine, own, other):
        lanes = lane_block(head, width)
        whole[:, lanes] = ref[x]
        rows_out[:, lanes] = ref[x, own_rows, :]
    grad[...] = mm(weight[...], whole[...], NT)
    token[...] = jnp.zeros(token.shape, FLOAT)


def hidden_kernel(rows_in, gain, first, second, third, fourth, hidden, unit, factor, normed):
    total = rows_in[...] + first[...] + second[...].astype(FLOAT) + third[...].astype(FLOAT) + fourth[...].astype(FLOAT)
    hidden[...] = total
    scale = lax.rsqrt(jnp.mean(total * total, axis=-1, keepdims=True) + EPS_NORM)
    factor[...] = scale
    unit[...] = total * scale
    normed[...] = (total * scale * gain[...]).astype(HALF)


def second_back_kernel(unit, factor, gain, cot_rows, first, second, third, fourth, d_hidden, gain_part):
    total = first[...] + second[...].astype(FLOAT) + third[...].astype(FLOAT) + fourth[...].astype(FLOAT)
    n = unit[...]
    gain_part[...] = jnp.sum(total * n, axis=0, keepdims=True)
    e = total * gain[...]
    mean = jnp.mean(e * n, axis=-1, keepdims=True)
    d_hidden[...] = (cot_rows[...].astype(FLOAT) + factor[...] * (e - n * mean)).astype(HALF)


def ffn_kernel(mine, own_in, other_in, gate_rows, up_rows, d_product, normed, product, d_gate, d_up, other, own, total):
    rows = own_in.shape[1]
    for head, ref, x in head_tiles(mine, own_in, other_in):
        normed[lane_block(head, rows), :] = ref[x]
    cols = gate_rows.shape[0]
    step = cols // 4
    for at in range(0, cols, step):
        span = slice(at, at + step)
        gate = mm(gate_rows[span, :], normed[...], NT)
        up = mm(up_rows[span, :], normed[...], NT)
        sig = sigmoid(gate)
        act = gate * sig
        product[span, :] = (act * up).astype(HALF)
        grad = d_product[span, :]
        dg = (grad * up * (sig * (1.0 + gate * (1.0 - sig)))).astype(HALF)
        du = (grad * act).astype(HALF)
        d_gate[span, :] = dg
        d_up[span, :] = du
    gate_turned = d_gate[...].T
    up_turned = d_up[...].T
    width = normed.shape[1]
    tile = width // 4
    core = mine[1]
    for at in range(0, width, tile):
        lanes = slice(at, at + tile)
        total[...] = mm(gate_turned, gate_rows[:, lanes]) + mm(up_turned, up_rows[:, lanes])
        spread_rows(core, total, own, other, rows, lanes)


def join_rows_kernel(mine, own, other, whole, own_cols):
    rows = own.shape[1]
    lanes = lane_block(mine[0] * 2 + mine[1], own_cols.shape[1])
    for head, ref, x in head_tiles(mine, own, other):
        whole[lane_block(head, rows), :] = ref[x]
        own_cols[lane_block(head, rows), :] = ref[x, :, lanes]


def split_sum_kernel(mine, own, arrived, *outs):
    for k in range(4):
        at = ring_place(mine[0], k)
        outs[k][...] = (own[at].astype(FLOAT) + arrived[at].astype(FLOAT)).astype(outs[k].dtype)
    outs[4][...] = jnp.zeros(outs[4].shape, FLOAT)


def head_scatter(own, other, mine, with_token=False):
    arrived = rotated(other, "c", 1)
    shape = own.shape[1:]
    shapes = (out(shape, FLOAT),) + (out(shape, HALF),) * 3 + (out((8, DK), FLOAT),)
    total, *sent, token = run(split_sum_kernel, shapes, (mine, own, arrived), scalars=1)
    parts = [total] + [rotated(part, "x", d) for d, part in zip(TURNS[1:], sent)]
    return (parts, token) if with_token else parts


def added(parts):
    total = parts[0]
    for part in parts[1:]:
        total = total + part.astype(FLOAT)
    return total


def dest_block(mine, k, o):
    core = mine[1]
    place = ring_place(jnp.where(core == 0, mine[3], mine[2]), k)
    return jnp.where(core == 0, o * 4 + place, place * 4 + o)


def mixer_grad_kernel(mine, d_branch, gated, normed, d_pre, gate_rows, *refs):
    outs, (gain_out, gated_turned, pre_turned) = refs[:4], refs[4:]
    gated_turned[...] = gated[...].T
    pre_turned[...] = d_pre[...].T
    cols = gated.shape[1]
    for k in range(4):
        for o in (0, 2):
            blocks = [lane_block(dest_block(mine, k, o + i), DK) for i in range(2)]
            mixer = mm(gated_turned[...], jnp.concatenate([d_branch[:, at] for at in blocks], axis=1))
            gate = mm(pre_turned[...], jnp.concatenate([normed[:, at] for at in blocks], axis=1))
            for i, at in enumerate(blocks):
                half = slice(i * DK, (i + 1) * DK)
                outs[k][o + i, :cols, :] = mixer[:, half].astype(HALF)
                outs[k][o + i, cols:, :] = gate[:, half].astype(HALF)
                gain_out[:, at] = jnp.sum(gate[:, half] * gate_rows[:, at].astype(FLOAT), axis=0, keepdims=True)


def in_grad_kernel(mine, normed, halo, dproj, d_logit, taps, mixer_gain, gate_gain, second_gain, first_gain, in_rows, beta_rows, *refs):
    outs, (token, turned_refs, extra) = refs[:4], refs[4:]
    token[...] = jnp.zeros(token.shape, FLOAT)
    cols = dproj.shape[1]
    heads = 2
    turned_refs[:cols, :] = dproj[...].T
    turned_refs[cols:, :] = d_logit[...].astype(HALF)
    extra[...] = jnp.zeros(extra.shape, FLOAT)
    per_tap = cols // DK
    for j in range(4):
        for i in range(per_tap):
            extra[j * per_tap + i : j * per_tap + i + 1, :] = taps[j : j + 1, i * DK : (i + 1) * DK]
    for i in range(mixer_gain.shape[1] // DK):
        extra[32 + i : 33 + i, :] = mixer_gain[:, i * DK : (i + 1) * DK]
    for k in range(4):
        for o in (0, 2):
            blocks = [lane_block(dest_block(mine, k, o + i), DK) for i in range(2)]
            left = jnp.concatenate(
                [jnp.concatenate([halo[:, at], normed[:, at]], axis=0) for at in blocks], axis=1
            )
            grads = mm(turned_refs[...], left)
            for i, at in enumerate(blocks):
                half = slice(i * DK, (i + 1) * DK)
                outs[k][o + i, :cols, :] = grads[:cols, half].astype(HALF)
                beta = grads[cols : cols + heads, half]
                gain = (
                    jnp.sum(grads[:cols, half] * in_rows[:, at].astype(FLOAT), axis=0, keepdims=True)
                    + jnp.sum(beta * beta_rows[:heads, at].astype(FLOAT), axis=0, keepdims=True)
                    + gate_gain[:, at]
                )
                extra[36 : 36 + heads, :] = beta
                extra[38:39, :] = gain / first_gain[:, at]
                extra[39:40, :] = second_gain[:, at]
                outs[k][o + i, cols:, :] = extra[...].astype(HALF)


def seq_sum_kernel(mine, *refs):
    rank = jnp.where(mine[1] == 0, mine[2], mine[3])
    parts, before, outs = refs[:4], refs[4:-4], refs[-4:]
    count = parts[0].shape[1]
    for k in range(4):
        place = ring_place(rank, k)
        total = parts[0][place].astype(FLOAT)
        for j in range(1, 4):
            total = total + parts[j][place].astype(FLOAT)
        at = outs[k].shape[0] - count
        if before:
            outs[k][:at, :] = before[k][...]
        outs[k][at:, :] = total.astype(outs[k].dtype)


def seq_sums(parts, before, mine, after):
    arrived = [parts[0]] + [turned(parts[i], True, TURNS[i]) for i in range(1, 4)]
    count = parts[0].shape[1] + (before[0].shape[0] if before else 0)
    shapes = (out((count, DK), FLOAT),) + (out((count, DK), HALF),) * 3
    return run(seq_sum_kernel, shapes, (mine, *arrived, *before), scalars=1, after=after, micros=2.0)


def unpack_kernel(own, first, second, third, mixer, gate, query, key, value, extra):
    total = own[...] + first[...].astype(FLOAT) + second[...].astype(FLOAT) + third[...].astype(FLOAT)
    at = 0
    for target in (mixer, gate, query, key, value):
        count = target.shape[1]
        target[...] = total[at : at + count, :].T
        at += count
    extra[...] = total[at:, :]


def ffn_grad_kernel(cot, normed, d_gate, d_up, product, after, grads, token):
    for k, (left, right) in enumerate(((normed, d_gate), (normed, d_up), (cot, product))):
        both = mm(right[...], left[...]).astype(HALF)
        grads[0, k] = both[:, :DK]
        grads[1, k] = both[:, DK:]
    token[...] = jnp.zeros(token.shape, FLOAT)


def ffn_grads(cot, normed, d_gate, d_up, product, after):
    tokens, width = cot.shape
    cols = d_gate.shape[0]
    left = pl.BlockSpec((tokens, 2 * DK), lambda i: (0, i))
    right = pl.BlockSpec((cols, tokens), lambda i: (0, 0))
    return pl.pallas_call(
        ffn_grad_kernel,
        grid=(width // (2 * DK),),
        out_shape=(pltpu.HBM((width // DK, 3, cols, DK), HALF), out((8, DK), FLOAT)),
        in_specs=[left, left, right, right, right, pl.BlockSpec(memory_space=pl.ANY)],
        out_specs=[
            pl.BlockSpec((2, 3, cols, DK), lambda i: (i, 0, 0, 0)),
            pl.BlockSpec((8, DK), lambda i: (0, 0)),
        ],
        compiler_params=pltpu.CompilerParams(vmem_limit_bytes=16 * 2**20),
        cost_estimate=cost(9.0),
    )(cot, normed, d_gate, d_up, product, after)


def tile_of(i, mine):
    return (i % 4) * 2 + jnp.where(i < 4, 1 - mine[1], mine[1])


def whole_block(shape):
    return pl.BlockSpec(shape, lambda i, mine: (0,) * len(shape))


def tile_outs(rows, width):
    return [
        pl.BlockSpec((1, rows, width), lambda i, mine: (jnp.minimum(i, 3), 0, 0)),
        pl.BlockSpec((1, rows, width), lambda i, mine: (jnp.maximum(i - 4, 0), 0, 0)),
    ]


def down_kernel(mine, product, weight, hidden, other, own, token, scratch):
    step = pl.program_id(0)
    rows = hidden.shape[0]

    @pl.when(step == 0)
    def _():
        scratch[...] = product[...].T

    part = mm(scratch[...], weight[...])
    here = lane_block(mine[0] * 2 + mine[1], rows)
    for target, wanted in ((other, step < 4), (own, step >= 4)):

        @pl.when(wanted)
        def _():
            target[0] = part.astype(HALF)
            target[0, here, :] = (target[0, here, :].astype(FLOAT) + hidden[...]).astype(HALF)

    token[...] = jnp.zeros(token.shape, FLOAT)


def down_tiles(mine, product, weight, hidden):
    cols, tokens = product.shape
    width = weight.shape[1] // 8
    spec = pltpu.PrefetchScalarGridSpec(
        num_scalar_prefetch=1,
        grid=(8,),
        in_specs=[
            whole_block(product.shape),
            pl.BlockSpec((cols, width), lambda i, mine: (0, tile_of(i, mine))),
            pl.BlockSpec((hidden.shape[0], width), lambda i, mine: (0, tile_of(i, mine))),
        ],
        out_specs=tile_outs(tokens, width) + [whole_block((8, DK))],
        scratch_shapes=[pltpu.VMEM((tokens, cols), HALF)],
    )
    tiles = out((4, tokens, width), HALF)
    return pl.pallas_call(
        down_kernel,
        grid_spec=spec,
        out_shape=(tiles, tiles, out((8, DK), FLOAT)),
        compiler_params=pltpu.CompilerParams(vmem_limit_bytes=16 * 2**20),
        cost_estimate=cost(4.0),
    )(mine, product, weight, hidden)


def d_first_kernel(mine, dproj, arrived, proj, d_pre, d_logit, sums, in_rows, gate_rows, beta_rows, after, other, own, scratch, sum_rows):
    step = pl.program_id(0)
    tokens = d_pre.shape[0]
    width = own.shape[2]

    @pl.when(step == 0)
    def _():
        scratch[: tokens - HALO, :] = dproj[HALO:tokens, :]
        last = dproj[tokens:, :].astype(FLOAT) + arrived[...]
        scratch[tokens - HALO :, :] = last.astype(HALF)
        late = jnp.sum(arrived[...] * proj[tokens - HALO :, :].astype(FLOAT), axis=-1, keepdims=True)
        column = jnp.concatenate([sums[: tokens - HALO, :], sums[tokens - HALO :, :] + late], axis=0)
        row = jnp.broadcast_to(column, (tokens, DK)).T
        sum_rows[...] = jnp.zeros(sum_rows.shape, FLOAT)
        for i in range(tokens // width):
            sum_rows[i : i + 1, :] = row[0:1, i * width : (i + 1) * width]

    part = mm(scratch[...], in_rows[...]) + mm(d_pre[...], gate_rows[...])
    for h in range(2):
        part = part + d_logit[:, h : h + 1] * beta_rows[h : h + 1, :].astype(FLOAT)
    for target, wanted in ((other, step < 4), (own, step >= 4)):

        @pl.when(wanted)
        def _():
            target[0, :tokens, :] = part.astype(HALF)
            target[0, tokens:, :] = sum_rows[...].astype(HALF)


def d_first_tiles(mine, dproj, arrived, proj, d_pre, d_logit, sums, in_rows, gate_rows, beta_rows, after):
    tokens = d_pre.shape[0]
    width = in_rows.shape[1] // 8

    def tile(rows):
        return pl.BlockSpec((rows, width), lambda i, mine: (0, tile_of(i, mine)))

    spec = pltpu.PrefetchScalarGridSpec(
        num_scalar_prefetch=1,
        grid=(8,),
        in_specs=[whole_block(a.shape) for a in (dproj, arrived, proj, d_pre, d_logit, sums)]
        + [tile(in_rows.shape[0]), tile(gate_rows.shape[0]), tile(beta_rows.shape[0])]
        + [pl.BlockSpec(memory_space=pl.ANY)],
        out_specs=tile_outs(tokens + HALO, width),
        scratch_shapes=[pltpu.VMEM((tokens, dproj.shape[1]), HALF), pltpu.VMEM((HALO, width), FLOAT)],
    )
    tiles = out((4, tokens + HALO, width), HALF)
    return pl.pallas_call(
        d_first_kernel,
        grid_spec=spec,
        out_shape=(tiles, tiles),
        compiler_params=pltpu.CompilerParams(vmem_limit_bytes=16 * 2**20),
        cost_estimate=cost(6.0),
    )(mine, dproj, arrived, proj, d_pre, d_logit, sums, in_rows, gate_rows, beta_rows, after)


def input_grad_kernel(mine, own, first, second, third, block_input, factor, gain, d_branch, grad):
    total = own[...] + first[...].astype(FLOAT) + second[...].astype(FLOAT) + third[...].astype(FLOAT)
    tokens, width = block_input.shape
    columns = []
    for i in range(tokens // width):
        row = total[tokens + i : tokens + i + 1, :]
        columns.append(jnp.broadcast_to(row, (DK, width)).T[:, 0:1])
    mean = jnp.concatenate(columns, axis=0) / (8 * width)
    scale = factor[...]
    unit = block_input[...].astype(FLOAT) * scale
    grad[...] = d_branch[...].astype(FLOAT) + scale * (total[:tokens, :] * gain[:, lane_block(mine[0] * 2 + mine[1], width)] - unit * mean)


def next_block(array, distance):
    size = 16
    route = [(i, i + distance) for i in range(size) if 0 <= i + distance < size]
    return lax.ppermute(array, SEQ, route)


def dot_nt(a, b):
    return lax.dot_general(a, b, NT, preferred_element_type=FLOAT)


def shards(
    block_input,
    log_decay,
    first_gain,
    query_weight,
    key_weight,
    value_weight,
    gate_weight,
    beta_weight,
    query_conv,
    key_conv,
    value_conv,
    mixer_gain,
    mixer_weight,
    second_gain,
    swiglu_gate,
    swiglu_up,
    swiglu_down,
    cotangent,
):
    heads = log_decay.shape[1]
    tokens, width = block_input.shape
    model = 8 * width
    chunks = tokens // CH
    rows = tokens // 8
    kq, vd = heads * DK, heads * DV
    cols = 2 * kq + vd
    hidden_cols = swiglu_gate.shape[1]
    mine = jnp.stack([lax.axis_index(name) for name in ("x", "c", "y", "z")]).astype(jnp.int32)

    token_out = out((8, DK), FLOAT)
    in_rows, gate_rows, gcol, grow, token = run(
        setup_kernel,
        (
            out((cols, model), HALF),
            out((vd, model), HALF),
            out((tokens, heads), FLOAT),
            out((heads * chunks, CH), FLOAT),
            token_out,
        ),
        (query_weight, key_weight, value_weight, gate_weight, log_decay.T),
        micros=3.0,
    )
    beta_rows = jnp.pad(beta_weight.T, ((0, HALO - heads), (0, 0)))
    taps = jnp.concatenate([query_conv.T, key_conv.T, value_conv.T], axis=1)
    gain_row = mixer_gain.reshape(1, -1)
    first_row = first_gain.reshape(1, -1)

    first_normed, first_factor, my_rows, logits, cot, halo_rows = run(
        first_norm_kernel,
        (
            out((tokens, model), HALF),
            out((tokens, 1), FLOAT),
            out((rows, model), FLOAT),
            out((tokens, HALO), FLOAT),
            out((tokens, width), HALF),
            out((HALO, model), HALF),
        ),
        (mine, first_row, beta_rows, cotangent, *head_gather(block_input, mine, (token,))),
        scalars=1,
        micros=3.0,
    )
    halo_normed = next_block(halo_rows, 1)
    proj = dot_nt(first_normed, in_rows).astype(HALF)
    halo_proj = dot_nt(halo_normed, in_rows).astype(HALF)
    gate_pre = dot_nt(first_normed, gate_rows)
    q, k, v, tri, n, b, w, u, p, pay = run(
        partial(prepare_kernel, heads, chunks),
        prepare_shapes(heads, chunks),
        (proj, halo_proj, taps, logits, gcol, grow),
        [pltpu.VMEM((HALO + tokens, cols), FLOAT)],
        micros=8.0,
        kept=range(9),
        megs=20,
    )
    near_pieces = ring_pieces(pay, "z")
    *cot_tiles, cot_token = head_gather(cot, mine, with_token=True)
    whole_cot, cot_rows, d_product, token = run(
        product_grad_kernel,
        (out((tokens, model), HALF), out((rows, model), HALF), out((hidden_cols, tokens), FLOAT), token_out),
        (mine, *cot_tiles, swiglu_down.T),
        scalars=1,
        micros=4.0,
    )
    before, group, near = run(
        partial(group_kernel, heads), group_shapes(heads), (mine, *near_pieces), scalars=1, after=(gate_pre[:8, :DK], cot_token), micros=2.0
    )
    half_tiles = out((4, rows, model), HALF)
    states, vns, mixed, gated, branch_other, branch_own, far = run(
        partial(mix_kernel, heads, chunks),
        mix_shapes(heads, chunks)[:4] + (half_tiles, half_tiles) + mix_shapes(heads, chunks)[4:],
        (mine, *ring_pieces(group, "y"), before, q, k, w, u, p, n, b, gcol, gate_pre, gain_row, mixer_weight),
        [pltpu.VMEM((tokens, model // 4), FLOAT)],
        scalars=1,
        after=(token,),
        kept=(0, 1, 2, 6),
        megs=16,
        micros=4.0,
    )
    branch = head_scatter(branch_own, branch_other, mine)
    wide_rows = out((rows, model), FLOAT)
    second_row = second_gain.reshape(1, -1)
    hidden, second_unit, second_factor, own_normed = run(
        hidden_kernel,
        (wide_rows, wide_rows, out((rows, 1), FLOAT), out((rows, model), HALF)),
        (my_rows, second_row, *branch),
    )
    turned_out = out((hidden_cols, tokens), HALF)
    second_normed, product, d_gate, d_up, second_other, second_own = run(
        ffn_kernel,
        (out((tokens, model), HALF), turned_out, turned_out, turned_out, half_tiles, half_tiles),
        (
            mine,
            *head_gather(own_normed, mine),
            swiglu_gate.T,
            swiglu_up.T,
            d_product,
        ),
        [pltpu.VMEM((tokens, model // 4), FLOAT)],
        scalars=1,
        micros=9.0,
        megs=20,
    )
    second_parts, second_token = head_scatter(second_own, second_other, mine, True)
    ffn_parts, token = ffn_grads(whole_cot, second_normed, d_gate, d_up, product, second_token)
    ffn_sum = lax.psum_scatter(ffn_parts, SEQ, scatter_dimension=0, tiled=True)[0].astype(FLOAT)
    d_hidden, second_gain_part = run(
        second_back_kernel,
        (out((rows, model), HALF), out((1, model), FLOAT)),
        (second_unit, second_factor, second_row, cot_rows, *second_parts),
        after=(token,),
    )
    down_other, down_own, down_token = down_tiles(mine, product, swiglu_down.T, hidden)
    d_branch, d_branch_own = run(
        join_rows_kernel,
        (out((tokens, model), HALF), out((tokens, width), HALF)),
        (mine, *head_gather(d_hidden, mine, (down_token,))),
        scalars=1,
    )
    d_gated = jnp.dot(d_branch, mixer_weight, preferred_element_type=FLOAT)
    dos, dvns, es, d_gate_pre, gain_part, gate_sums, ends = run(
        partial(gate_back_kernel, heads, chunks),
        gate_back_shapes(heads, chunks),
        (d_gated, mixed, gate_pre, gain_row, q, w, p, n, gcol),
        micros=4.0,
    )
    tile = out((4, 2 * vd, DK), HALF)
    *mixer_parts, gate_gain = run(
        mixer_grad_kernel,
        (tile,) * 4 + (out((1, model), FLOAT),),
        (mine, d_branch, gated, first_normed, d_gate_pre, gate_rows),
        [pltpu.VMEM((vd, tokens), HALF), pltpu.VMEM((vd, tokens), HALF)],
        scalars=1,
        micros=5.0,
    )
    after, group_end, _ = run(
        partial(group_back_kernel, heads),
        group_back_shapes(heads),
        (mine, near, *ring_pieces(ends, "z")),
        scalars=1,
        after=(gate_gain,),
        micros=2.0,
    )
    output = added(head_scatter(down_own, down_other, mine)).astype(HALF)
    dproj, halo_grad, d_logit, logit_rows, taps_part, sums = run(
        partial(back_kernel, heads, chunks),
        back_shapes(heads, chunks),
        (mine, far, *ring_pieces(group_end, "y"), after, q, k, v, logits, gate_sums, gcol, grow, tri, states, vns, dos, dvns, es, n, proj, halo_proj, taps),
        back_scratch(heads, chunks),
        scalars=1,
        after=(output,),
        micros=11.0,
        megs=30,
    )
    tile = out((4, cols + EXTRA, DK), HALF)
    *in_parts, in_token = run(
        in_grad_kernel,
        (tile,) * 4 + (token_out,),
        (mine, first_normed, halo_normed, dproj, logit_rows, taps_part, gain_part, gate_gain, second_gain_part, first_row, in_rows, beta_rows),
        [pltpu.VMEM((cols + HALO, HALO + tokens), HALF), pltpu.VMEM((EXTRA, DK), FLOAT)],
        scalars=1,
        micros=6.0,
        megs=16,
    )
    mixer_sums = seq_sums(mixer_parts, (), mine, ())
    arrived = next_block(halo_grad, -1)
    first_other, first_own = d_first_tiles(
        mine, dproj, arrived, proj, d_gate_pre, d_logit, sums, in_rows, gate_rows, beta_rows, in_token
    )
    first_parts, first_token = head_scatter(first_own, first_other, mine, True)

    sums_out = seq_sums(in_parts, mixer_sums, mine, (first_token,))
    totals = [sums_out[0]] + [turned(sums_out[i], False, TURNS[i]) for i in range(1, 4)]
    grad_mixer_weight, grad_gate_weight, grad_query, grad_key, grad_value, extra = run(
        unpack_kernel,
        tuple(out((DK, count), FLOAT) for count in (vd, vd, kq, kq, vd)) + (out((EXTRA, DK), FLOAT),),
        totals,
    )
    grad_input = run(
        input_grad_kernel,
        (out((tokens, width), FLOAT),),
        (mine, *first_parts, block_input, first_factor, first_row, d_branch_own),
        scalars=1,
    )[0]
    taps_grad = extra[: 4 * cols // DK].reshape(4, cols)
    grad_mixer_gain = extra[32:36].reshape(-1)
    grad_beta = extra[36 : 36 + heads].T
    gains = lax.all_to_all(jnp.broadcast_to(extra[None, 38:40], (8, 2, DK)), HEAD, 0, 0, tiled=True).sum(axis=0)
    return (
        output,
        grad_input,
        gains[0],
        grad_query,
        grad_key,
        grad_value,
        grad_gate_weight,
        grad_beta,
        taps_grad[:, :kq].T,
        taps_grad[:, kq : 2 * kq].T,
        taps_grad[:, 2 * kq :].T,
        grad_mixer_gain,
        grad_mixer_weight,
        gains[1],
        ffn_sum[0].T,
        ffn_sum[1].T,
        ffn_sum[2].T,
    )


def solution(mesh):
    torus = Mesh(mesh.devices.reshape(4, 4, 4, 2), SEQ + HEAD)
    in_specs = (
        P(SEQ, HEAD),
        P(SEQ, HEAD),
        P(),
        P(None, HEAD),
        P(None, HEAD),
        P(None, HEAD),
        P(None, HEAD),
        P(None, HEAD),
        P(HEAD, None),
        P(HEAD, None),
        P(HEAD, None),
        P(HEAD),
        P(None, HEAD),
        P(),
        P(None, HEAD),
        P(None, HEAD),
        P(None, HEAD),
        P(SEQ, HEAD),
    )
    out_specs = (
        P(SEQ, HEAD),
        P(SEQ, HEAD),
        P(SEQ),
        P(SEQ, HEAD),
        P(SEQ, HEAD),
        P(SEQ, HEAD),
        P(SEQ, HEAD),
        P(SEQ, HEAD),
        P(HEAD, None),
        P(HEAD, None),
        P(HEAD, None),
        P(HEAD),
        P(SEQ, HEAD),
        P(SEQ),
        P(SEQ, HEAD),
        P(SEQ, HEAD),
        P(SEQ, HEAD),
    )
    return jax.shard_map(
        shards, mesh=torus, in_specs=in_specs, out_specs=out_specs, check_vma=False
    )
```

```python
from functools import partial

import jax
import jax.numpy as jnp
from jax import lax
from jax.experimental import pallas as pl
from jax.experimental.pallas import tpu as pltpu
from jax.sharding import Mesh
from jax.sharding import PartitionSpec as P

DK = 128
DV = 256
CH = 128
EPS_NORM = 1e-06
EPS_GATE = 1e-05
FLOAT = jnp.float32
HALF = jnp.bfloat16
NN = (((1,), (0,)), ((), ()))
NT = (((1,), (1,)), ((), ()))
TN = (((0,), (0,)), ((), ()))


def mm(a, b, dims=NN):
    return lax.dot_general(a.astype(HALF), b.astype(HALF), dims, preferred_element_type=FLOAT)


def halves(a):
    high = a.astype(HALF)
    return high, (a - high.astype(FLOAT)).astype(HALF)


def mm2(a, b, dims=NN):
    high, low = halves(b)
    return mm(a, high, dims) + mm(a, low, dims)


def mm3(a, b, dims=NN):
    a_high, a_low = halves(a)
    b_high, b_low = halves(b)
    return mm(a_high, b_high, dims) + (mm(a_high, b_low, dims) + mm(a_low, b_high, dims))


def sigmoid(v):
    return 1.0 / (1.0 + jnp.exp(-v))


def square_masks():
    rows = lax.broadcasted_iota(jnp.int32, (CH, CH), 0)
    cols = lax.broadcasted_iota(jnp.int32, (CH, CH), 1)
    return rows, cols


def decay_matrix(gcol, grow):
    rows, cols = square_masks()
    return jnp.where(rows >= cols, jnp.exp(jnp.minimum(gcol - grow, 0.0)), 0.0)


def conv_of(wide, taps, start, count, lanes):
    total = wide[HALO - 3 + start : HALO - 3 + start + count, lanes] * taps[0:1, lanes]
    for j in range(1, 4):
        total = total + wide[HALO - 3 + j + start : HALO - 3 + j + start + count, lanes] * taps[j : j + 1, lanes]
    return total


def prepare_kernel(heads, chunks, proj, halo, taps, logits, gcol, grow, q_out, k_out, v_out, t_out, n_out, b_out, w_out, u_out, p_out, pay, token, wide):
    token[...] = jnp.zeros(token.shape, FLOAT)
    rows, cols = square_masks()
    differ = rows ^ cols
    eye = jnp.where(rows == cols, 1.0, 0.0)
    wide[:HALO, :] = halo[...].astype(FLOAT)
    wide[HALO:, :] = proj[...].astype(FLOAT)
    kq = heads * DK
    work = [(h, c) for h in range(heads) for c in range(chunks)]
    low, keys, sides = {}, {}, {}
    for h, c in work:
        span = slice(c * CH, (c + 1) * CH)
        ql, kl, vl = (
            slice(h * DK, (h + 1) * DK),
            slice(kq + h * DK, kq + (h + 1) * DK),
            slice(2 * kq + h * DV, 2 * kq + (h + 1) * DV),
        )
        cq = conv_of(wide, taps, c * CH, CH, ql)
        query = (cq * sigmoid(cq)).astype(HALF)
        ck = conv_of(wide, taps, c * CH, CH, kl)
        act = ck * sigmoid(ck)
        key = (act * lax.rsqrt(jnp.sum(act * act, axis=-1, keepdims=True) + EPS_NORM)).astype(HALF)
        cv = conv_of(wide, taps, c * CH, CH, vl)
        value = (cv * sigmoid(cv)).astype(HALF)
        q_out[span, ql] = query
        k_out[span, ql] = key
        v_out[span, h * DV : (h + 1) * DV] = value
        beta = sigmoid(logits[span, h : h + 1])
        g = gcol[span, h : h + 1]
        spread = decay_matrix(g, grow[h * chunks + c : h * chunks + c + 1, :])
        inner = mm(key, key, NT)
        low[h, c] = jnp.where(rows > cols, beta * spread * inner, 0.0)
        p_out[h * chunks + c] = (spread * mm(query, key, NT)).astype(HALF)
        keys[h, c] = key
        sides[h, c] = jnp.concatenate([(beta * jnp.exp(g)) * key.astype(FLOAT), beta * value.astype(FLOAT)], axis=1)
    tri = {at: eye - jnp.where(differ < 2, low[at], 0.0) for at in work}
    size = 2
    while size < CH:
        part = {at: mm3(jnp.where((differ >= size) & (differ < 2 * size), low[at], 0.0), tri[at]) for at in work}
        tri = {at: tri[at] - mm3(tri[at], part[at]) for at in work}
        size *= 2
    steps = {}
    for h, c in work:
        at = h * chunks + c
        t_out[at] = tri[h, c].astype(HALF)
        solved = mm3(tri[h, c], sides[h, c])
        w_out[at] = solved[:, :DK].astype(HALF)
        u_out[at] = solved[:, DK:].astype(HALF)
        g = gcol[c * CH : (c + 1) * CH, h : h + 1]
        last = gcol[(c + 1) * CH - 1 : (c + 1) * CH, h : h + 1]
        step = mm2(keys[h, c], jnp.exp(last - g) * solved, TN)
        n_out[at] = step[:, :DK].astype(HALF)
        b_out[at] = step[:, DK:]
        steps[h, c] = (jnp.exp(last), step)
    zero = jnp.zeros((DK, DK), FLOAT)
    for h in range(heads):
        decay, step = steps[h, 0]
        total = jnp.concatenate([decay * eye - step[:, :DK], step[:, DK:]], axis=1)
        whole = decay
        for c in range(1, chunks):
            decay, step = steps[h, c]
            total = decay * total - mm3(step[:, :DK], total) + jnp.concatenate([zero, step[:, DK:]], axis=1)
            whole = whole * decay
        pack_map(pay, h, total, whole, eye)


def whole_decay(pay, j, h):
    return pay[j, h, DK : DK + 1, 0:1].astype(FLOAT) + pay[j, h, DK + 8 : DK + 9, 0:1].astype(FLOAT)


def apply_whole(pay, j, h, state, dims):
    return whole_decay(pay, j, h) * state + mm(pay[j, h, :DK, :DK], state, dims)


def pack_map(pay, h, total, whole, eye):
    pay[h, :DK, :] = jnp.concatenate([total[:, :DK] - whole * eye, total[:, DK:]], axis=1).astype(HALF)
    rest = jnp.broadcast_to(whole, (8, DK + DV))
    first = rest.astype(HALF).astype(FLOAT)
    pay[h, DK:, :] = jnp.concatenate([first, rest - first], axis=0).astype(HALF)


def group_kernel(heads, mine, p0, p1, p2, p3, before, group, near):
    me = mine[3]
    for k, piece in enumerate((p0, p1, p2, p3)):
        near[ring_place(me, k)] = piece[...]
    rows, cols = square_masks()
    eye = jnp.where(rows == cols, 1.0, 0.0)
    zero = jnp.zeros((DK, DK), FLOAT)
    start = jnp.concatenate([eye, jnp.zeros((DK, DV), FLOAT)], axis=1)
    totals, keeps, wholes = [start] * heads, [start] * heads, [jnp.ones((1, 1), FLOAT)] * heads
    for j in range(near.shape[0]):
        for h in range(heads):
            added = jnp.concatenate([zero, near[j, h, :DK, DK:].astype(FLOAT)], axis=1)
            if j == 0:
                moved = jnp.concatenate([whole_decay(near, j, h) * eye + near[j, h, :DK, :DK].astype(FLOAT), added[:, DK:]], axis=1)
            else:
                moved = apply_whole(near, j, h, totals[h], NN) + added
            totals[h] = moved
            wholes[h] = wholes[h] * whole_decay(near, j, h)
            keeps[h] = jnp.where(me == j + 1, moved, keeps[h])
    for h in range(heads):
        before[h] = keeps[h]
        pack_map(group, h, totals[h], wholes[h], eye)


def group_back_kernel(heads, mine, near, p0, p1, p2, p3, after, group, ends, token):
    token[...] = jnp.zeros(token.shape, FLOAT)
    me = mine[3]
    for k, piece in enumerate((p0, p1, p2, p3)):
        ends[ring_place(me, k)] = piece[...]
    rows, cols = square_masks()
    eye = jnp.where(rows == cols, 1.0, 0.0)
    zero = jnp.zeros((DK, DK), FLOAT)
    start = jnp.concatenate([eye, jnp.zeros((DK, DV), FLOAT)], axis=1)
    totals, keeps = [start] * heads, [start] * heads
    for j in reversed(range(near.shape[0])):
        for h in range(heads):
            keeps[h] = jnp.where(me == j, totals[h], keeps[h])
            added = jnp.concatenate([zero, ends[j, h].astype(FLOAT)], axis=1)
            totals[h] = apply_whole(near, j, h, totals[h], TN) + added
    for h in range(heads):
        after[h] = keeps[h]
        group[h] = totals[h][:, DK:].astype(HALF)


def spread_rows(core, total, own, other, rows, lanes):
    for x in range(4):
        mine = pl.ds(pl.multiple_of((2 * x + core) * rows, rows), rows)
        away = pl.ds(pl.multiple_of((2 * x + 1 - core) * rows, rows), rows)
        own[x, :, lanes] = total[mine, :].astype(HALF)
        other[x, :, lanes] = total[away, :].astype(HALF)


def mix_kernel(heads, chunks, mine, p0, p1, p2, p3, before, q, k, w, u, p, n, b, gcol, gate, gain, weight, s_out, vn_out, o_out, gated, other, own, pay, total):
    ranks = pay.shape[0]
    me = mine[2]
    for at, piece in enumerate((p0, p1, p2, p3)):
        pay[ring_place(me, at)] = piece[...]
    states = [jnp.zeros((DK, DV), FLOAT) for h in range(heads)]
    for j in range(ranks - 1):
        passed = j < me
        for h in range(heads):
            moved = apply_whole(pay, j, h, states[h], NN) + pay[j, h, :DK, DK:].astype(FLOAT)
            states[h] = jnp.where(passed, moved, states[h])
    for h in range(heads):
        states[h] = mm3(before[h, :, :DK], states[h]) + before[h, :, DK:]
    for c in range(chunks):
        span = slice(c * CH, (c + 1) * CH)
        for h in range(heads):
            at = h * chunks + c
            state = states[h].astype(HALF)
            s_out[at] = state
            g = gcol[span, h : h + 1]
            last = gcol[(c + 1) * CH - 1 : (c + 1) * CH, h : h + 1]
            vn = (u[at].astype(FLOAT) - mm(w[at], state)).astype(HALF)
            vn_out[at] = vn
            out = jnp.exp(g) * mm(q[span, h * DK : (h + 1) * DK], state) + mm(p[at], vn)
            vl = slice(h * DV, (h + 1) * DV)
            o_out[span, vl] = out
            factor = lax.rsqrt(jnp.mean(out * out, axis=-1, keepdims=True) + EPS_GATE)
            pre = gate[span, vl]
            gated[span, vl] = (out * factor * gain[:, vl] * (pre * sigmoid(pre))).astype(HALF)
            if c + 1 < chunks:
                states[h] = jnp.exp(last) * states[h] - mm(n[at], state) + b[at]
    width = weight.shape[0]
    tile = total.shape[1]
    rows = own.shape[1]
    for at in range(0, width, tile):
        lanes = slice(at, at + tile)
        total[...] = mm(gated[...], weight[lanes, :], NT)
        spread_rows(mine[1], total, own, other, rows, lanes)


def gate_back_kernel(heads, chunks, d_gated, out, gate, gain, q, w, p, n, gcol, do_out, dvn_out, e_out, dpre_out, dgain_out, sums_out, pay):
    dgain = [jnp.zeros((1, DV), FLOAT) for h in range(heads)]
    ends = [None] * heads
    for c in reversed(range(chunks)):
        span = slice(c * CH, (c + 1) * CH)
        for h in range(heads):
            at = h * chunks + c
            vl = slice(h * DV, (h + 1) * DV)
            dg, o, pre, gn = d_gated[span, vl], out[span, vl], gate[span, vl], gain[:, vl]
            sig = sigmoid(pre)
            factor = lax.rsqrt(jnp.mean(o * o, axis=-1, keepdims=True) + EPS_GATE)
            m = o * factor
            s = pre * sig
            dgm = dg * m
            dgain[h] = dgain[h] + jnp.sum(dgm * s, axis=0, keepdims=True)
            dpre = dgm * gn * (sig * (1.0 + pre * (1.0 - sig)))
            dpre_out[span, vl] = dpre.astype(HALF)
            row_sum = jnp.sum(dpre * pre, axis=-1, keepdims=True)
            sums_out[span, :] = row_sum if h == 0 else sums_out[span, :] + row_sum
            e = dg * gn * s
            dout = factor * (e - m * jnp.mean(e * m, axis=-1, keepdims=True))
            do_out[span, vl] = dout.astype(HALF)
            g = gcol[span, h : h + 1]
            last = gcol[(c + 1) * CH - 1 : (c + 1) * CH, h : h + 1]
            dvn = mm(p[at], dout, TN)
            dvn_out[at] = dvn
            source = mm(q[span, h * DK : (h + 1) * DK], jnp.exp(g) * dout, TN) - mm(w[at], dvn, TN)
            e_out[at] = source
            if ends[h] is None:
                ends[h] = source
            else:
                ends[h] = jnp.exp(last) * ends[h] - mm(n[at], ends[h], TN) + source
    for h in range(heads):
        pay[h] = ends[h].astype(HALF)
        dgain_out[0:1, h * DV : (h + 1) * DV] = dgain[h]


def back_kernel(heads, chunks, mine, pay, p0, p1, p2, p3, after, q, k, v, logits, gate_sums, gcol, grow, tri, states, vns, dos, dvns, es, ns, proj, halo, taps, dproj_out, dlogit_out, logit_rows, dtaps_out, sums_out, wide, dconv, late, rowsum):
    ranks = pay.shape[0]
    tokens = chunks * CH
    me = mine[2]
    for at, piece in enumerate((p0, p1, p2, p3)):
        late[ring_place(me, at)] = piece[...]
    kq = heads * DK
    width = 2 * kq + heads * DV
    rows, cols = square_masks()
    grads = [jnp.zeros((DK, DV), FLOAT) for h in range(heads)]
    for j in reversed(range(1, ranks)):
        passed = j > me
        for h in range(heads):
            moved = apply_whole(pay, j, h, grads[h], TN) + late[j, h].astype(FLOAT)
            grads[h] = jnp.where(passed, moved, grads[h])
    for h in range(heads):
        grads[h] = mm3(after[h, :, :DK], grads[h]) + after[h, :, DK:]
    wide[:HALO, :] = halo[...].astype(FLOAT)
    wide[HALO:, :] = proj[...].astype(FLOAT)
    logit_rows[...] = jnp.zeros(logit_rows.shape, FLOAT)
    dconv[0:HALO, :] = jnp.zeros((HALO, width), FLOAT)
    dconv[HALO + tokens :, :] = jnp.zeros((8, width), FLOAT)
    for c in reversed(range(chunks)):
        span = slice(c * CH, (c + 1) * CH)
        for h in range(heads):
            at = h * chunks + c
            ql, kl, vl, ol = (
                slice(h * DK, (h + 1) * DK),
                slice(kq + h * DK, kq + (h + 1) * DK),
                slice(2 * kq + h * DV, 2 * kq + (h + 1) * DV),
                slice(h * DV, (h + 1) * DV),
            )
            grad = grads[h].astype(HALF)
            query, key, value = q[span, ql], k[span, ql], v[span, ol]
            state, vn, dout = states[at], vns[at], dos[span, ol]
            logit = logits[span, h : h + 1]
            beta = sigmoid(logit)
            g = gcol[span, h : h + 1]
            last = gcol[(c + 1) * CH - 1 : (c + 1) * CH, h : h + 1]
            eg, ed = jnp.exp(g), jnp.exp(last - g)
            spread = decay_matrix(g, grow[at : at + 1, :])
            strict = jnp.where(rows > cols, spread, 0.0)
            inner = mm(key, key, NT)
            dvn = dvns[at] + ed * mm(key, grad)
            dr = mm(tri[at], dvn, TN)
            drh = dr.astype(HALF)
            ks = mm(key, state)
            dval = beta * dr
            both = mm(jnp.concatenate([dout, drh], axis=0), state, NT)
            dkeep = mm(vn, grad, NT)
            pair = mm(jnp.concatenate([dout, drh], axis=0), vn, NT)
            dqk = spread * pair[:CH]
            da = -(strict * pair[CH:])
            dkk = beta * da
            dbeta = jnp.sum(dr * (value.astype(FLOAT) - eg * ks), axis=-1, keepdims=True) + jnp.sum(
                da * inner, axis=-1, keepdims=True
            )
            dqkh = dqk.astype(HALF)
            dkkh = dkk.astype(HALF)
            dquery = eg * both[:CH] + mm(dqkh, key)
            dkey = (
                ed * dkeep
                - (beta * eg) * both[CH:]
                + mm(dqkh, query, TN)
                + mm(dkkh, key)
                + mm(dkkh, key, TN)
            )
            if c > 0:
                grads[h] = jnp.exp(last) * grads[h] - mm(ns[at], grad, TN) + es[at]
            dlogit = dbeta * beta * (1.0 - beta)
            dlogit_out[span, h : h + 1] = dlogit
            logit_rows[h : h + 1, HALO + c * CH : HALO + (c + 1) * CH] = jnp.broadcast_to(dlogit, (CH, DK)).T[0:1]
            extra_sum = dlogit * logit
            far_span = slice(HALO + c * CH, HALO + (c + 1) * CH)
            sums_out[far_span, :] = (gate_sums[span, :] if h == 0 else sums_out[far_span, :]) + extra_sum
            there = slice(HALO + c * CH, HALO + (c + 1) * CH)
            cq = conv_of(wide, taps, c * CH, CH, ql)
            sig = sigmoid(cq)
            dconv[there, ql] = dquery * (sig * (1.0 + cq * (1.0 - sig)))
            cv = conv_of(wide, taps, c * CH, CH, vl)
            sig = sigmoid(cv)
            dconv[there, vl] = dval * (sig * (1.0 + cv * (1.0 - sig)))
            ck = conv_of(wide, taps, c * CH, CH, kl)
            sig = sigmoid(ck)
            act = ck * sig
            unit = lax.rsqrt(jnp.sum(act * act, axis=-1, keepdims=True) + EPS_NORM)
            u = act * unit
            dact = unit * (dkey - u * jnp.sum(dkey * u, axis=-1, keepdims=True))
            dconv[there, kl] = dact * (sig * (1.0 + ck * (1.0 - sig)))
    dtaps_out[4:8, :] = jnp.zeros((4, width), FLOAT)
    rowsum[...] = jnp.zeros((HALO + tokens, 1), FLOAT)
    for at in range(0, width, DK):
        lanes = slice(at, at + DK)
        for j in range(4):
            dtaps_out[j : j + 1, lanes] = jnp.sum(
                dconv[HALO : HALO + tokens, lanes] * wide[HALO - 3 + j : HALO - 3 + j + tokens, lanes], axis=0, keepdims=True
            )
        total = dconv[3 : 3 + HALO + tokens, lanes] * taps[0:1, lanes]
        for j in range(1, 4):
            total = total + dconv[3 - j : 3 - j + HALO + tokens, lanes] * taps[j : j + 1, lanes]
        small = total.astype(HALF)
        dproj_out[:, lanes] = small
        rowsum[...] += jnp.sum(small.astype(FLOAT) * wide[:, lanes], axis=-1, keepdims=True)
    sums_out[HALO:, :] += rowsum[HALO:, :]
    sums_out[:HALO, :] = rowsum[:HALO, :]


def out(shape, dtype):
    return jax.ShapeDtypeStruct(shape, dtype)


def cost(micros):
    return pl.CostEstimate(flops=int(micros * 1.1e7), bytes_accessed=0, transcendentals=0)


def run(kernel, shapes, args, scratch=(), scalars=0, after=(), micros=1.0, megs=12, kept=()):
    vmem = pl.BlockSpec(memory_space=pltpu.VMEM)
    smem = pl.BlockSpec(memory_space=pltpu.SMEM)
    count = len(args)

    def body(*refs):
        kernel(*refs[:count], *refs[count + len(after) :])

    return pl.pallas_call(
        body,
        out_shape=tuple(pltpu.HBM(a.shape, a.dtype) if i in kept else a for i, a in enumerate(shapes)),
        in_specs=[smem] * scalars + [vmem] * (count - scalars) + [pl.BlockSpec(memory_space=pl.ANY)] * len(after),
        out_specs=[pl.BlockSpec() if i in kept else vmem for i in range(len(shapes))],
        scratch_shapes=list(scratch),
        compiler_params=pltpu.CompilerParams(vmem_limit_bytes=megs * 2**20),
        cost_estimate=cost(micros),
    )(*args, *after)


def passed(arrays, after):
    count = len(arrays)
    anywhere = pl.BlockSpec(memory_space=pl.ANY)

    def body(*refs):
        token = refs[-1]
        token[...] = jnp.zeros(token.shape, FLOAT)

    *same, token = pl.pallas_call(
        body,
        out_shape=tuple(out(a.shape, a.dtype) for a in arrays) + (out((8, DK), FLOAT),),
        in_specs=[anywhere] * (count + len(after)),
        out_specs=[anywhere] * count + [pl.BlockSpec(memory_space=pltpu.VMEM)],
        input_output_aliases={i: i for i in range(count)},
        compiler_params=pltpu.CompilerParams(vmem_limit_bytes=2**20),
        cost_estimate=cost(0.1),
    )(*arrays, *after)
    return same, token


def prepare_shapes(heads, chunks):
    tokens, pairs = chunks * CH, heads * chunks
    return (
        out((tokens, heads * DK), HALF),
        out((tokens, heads * DK), HALF),
        out((tokens, heads * DV), HALF),
        out((pairs, CH, CH), HALF),
        out((pairs, DK, DK), HALF),
        out((pairs, DK, DV), FLOAT),
        out((pairs, CH, DK), HALF),
        out((pairs, CH, DV), HALF),
        out((pairs, CH, CH), HALF),
        out((heads, DK + 16, DK + DV), HALF),
    )


def mix_shapes(heads, chunks):
    tokens, pairs = chunks * CH, heads * chunks
    return (
        out((pairs, DK, DV), HALF),
        out((pairs, CH, DV), HALF),
        out((tokens, heads * DV), FLOAT),
        out((tokens, heads * DV), HALF),
        out((4, heads, DK + 16, DK + DV), HALF),
    )


def gate_back_shapes(heads, chunks):
    tokens, pairs = chunks * CH, heads * chunks
    return (
        out((tokens, heads * DV), HALF),
        out((pairs, CH, DV), FLOAT),
        out((pairs, DK, DV), FLOAT),
        out((tokens, heads * DV), HALF),
        out((1, heads * DV), FLOAT),
        out((tokens, 1), FLOAT),
        out((heads, DK, DV), HALF),
    )


def back_shapes(heads, chunks):
    tokens = chunks * CH
    width = heads * (2 * DK + DV)
    return (
        out((HALO + tokens, width), HALF),
        out((tokens, heads), FLOAT),
        out((HALO, HALO + tokens), FLOAT),
        out((8, width), FLOAT),
        out((HALO + tokens, 1), FLOAT),
    )


def back_scratch(heads, chunks):
    tokens = chunks * CH
    width = heads * (2 * DK + DV)
    return (pltpu.VMEM((HALO + tokens, width), FLOAT), pltpu.VMEM((HALO + tokens + 8, width), FLOAT), pltpu.VMEM((4, heads, DK, DV), HALF), pltpu.VMEM((HALO + tokens, 1), FLOAT))


def group_shapes(heads):
    pay = (heads, DK + 16, DK + DV)
    return (out((heads, DK, DK + DV), FLOAT), out(pay, HALF), out((4, *pay), HALF))


def group_back_shapes(heads):
    return (
        out((heads, DK, DK + DV), FLOAT),
        out((heads, DK, DV), HALF),
        out((4, heads, DK, DV), HALF),
    )


HEAD = ("x", "c")
SEQ = ("y", "z")
PLANE = ("y", "z", "c")
HALO = 16
EXTRA = 64
TURNS = (0, 1, -1, 2)


def rotated(array, axis, distance):
    size = lax.axis_size(axis)
    return lax.ppermute(array, axis, [(i, (i + distance) % size) for i in range(size)])


def ring_pieces(array, axis):
    return [array] + [rotated(array, axis, -d) for d in TURNS[1:]]


def join_kernel(mine, *refs):
    for k in range(4):
        refs[4][ring_place(mine[0], k)] = refs[k][...]


def head_gather(array, mine, after=()):
    shapes = (out((4, *array.shape), array.dtype),)
    own = run(join_kernel, shapes, (mine, *ring_pieces(array, "x")), scalars=1, after=after)[0]
    return own, rotated(own, "c", 1)


def head_tiles(mine, own, other):
    core = mine[1]
    return [(2 * x + which, ref, x) for which, ref in ((core, own), (1 - core, other)) for x in range(4)]


def turned(array, first, distance):
    pairs = []
    for y in range(4):
        for z in range(4):
            for core in range(2):
                along_z = (core == 0) == first
                to = (y, (z + distance) % 4) if along_z else ((y + distance) % 4, z)
                pairs.append(((y * 4 + z) * 2 + core, (to[0] * 4 + to[1]) * 2 + core))
    return lax.ppermute(array, PLANE, pairs)


def ring_place(mine, k):
    return lax.rem(mine + TURNS[k] + 4, 4)


def lane_block(at, width):
    return pl.ds(pl.multiple_of(at * width, width), width)


def setup_kernel(query, key, value, gate, decay, in_out, gate_out, gcol, grow, token):
    at = 0
    for weight in (query, key, value):
        count = weight.shape[1]
        in_out[at : at + count, :] = weight[...].T
        at += count
    gate_out[...] = gate[...].T
    rows, cols = square_masks()
    heads, tokens = decay.shape
    chunks = tokens // CH
    for h in range(heads):
        for c in range(chunks):
            span = slice(c * CH, (c + 1) * CH)
            flat = jnp.broadcast_to(decay[h : h + 1, span], (CH, CH))
            grow[h * chunks + c : h * chunks + c + 1, :] = jnp.sum(
                jnp.where(rows <= cols, flat.T, 0.0), axis=0, keepdims=True
            )
            gcol[span, h : h + 1] = jnp.sum(jnp.where(cols <= rows, flat, 0.0), axis=1, keepdims=True)
    token[...] = jnp.zeros(token.shape, FLOAT)


def first_norm_kernel(mine, gain, beta_rows, cot, own, other, normed, factor, rows_out, logits, cot_out, halo_out):
    width = own.shape[2]
    rows = rows_out.shape[0]
    own_rows = lane_block(mine[0] * 2 + mine[1], rows)
    square = 0.0
    for _, ref, x in head_tiles(mine, own, other):
        wide = ref[x].astype(FLOAT)
        square = square + jnp.sum(wide * wide, axis=-1, keepdims=True)
    scale = lax.rsqrt(square / (8 * width) + EPS_NORM)
    factor[...] = scale
    total = 0.0
    for head, ref, x in head_tiles(mine, own, other):
        lanes = lane_block(head, width)
        small = (ref[x].astype(FLOAT) * scale * gain[:, lanes]).astype(HALF)
        normed[:, lanes] = small
        total = total + mm(small, beta_rows[:, lanes], NT)
        rows_out[:, lanes] = ref[x, own_rows, :].astype(FLOAT)
    logits[...] = total
    cot_out[...] = cot[...]
    halo_out[...] = normed[normed.shape[0] - HALO :, :]


def product_grad_kernel(mine, own, other, weight, whole, rows_out, grad, token):
    width = own.shape[2]
    rows = rows_out.shape[0]
    own_rows = lane_block(mine[0] * 2 + mine[1], rows)
    for head, ref, x in head_tiles(mine, own, other):
        lanes = lane_block(head, width)
        whole[:, lanes] = ref[x]
        rows_out[:, lanes] = ref[x, own_rows, :]
    grad[...] = mm(weight[...], whole[...], NT)
    token[...] = jnp.zeros(token.shape, FLOAT)


def hidden_kernel(rows_in, gain, first, second, third, fourth, hidden, unit, factor, normed):
    total = rows_in[...] + first[...] + second[...].astype(FLOAT) + third[...].astype(FLOAT) + fourth[...].astype(FLOAT)
    hidden[...] = total
    scale = lax.rsqrt(jnp.mean(total * total, axis=-1, keepdims=True) + EPS_NORM)
    factor[...] = scale
    unit[...] = total * scale
    normed[...] = (total * scale * gain[...]).astype(HALF)


def second_back_kernel(unit, factor, gain, cot_rows, first, second, third, fourth, d_hidden, gain_part, token):
    token[...] = jnp.zeros(token.shape, FLOAT)
    total = first[...] + second[...].astype(FLOAT) + third[...].astype(FLOAT) + fourth[...].astype(FLOAT)
    n = unit[...]
    gain_part[...] = jnp.sum(total * n, axis=0, keepdims=True)
    e = total * gain[...]
    mean = jnp.mean(e * n, axis=-1, keepdims=True)
    d_hidden[...] = (cot_rows[...].astype(FLOAT) + factor[...] * (e - n * mean)).astype(HALF)


def ffn_kernel(mine, own_in, other_in, gate_rows, up_rows, d_product, normed, product, d_gate, d_up, other, own, token, total):
    rows = own_in.shape[1]
    for head, ref, x in head_tiles(mine, own_in, other_in):
        normed[lane_block(head, rows), :] = ref[x]
    cols = gate_rows.shape[0]
    step = cols // 2
    for at in range(0, cols, step):
        span = slice(at, at + step)
        gate = mm(gate_rows[span, :], normed[...], NT)
        up = mm(up_rows[span, :], normed[...], NT)
        sig = sigmoid(gate)
        act = gate * sig
        product[span, :] = (act * up).astype(HALF)
        grad = d_product[span, :]
        dg = (grad * up * (sig * (1.0 + gate * (1.0 - sig)))).astype(HALF)
        du = (grad * act).astype(HALF)
        d_gate[span, :] = dg
        d_up[span, :] = du
    token[...] = jnp.zeros(token.shape, FLOAT)
    gate_turned = d_gate[...].T
    up_turned = d_up[...].T
    width = normed.shape[1]
    tile = width // 4
    core = mine[1]
    for at in range(0, width, tile):
        lanes = slice(at, at + tile)
        total[...] = mm(gate_turned, gate_rows[:, lanes]) + mm(up_turned, up_rows[:, lanes])
        spread_rows(core, total, own, other, rows, lanes)


def join_rows_kernel(mine, own, other, whole, own_cols):
    rows = own.shape[1]
    lanes = lane_block(mine[0] * 2 + mine[1], own_cols.shape[1])
    for head, ref, x in head_tiles(mine, own, other):
        whole[lane_block(head, rows), :] = ref[x]
        own_cols[lane_block(head, rows), :] = ref[x, :, lanes]


def split_sum_kernel(mine, own, arrived, *outs):
    for k in range(4):
        at = ring_place(mine[0], k)
        outs[k][...] = (own[at].astype(FLOAT) + arrived[at].astype(FLOAT)).astype(outs[k].dtype)
    outs[4][...] = jnp.zeros(outs[4].shape, FLOAT)


def tile_sum_kernel(own, arrived, total):
    total[...] = (own[...].astype(FLOAT) + arrived[...].astype(FLOAT)).astype(HALF)


def head_scatter(own, other, mine, with_token=False, after=()):
    arrived = rotated(other, "c", 1)
    shape = own.shape[1:]
    shapes = (out(shape, FLOAT),) + (out(shape, HALF),) * 3 + (out((8, DK), FLOAT),)
    total, *sent, token = run(split_sum_kernel, shapes, (mine, own, arrived), scalars=1, after=after)
    parts = [total] + [rotated(part, "x", d) for d, part in zip(TURNS[1:], sent)]
    return (parts, token) if with_token else parts


def added(parts):
    total = parts[0]
    for part in parts[1:]:
        total = total + part.astype(FLOAT)
    return total


def dest_block(mine, k, o):
    core = mine[1]
    place = ring_place(jnp.where(core == 0, mine[3], mine[2]), k)
    return jnp.where(core == 0, o * 4 + place, place * 4 + o)


def store_tile(outs, k, o, early, value):
    count = early.shape[0]
    if k < 3:
        outs[k][o, :count, :] = early
        outs[k][o, count:, :] = value
    else:
        spare = outs[3].shape[1] - count
        outs[3][o, :count, :] = early
        outs[3][o, count:, :] = value[:spare]
        outs[4][o] = value[spare:]


def mixer_grad_kernel(mine, d_branch, gated, normed, d_pre, gate_rows, *refs):
    outs, (gain_out, gated_turned, pre_turned) = refs[:4], refs[4:]
    gated_turned[...] = gated[...].T
    pre_turned[...] = d_pre[...].T
    for k in range(4):
        for o in (0, 2):
            blocks = [lane_block(dest_block(mine, k, o + i), DK) for i in range(2)]
            mixer = mm(gated_turned[...], jnp.concatenate([d_branch[:, at] for at in blocks], axis=1))
            gate = mm(pre_turned[...], jnp.concatenate([normed[:, at] for at in blocks], axis=1))
            for i, at in enumerate(blocks):
                half = slice(i * DK, (i + 1) * DK)
                outs[k][o + i] = jnp.concatenate([mixer[:, half], gate[:, half]], axis=0).astype(HALF)
                gain_out[:, at] = jnp.sum(gate[:, half] * gate_rows[:, at].astype(FLOAT), axis=0, keepdims=True)


def in_grad_kernel(mine, normed, halo, dproj, d_logit, taps, mixer_gain, gate_gain, second_gain, first_gain, in_rows, beta_rows, *refs):
    early, outs, (token, turned_refs, extra) = refs[:4], refs[4:9], refs[9:]
    token[...] = jnp.zeros(token.shape, FLOAT)
    cols = dproj.shape[1]
    heads = 2
    turned_refs[:cols, :] = dproj[...].T
    turned_refs[cols:, :] = d_logit[...].astype(HALF)
    extra[...] = jnp.zeros(extra.shape, FLOAT)
    per_tap = cols // DK
    for j in range(4):
        for i in range(per_tap):
            extra[j * per_tap + i : j * per_tap + i + 1, :] = taps[j : j + 1, i * DK : (i + 1) * DK]
    for i in range(mixer_gain.shape[1] // DK):
        extra[32 + i : 33 + i, :] = mixer_gain[:, i * DK : (i + 1) * DK]
    for k in range(4):
        for o in (0, 2):
            blocks = [lane_block(dest_block(mine, k, o + i), DK) for i in range(2)]
            left = jnp.concatenate(
                [jnp.concatenate([halo[:, at], normed[:, at]], axis=0) for at in blocks], axis=1
            )
            grads = mm(turned_refs[...], left)
            for i, at in enumerate(blocks):
                half = slice(i * DK, (i + 1) * DK)
                beta = grads[cols : cols + heads, half]
                gain = (
                    jnp.sum(grads[:cols, half] * in_rows[:, at].astype(FLOAT), axis=0, keepdims=True)
                    + jnp.sum(beta * beta_rows[:heads, at].astype(FLOAT), axis=0, keepdims=True)
                    + gate_gain[:, at]
                )
                extra[36 : 36 + heads, :] = beta
                extra[40:41, :] = gain / first_gain[:, at]
                extra[41:42, :] = second_gain[:, at]
                store_tile(
                    outs, k, o + i, early[k][o + i], jnp.concatenate([grads[:cols, half], extra[...]], axis=0).astype(HALF)
                )


def ffn_grad_kernel(turns, mine, cot, normed, d_gate, d_up, product, *refs):
    outs, token = refs[:-1], refs[-1]
    token[...] = jnp.zeros(token.shape, FLOAT)
    cols = d_gate.shape[0]
    half_rows = 3 * cols // 2
    for k in turns:
        for o in (0, 2):
            blocks = [lane_block(dest_block(mine, k, o + i), DK) for i in range(2)]
            lefts = [jnp.concatenate([ref[:, at] for at in blocks], axis=1) for ref in (normed, cot)]
            for n, (right, left) in enumerate(((d_gate, lefts[0]), (d_up, lefts[0]), (product, lefts[1]))):
                both = mm(right[...], left).astype(HALF)
                for i in range(2):
                    tile = both[:, i * DK : (i + 1) * DK]
                    first = n * cols
                    if k < 3:
                        outs[turns.index(k)][o + i, first : first + cols, :] = tile
                    elif first + cols <= half_rows:
                        outs[0][o + i, first : first + cols, :] = tile
                    elif first >= half_rows:
                        outs[1][o + i, first - half_rows : first - half_rows + cols, :] = tile
                    else:
                        outs[0][o + i, first:, :] = tile[: half_rows - first]
                        outs[1][o + i, : first + cols - half_rows, :] = tile[half_rows - first :]


def ffn_grads(turns, mine, cot, normed, d_gate, d_up, product, after):
    rows = 3 * d_gate.shape[0]
    if turns == (3,):
        shapes = (out((4, rows // 2, DK), HALF),) * 2
    else:
        shapes = (out((4, rows, DK), HALF),) * len(turns)
    return run(
        partial(ffn_grad_kernel, turns),
        shapes + (out((8, DK), FLOAT),),
        (mine, cot, normed, d_gate, d_up, product),
        scalars=1,
        after=(after,),
    )


def gain_rows(ref):
    first = ref.shape[1] - EXTRA + 40
    return ref[:, first : first + 8, :].astype(FLOAT)


def last_relay_kernel(own, plus, minus, first, second, plus_out, minus_out, token, rows):
    relay_kernel(plus, minus, first, second, plus_out, minus_out, token)
    for i, ref in enumerate((own, plus_out, minus_out)):
        rows[i] = gain_rows(ref)


def quad_sum_kernel(tiles, own, plus, minus):
    for i, target in enumerate((own, plus, minus)):
        target[...] = (tiles[0, i] + tiles[1, i]) + (tiles[2, i] + tiles[3, i])


def gains_over_chips(rows):
    tiles = lax.all_to_all(jnp.broadcast_to(rows[None], (4, *rows.shape)), "x", 0, 0, tiled=True)
    own, plus, minus = run(quad_sum_kernel, (out((4, 8, DK), FLOAT),) * 3, (tiles,))
    return own, turned(plus, True, 1), turned(minus, True, -1)


def relay_kernel(plus, minus, first, second, plus_out, minus_out, token):
    half = first.shape[1]
    plus_out[:, :half, :] = (plus[:, :half, :].astype(FLOAT) + first[...].astype(FLOAT)).astype(HALF)
    plus_out[:, half:, :] = plus[:, half:, :]
    minus_out[:, :half, :] = minus[:, :half, :]
    minus_out[:, half:, :] = (minus[:, half:, :].astype(FLOAT) + second[...].astype(FLOAT)).astype(HALF)
    token[...] = jnp.zeros(token.shape, FLOAT)


def relayed(parts, after, micros):
    shape = out(parts[1].shape, HALF)
    first, second = turned(parts[3], True, 1), turned(parts[4], True, -1)
    plus, minus, token = run(
        relay_kernel,
        (shape, shape, out((8, DK), FLOAT)),
        (parts[1], parts[2], first, second),
        after=after,
        micros=micros,
    )
    return (parts[0], turned(plus, True, 1), turned(minus, True, -1)), token


def last_sum_kernel(mine, own, plus, minus, own_rows, plus_rows, minus_rows, *outs):
    seq_sum_kernel(0, mine, own, plus, minus, *outs)
    rank = jnp.where(mine[1] == 0, mine[2], mine[3])
    first = outs[0].shape[0] - EXTRA + 32
    for k in range(4):
        place = ring_place(rank, k)
        old = own[place, first : first + 16, :].astype(FLOAT)
        old = old + plus[place, first : first + 16, :].astype(FLOAT) + minus[place, first : first + 16, :].astype(FLOAT)
        new = own_rows[place] + plus_rows[place] + minus_rows[place]
        outs[k][first : first + 16, :] = jnp.concatenate([old[:8], new], axis=0).astype(outs[k].dtype)


def seq_sum_kernel(early, mine, *refs):
    rank = jnp.where(mine[1] == 0, mine[2], mine[3])
    group, before = refs[:3], refs[3 : 3 + 4 * early]
    outs = refs[3 + 4 * early : 7 + 4 * early]
    refs[-1][...] = jnp.zeros(refs[-1].shape, FLOAT)
    for k in range(4):
        place = ring_place(rank, k)
        at = 0
        for i in range(early):
            source = before[4 * i + k]
            outs[k][at : at + source.shape[0], :] = source[...]
            at += source.shape[0]
        total = group[0][place].astype(FLOAT) + group[1][place].astype(FLOAT) + group[2][place].astype(FLOAT)
        outs[k][at:, :] = total.astype(outs[k].dtype)


def seq_sums(group, before, mine, after, micros):
    count = group[0].shape[1] + sum(sums[0].shape[0] for sums in before)
    shapes = (out((count, DK), FLOAT),) + (out((count, DK), HALF),) * 3
    shapes += (out((8, DK), FLOAT),)
    flat = [piece for sums in before for piece in sums]
    return run(
        partial(seq_sum_kernel, len(before)), shapes, (mine, *group, *flat), scalars=1, after=after, micros=micros
    )


def second_round(sums):
    return [sums[0]] + [turned(sums[i], False, TURNS[i]) for i in range(1, 4)]


def unpack_kernel(own, first, second, third, *outs):
    total = own[...] + first[...].astype(FLOAT) + second[...].astype(FLOAT) + third[...].astype(FLOAT)
    at = 0
    for target in outs[:5]:
        count = target.shape[1]
        target[...] = total[at : at + count, :].T
        at += count
    extra = total[at:, :]
    per_tap = 8
    first = 0
    for target in outs[5:8]:
        blocks = target.shape[1] // DK
        for j in range(4):
            for i in range(blocks):
                row = j * per_tap + first + i
                target[j : j + 1, i * DK : (i + 1) * DK] = extra[row : row + 1, :]
        first += blocks
    for i in range(outs[8].shape[1] // DK):
        outs[8][:, i * DK : (i + 1) * DK] = extra[32 + i : 33 + i, :]
    outs[9][...] = extra[36:38, :]
    outs[10][...] = extra[40:48, :]


def ffn_unpack_kernel(own, first, second, third, gate, up, down, token):
    cols = gate.shape[0]
    token[...] = jnp.zeros(token.shape, FLOAT)
    for n, target in enumerate((gate, up, down)):
        span = slice(n * cols, (n + 1) * cols)
        target[...] = (
            own[span, :]
            + first[span, :].astype(FLOAT)
            + second[span, :].astype(FLOAT)
            + third[span, :].astype(FLOAT)
        )


def output_kernel(own, first, second, third, total, token):
    token[...] = jnp.zeros(token.shape, FLOAT)
    total[...] = (
        own[...] + first[...].astype(FLOAT) + second[...].astype(FLOAT) + third[...].astype(FLOAT)
    ).astype(HALF)


def tile_of(i, mine):
    return (i % 4) * 2 + jnp.where(i < 4, 1 - mine[1], mine[1])


def whole_block(shape):
    return pl.BlockSpec(shape, lambda i, mine: (0,) * len(shape))


def tile_outs(rows, width):
    return [
        pl.BlockSpec((1, rows, width), lambda i, mine: (jnp.minimum(i, 3), 0, 0)),
        pl.BlockSpec((1, rows, width), lambda i, mine: (jnp.maximum(i - 4, 0), 0, 0)),
    ]


def down_kernel(mine, product, weight, hidden, other, own, token, scratch):
    step = pl.program_id(0)
    rows = hidden.shape[0]

    @pl.when(step == 0)
    def _():
        scratch[...] = product[...].T

    part = mm(scratch[...], weight[...])
    here = lane_block(mine[0] * 2 + mine[1], rows)
    for target, wanted in ((other, step < 4), (own, step >= 4)):

        @pl.when(wanted)
        def _():
            target[0] = part.astype(HALF)
            target[0, here, :] = (target[0, here, :].astype(FLOAT) + hidden[...]).astype(HALF)

    token[...] = jnp.zeros(token.shape, FLOAT)


def down_tiles(mine, product, weight, hidden):
    cols, tokens = product.shape
    width = weight.shape[1] // 8
    spec = pltpu.PrefetchScalarGridSpec(
        num_scalar_prefetch=1,
        grid=(8,),
        in_specs=[
            whole_block(product.shape),
            pl.BlockSpec((cols, width), lambda i, mine: (0, tile_of(i, mine))),
            pl.BlockSpec((hidden.shape[0], width), lambda i, mine: (0, tile_of(i, mine))),
        ],
        out_specs=tile_outs(tokens, width) + [whole_block((8, DK))],
        scratch_shapes=[pltpu.VMEM((tokens, cols), HALF)],
    )
    tiles = out((4, tokens, width), HALF)
    return pl.pallas_call(
        down_kernel,
        grid_spec=spec,
        out_shape=(tiles, tiles, out((8, DK), FLOAT)),
        compiler_params=pltpu.CompilerParams(vmem_limit_bytes=16 * 2**20),
        cost_estimate=cost(4.0),
    )(mine, product, weight, hidden)


def d_first_kernel(mine, dproj, d_pre, d_logit, sums, in_rows, gate_rows, beta_rows, after, other, own, token, sum_rows):
    step = pl.program_id(0)
    tokens = d_pre.shape[0]
    width = own.shape[2]

    @pl.when(step == 0)
    def _():
        row = jnp.broadcast_to(sums[HALO:, :], (tokens, DK)).T
        sum_rows[...] = jnp.zeros(sum_rows.shape, FLOAT)
        for i in range(tokens // width):
            sum_rows[i : i + 1, :] = row[0:1, i * width : (i + 1) * width]
        sum_rows[2:3, 0:HALO] = jnp.broadcast_to(sums[:HALO, :], (HALO, DK)).T[0:1, :]

    part = mm(dproj[...], in_rows[...])
    late = mm(d_pre[...], gate_rows[...])
    for h in range(2):
        late = late + d_logit[:, h : h + 1] * beta_rows[h : h + 1, :].astype(FLOAT)
    for target, wanted in ((other, step < 4), (own, step >= 4)):

        @pl.when(wanted)
        def _():
            target[0, :HALO, :] = part[:HALO].astype(HALF)
            target[0, HALO : HALO + tokens, :] = (part[HALO:] + late).astype(HALF)
            target[0, HALO + tokens :, :] = sum_rows[...].astype(HALF)

    token[...] = jnp.zeros(token.shape, FLOAT)


def d_first_tiles(mine, dproj, d_pre, d_logit, sums, in_rows, gate_rows, beta_rows, after):
    tokens = d_pre.shape[0]
    width = in_rows.shape[1] // 8
    count = tokens + 2 * HALO

    def tile(rows):
        return pl.BlockSpec((rows, width), lambda i, mine: (0, tile_of(i, mine)))

    spec = pltpu.PrefetchScalarGridSpec(
        num_scalar_prefetch=1,
        grid=(8,),
        in_specs=[whole_block(a.shape) for a in (dproj, d_pre, d_logit, sums)]
        + [tile(in_rows.shape[0]), tile(gate_rows.shape[0]), tile(beta_rows.shape[0])]
        + [pl.BlockSpec(memory_space=pl.ANY)],
        out_specs=tile_outs(count, width) + [whole_block((8, DK))],
        scratch_shapes=[pltpu.VMEM((HALO, width), FLOAT)],
    )
    tiles = out((4, count, width), HALF)
    return pl.pallas_call(
        d_first_kernel,
        grid_spec=spec,
        out_shape=(tiles, tiles, out((8, DK), FLOAT)),
        compiler_params=pltpu.CompilerParams(vmem_limit_bytes=16 * 2**20),
        cost_estimate=cost(6.0),
    )(mine, dproj, d_pre, d_logit, sums, in_rows, gate_rows, beta_rows, after)


def first_total_kernel(tiles, total, pack):
    whole = sum(tiles[x].astype(FLOAT) for x in range(4))
    total[...] = whole
    pack[:HALO, :] = whole[:HALO]
    at = whole.shape[0] - HALO
    pack[HALO:, :] = whole[at : at + 8]


def input_grad_kernel(mine, total, arrived, block_input, factor, gain, d_branch, grad):
    tokens, width = block_input.shape
    columns = []
    for i in range(tokens // width):
        row = total[HALO + tokens + i : HALO + tokens + i + 1, :]
        columns.append(jnp.broadcast_to(row, (DK, width)).T[:, 0:1])
    late_row = jnp.broadcast_to(arrived[HALO + 2 : HALO + 3, :], (DK, width)).T[:HALO, 0:1]
    mean = jnp.concatenate(columns, axis=0) / (8 * width)
    scale = factor[...]
    unit = block_input[...].astype(FLOAT) * scale
    gain_own = gain[:, lane_block(mine[0] * 2 + mine[1], width)]
    grad[...] = d_branch[...].astype(FLOAT) + scale * (total[HALO : HALO + tokens, :] * gain_own - unit * mean)
    last = slice(tokens - HALO, tokens)
    grad[last, :] += scale[last] * (arrived[:HALO, :] * gain_own - unit[last] * (late_row / (8 * width)))


def next_block(array, distance):
    size = 16
    route = [(i, i + distance) for i in range(size) if 0 <= i + distance < size]
    return lax.ppermute(array, SEQ, route)


def dot_nt(a, b):
    return lax.dot_general(a, b, NT, preferred_element_type=FLOAT)


def shards(
    block_input,
    log_decay,
    first_gain,
    query_weight,
    key_weight,
    value_weight,
    gate_weight,
    beta_weight,
    query_conv,
    key_conv,
    value_conv,
    mixer_gain,
    mixer_weight,
    second_gain,
    swiglu_gate,
    swiglu_up,
    swiglu_down,
    cotangent,
):
    heads = log_decay.shape[1]
    tokens, width = block_input.shape
    model = 8 * width
    chunks = tokens // CH
    rows = tokens // 8
    kq, vd = heads * DK, heads * DV
    cols = 2 * kq + vd
    hidden_cols = swiglu_gate.shape[1]
    mine = jnp.stack([lax.axis_index(name) for name in ("x", "c", "y", "z")]).astype(jnp.int32)

    token_out = out((8, DK), FLOAT)
    in_rows, gate_rows, gcol, grow, token = run(
        setup_kernel,
        (
            out((cols, model), HALF),
            out((vd, model), HALF),
            out((tokens, heads), FLOAT),
            out((heads * chunks, CH), FLOAT),
            token_out,
        ),
        (query_weight, key_weight, value_weight, gate_weight, log_decay.T),
        micros=3.0,
    )
    beta_rows = jnp.pad(beta_weight.T, ((0, HALO - heads), (0, 0)))
    taps = jnp.concatenate([query_conv.T, key_conv.T, value_conv.T], axis=1)
    gain_row = mixer_gain.reshape(1, -1)
    first_row = first_gain.reshape(1, -1)

    first_normed, first_factor, my_rows, logits, cot, halo_rows = run(
        first_norm_kernel,
        (
            out((tokens, model), HALF),
            out((tokens, 1), FLOAT),
            out((rows, model), FLOAT),
            out((tokens, HALO), FLOAT),
            out((tokens, width), HALF),
            out((HALO, model), HALF),
        ),
        (mine, first_row, beta_rows, cotangent, *head_gather(block_input, mine, (token,))),
        scalars=1,
        micros=3.0,
    )
    halo_normed = next_block(halo_rows, 1)
    proj = dot_nt(first_normed, in_rows).astype(HALF)
    halo_proj = dot_nt(halo_normed, in_rows).astype(HALF)
    gate_pre = dot_nt(first_normed, gate_rows)
    q, k, v, tri, n, b, w, u, p, pay, pay_token = run(
        partial(prepare_kernel, heads, chunks),
        prepare_shapes(heads, chunks) + (token_out,),
        (proj, halo_proj, taps, logits, gcol, grow),
        [pltpu.VMEM((HALO + tokens, cols), FLOAT)],
        micros=8.0,
        kept=range(9),
        megs=20,
    )
    near_pieces = ring_pieces(pay, "z")
    cot_tiles = head_gather(cot, mine, (pay_token,))
    whole_cot, cot_rows, d_product, token = run(
        product_grad_kernel,
        (out((tokens, model), HALF), out((rows, model), HALF), out((hidden_cols, tokens), FLOAT), token_out),
        (mine, *cot_tiles, swiglu_down.T),
        scalars=1,
        micros=4.0,
    )
    before, group, near = run(
        partial(group_kernel, heads), group_shapes(heads), (mine, *near_pieces), scalars=1, after=(gate_pre[:8, :DK],), micros=2.0
    )
    half_tiles = out((4, rows, model), HALF)
    states, vns, mixed, gated, branch_other, branch_own, far = run(
        partial(mix_kernel, heads, chunks),
        mix_shapes(heads, chunks)[:4] + (half_tiles, half_tiles) + mix_shapes(heads, chunks)[4:],
        (mine, *ring_pieces(group, "y"), before, q, k, w, u, p, n, b, gcol, gate_pre, gain_row, mixer_weight),
        [pltpu.VMEM((tokens, model // 4), FLOAT)],
        scalars=1,
        after=(token,),
        kept=(0, 1, 2, 6),
        megs=16,
        micros=4.0,
    )
    branch = head_scatter(branch_own, branch_other, mine)
    wide_rows = out((rows, model), FLOAT)
    second_row = second_gain.reshape(1, -1)
    hidden, second_unit, second_factor, own_normed = run(
        hidden_kernel,
        (wide_rows, wide_rows, out((rows, 1), FLOAT), out((rows, model), HALF)),
        (my_rows, second_row, *branch),
    )
    turned_out = out((hidden_cols, tokens), HALF)
    second_normed, product, d_gate, d_up, second_other, second_own, ffn_token = run(
        ffn_kernel,
        (out((tokens, model), HALF), turned_out, turned_out, turned_out, half_tiles, half_tiles, token_out),
        (
            mine,
            *head_gather(own_normed, mine),
            swiglu_gate.T,
            swiglu_up.T,
            d_product,
        ),
        [pltpu.VMEM((tokens, model // 4), FLOAT)],
        scalars=1,
        micros=9.0,
        megs=20,
    )
    second_parts, token = head_scatter(second_own, second_other, mine, True)
    grad_args = (mine, whole_cot, second_normed, d_gate, d_up, product)
    *ffn_ends, token = ffn_grads((3,), *grad_args, token)
    ffn_plus, ffn_minus, token = ffn_grads((1, 2), *grad_args, token)
    d_hidden, second_gain_part, back_token = run(
        second_back_kernel,
        (out((rows, model), HALF), out((1, model), FLOAT), token_out),
        (second_unit, second_factor, second_row, cot_rows, *second_parts),
        after=(token,),
    )
    ffn_group, ffn_token = relayed([None, ffn_plus, ffn_minus, *ffn_ends], (back_token,), 3.0)
    down_other, down_own, down_token = down_tiles(mine, product, swiglu_down.T, hidden)
    d_branch, d_branch_own = run(
        join_rows_kernel,
        (out((tokens, model), HALF), out((tokens, width), HALF)),
        (mine, *head_gather(d_hidden, mine, (down_token, ffn_token))),
        scalars=1,
    )
    d_gated = jnp.dot(d_branch, mixer_weight, preferred_element_type=FLOAT)
    dos, dvns, es, d_gate_pre, gain_part, gate_sums, ends = run(
        partial(gate_back_kernel, heads, chunks),
        gate_back_shapes(heads, chunks),
        (d_gated, mixed, gate_pre, gain_row, q, w, p, n, gcol),
        micros=4.0,
    )
    ffn_own, token = ffn_grads((0,), *grad_args, gate_sums[:8])
    *ffn_sums, ffn_token = seq_sums((ffn_own, *ffn_group[1:]), (), mine, (), 3.0)
    tile = out((4, 2 * vd, DK), HALF)
    *mixer_parts, gate_gain = run(
        mixer_grad_kernel,
        (tile,) * 4 + (out((1, model), FLOAT),),
        (mine, d_branch, gated, first_normed, d_gate_pre, gate_rows),
        [pltpu.VMEM((vd, tokens), HALF), pltpu.VMEM((vd, tokens), HALF)],
        scalars=1,
        micros=5.0,
    )
    after, group_end, _, group_token = run(
        partial(group_back_kernel, heads),
        group_back_shapes(heads) + (token_out,),
        (mine, near, *ring_pieces(ends, "z")),
        scalars=1,
        after=(gate_gain, ffn_token),
        micros=2.0,
    )
    end_pieces = ring_pieces(group_end, "y")
    passed_sums, ffn_token = passed(ffn_sums, tuple(end_pieces[1:]))
    dproj, d_logit, logit_rows, taps_part, sums = run(
        partial(back_kernel, heads, chunks),
        back_shapes(heads, chunks),
        (mine, far, *end_pieces, after, q, k, v, logits, gate_sums, gcol, grow, tri, states, vns, dos, dvns, es, n, proj, halo_proj, taps),
        back_scratch(heads, chunks),
        scalars=1,
        after=(ffn_token,),
        micros=11.0,
        megs=30,
    )
    ffn_grad_out = out((hidden_cols, DK), FLOAT)
    grad_gate, grad_up, grad_down, ffn_token = run(
        ffn_unpack_kernel, (ffn_grad_out,) * 3 + (token_out,), second_round(passed_sums), after=(sums[:8],)
    )
    packed = 2 * vd + cols + EXTRA
    tile, half_tile = out((4, packed, DK), HALF), out((4, packed // 2, DK), HALF)
    *in_parts, in_token = run(
        in_grad_kernel,
        (tile,) * 3 + (half_tile,) * 2 + (token_out,),
        (mine, first_normed, halo_normed, dproj, logit_rows, taps_part, gain_part, gate_gain, second_gain_part, first_row, in_rows, beta_rows, *mixer_parts),
        [pltpu.VMEM((cols + HALO, HALO + tokens), HALF), pltpu.VMEM((EXTRA, DK), FLOAT)],
        scalars=1,
        after=(ffn_token,),
        micros=6.0,
        megs=16,
    )
    first_other, first_own, first_token = d_first_tiles(
        mine, dproj, d_gate_pre, d_logit, sums, in_rows, gate_rows, beta_rows, in_token
    )
    output, out_token = run(
        output_kernel,
        (out((tokens, width), HALF), token_out),
        head_scatter(down_own, down_other, mine, after=(in_token,)),
    )
    tile = out((4, packed, DK), HALF)
    plus, minus, in_token, rows_left = run(
        last_relay_kernel,
        (tile, tile, token_out, out((3, 4, 8, DK), FLOAT)),
        (*in_parts[:3], turned(in_parts[3], True, 1), turned(in_parts[4], True, -1)),
        after=(first_token, out_token),
    )
    in_group = (in_parts[0], turned(plus, True, 1), turned(minus, True, -1))
    first_sum = run(
        tile_sum_kernel,
        (out((4, tokens + 2 * HALO, width), HALF),),
        (first_own, rotated(first_other, "c", 1)),
        after=(in_token,),
    )[0]
    first_tiles = lax.all_to_all(first_sum, "x", 0, 0, tiled=True)
    total, pack = run(
        first_total_kernel,
        (out((tokens + 2 * HALO, width), FLOAT), out((HALO + 8, width), FLOAT)),
        (first_tiles,),
    )
    *sums_out, sum_token = run(
        last_sum_kernel,
        (out((packed, DK), FLOAT),) + (out((packed, DK), HALF),) * 3 + (token_out,),
        (mine, *in_group, *gains_over_chips(rows_left)),
        scalars=1,
    )
    totals = [sums_out[0]] + [turned(sums_out[i], False, TURNS[i]) for i in range(1, 4)]
    grad_mixer_weight, grad_gate_weight, grad_query, grad_key, grad_value, *taps_grad, gain_grad, beta_grad, both = run(
        unpack_kernel,
        tuple(out((DK, count), FLOAT) for count in (vd, vd, kq, kq, vd)) + tuple(out((rows_, count), FLOAT) for rows_, count in ((4, kq), (4, kq), (4, vd), (1, vd), (heads, DK), (8, DK))),
        totals,
    )
    grad_input = run(
        input_grad_kernel,
        (out((tokens, width), FLOAT),),
        (mine, total, next_block(pack, -1), block_input, first_factor, first_row, d_branch_own),
        scalars=1,
    )[0]
    both = both + rotated(both, "c", 1)
    return (
        output,
        grad_input,
        both[0],
        grad_query,
        grad_key,
        grad_value,
        grad_gate_weight,
        beta_grad.T,
        taps_grad[0].T,
        taps_grad[1].T,
        taps_grad[2].T,
        gain_grad.reshape(-1),
        grad_mixer_weight,
        both[1],
        grad_gate.T,
        grad_up.T,
        grad_down.T,
    )


def solution(mesh):
    torus = Mesh(mesh.devices.reshape(4, 4, 4, 2), SEQ + HEAD)
    in_specs = (
        P(SEQ, HEAD),
        P(SEQ, HEAD),
        P(),
        P(None, HEAD),
        P(None, HEAD),
        P(None, HEAD),
        P(None, HEAD),
        P(None, HEAD),
        P(HEAD, None),
        P(HEAD, None),
        P(HEAD, None),
        P(HEAD),
        P(None, HEAD),
        P(),
        P(None, HEAD),
        P(None, HEAD),
        P(None, HEAD),
        P(SEQ, HEAD),
    )
    out_specs = (
        P(SEQ, HEAD),
        P(SEQ, HEAD),
        P(SEQ),
        P(SEQ, HEAD),
        P(SEQ, HEAD),
        P(SEQ, HEAD),
        P(SEQ, HEAD),
        P(SEQ, HEAD),
        P(HEAD, None),
        P(HEAD, None),
        P(HEAD, None),
        P(HEAD),
        P(SEQ, HEAD),
        P(SEQ),
        P(SEQ, HEAD),
        P(SEQ, HEAD),
        P(SEQ, HEAD),
    )
    return jax.shard_map(
        shards, mesh=torus, in_specs=in_specs, out_specs=out_specs, check_vma=False
    )
```

```python
from functools import partial

import jax
import jax.numpy as jnp
from jax import lax
from jax.experimental import pallas as pl
from jax.experimental.pallas import tpu as pltpu
from jax.sharding import Mesh
from jax.sharding import PartitionSpec as P

DK = 128
DV = 256
CH = 128
EPS_NORM = 1e-06
EPS_GATE = 1e-05
FLOAT = jnp.float32
HALF = jnp.bfloat16
NN = (((1,), (0,)), ((), ()))
NT = (((1,), (1,)), ((), ()))
TN = (((0,), (0,)), ((), ()))


def mm(a, b, dims=NN):
    return lax.dot_general(a.astype(HALF), b.astype(HALF), dims, preferred_element_type=FLOAT)


def halves(a):
    high = a.astype(HALF)
    return high, (a - high.astype(FLOAT)).astype(HALF)


def mm2(a, b, dims=NN):
    high, low = halves(b)
    return mm(a, high, dims) + mm(a, low, dims)


def mm3(a, b, dims=NN):
    a_high, a_low = halves(a)
    b_high, b_low = halves(b)
    return mm(a_high, b_high, dims) + (mm(a_high, b_low, dims) + mm(a_low, b_high, dims))


def sigmoid(v):
    return 1.0 / (1.0 + jnp.exp(-v))


def square_masks():
    rows = lax.broadcasted_iota(jnp.int32, (CH, CH), 0)
    cols = lax.broadcasted_iota(jnp.int32, (CH, CH), 1)
    return rows, cols


def decay_matrix(gcol, grow):
    rows, cols = square_masks()
    return jnp.where(rows >= cols, jnp.exp(jnp.minimum(gcol - grow, 0.0)), 0.0)


def conv_of(wide, taps, start, count, lanes):
    total = wide[HALO - 3 + start : HALO - 3 + start + count, lanes] * taps[0:1, lanes]
    for j in range(1, 4):
        total = total + wide[HALO - 3 + j + start : HALO - 3 + j + start + count, lanes] * taps[j : j + 1, lanes]
    return total


def query_kernel(heads, chunks, proj, halo, taps, k, gcol, grow, q_out, p_out, token, wide):
    token[...] = jnp.zeros(token.shape, FLOAT)
    kq = heads * DK
    wide[:HALO, :] = halo[:, :kq].astype(FLOAT)
    wide[HALO:, :] = proj[:, :kq].astype(FLOAT)
    for h in range(heads):
        for c in range(chunks):
            span = slice(c * CH, (c + 1) * CH)
            lanes = slice(h * DK, (h + 1) * DK)
            at = h * chunks + c
            cq = conv_of(wide, taps, c * CH, CH, lanes)
            query = (cq * sigmoid(cq)).astype(HALF)
            q_out[span, lanes] = query
            spread = decay_matrix(gcol[span, h : h + 1], grow[at : at + 1, :])
            p_out[at] = (spread * mm(query, k[span, lanes], NT)).astype(HALF)


def prepare_kernel(heads, chunks, proj, halo, taps, logits, gcol, grow, k_out, v_out, t_out, n_out, b_out, w_out, u_out, pay, token, wide):
    token[...] = jnp.zeros(token.shape, FLOAT)
    rows, cols = square_masks()
    differ = rows ^ cols
    eye = jnp.where(rows == cols, 1.0, 0.0)
    wide[:HALO, :] = halo[...].astype(FLOAT)
    wide[HALO:, :] = proj[...].astype(FLOAT)
    kq = heads * DK
    work = [(h, c) for h in range(heads) for c in range(chunks)]
    low, keys, sides = {}, {}, {}
    for h, c in work:
        span = slice(c * CH, (c + 1) * CH)
        ql, kl, vl = (
            slice(h * DK, (h + 1) * DK),
            slice(kq + h * DK, kq + (h + 1) * DK),
            slice(2 * kq + h * DV, 2 * kq + (h + 1) * DV),
        )
        ck = conv_of(wide, taps, c * CH, CH, kl)
        act = ck * sigmoid(ck)
        key = (act * lax.rsqrt(jnp.sum(act * act, axis=-1, keepdims=True) + EPS_NORM)).astype(HALF)
        cv = conv_of(wide, taps, c * CH, CH, vl)
        value = (cv * sigmoid(cv)).astype(HALF)
        k_out[span, ql] = key
        v_out[span, h * DV : (h + 1) * DV] = value
        beta = sigmoid(logits[span, h : h + 1])
        g = gcol[span, h : h + 1]
        spread = decay_matrix(g, grow[h * chunks + c : h * chunks + c + 1, :])
        inner = mm(key, key, NT)
        low[h, c] = jnp.where(rows > cols, beta * spread * inner, 0.0)
        keys[h, c] = key
        sides[h, c] = jnp.concatenate([(beta * jnp.exp(g)) * key.astype(FLOAT), beta * value.astype(FLOAT)], axis=1)
    tri = {at: eye - jnp.where(differ < 2, low[at], 0.0) for at in work}
    size = 2
    while size < CH:
        part = {at: mm3(jnp.where((differ >= size) & (differ < 2 * size), low[at], 0.0), tri[at]) for at in work}
        tri = {at: tri[at] - mm3(tri[at], part[at]) for at in work}
        size *= 2
    steps = {}
    for h, c in work:
        at = h * chunks + c
        t_out[at] = tri[h, c].astype(HALF)
        solved = mm3(tri[h, c], sides[h, c])
        w_out[at] = solved[:, :DK].astype(HALF)
        u_out[at] = solved[:, DK:].astype(HALF)
        g = gcol[c * CH : (c + 1) * CH, h : h + 1]
        last = gcol[(c + 1) * CH - 1 : (c + 1) * CH, h : h + 1]
        step = mm2(keys[h, c], jnp.exp(last - g) * solved, TN)
        n_out[at] = step[:, :DK].astype(HALF)
        b_out[at] = step[:, DK:]
        steps[h, c] = (jnp.exp(last), step)
    zero = jnp.zeros((DK, DK), FLOAT)
    for h in range(heads):
        decay, step = steps[h, 0]
        total = jnp.concatenate([decay * eye - step[:, :DK], step[:, DK:]], axis=1)
        whole = decay
        for c in range(1, chunks):
            decay, step = steps[h, c]
            total = decay * total - mm3(step[:, :DK], total) + jnp.concatenate([zero, step[:, DK:]], axis=1)
            whole = whole * decay
        pack_map(pay, h, total, whole, eye)


def whole_decay(pay, j, h):
    return pay[j, h, DK : DK + 1, 0:1].astype(FLOAT) + pay[j, h, DK + 8 : DK + 9, 0:1].astype(FLOAT)


def apply_whole(pay, j, h, state, dims):
    return whole_decay(pay, j, h) * state + mm(pay[j, h, :DK, :DK], state, dims)


def pack_map(pay, h, total, whole, eye):
    pay[h, :DK, :] = jnp.concatenate([total[:, :DK] - whole * eye, total[:, DK:]], axis=1).astype(HALF)
    rest = jnp.broadcast_to(whole, (8, DK + DV))
    first = rest.astype(HALF).astype(FLOAT)
    pay[h, DK:, :] = jnp.concatenate([first, rest - first], axis=0).astype(HALF)


def group_kernel(heads, mine, p0, p1, p2, p3, before, group, near, token):
    token[...] = jnp.zeros(token.shape, FLOAT)
    me = mine[3]
    for k, piece in enumerate((p0, p1, p2, p3)):
        near[ring_place(me, k)] = piece[...]
    rows, cols = square_masks()
    eye = jnp.where(rows == cols, 1.0, 0.0)
    zero = jnp.zeros((DK, DK), FLOAT)
    start = jnp.concatenate([eye, jnp.zeros((DK, DV), FLOAT)], axis=1)
    totals, keeps, wholes = [start] * heads, [start] * heads, [jnp.ones((1, 1), FLOAT)] * heads
    for j in range(near.shape[0]):
        for h in range(heads):
            added = jnp.concatenate([zero, near[j, h, :DK, DK:].astype(FLOAT)], axis=1)
            if j == 0:
                moved = jnp.concatenate([whole_decay(near, j, h) * eye + near[j, h, :DK, :DK].astype(FLOAT), added[:, DK:]], axis=1)
            else:
                moved = apply_whole(near, j, h, totals[h], NN) + added
            totals[h] = moved
            wholes[h] = wholes[h] * whole_decay(near, j, h)
            keeps[h] = jnp.where(me == j + 1, moved, keeps[h])
    for h in range(heads):
        before[h] = keeps[h]
        pack_map(group, h, totals[h], wholes[h], eye)


def group_back_kernel(heads, mine, near, p0, p1, p2, p3, after, group, ends, token):
    token[...] = jnp.zeros(token.shape, FLOAT)
    me = mine[3]
    for k, piece in enumerate((p0, p1, p2, p3)):
        ends[ring_place(me, k)] = piece[...]
    rows, cols = square_masks()
    eye = jnp.where(rows == cols, 1.0, 0.0)
    zero = jnp.zeros((DK, DK), FLOAT)
    start = jnp.concatenate([eye, jnp.zeros((DK, DV), FLOAT)], axis=1)
    totals, keeps = [start] * heads, [start] * heads
    for j in reversed(range(near.shape[0])):
        for h in range(heads):
            keeps[h] = jnp.where(me == j, totals[h], keeps[h])
            added = jnp.concatenate([zero, ends[j, h].astype(FLOAT)], axis=1)
            totals[h] = apply_whole(near, j, h, totals[h], TN) + added
    for h in range(heads):
        after[h] = keeps[h]
        group[h] = totals[h][:, DK:].astype(HALF)


def spread_rows(core, total, own, other, rows, lanes):
    for x in range(4):
        mine = pl.ds(pl.multiple_of((2 * x + core) * rows, rows), rows)
        away = pl.ds(pl.multiple_of((2 * x + 1 - core) * rows, rows), rows)
        own[x, :, lanes] = total[mine, :].astype(HALF)
        other[x, :, lanes] = total[away, :].astype(HALF)


def mix_kernel(heads, chunks, mine, p0, p1, p2, p3, before, q, k, w, u, p, n, b, gcol, gate, gain, weight, s_out, vn_out, o_out, gated, other, own, pay, token, total):
    token[...] = jnp.zeros(token.shape, FLOAT)
    ranks = pay.shape[0]
    me = mine[2]
    for at, piece in enumerate((p0, p1, p2, p3)):
        pay[ring_place(me, at)] = piece[...]
    states = [jnp.zeros((DK, DV), FLOAT) for h in range(heads)]
    for j in range(ranks - 1):
        passed = j < me
        for h in range(heads):
            moved = apply_whole(pay, j, h, states[h], NN) + pay[j, h, :DK, DK:].astype(FLOAT)
            states[h] = jnp.where(passed, moved, states[h])
    for h in range(heads):
        states[h] = mm3(before[h, :, :DK], states[h]) + before[h, :, DK:]
    for c in range(chunks):
        span = slice(c * CH, (c + 1) * CH)
        for h in range(heads):
            at = h * chunks + c
            state = states[h].astype(HALF)
            s_out[at] = state
            g = gcol[span, h : h + 1]
            last = gcol[(c + 1) * CH - 1 : (c + 1) * CH, h : h + 1]
            vn = (u[at].astype(FLOAT) - mm(w[at], state)).astype(HALF)
            vn_out[at] = vn
            out = jnp.exp(g) * mm(q[span, h * DK : (h + 1) * DK], state) + mm(p[at], vn)
            vl = slice(h * DV, (h + 1) * DV)
            o_out[span, vl] = out
            factor = lax.rsqrt(jnp.mean(out * out, axis=-1, keepdims=True) + EPS_GATE)
            pre = gate[span, vl]
            gated[span, vl] = (out * factor * gain[:, vl] * (pre * sigmoid(pre))).astype(HALF)
            if c + 1 < chunks:
                states[h] = jnp.exp(last) * states[h] - mm(n[at], state) + b[at]
    width = weight.shape[0]
    tile = total.shape[1]
    rows = own.shape[1]
    for at in range(0, width, tile):
        lanes = slice(at, at + tile)
        total[...] = mm(gated[...], weight[lanes, :], NT)
        spread_rows(mine[1], total, own, other, rows, lanes)


def gate_back_kernel(heads, chunks, d_gated, out, gate, gain, q, w, p, n, gcol, do_out, dvn_out, e_out, dpre_out, dgain_out, sums_out, pay):
    dgain = [jnp.zeros((1, DV), FLOAT) for h in range(heads)]
    ends = [None] * heads
    for c in reversed(range(chunks)):
        span = slice(c * CH, (c + 1) * CH)
        for h in range(heads):
            at = h * chunks + c
            vl = slice(h * DV, (h + 1) * DV)
            dg, o, pre, gn = d_gated[span, vl], out[span, vl], gate[span, vl], gain[:, vl]
            sig = sigmoid(pre)
            factor = lax.rsqrt(jnp.mean(o * o, axis=-1, keepdims=True) + EPS_GATE)
            m = o * factor
            s = pre * sig
            dgm = dg * m
            dgain[h] = dgain[h] + jnp.sum(dgm * s, axis=0, keepdims=True)
            dpre = dgm * gn * (sig * (1.0 + pre * (1.0 - sig)))
            dpre_out[span, vl] = dpre.astype(HALF)
            row_sum = jnp.sum(dpre * pre, axis=-1, keepdims=True)
            sums_out[span, :] = row_sum if h == 0 else sums_out[span, :] + row_sum
            e = dg * gn * s
            dout = factor * (e - m * jnp.mean(e * m, axis=-1, keepdims=True))
            do_out[span, vl] = dout.astype(HALF)
            g = gcol[span, h : h + 1]
            last = gcol[(c + 1) * CH - 1 : (c + 1) * CH, h : h + 1]
            dvn = mm(p[at], dout, TN)
            dvn_out[at] = dvn
            source = mm(q[span, h * DK : (h + 1) * DK], jnp.exp(g) * dout, TN) - mm(w[at], dvn, TN)
            e_out[at] = source
            if ends[h] is None:
                ends[h] = source
            else:
                ends[h] = jnp.exp(last) * ends[h] - mm(n[at], ends[h], TN) + source
    for h in range(heads):
        pay[h] = ends[h].astype(HALF)
        dgain_out[0:1, h * DV : (h + 1) * DV] = dgain[h]


def slopes_kernel(heads, chunks, k, v, states, gcol, grow, proj, halo, taps, slopes, inner_out, spread_out, rest, token, wide):
    token[...] = jnp.zeros(token.shape, FLOAT)
    kq = heads * DK
    wide[:HALO, :] = halo[...].astype(FLOAT)
    wide[HALO:, :] = proj[...].astype(FLOAT)
    for h in range(heads):
        for c in range(chunks):
            span = slice(c * CH, (c + 1) * CH)
            at = h * chunks + c
            kl = slice(kq + h * DK, kq + (h + 1) * DK)
            for lanes in (slice(h * DK, (h + 1) * DK), slice(2 * kq + h * DV, 2 * kq + (h + 1) * DV)):
                pre = conv_of(wide, taps, c * CH, CH, lanes)
                sig = sigmoid(pre)
                slopes[span, lanes] = sig * (1.0 + pre * (1.0 - sig))
            pre = conv_of(wide, taps, c * CH, CH, kl)
            sig = sigmoid(pre)
            act = pre * sig
            unit = lax.rsqrt(jnp.sum(act * act, axis=-1, keepdims=True) + EPS_NORM)
            slopes[span, kl] = unit * (sig * (1.0 + pre * (1.0 - sig)))
            key = k[span, h * DK : (h + 1) * DK]
            g = gcol[span, h : h + 1]
            inner_out[at] = mm(key, key, NT)
            spread_out[at] = decay_matrix(g, grow[at : at + 1, :])
            vl = slice(h * DV, (h + 1) * DV)
            rest[span, vl] = v[span, vl].astype(FLOAT) - jnp.exp(g) * mm(key, states[at])


def back_kernel(heads, chunks, mine, pay, p0, p1, p2, p3, after, q, k, logits, gate_sums, gcol, tri, states, vns, dos, dvns, es, ns, proj, halo, taps, slopes, inner_in, spread_in, rest, dproj_out, dlogit_out, logit_rows, dtaps_out, sums_out, wide, dconv, late, rowsum):
    ranks = pay.shape[0]
    tokens = chunks * CH
    me = mine[2]
    for at, piece in enumerate((p0, p1, p2, p3)):
        late[ring_place(me, at)] = piece[...]
    kq = heads * DK
    width = 2 * kq + heads * DV
    rows, cols = square_masks()
    grads = [jnp.zeros((DK, DV), FLOAT) for h in range(heads)]
    for j in reversed(range(1, ranks)):
        passed = j > me
        for h in range(heads):
            moved = apply_whole(pay, j, h, grads[h], TN) + late[j, h].astype(FLOAT)
            grads[h] = jnp.where(passed, moved, grads[h])
    for h in range(heads):
        grads[h] = mm3(after[h, :, :DK], grads[h]) + after[h, :, DK:]
    wide[:HALO, :] = halo[...].astype(FLOAT)
    wide[HALO:, :] = proj[...].astype(FLOAT)
    logit_rows[...] = jnp.zeros(logit_rows.shape, FLOAT)
    dconv[0:HALO, :] = jnp.zeros((HALO, width), FLOAT)
    dconv[HALO + tokens :, :] = jnp.zeros((8, width), FLOAT)
    for c in reversed(range(chunks)):
        span = slice(c * CH, (c + 1) * CH)
        for h in range(heads):
            at = h * chunks + c
            ql, kl, vl, ol = (
                slice(h * DK, (h + 1) * DK),
                slice(kq + h * DK, kq + (h + 1) * DK),
                slice(2 * kq + h * DV, 2 * kq + (h + 1) * DV),
                slice(h * DV, (h + 1) * DV),
            )
            grad = grads[h].astype(HALF)
            query, key = q[span, ql], k[span, ql]
            state, vn, dout = states[at], vns[at], dos[span, ol]
            logit = logits[span, h : h + 1]
            beta = sigmoid(logit)
            g = gcol[span, h : h + 1]
            last = gcol[(c + 1) * CH - 1 : (c + 1) * CH, h : h + 1]
            eg, ed = jnp.exp(g), jnp.exp(last - g)
            spread = spread_in[at]
            strict = jnp.where(rows > cols, spread, 0.0)
            inner = inner_in[at]
            dvn = dvns[at] + ed * mm(key, grad)
            dr = mm(tri[at], dvn, TN)
            drh = dr.astype(HALF)
            dval = beta * dr
            both = mm(jnp.concatenate([dout, drh], axis=0), state, NT)
            dkeep = mm(vn, grad, NT)
            pair = mm(jnp.concatenate([dout, drh], axis=0), vn, NT)
            dqk = spread * pair[:CH]
            da = -(strict * pair[CH:])
            dkk = beta * da
            dbeta = jnp.sum(dr * rest[span, ol], axis=-1, keepdims=True) + jnp.sum(
                da * inner, axis=-1, keepdims=True
            )
            dqkh = dqk.astype(HALF)
            dkkh = dkk.astype(HALF)
            dquery = eg * both[:CH] + mm(dqkh, key)
            dkey = (
                ed * dkeep
                - (beta * eg) * both[CH:]
                + mm(dqkh, query, TN)
                + mm(dkkh, key)
                + mm(dkkh, key, TN)
            )
            if c > 0:
                grads[h] = jnp.exp(last) * grads[h] - mm(ns[at], grad, TN) + es[at]
            dlogit = dbeta * beta * (1.0 - beta)
            dlogit_out[span, h : h + 1] = dlogit
            logit_rows[h : h + 1, HALO + c * CH : HALO + (c + 1) * CH] = jnp.broadcast_to(dlogit, (CH, DK)).T[0:1]
            extra_sum = dlogit * logit
            far_span = slice(HALO + c * CH, HALO + (c + 1) * CH)
            sums_out[far_span, :] = (gate_sums[span, :] if h == 0 else sums_out[far_span, :]) + extra_sum
            there = slice(HALO + c * CH, HALO + (c + 1) * CH)
            dconv[there, ql] = dquery * slopes[span, ql]
            dconv[there, vl] = dval * slopes[span, vl]
            unit = key.astype(FLOAT)
            dconv[there, kl] = (dkey - unit * jnp.sum(dkey * unit, axis=-1, keepdims=True)) * slopes[span, kl]
    dtaps_out[4:8, :] = jnp.zeros((4, width), FLOAT)
    rowsum[...] = jnp.zeros((HALO + tokens, 1), FLOAT)
    for at in range(0, width, DK):
        lanes = slice(at, at + DK)
        for j in range(4):
            dtaps_out[j : j + 1, lanes] = jnp.sum(
                dconv[HALO : HALO + tokens, lanes] * wide[HALO - 3 + j : HALO - 3 + j + tokens, lanes], axis=0, keepdims=True
            )
        total = dconv[3 : 3 + HALO + tokens, lanes] * taps[0:1, lanes]
        for j in range(1, 4):
            total = total + dconv[3 - j : 3 - j + HALO + tokens, lanes] * taps[j : j + 1, lanes]
        small = total.astype(HALF)
        dproj_out[:, lanes] = small
        rowsum[...] += jnp.sum(small.astype(FLOAT) * wide[:, lanes], axis=-1, keepdims=True)
    sums_out[HALO:, :] += rowsum[HALO:, :]
    sums_out[:HALO, :] = rowsum[:HALO, :]


def out(shape, dtype):
    return jax.ShapeDtypeStruct(shape, dtype)


def cost(micros):
    return pl.CostEstimate(flops=int(micros * 1.1e7), bytes_accessed=0, transcendentals=0)


def run(kernel, shapes, args, scratch=(), scalars=0, after=(), micros=1.0, megs=12, kept=()):
    vmem = pl.BlockSpec(memory_space=pltpu.VMEM)
    smem = pl.BlockSpec(memory_space=pltpu.SMEM)
    count = len(args)

    def body(*refs):
        kernel(*refs[:count], *refs[count + len(after) :])

    return pl.pallas_call(
        body,
        out_shape=tuple(pltpu.HBM(a.shape, a.dtype) if i in kept else a for i, a in enumerate(shapes)),
        in_specs=[smem] * scalars + [vmem] * (count - scalars) + [pl.BlockSpec(memory_space=pl.ANY)] * len(after),
        out_specs=[pl.BlockSpec() if i in kept else vmem for i in range(len(shapes))],
        scratch_shapes=list(scratch),
        compiler_params=pltpu.CompilerParams(vmem_limit_bytes=megs * 2**20),
        cost_estimate=cost(micros),
    )(*args, *after)


def passed(arrays, after):
    count = len(arrays)
    anywhere = pl.BlockSpec(memory_space=pl.ANY)

    def body(*refs):
        token = refs[-1]
        token[...] = jnp.zeros(token.shape, FLOAT)

    *same, token = pl.pallas_call(
        body,
        out_shape=tuple(out(a.shape, a.dtype) for a in arrays) + (out((8, DK), FLOAT),),
        in_specs=[anywhere] * (count + len(after)),
        out_specs=[anywhere] * count + [pl.BlockSpec(memory_space=pltpu.VMEM)],
        input_output_aliases={i: i for i in range(count)},
        compiler_params=pltpu.CompilerParams(vmem_limit_bytes=2**20),
        cost_estimate=cost(0.1),
    )(*arrays, *after)
    return same, token


def prepare_shapes(heads, chunks):
    tokens, pairs = chunks * CH, heads * chunks
    return (
        out((tokens, heads * DK), HALF),
        out((tokens, heads * DV), HALF),
        out((pairs, CH, CH), HALF),
        out((pairs, DK, DK), HALF),
        out((pairs, DK, DV), FLOAT),
        out((pairs, CH, DK), HALF),
        out((pairs, CH, DV), HALF),
        out((heads, DK + 16, DK + DV), HALF),
    )


def mix_shapes(heads, chunks):
    tokens, pairs = chunks * CH, heads * chunks
    return (
        out((pairs, DK, DV), HALF),
        out((pairs, CH, DV), HALF),
        out((tokens, heads * DV), FLOAT),
        out((tokens, heads * DV), HALF),
        out((4, heads, DK + 16, DK + DV), HALF),
    )


def gate_back_shapes(heads, chunks):
    tokens, pairs = chunks * CH, heads * chunks
    return (
        out((tokens, heads * DV), HALF),
        out((pairs, CH, DV), FLOAT),
        out((pairs, DK, DV), FLOAT),
        out((tokens, heads * DV), HALF),
        out((1, heads * DV), FLOAT),
        out((tokens, 1), FLOAT),
        out((heads, DK, DV), HALF),
    )


def back_shapes(heads, chunks):
    tokens = chunks * CH
    width = heads * (2 * DK + DV)
    return (
        out((HALO + tokens, width), HALF),
        out((tokens, heads), FLOAT),
        out((HALO, HALO + tokens), FLOAT),
        out((8, width), FLOAT),
        out((HALO + tokens, 1), FLOAT),
    )


def back_scratch(heads, chunks):
    tokens = chunks * CH
    width = heads * (2 * DK + DV)
    return (pltpu.VMEM((HALO + tokens, width), FLOAT), pltpu.VMEM((HALO + tokens + 8, width), FLOAT), pltpu.VMEM((4, heads, DK, DV), HALF), pltpu.VMEM((HALO + tokens, 1), FLOAT))


def group_shapes(heads):
    pay = (heads, DK + 16, DK + DV)
    return (out((heads, DK, DK + DV), FLOAT), out(pay, HALF), out((4, *pay), HALF))


def group_back_shapes(heads):
    return (
        out((heads, DK, DK + DV), FLOAT),
        out((heads, DK, DV), HALF),
        out((4, heads, DK, DV), HALF),
    )


HEAD = ("x", "c")
SEQ = ("y", "z")
PLANE = ("y", "z", "c")
HALO = 16
EXTRA = 64
TURNS = (0, 1, -1, 2)


def rotated(array, axis, distance):
    size = lax.axis_size(axis)
    return lax.ppermute(array, axis, [(i, (i + distance) % size) for i in range(size)])


def ring_pieces(array, axis):
    return [array] + [rotated(array, axis, -d) for d in TURNS[1:]]


def join_kernel(mine, *refs):
    for k in range(4):
        refs[4][ring_place(mine[0], k)] = refs[k][...]


def head_gather(array, mine, after=()):
    shapes = (out((4, *array.shape), array.dtype),)
    own = run(join_kernel, shapes, (mine, *ring_pieces(array, "x")), scalars=1, after=after)[0]
    return own, rotated(own, "c", 1)


def head_tiles(mine, own, other):
    core = mine[1]
    return [(2 * x + which, ref, x) for which, ref in ((core, own), (1 - core, other)) for x in range(4)]


def turned(array, first, distance):
    pairs = []
    for y in range(4):
        for z in range(4):
            for core in range(2):
                along_z = (core == 0) == first
                to = (y, (z + distance) % 4) if along_z else ((y + distance) % 4, z)
                pairs.append(((y * 4 + z) * 2 + core, (to[0] * 4 + to[1]) * 2 + core))
    return lax.ppermute(array, PLANE, pairs)


def ring_place(mine, k):
    return lax.rem(mine + TURNS[k] + 4, 4)


def lane_block(at, width):
    return pl.ds(pl.multiple_of(at * width, width), width)


def setup_kernel(query, key, value, gate, decay, in_out, gate_out, gcol, grow, token):
    at = 0
    for weight in (query, key, value):
        count = weight.shape[1]
        in_out[at : at + count, :] = weight[...].T
        at += count
    gate_out[...] = gate[...].T
    rows, cols = square_masks()
    heads, tokens = decay.shape
    chunks = tokens // CH
    for h in range(heads):
        for c in range(chunks):
            span = slice(c * CH, (c + 1) * CH)
            flat = jnp.broadcast_to(decay[h : h + 1, span], (CH, CH))
            grow[h * chunks + c : h * chunks + c + 1, :] = jnp.sum(
                jnp.where(rows <= cols, flat.T, 0.0), axis=0, keepdims=True
            )
            gcol[span, h : h + 1] = jnp.sum(jnp.where(cols <= rows, flat, 0.0), axis=1, keepdims=True)
    token[...] = jnp.zeros(token.shape, FLOAT)


def first_norm_kernel(mine, gain, beta_rows, own, other, normed, factor, rows_out, logits, halo_out):
    width = own.shape[2]
    rows = rows_out.shape[0]
    own_rows = lane_block(mine[0] * 2 + mine[1], rows)
    square = 0.0
    for _, ref, x in head_tiles(mine, own, other):
        wide = ref[x].astype(FLOAT)
        square = square + jnp.sum(wide * wide, axis=-1, keepdims=True)
    scale = lax.rsqrt(square / (8 * width) + EPS_NORM)
    factor[...] = scale
    total = 0.0
    for head, ref, x in head_tiles(mine, own, other):
        lanes = lane_block(head, width)
        small = (ref[x].astype(FLOAT) * scale * gain[:, lanes]).astype(HALF)
        normed[:, lanes] = small
        total = total + mm(small, beta_rows[:, lanes], NT)
        rows_out[:, lanes] = ref[x, own_rows, :].astype(FLOAT)
    logits[...] = total
    halo_out[...] = normed[normed.shape[0] - HALO :, :]


def product_grad_kernel(mine, own, other, weight, whole, rows_out, grad, token):
    width = own.shape[2]
    rows = rows_out.shape[0]
    own_rows = lane_block(mine[0] * 2 + mine[1], rows)
    for head, ref, x in head_tiles(mine, own, other):
        lanes = lane_block(head, width)
        whole[:, lanes] = ref[x]
        rows_out[:, lanes] = ref[x, own_rows, :]
    grad[...] = mm(weight[...], whole[...], NT)
    token[...] = jnp.zeros(token.shape, FLOAT)


def hidden_kernel(rows_in, gain, first, second, third, fourth, hidden, unit, factor, normed):
    total = rows_in[...] + first[...] + second[...].astype(FLOAT) + third[...].astype(FLOAT) + fourth[...].astype(FLOAT)
    hidden[...] = total
    scale = lax.rsqrt(jnp.mean(total * total, axis=-1, keepdims=True) + EPS_NORM)
    factor[...] = scale
    unit[...] = total * scale
    normed[...] = (total * scale * gain[...]).astype(HALF)


def second_back_kernel(unit, factor, gain, cot_rows, first, second, third, fourth, d_hidden, gain_part, token):
    token[...] = jnp.zeros(token.shape, FLOAT)
    total = first[...] + second[...].astype(FLOAT) + third[...].astype(FLOAT) + fourth[...].astype(FLOAT)
    n = unit[...]
    gain_part[...] = jnp.sum(total * n, axis=0, keepdims=True)
    e = total * gain[...]
    mean = jnp.mean(e * n, axis=-1, keepdims=True)
    d_hidden[...] = (cot_rows[...].astype(FLOAT) + factor[...] * (e - n * mean)).astype(HALF)


def ffn_kernel(mine, own_in, other_in, gate_rows, up_rows, d_product, normed, product, d_gate, d_up, other, own, token, total):
    rows = own_in.shape[1]
    for head, ref, x in head_tiles(mine, own_in, other_in):
        normed[lane_block(head, rows), :] = ref[x]
    cols = gate_rows.shape[0]
    step = cols // 2
    for at in range(0, cols, step):
        span = slice(at, at + step)
        gate = mm(gate_rows[span, :], normed[...], NT)
        up = mm(up_rows[span, :], normed[...], NT)
        sig = sigmoid(gate)
        act = gate * sig
        product[span, :] = (act * up).astype(HALF)
        grad = d_product[span, :]
        dg = (grad * up * (sig * (1.0 + gate * (1.0 - sig)))).astype(HALF)
        du = (grad * act).astype(HALF)
        d_gate[span, :] = dg
        d_up[span, :] = du
    token[...] = jnp.zeros(token.shape, FLOAT)
    gate_turned = d_gate[...].T
    up_turned = d_up[...].T
    width = normed.shape[1]
    tile = width // 4
    core = mine[1]
    for at in range(0, width, tile):
        lanes = slice(at, at + tile)
        total[...] = mm(gate_turned, gate_rows[:, lanes]) + mm(up_turned, up_rows[:, lanes])
        spread_rows(core, total, own, other, rows, lanes)


def join_rows_kernel(mine, own, other, whole, own_cols):
    rows = own.shape[1]
    lanes = lane_block(mine[0] * 2 + mine[1], own_cols.shape[1])
    for head, ref, x in head_tiles(mine, own, other):
        whole[lane_block(head, rows), :] = ref[x]
        own_cols[lane_block(head, rows), :] = ref[x, :, lanes]


def split_sum_kernel(mine, own, arrived, *outs):
    for k in range(4):
        at = ring_place(mine[0], k)
        outs[k][...] = (own[at].astype(FLOAT) + arrived[at].astype(FLOAT)).astype(outs[k].dtype)
    outs[4][...] = jnp.zeros(outs[4].shape, FLOAT)


def head_scatter(own, other, mine, with_token=False, after=()):
    arrived = rotated(other, "c", 1)
    shape = own.shape[1:]
    shapes = (out(shape, FLOAT),) + (out(shape, HALF),) * 3 + (out((8, DK), FLOAT),)
    total, *sent, token = run(split_sum_kernel, shapes, (mine, own, arrived), scalars=1, after=after)
    parts = [total] + [rotated(part, "x", d) for d, part in zip(TURNS[1:], sent)]
    return (parts, token) if with_token else parts


def swapped(array, mask):
    return lax.ppermute(array, "x", [(i, i ^ mask) for i in range(4)])


def first_half_kernel(mine, own, arrived, keep, send):
    base = jnp.where(mine[0] < 2, 0, 2)
    for target, at in ((keep, base), (send, 2 - base)):
        for i in range(2):
            target[i] = (own[at + i].astype(FLOAT) + arrived[at + i].astype(FLOAT)).astype(target.dtype)


def second_half_kernel(mine, keep, arrived, own, send):
    at = lax.rem(mine[0], 2)
    own[...] = keep[at].astype(FLOAT) + arrived[at].astype(FLOAT)
    send[...] = (keep[1 - at].astype(FLOAT) + arrived[1 - at].astype(FLOAT)).astype(HALF)


def head_halving(own, other, mine, after):
    shape = own.shape[1:]
    pair = out((2, *shape), HALF)
    keep, send = run(
        first_half_kernel, (pair, pair), (mine, own, rotated(other, "c", 1)), scalars=1, after=after
    )
    total, send = run(
        second_half_kernel, (out(shape, FLOAT), out(shape, HALF)), (mine, keep, swapped(send, 2)), scalars=1
    )
    return [total, swapped(send, 1)]


def added(parts):
    total = parts[0]
    for part in parts[1:]:
        total = total + part.astype(FLOAT)
    return total


def dest_block(mine, k, o):
    core = mine[1]
    place = ring_place(jnp.where(core == 0, mine[3], mine[2]), k)
    return jnp.where(core == 0, o * 4 + place, place * 4 + o)


def store_tile(outs, k, o, early, value):
    count = early.shape[0]
    if k < 3:
        outs[k][o, :count, :] = early
        outs[k][o, count:, :] = value
    else:
        spare = outs[3].shape[1] - count
        outs[3][o, :count, :] = early
        outs[3][o, count:, :] = value[:spare]
        outs[4][o] = value[spare:]


def mixer_grad_kernel(mine, d_branch, gated, normed, d_pre, gate_rows, *refs):
    outs, (gain_out, gated_turned, pre_turned) = refs[:4], refs[4:]
    gated_turned[...] = gated[...].T
    pre_turned[...] = d_pre[...].T
    for k in range(4):
        for o in (0, 2):
            blocks = [lane_block(dest_block(mine, k, o + i), DK) for i in range(2)]
            mixer = mm(gated_turned[...], jnp.concatenate([d_branch[:, at] for at in blocks], axis=1))
            gate = mm(pre_turned[...], jnp.concatenate([normed[:, at] for at in blocks], axis=1))
            for i, at in enumerate(blocks):
                half = slice(i * DK, (i + 1) * DK)
                outs[k][o + i] = jnp.concatenate([mixer[:, half], gate[:, half]], axis=0).astype(HALF)
                gain_out[:, at] = jnp.sum(gate[:, half] * gate_rows[:, at].astype(FLOAT), axis=0, keepdims=True)


def in_grad_kernel(mine, normed, halo, dproj, d_logit, taps, mixer_gain, gate_gain, second_gain, first_gain, in_rows, beta_rows, *refs):
    early, outs, (token, turned_refs, extra) = refs[:4], refs[4:9], refs[9:]
    token[...] = jnp.zeros(token.shape, FLOAT)
    cols = dproj.shape[1]
    heads = 2
    turned_refs[:cols, :] = dproj[...].T
    turned_refs[cols:, :] = d_logit[...].astype(HALF)
    extra[...] = jnp.zeros(extra.shape, FLOAT)
    per_tap = cols // DK
    for j in range(4):
        for i in range(per_tap):
            extra[j * per_tap + i : j * per_tap + i + 1, :] = taps[j : j + 1, i * DK : (i + 1) * DK]
    for i in range(mixer_gain.shape[1] // DK):
        extra[32 + i : 33 + i, :] = mixer_gain[:, i * DK : (i + 1) * DK]
    for k in range(4):
        for o in (0, 2):
            blocks = [lane_block(dest_block(mine, k, o + i), DK) for i in range(2)]
            left = jnp.concatenate(
                [jnp.concatenate([halo[:, at], normed[:, at]], axis=0) for at in blocks], axis=1
            )
            grads = mm(turned_refs[...], left)
            for i, at in enumerate(blocks):
                half = slice(i * DK, (i + 1) * DK)
                beta = grads[cols : cols + heads, half]
                gain = (
                    jnp.sum(grads[:cols, half] * in_rows[:, at].astype(FLOAT), axis=0, keepdims=True)
                    + jnp.sum(beta * beta_rows[:heads, at].astype(FLOAT), axis=0, keepdims=True)
                    + gate_gain[:, at]
                )
                extra[36 : 36 + heads, :] = beta
                extra[40:41, :] = gain / first_gain[:, at]
                extra[41:42, :] = second_gain[:, at]
                store_tile(
                    outs, k, o + i, early[k][o + i], jnp.concatenate([grads[:cols, half], extra[...]], axis=0).astype(HALF)
                )


def ffn_grad_kernel(turns, mine, cot, normed, d_gate, d_up, product, *refs):
    outs, token = refs[:-1], refs[-1]
    token[...] = jnp.zeros(token.shape, FLOAT)
    cols = d_gate.shape[0]
    half_rows = 3 * cols // 2
    for k in turns:
        for o in (0, 2):
            blocks = [lane_block(dest_block(mine, k, o + i), DK) for i in range(2)]
            lefts = [jnp.concatenate([ref[:, at] for at in blocks], axis=1) for ref in (normed, cot)]
            for n, (right, left) in enumerate(((d_gate, lefts[0]), (d_up, lefts[0]), (product, lefts[1]))):
                both = mm(right[...], left).astype(HALF)
                for i in range(2):
                    tile = both[:, i * DK : (i + 1) * DK]
                    first = n * cols
                    if k < 3:
                        outs[turns.index(k)][o + i, first : first + cols, :] = tile
                    elif first + cols <= half_rows:
                        outs[0][o + i, first : first + cols, :] = tile
                    elif first >= half_rows:
                        outs[1][o + i, first - half_rows : first - half_rows + cols, :] = tile
                    else:
                        outs[0][o + i, first:, :] = tile[: half_rows - first]
                        outs[1][o + i, : first + cols - half_rows, :] = tile[half_rows - first :]


def ffn_grads(turns, mine, cot, normed, d_gate, d_up, product, after):
    rows = 3 * d_gate.shape[0]
    if turns == (3,):
        shapes = (out((4, rows // 2, DK), HALF),) * 2
    else:
        shapes = (out((4, rows, DK), HALF),) * len(turns)
    return run(
        partial(ffn_grad_kernel, turns),
        shapes + (out((8, DK), FLOAT),),
        (mine, cot, normed, d_gate, d_up, product),
        scalars=1,
        after=(after,),
    )


def gain_rows(ref):
    first = ref.shape[1] - EXTRA + 40
    return ref[:, first : first + 8, :].astype(FLOAT)


def last_relay_kernel(own, plus, minus, first, second, plus_out, minus_out, token, rows):
    relay_kernel(plus, minus, first, second, plus_out, minus_out, token)
    for i, ref in enumerate((own, plus_out, minus_out)):
        rows[i] = gain_rows(ref)


def quad_sum_kernel(first, second, third, fourth, own, plus, minus, token):
    token[...] = jnp.zeros(token.shape, FLOAT)
    for i, target in enumerate((own, plus, minus)):
        target[...] = (first[i] + second[i]) + (third[i] + fourth[i])


def relay_kernel(plus, minus, first, second, plus_out, minus_out, token):
    half = first.shape[1]
    plus_out[:, :half, :] = (plus[:, :half, :].astype(FLOAT) + first[...].astype(FLOAT)).astype(HALF)
    plus_out[:, half:, :] = plus[:, half:, :]
    minus_out[:, :half, :] = minus[:, :half, :]
    minus_out[:, half:, :] = (minus[:, half:, :].astype(FLOAT) + second[...].astype(FLOAT)).astype(HALF)
    token[...] = jnp.zeros(token.shape, FLOAT)


def relayed(parts, after, micros):
    shape = out(parts[1].shape, HALF)
    first, second = turned(parts[3], True, 1), turned(parts[4], True, -1)
    plus, minus, token = run(
        relay_kernel,
        (shape, shape, out((8, DK), FLOAT)),
        (parts[1], parts[2], first, second),
        after=after,
        micros=micros,
    )
    return (parts[0], turned(plus, True, 1), turned(minus, True, -1)), token


def last_sum_kernel(mine, own, plus, minus, own_rows, plus_rows, minus_rows, *outs):
    seq_sum_kernel(0, mine, own, plus, minus, *outs)
    rank = jnp.where(mine[1] == 0, mine[2], mine[3])
    first = outs[0].shape[0] - EXTRA + 32
    for k in range(4):
        place = ring_place(rank, k)
        old = own[place, first : first + 16, :].astype(FLOAT)
        old = old + plus[place, first : first + 16, :].astype(FLOAT) + minus[place, first : first + 16, :].astype(FLOAT)
        new = own_rows[place] + plus_rows[place] + minus_rows[place]
        outs[k][first : first + 16, :] = jnp.concatenate([old[:8], new], axis=0).astype(outs[k].dtype)


def seq_sum_kernel(early, mine, *refs):
    rank = jnp.where(mine[1] == 0, mine[2], mine[3])
    group, before = refs[:3], refs[3 : 3 + 4 * early]
    outs = refs[3 + 4 * early : 7 + 4 * early]
    refs[-1][...] = jnp.zeros(refs[-1].shape, FLOAT)
    for k in range(4):
        place = ring_place(rank, k)
        at = 0
        for i in range(early):
            source = before[4 * i + k]
            outs[k][at : at + source.shape[0], :] = source[...]
            at += source.shape[0]
        total = group[0][place].astype(FLOAT) + group[1][place].astype(FLOAT) + group[2][place].astype(FLOAT)
        outs[k][at:, :] = total.astype(outs[k].dtype)


def seq_sums(group, before, mine, after, micros):
    count = group[0].shape[1] + sum(sums[0].shape[0] for sums in before)
    shapes = (out((count, DK), FLOAT),) + (out((count, DK), HALF),) * 3
    shapes += (out((8, DK), FLOAT),)
    flat = [piece for sums in before for piece in sums]
    return run(
        partial(seq_sum_kernel, len(before)), shapes, (mine, *group, *flat), scalars=1, after=after, micros=micros
    )


def second_round(sums):
    return [sums[0]] + [turned(sums[i], False, TURNS[i]) for i in range(1, 4)]


def unpack_kernel(own, first, second, third, *outs):
    total = own[...] + first[...].astype(FLOAT) + second[...].astype(FLOAT) + third[...].astype(FLOAT)
    at = 0
    for target in outs[:5]:
        count = target.shape[1]
        target[...] = total[at : at + count, :].T
        at += count
    extra = total[at:, :]
    per_tap = 8
    first = 0
    for target in outs[5:8]:
        blocks = target.shape[1] // DK
        for j in range(4):
            for i in range(blocks):
                row = j * per_tap + first + i
                target[j : j + 1, i * DK : (i + 1) * DK] = extra[row : row + 1, :]
        first += blocks
    for i in range(outs[8].shape[1] // DK):
        outs[8][:, i * DK : (i + 1) * DK] = extra[32 + i : 33 + i, :]
    outs[9][...] = extra[36:38, :]
    outs[10][...] = extra[40:48, :]


def ffn_unpack_kernel(own, first, second, third, gate, up, down, token):
    cols = gate.shape[0]
    token[...] = jnp.zeros(token.shape, FLOAT)
    for n, target in enumerate((gate, up, down)):
        span = slice(n * cols, (n + 1) * cols)
        target[...] = (
            own[span, :]
            + first[span, :].astype(FLOAT)
            + second[span, :].astype(FLOAT)
            + third[span, :].astype(FLOAT)
        )


def output_kernel(own, first, second, third, total, token):
    token[...] = jnp.zeros(token.shape, FLOAT)
    total[...] = (
        own[...] + first[...].astype(FLOAT) + second[...].astype(FLOAT) + third[...].astype(FLOAT)
    ).astype(HALF)


def tile_of(i, mine):
    return (i % 4) * 2 + jnp.where(i < 4, 1 - mine[1], mine[1])


def whole_block(shape):
    return pl.BlockSpec(shape, lambda i, mine: (0,) * len(shape))


def tile_outs(rows, width):
    return [
        pl.BlockSpec((1, rows, width), lambda i, mine: (jnp.minimum(i, 3), 0, 0)),
        pl.BlockSpec((1, rows, width), lambda i, mine: (jnp.maximum(i - 4, 0), 0, 0)),
    ]


def down_kernel(mine, product, weight, hidden, other, own, token, scratch):
    step = pl.program_id(0)
    rows = hidden.shape[0]

    @pl.when(step == 0)
    def _():
        scratch[...] = product[...].T

    part = mm(scratch[...], weight[...])
    here = lane_block(mine[0] * 2 + mine[1], rows)
    for target, wanted in ((other, step < 4), (own, step >= 4)):

        @pl.when(wanted)
        def _():
            target[0] = part.astype(HALF)
            target[0, here, :] = (target[0, here, :].astype(FLOAT) + hidden[...]).astype(HALF)

    token[...] = jnp.zeros(token.shape, FLOAT)


def down_tiles(mine, product, weight, hidden):
    cols, tokens = product.shape
    width = weight.shape[1] // 8
    spec = pltpu.PrefetchScalarGridSpec(
        num_scalar_prefetch=1,
        grid=(8,),
        in_specs=[
            whole_block(product.shape),
            pl.BlockSpec((cols, width), lambda i, mine: (0, tile_of(i, mine))),
            pl.BlockSpec((hidden.shape[0], width), lambda i, mine: (0, tile_of(i, mine))),
        ],
        out_specs=tile_outs(tokens, width) + [whole_block((8, DK))],
        scratch_shapes=[pltpu.VMEM((tokens, cols), HALF)],
    )
    tiles = out((4, tokens, width), HALF)
    return pl.pallas_call(
        down_kernel,
        grid_spec=spec,
        out_shape=(tiles, tiles, out((8, DK), FLOAT)),
        compiler_params=pltpu.CompilerParams(vmem_limit_bytes=16 * 2**20),
        cost_estimate=cost(4.0),
    )(mine, product, weight, hidden)


def d_first_kernel(mine, dproj, d_pre, d_logit, sums, in_rows, gate_rows, beta_rows, after, other, own, token, sum_rows):
    step = pl.program_id(0)
    tokens = d_pre.shape[0]
    width = own.shape[2]

    @pl.when(step == 0)
    def _():
        row = jnp.broadcast_to(sums[HALO:, :], (tokens, DK)).T
        sum_rows[...] = jnp.zeros(sum_rows.shape, FLOAT)
        for i in range(tokens // width):
            sum_rows[i : i + 1, :] = row[0:1, i * width : (i + 1) * width]
        sum_rows[2:3, 0:HALO] = jnp.broadcast_to(sums[:HALO, :], (HALO, DK)).T[0:1, :]

    part = mm(dproj[...], in_rows[...])
    late = mm(d_pre[...], gate_rows[...])
    for h in range(2):
        late = late + d_logit[:, h : h + 1] * beta_rows[h : h + 1, :].astype(FLOAT)
    for target, wanted in ((other, step < 4), (own, step >= 4)):

        @pl.when(wanted)
        def _():
            target[0, :HALO, :] = part[:HALO].astype(HALF)
            target[0, HALO : HALO + tokens, :] = (part[HALO:] + late).astype(HALF)
            target[0, HALO + tokens :, :] = sum_rows[...].astype(HALF)

    token[...] = jnp.zeros(token.shape, FLOAT)


def d_first_tiles(mine, dproj, d_pre, d_logit, sums, in_rows, gate_rows, beta_rows, after):
    tokens = d_pre.shape[0]
    width = in_rows.shape[1] // 8
    count = tokens + 2 * HALO

    def tile(rows):
        return pl.BlockSpec((rows, width), lambda i, mine: (0, tile_of(i, mine)))

    spec = pltpu.PrefetchScalarGridSpec(
        num_scalar_prefetch=1,
        grid=(8,),
        in_specs=[whole_block(a.shape) for a in (dproj, d_pre, d_logit, sums)]
        + [tile(in_rows.shape[0]), tile(gate_rows.shape[0]), tile(beta_rows.shape[0])]
        + [pl.BlockSpec(memory_space=pl.ANY)],
        out_specs=tile_outs(count, width) + [whole_block((8, DK))],
        scratch_shapes=[pltpu.VMEM((HALO, width), FLOAT)],
    )
    tiles = out((4, count, width), HALF)
    return pl.pallas_call(
        d_first_kernel,
        grid_spec=spec,
        out_shape=(tiles, tiles, out((8, DK), FLOAT)),
        compiler_params=pltpu.CompilerParams(vmem_limit_bytes=16 * 2**20),
        cost_estimate=cost(6.0),
    )(mine, dproj, d_pre, d_logit, sums, in_rows, gate_rows, beta_rows, after)


def first_total_kernel(own, arrived, total, pack, token):
    token[...] = jnp.zeros(token.shape, FLOAT)
    whole = own[...] + arrived[...].astype(FLOAT)
    total[...] = whole
    pack[:HALO, :] = whole[:HALO]
    at = whole.shape[0] - HALO
    pack[HALO:, :] = whole[at : at + 8]


def input_grad_kernel(mine, total, arrived, block_input, factor, gain, d_branch, grad):
    tokens, width = block_input.shape
    columns = []
    for i in range(tokens // width):
        row = total[HALO + tokens + i : HALO + tokens + i + 1, :]
        columns.append(jnp.broadcast_to(row, (DK, width)).T[:, 0:1])
    late_row = jnp.broadcast_to(arrived[HALO + 2 : HALO + 3, :], (DK, width)).T[:HALO, 0:1]
    mean = jnp.concatenate(columns, axis=0) / (8 * width)
    scale = factor[...]
    unit = block_input[...].astype(FLOAT) * scale
    gain_own = gain[:, lane_block(mine[0] * 2 + mine[1], width)]
    grad[...] = d_branch[...].astype(FLOAT) + scale * (total[HALO : HALO + tokens, :] * gain_own - unit * mean)
    last = slice(tokens - HALO, tokens)
    grad[last, :] += scale[last] * (arrived[:HALO, :] * gain_own - unit[last] * (late_row / (8 * width)))


def next_block(array, distance):
    size = 16
    route = [(i, i + distance) for i in range(size) if 0 <= i + distance < size]
    return lax.ppermute(array, SEQ, route)


def dot_nt(a, b):
    return lax.dot_general(a, b, NT, preferred_element_type=FLOAT)


def shards(
    block_input,
    log_decay,
    first_gain,
    query_weight,
    key_weight,
    value_weight,
    gate_weight,
    beta_weight,
    query_conv,
    key_conv,
    value_conv,
    mixer_gain,
    mixer_weight,
    second_gain,
    swiglu_gate,
    swiglu_up,
    swiglu_down,
    cotangent,
):
    heads = log_decay.shape[1]
    tokens, width = block_input.shape
    model = 8 * width
    chunks = tokens // CH
    rows = tokens // 8
    kq, vd = heads * DK, heads * DV
    cols = 2 * kq + vd
    hidden_cols = swiglu_gate.shape[1]
    mine = jnp.stack([lax.axis_index(name) for name in ("x", "c", "y", "z")]).astype(jnp.int32)

    token_out = out((8, DK), FLOAT)
    in_rows, gate_rows, gcol, grow, token = run(
        setup_kernel,
        (
            out((cols, model), HALF),
            out((vd, model), HALF),
            out((tokens, heads), FLOAT),
            out((heads * chunks, CH), FLOAT),
            token_out,
        ),
        (query_weight, key_weight, value_weight, gate_weight, log_decay.T),
        micros=3.0,
    )
    beta_rows = jnp.pad(beta_weight.T, ((0, HALO - heads), (0, 0)))
    taps = jnp.concatenate([query_conv.T, key_conv.T, value_conv.T], axis=1)
    gain_row = mixer_gain.reshape(1, -1)
    first_row = first_gain.reshape(1, -1)

    first_normed, first_factor, my_rows, logits, halo_rows = run(
        first_norm_kernel,
        (
            out((tokens, model), HALF),
            out((tokens, 1), FLOAT),
            out((rows, model), FLOAT),
            out((tokens, HALO), FLOAT),
            out((HALO, model), HALF),
        ),
        (mine, first_row, beta_rows, *head_gather(block_input, mine, (token,))),
        scalars=1,
        micros=3.0,
    )
    halo_normed = next_block(halo_rows, 1)
    proj = dot_nt(first_normed, in_rows).astype(HALF)
    halo_proj = dot_nt(halo_normed, in_rows).astype(HALF)
    gate_pre = dot_nt(first_normed, gate_rows)
    k, v, tri, n, b, w, u, pay, pay_token = run(
        partial(prepare_kernel, heads, chunks),
        prepare_shapes(heads, chunks) + (token_out,),
        (proj, halo_proj, taps, logits, gcol, grow),
        [pltpu.VMEM((HALO + tokens, cols), FLOAT)],
        micros=8.0,
        kept=range(7),
        megs=20,
    )
    near_pieces = ring_pieces(pay, "z")
    q, p, query_token = run(
        partial(query_kernel, heads, chunks),
        (out((tokens, kq), HALF), out((heads * chunks, CH, CH), HALF), token_out),
        (proj, halo_proj, taps, k, gcol, grow),
        [pltpu.VMEM((HALO + tokens, kq), FLOAT)],
        after=(pay_token,),
    )
    before, group, near, group_token = run(
        partial(group_kernel, heads), group_shapes(heads) + (token_out,), (mine, *near_pieces), scalars=1, after=(gate_pre[:8, :DK], query_token), micros=2.0
    )
    half_tiles = out((4, rows, model), HALF)
    states, vns, mixed, gated, branch_other, branch_own, far, mix_token = run(
        partial(mix_kernel, heads, chunks),
        mix_shapes(heads, chunks)[:4] + (half_tiles, half_tiles) + mix_shapes(heads, chunks)[4:] + (token_out,),
        (mine, *ring_pieces(group, "y"), before, q, k, w, u, p, n, b, gcol, gate_pre, gain_row, mixer_weight),
        [pltpu.VMEM((tokens, model // 4), FLOAT)],
        scalars=1,
        kept=(0, 1, 2, 6),
        megs=16,
        micros=4.0,
    )
    branch = head_scatter(branch_own, branch_other, mine)
    (cot,), _ = passed([cotangent], (group_token,))
    cot_tiles = head_gather(cot, mine, (mix_token,))
    whole_cot, cot_rows, d_product, token = run(
        product_grad_kernel,
        (out((tokens, model), HALF), out((rows, model), HALF), out((hidden_cols, tokens), FLOAT), token_out),
        (mine, *cot_tiles, swiglu_down.T),
        scalars=1,
        micros=4.0,
    )
    wide_rows = out((rows, model), FLOAT)
    second_row = second_gain.reshape(1, -1)
    hidden, second_unit, second_factor, own_normed = run(
        hidden_kernel,
        (wide_rows, wide_rows, out((rows, 1), FLOAT), out((rows, model), HALF)),
        (my_rows, second_row, *branch),
        after=(token,),
    )
    turned_out = out((hidden_cols, tokens), HALF)
    second_normed, product, d_gate, d_up, second_other, second_own, ffn_token = run(
        ffn_kernel,
        (out((tokens, model), HALF), turned_out, turned_out, turned_out, half_tiles, half_tiles, token_out),
        (
            mine,
            *head_gather(own_normed, mine),
            swiglu_gate.T,
            swiglu_up.T,
            d_product,
        ),
        [pltpu.VMEM((tokens, model // 4), FLOAT)],
        scalars=1,
        micros=9.0,
        megs=20,
    )
    second_parts, token = head_scatter(second_own, second_other, mine, True)
    grad_args = (mine, whole_cot, second_normed, d_gate, d_up, product)
    *ffn_ends, token = ffn_grads((3,), *grad_args, token)
    ffn_plus, ffn_minus, token = ffn_grads((1, 2), *grad_args, token)
    d_hidden, second_gain_part, back_token = run(
        second_back_kernel,
        (out((rows, model), HALF), out((1, model), FLOAT), token_out),
        (second_unit, second_factor, second_row, cot_rows, *second_parts),
        after=(token,),
    )
    ffn_group, ffn_token = relayed([None, ffn_plus, ffn_minus, *ffn_ends], (back_token,), 3.0)
    down_other, down_own, down_token = down_tiles(mine, product, swiglu_down.T, hidden)
    d_branch, d_branch_own = run(
        join_rows_kernel,
        (out((tokens, model), HALF), out((tokens, width), HALF)),
        (mine, *head_gather(d_hidden, mine, (down_token, ffn_token))),
        scalars=1,
    )
    d_gated = jnp.dot(d_branch, mixer_weight, preferred_element_type=FLOAT)
    dos, dvns, es, d_gate_pre, gain_part, gate_sums, ends = run(
        partial(gate_back_kernel, heads, chunks),
        gate_back_shapes(heads, chunks),
        (d_gated, mixed, gate_pre, gain_row, q, w, p, n, gcol),
        micros=4.0,
    )
    ffn_own, token = ffn_grads((0,), *grad_args, gate_sums[:8])
    *ffn_sums, ffn_token = seq_sums((ffn_own, *ffn_group[1:]), (), mine, (), 3.0)
    tile = out((4, 2 * vd, DK), HALF)
    *mixer_parts, gate_gain = run(
        mixer_grad_kernel,
        (tile,) * 4 + (out((1, model), FLOAT),),
        (mine, d_branch, gated, first_normed, d_gate_pre, gate_rows),
        [pltpu.VMEM((vd, tokens), HALF), pltpu.VMEM((vd, tokens), HALF)],
        scalars=1,
        micros=5.0,
    )
    after, group_end, _, group_token = run(
        partial(group_back_kernel, heads),
        group_back_shapes(heads) + (token_out,),
        (mine, near, *ring_pieces(ends, "z")),
        scalars=1,
        after=(gate_gain, ffn_token),
        micros=2.0,
    )
    end_pieces = ring_pieces(group_end, "y")
    square = out((heads * chunks, CH, CH), FLOAT)
    *slopes, slope_token = run(
        partial(slopes_kernel, heads, chunks),
        (out((tokens, cols), FLOAT), square, square, out((tokens, vd), FLOAT), token_out),
        (k, v, states, gcol, grow, proj, halo_proj, taps),
        [pltpu.VMEM((HALO + tokens, cols), FLOAT)],
        after=(group_token,),
    )
    passed_sums, ffn_token = passed(ffn_sums, (*end_pieces[1:], slope_token))
    dproj, d_logit, logit_rows, taps_part, sums = run(
        partial(back_kernel, heads, chunks),
        back_shapes(heads, chunks),
        (mine, far, *end_pieces, after, q, k, logits, gate_sums, gcol, tri, states, vns, dos, dvns, es, n, proj, halo_proj, taps, *slopes),
        back_scratch(heads, chunks),
        scalars=1,
        after=(ffn_token,),
        micros=11.0,
        megs=30,
    )
    packed = 2 * vd + cols + EXTRA
    tile, half_tile = out((4, packed, DK), HALF), out((4, packed // 2, DK), HALF)
    *in_parts, in_token = run(
        in_grad_kernel,
        (tile,) * 3 + (half_tile,) * 2 + (token_out,),
        (mine, first_normed, halo_normed, dproj, logit_rows, taps_part, gain_part, gate_gain, second_gain_part, first_row, in_rows, beta_rows, *mixer_parts),
        [pltpu.VMEM((cols + HALO, HALO + tokens), HALF), pltpu.VMEM((EXTRA, DK), FLOAT)],
        scalars=1,
        micros=6.0,
        megs=16,
    )
    ffn_grad_out = out((hidden_cols, DK), FLOAT)
    grad_gate, grad_up, grad_down, ffn_token = run(
        ffn_unpack_kernel, (ffn_grad_out,) * 3 + (token_out,), second_round(passed_sums), after=(in_token,)
    )
    in_ends, in_token = passed(in_parts[3:], (ffn_token,))
    in_parts = in_parts[:3] + in_ends
    first_other, first_own, first_token = d_first_tiles(
        mine, dproj, d_gate_pre, d_logit, sums, in_rows, gate_rows, beta_rows, in_token
    )
    output, out_token = run(
        output_kernel,
        (out((tokens, width), HALF), token_out),
        head_scatter(down_own, down_other, mine, after=(in_token,)),
    )
    tile = out((4, packed, DK), HALF)
    plus, minus, in_token, rows_left = run(
        last_relay_kernel,
        (tile, tile, token_out, out((3, 4, 8, DK), FLOAT)),
        (*in_parts[:3], turned(in_parts[3], True, 1), turned(in_parts[4], True, -1)),
        after=(first_token, out_token),
    )
    in_group = (in_parts[0], turned(plus, True, 1), turned(minus, True, -1))
    own_rows, plus_rows, minus_rows, gain_token = run(
        quad_sum_kernel, (out((4, 8, DK), FLOAT),) * 3 + (token_out,), ring_pieces(rows_left, "x"), after=(in_token,)
    )
    total, pack, first_token = run(
        first_total_kernel,
        (out((tokens + 2 * HALO, width), FLOAT), out((HALO + 8, width), FLOAT), token_out),
        head_halving(first_own, first_other, mine, (gain_token,)),
    )
    *sums_out, sum_token = run(
        last_sum_kernel,
        (out((packed, DK), FLOAT),) + (out((packed, DK), HALF),) * 3 + (token_out,),
        (mine, *in_group, own_rows, turned(plus_rows, True, 1), turned(minus_rows, True, -1)),
        scalars=1,
    )
    totals = [sums_out[0]] + [turned(sums_out[i], False, TURNS[i]) for i in range(1, 4)]
    grad_mixer_weight, grad_gate_weight, grad_query, grad_key, grad_value, *taps_grad, gain_grad, beta_grad, both = run(
        unpack_kernel,
        tuple(out((DK, count), FLOAT) for count in (vd, vd, kq, kq, vd)) + tuple(out((rows_, count), FLOAT) for rows_, count in ((4, kq), (4, kq), (4, vd), (1, vd), (heads, DK), (8, DK))),
        totals,
    )
    grad_input = run(
        input_grad_kernel,
        (out((tokens, width), FLOAT),),
        (mine, total, next_block(pack, -1), block_input, first_factor, first_row, d_branch_own),
        scalars=1,
    )[0]
    both = both + rotated(both, "c", 1)
    return (
        output,
        grad_input,
        both[0],
        grad_query,
        grad_key,
        grad_value,
        grad_gate_weight,
        beta_grad.T,
        taps_grad[0].T,
        taps_grad[1].T,
        taps_grad[2].T,
        gain_grad.reshape(-1),
        grad_mixer_weight,
        both[1],
        grad_gate.T,
        grad_up.T,
        grad_down.T,
    )


def solution(mesh):
    torus = Mesh(mesh.devices.reshape(4, 4, 4, 2), SEQ + HEAD)
    in_specs = (
        P(SEQ, HEAD),
        P(SEQ, HEAD),
        P(),
        P(None, HEAD),
        P(None, HEAD),
        P(None, HEAD),
        P(None, HEAD),
        P(None, HEAD),
        P(HEAD, None),
        P(HEAD, None),
        P(HEAD, None),
        P(HEAD),
        P(None, HEAD),
        P(),
        P(None, HEAD),
        P(None, HEAD),
        P(None, HEAD),
        P(SEQ, HEAD),
    )
    out_specs = (
        P(SEQ, HEAD),
        P(SEQ, HEAD),
        P(SEQ),
        P(SEQ, HEAD),
        P(SEQ, HEAD),
        P(SEQ, HEAD),
        P(SEQ, HEAD),
        P(SEQ, HEAD),
        P(HEAD, None),
        P(HEAD, None),
        P(HEAD, None),
        P(HEAD),
        P(SEQ, HEAD),
        P(SEQ),
        P(SEQ, HEAD),
        P(SEQ, HEAD),
        P(SEQ, HEAD),
    )
    return jax.shard_map(
        shards, mesh=torus, in_specs=in_specs, out_specs=out_specs, check_vma=False
    )
```

```python
from functools import partial

import jax
import jax.numpy as jnp
from jax import lax
from jax.experimental import pallas as pl
from jax.experimental.pallas import tpu as pltpu
from jax.sharding import Mesh
from jax.sharding import PartitionSpec as P

DK = 128
DV = 256
CH = 128
EPS_NORM = 1e-06
EPS_GATE = 1e-05
FLOAT = jnp.float32
HALF = jnp.bfloat16
NN = (((1,), (0,)), ((), ()))
NT = (((1,), (1,)), ((), ()))
TN = (((0,), (0,)), ((), ()))


def mm(a, b, dims=NN):
    return lax.dot_general(a.astype(HALF), b.astype(HALF), dims, preferred_element_type=FLOAT)


def halves(a):
    high = a.astype(HALF)
    return high, (a - high.astype(FLOAT)).astype(HALF)


def mm2(a, b, dims=NN):
    high, low = halves(b)
    return mm(a, high, dims) + mm(a, low, dims)


def mm3(a, b, dims=NN):
    a_high, a_low = halves(a)
    b_high, b_low = halves(b)
    return mm(a_high, b_high, dims) + (mm(a_high, b_low, dims) + mm(a_low, b_high, dims))


def sigmoid(v):
    return 1.0 / (1.0 + jnp.exp(-v))


def square_masks():
    rows = lax.broadcasted_iota(jnp.int32, (CH, CH), 0)
    cols = lax.broadcasted_iota(jnp.int32, (CH, CH), 1)
    return rows, cols


def decay_matrix(gcol, grow):
    rows, cols = square_masks()
    return jnp.where(rows >= cols, jnp.exp(jnp.minimum(gcol - grow, 0.0)), 0.0)


def conv_of(wide, taps, start, count, lanes):
    total = wide[HALO - 3 + start : HALO - 3 + start + count, lanes] * taps[0:1, lanes]
    for j in range(1, 4):
        total = total + wide[HALO - 3 + j + start : HALO - 3 + j + start + count, lanes] * taps[j : j + 1, lanes]
    return total


def query_kernel(heads, chunks, proj, halo, taps, k, gcol, grow, q_out, p_out, token, wide):
    token[...] = jnp.zeros(token.shape, FLOAT)
    kq = heads * DK
    wide[:HALO, :] = halo[:, :kq].astype(FLOAT)
    wide[HALO:, :] = proj[:, :kq].astype(FLOAT)
    for h in range(heads):
        for c in range(chunks):
            span = slice(c * CH, (c + 1) * CH)
            lanes = slice(h * DK, (h + 1) * DK)
            at = h * chunks + c
            cq = conv_of(wide, taps, c * CH, CH, lanes)
            query = (cq * sigmoid(cq)).astype(HALF)
            q_out[span, lanes] = query
            spread = decay_matrix(gcol[span, h : h + 1], grow[at : at + 1, :])
            p_out[at] = (spread * mm(query, k[span, lanes], NT)).astype(HALF)


def prepare_kernel(heads, chunks, proj, halo, taps, logits, gcol, grow, k_out, v_out, t_out, n_out, b_out, w_out, u_out, pay, token, wide):
    token[...] = jnp.zeros(token.shape, FLOAT)
    rows, cols = square_masks()
    differ = rows ^ cols
    eye = jnp.where(rows == cols, 1.0, 0.0)
    wide[:HALO, :] = halo[...].astype(FLOAT)
    wide[HALO:, :] = proj[...].astype(FLOAT)
    kq = heads * DK
    work = [(h, c) for h in range(heads) for c in range(chunks)]
    low, keys, sides = {}, {}, {}
    for h, c in work:
        span = slice(c * CH, (c + 1) * CH)
        ql, kl, vl = (
            slice(h * DK, (h + 1) * DK),
            slice(kq + h * DK, kq + (h + 1) * DK),
            slice(2 * kq + h * DV, 2 * kq + (h + 1) * DV),
        )
        ck = conv_of(wide, taps, c * CH, CH, kl)
        act = ck * sigmoid(ck)
        key = (act * lax.rsqrt(jnp.sum(act * act, axis=-1, keepdims=True) + EPS_NORM)).astype(HALF)
        cv = conv_of(wide, taps, c * CH, CH, vl)
        value = (cv * sigmoid(cv)).astype(HALF)
        k_out[span, ql] = key
        v_out[span, h * DV : (h + 1) * DV] = value
        beta = sigmoid(logits[span, h : h + 1])
        g = gcol[span, h : h + 1]
        spread = decay_matrix(g, grow[h * chunks + c : h * chunks + c + 1, :])
        inner = mm(key, key, NT)
        low[h, c] = jnp.where(rows > cols, beta * spread * inner, 0.0)
        keys[h, c] = key
        sides[h, c] = jnp.concatenate([(beta * jnp.exp(g)) * key.astype(FLOAT), beta * value.astype(FLOAT)], axis=1)
    tri = {at: eye - jnp.where(differ < 2, low[at], 0.0) for at in work}
    size = 2
    while size < CH:
        part = {at: mm3(jnp.where((differ >= size) & (differ < 2 * size), low[at], 0.0), tri[at]) for at in work}
        tri = {at: tri[at] - mm3(tri[at], part[at]) for at in work}
        size *= 2
    steps = {}
    for h, c in work:
        at = h * chunks + c
        t_out[at] = tri[h, c].astype(HALF)
        solved = mm3(tri[h, c], sides[h, c])
        w_out[at] = solved[:, :DK].astype(HALF)
        u_out[at] = solved[:, DK:].astype(HALF)
        g = gcol[c * CH : (c + 1) * CH, h : h + 1]
        last = gcol[(c + 1) * CH - 1 : (c + 1) * CH, h : h + 1]
        step = mm2(keys[h, c], jnp.exp(last - g) * solved, TN)
        n_out[at] = step[:, :DK].astype(HALF)
        b_out[at] = step[:, DK:]
        steps[h, c] = (jnp.exp(last), step)
    zero = jnp.zeros((DK, DK), FLOAT)
    for h in range(heads):
        decay, step = steps[h, 0]
        total = jnp.concatenate([decay * eye - step[:, :DK], step[:, DK:]], axis=1)
        whole = decay
        for c in range(1, chunks):
            decay, step = steps[h, c]
            total = decay * total - mm3(step[:, :DK], total) + jnp.concatenate([zero, step[:, DK:]], axis=1)
            whole = whole * decay
        pack_map(pay, h, total, whole, eye)


def whole_decay(pay, j, h):
    return pay[j, h, DK : DK + 1, 0:1].astype(FLOAT) + pay[j, h, DK + 8 : DK + 9, 0:1].astype(FLOAT)


def apply_whole(pay, j, h, state, dims):
    return whole_decay(pay, j, h) * state + mm(pay[j, h, :DK, :DK], state, dims)


def pack_map(pay, h, total, whole, eye):
    pay[h, :DK, :] = jnp.concatenate([total[:, :DK] - whole * eye, total[:, DK:]], axis=1).astype(HALF)
    rest = jnp.broadcast_to(whole, (8, DK + DV))
    first = rest.astype(HALF).astype(FLOAT)
    pay[h, DK:, :] = jnp.concatenate([first, rest - first], axis=0).astype(HALF)


def group_kernel(heads, mine, p0, p1, p2, p3, before, group, near, token):
    token[...] = jnp.zeros(token.shape, FLOAT)
    me = mine[3]
    for k, piece in enumerate((p0, p1, p2, p3)):
        near[ring_place(me, k)] = piece[...]
    rows, cols = square_masks()
    eye = jnp.where(rows == cols, 1.0, 0.0)
    zero = jnp.zeros((DK, DK), FLOAT)
    start = jnp.concatenate([eye, jnp.zeros((DK, DV), FLOAT)], axis=1)
    totals, keeps, wholes = [start] * heads, [start] * heads, [jnp.ones((1, 1), FLOAT)] * heads
    for j in range(near.shape[0]):
        for h in range(heads):
            added = jnp.concatenate([zero, near[j, h, :DK, DK:].astype(FLOAT)], axis=1)
            if j == 0:
                moved = jnp.concatenate([whole_decay(near, j, h) * eye + near[j, h, :DK, :DK].astype(FLOAT), added[:, DK:]], axis=1)
            else:
                moved = apply_whole(near, j, h, totals[h], NN) + added
            totals[h] = moved
            wholes[h] = wholes[h] * whole_decay(near, j, h)
            keeps[h] = jnp.where(me == j + 1, moved, keeps[h])
    for h in range(heads):
        before[h] = keeps[h]
        pack_map(group, h, totals[h], wholes[h], eye)


def group_back_kernel(heads, mine, near, p0, p1, p2, p3, after, group, ends, token):
    token[...] = jnp.zeros(token.shape, FLOAT)
    me = mine[3]
    for k, piece in enumerate((p0, p1, p2, p3)):
        ends[ring_place(me, k)] = piece[...]
    rows, cols = square_masks()
    eye = jnp.where(rows == cols, 1.0, 0.0)
    zero = jnp.zeros((DK, DK), FLOAT)
    start = jnp.concatenate([eye, jnp.zeros((DK, DV), FLOAT)], axis=1)
    totals, keeps = [start] * heads, [start] * heads
    for j in reversed(range(near.shape[0])):
        for h in range(heads):
            keeps[h] = jnp.where(me == j, totals[h], keeps[h])
            added = jnp.concatenate([zero, ends[j, h].astype(FLOAT)], axis=1)
            totals[h] = apply_whole(near, j, h, totals[h], TN) + added
    for h in range(heads):
        after[h] = keeps[h]
        group[h] = totals[h][:, DK:].astype(HALF)


def spread_rows(core, total, own, other, rows, lanes):
    for x in range(4):
        mine = pl.ds(pl.multiple_of((2 * x + core) * rows, rows), rows)
        away = pl.ds(pl.multiple_of((2 * x + 1 - core) * rows, rows), rows)
        own[x, :, lanes] = total[mine, :].astype(HALF)
        other[x, :, lanes] = total[away, :].astype(HALF)


def mix_kernel(heads, chunks, mine, p0, p1, p2, p3, before, q, k, w, u, p, n, b, gcol, gate, gain, weight, s_out, vn_out, o_out, gated, other, own, pay, token, total):
    token[...] = jnp.zeros(token.shape, FLOAT)
    ranks = pay.shape[0]
    me = mine[2]
    for at, piece in enumerate((p0, p1, p2, p3)):
        pay[ring_place(me, at)] = piece[...]
    states = [jnp.zeros((DK, DV), FLOAT) for h in range(heads)]
    for j in range(ranks - 1):
        passed = j < me
        for h in range(heads):
            moved = apply_whole(pay, j, h, states[h], NN) + pay[j, h, :DK, DK:].astype(FLOAT)
            states[h] = jnp.where(passed, moved, states[h])
    for h in range(heads):
        states[h] = mm3(before[h, :, :DK], states[h]) + before[h, :, DK:]
    for c in range(chunks):
        span = slice(c * CH, (c + 1) * CH)
        for h in range(heads):
            at = h * chunks + c
            state = states[h].astype(HALF)
            s_out[at] = state
            g = gcol[span, h : h + 1]
            last = gcol[(c + 1) * CH - 1 : (c + 1) * CH, h : h + 1]
            vn = (u[at].astype(FLOAT) - mm(w[at], state)).astype(HALF)
            vn_out[at] = vn
            out = jnp.exp(g) * mm(q[span, h * DK : (h + 1) * DK], state) + mm(p[at], vn)
            vl = slice(h * DV, (h + 1) * DV)
            o_out[span, vl] = out
            factor = lax.rsqrt(jnp.mean(out * out, axis=-1, keepdims=True) + EPS_GATE)
            pre = gate[span, vl]
            gated[span, vl] = (out * factor * gain[:, vl] * (pre * sigmoid(pre))).astype(HALF)
            if c + 1 < chunks:
                states[h] = jnp.exp(last) * states[h] - mm(n[at], state) + b[at]
    width = weight.shape[0]
    tile = total.shape[1]
    rows = own.shape[1]
    for at in range(0, width, tile):
        lanes = slice(at, at + tile)
        total[...] = mm(gated[...], weight[lanes, :], NT)
        spread_rows(mine[1], total, own, other, rows, lanes)


def gate_back_kernel(heads, chunks, d_gated, out, gate, gain, q, w, p, n, gcol, do_out, dvn_out, e_out, dpre_out, dgain_out, sums_out, pay):
    dgain = [jnp.zeros((1, DV), FLOAT) for h in range(heads)]
    ends = [None] * heads
    for c in reversed(range(chunks)):
        span = slice(c * CH, (c + 1) * CH)
        for h in range(heads):
            at = h * chunks + c
            vl = slice(h * DV, (h + 1) * DV)
            dg, o, pre, gn = d_gated[span, vl], out[span, vl], gate[span, vl], gain[:, vl]
            sig = sigmoid(pre)
            factor = lax.rsqrt(jnp.mean(o * o, axis=-1, keepdims=True) + EPS_GATE)
            m = o * factor
            s = pre * sig
            dgm = dg * m
            dgain[h] = dgain[h] + jnp.sum(dgm * s, axis=0, keepdims=True)
            dpre = dgm * gn * (sig * (1.0 + pre * (1.0 - sig)))
            dpre_out[span, vl] = dpre.astype(HALF)
            row_sum = jnp.sum(dpre * pre, axis=-1, keepdims=True)
            sums_out[span, :] = row_sum if h == 0 else sums_out[span, :] + row_sum
            e = dg * gn * s
            dout = factor * (e - m * jnp.mean(e * m, axis=-1, keepdims=True))
            do_out[span, vl] = dout.astype(HALF)
            g = gcol[span, h : h + 1]
            last = gcol[(c + 1) * CH - 1 : (c + 1) * CH, h : h + 1]
            dvn = mm(p[at], dout, TN)
            dvn_out[at] = dvn
            source = mm(q[span, h * DK : (h + 1) * DK], jnp.exp(g) * dout, TN) - mm(w[at], dvn, TN)
            e_out[at] = source
            if ends[h] is None:
                ends[h] = source
            else:
                ends[h] = jnp.exp(last) * ends[h] - mm(n[at], ends[h], TN) + source
    for h in range(heads):
        pay[h] = ends[h].astype(HALF)
        dgain_out[0:1, h * DV : (h + 1) * DV] = dgain[h]


def slopes_kernel(heads, chunks, k, v, states, gcol, grow, proj, halo, taps, slopes, inner_out, spread_out, rest, token, wide):
    token[...] = jnp.zeros(token.shape, FLOAT)
    kq = heads * DK
    wide[:HALO, :] = halo[...].astype(FLOAT)
    wide[HALO:, :] = proj[...].astype(FLOAT)
    for h in range(heads):
        for c in range(chunks):
            span = slice(c * CH, (c + 1) * CH)
            at = h * chunks + c
            kl = slice(kq + h * DK, kq + (h + 1) * DK)
            for lanes in (slice(h * DK, (h + 1) * DK), slice(2 * kq + h * DV, 2 * kq + (h + 1) * DV)):
                pre = conv_of(wide, taps, c * CH, CH, lanes)
                sig = sigmoid(pre)
                slopes[span, lanes] = sig * (1.0 + pre * (1.0 - sig))
            pre = conv_of(wide, taps, c * CH, CH, kl)
            sig = sigmoid(pre)
            act = pre * sig
            unit = lax.rsqrt(jnp.sum(act * act, axis=-1, keepdims=True) + EPS_NORM)
            slopes[span, kl] = unit * (sig * (1.0 + pre * (1.0 - sig)))
            key = k[span, h * DK : (h + 1) * DK]
            g = gcol[span, h : h + 1]
            inner_out[at] = mm(key, key, NT)
            spread_out[at] = decay_matrix(g, grow[at : at + 1, :])
            vl = slice(h * DV, (h + 1) * DV)
            rest[span, vl] = v[span, vl].astype(FLOAT) - jnp.exp(g) * mm(key, states[at])


def back_kernel(heads, chunks, mine, pay, p0, p1, p2, p3, after, q, k, logits, gate_sums, gcol, tri, states, vns, dos, dvns, es, ns, proj, halo, taps, slopes, inner_in, spread_in, rest, dproj_out, halo_out, dlogit_out, logit_rows, dtaps_out, sums_out, wide, dconv, late, rowsum):
    ranks = pay.shape[0]
    tokens = chunks * CH
    me = mine[2]
    for at, piece in enumerate((p0, p1, p2, p3)):
        late[ring_place(me, at)] = piece[...]
    kq = heads * DK
    width = 2 * kq + heads * DV
    rows, cols = square_masks()
    grads = [jnp.zeros((DK, DV), FLOAT) for h in range(heads)]
    for j in reversed(range(1, ranks)):
        passed = j > me
        for h in range(heads):
            moved = apply_whole(pay, j, h, grads[h], TN) + late[j, h].astype(FLOAT)
            grads[h] = jnp.where(passed, moved, grads[h])
    for h in range(heads):
        grads[h] = mm3(after[h, :, :DK], grads[h]) + after[h, :, DK:]
    wide[:HALO, :] = halo[...].astype(FLOAT)
    wide[HALO:, :] = proj[...].astype(FLOAT)
    logit_rows[...] = jnp.zeros(logit_rows.shape, FLOAT)
    dconv[0:HALO, :] = jnp.zeros((HALO, width), FLOAT)
    dconv[HALO + tokens :, :] = jnp.zeros((8, width), FLOAT)
    for c in reversed(range(chunks)):
        span = slice(c * CH, (c + 1) * CH)
        for h in range(heads):
            at = h * chunks + c
            ql, kl, vl, ol = (
                slice(h * DK, (h + 1) * DK),
                slice(kq + h * DK, kq + (h + 1) * DK),
                slice(2 * kq + h * DV, 2 * kq + (h + 1) * DV),
                slice(h * DV, (h + 1) * DV),
            )
            grad = grads[h].astype(HALF)
            query, key = q[span, ql], k[span, ql]
            state, vn, dout = states[at], vns[at], dos[span, ol]
            logit = logits[span, h : h + 1]
            beta = sigmoid(logit)
            g = gcol[span, h : h + 1]
            last = gcol[(c + 1) * CH - 1 : (c + 1) * CH, h : h + 1]
            eg, ed = jnp.exp(g), jnp.exp(last - g)
            spread = spread_in[at]
            strict = jnp.where(rows > cols, spread, 0.0)
            inner = inner_in[at]
            dvn = dvns[at] + ed * mm(key, grad)
            dr = mm(tri[at], dvn, TN)
            drh = dr.astype(HALF)
            dval = beta * dr
            both = mm(jnp.concatenate([dout, drh], axis=0), state, NT)
            dkeep = mm(vn, grad, NT)
            pair = mm(jnp.concatenate([dout, drh], axis=0), vn, NT)
            dqk = spread * pair[:CH]
            da = -(strict * pair[CH:])
            dkk = beta * da
            dbeta = jnp.sum(dr * rest[span, ol], axis=-1, keepdims=True) + jnp.sum(
                da * inner, axis=-1, keepdims=True
            )
            dqkh = dqk.astype(HALF)
            dkkh = dkk.astype(HALF)
            dquery = eg * both[:CH] + mm(dqkh, key)
            dkey = (
                ed * dkeep
                - (beta * eg) * both[CH:]
                + mm(dqkh, query, TN)
                + mm(dkkh, key)
                + mm(dkkh, key, TN)
            )
            if c > 0:
                grads[h] = jnp.exp(last) * grads[h] - mm(ns[at], grad, TN) + es[at]
            dlogit = dbeta * beta * (1.0 - beta)
            dlogit_out[span, h : h + 1] = dlogit
            logit_rows[h : h + 1, HALO + c * CH : HALO + (c + 1) * CH] = jnp.broadcast_to(dlogit, (CH, DK)).T[0:1]
            extra_sum = dlogit * logit
            far_span = slice(HALO + c * CH, HALO + (c + 1) * CH)
            sums_out[far_span, :] = (gate_sums[span, :] if h == 0 else sums_out[far_span, :]) + extra_sum
            there = slice(HALO + c * CH, HALO + (c + 1) * CH)
            dconv[there, ql] = dquery * slopes[span, ql]
            dconv[there, vl] = dval * slopes[span, vl]
            unit = key.astype(FLOAT)
            dconv[there, kl] = (dkey - unit * jnp.sum(dkey * unit, axis=-1, keepdims=True)) * slopes[span, kl]
    dtaps_out[4:8, :] = jnp.zeros((4, width), FLOAT)
    rowsum[...] = jnp.zeros((HALO + tokens, 1), FLOAT)
    for at in range(0, width, DK):
        lanes = slice(at, at + DK)
        for j in range(4):
            dtaps_out[j : j + 1, lanes] = jnp.sum(
                dconv[HALO : HALO + tokens, lanes] * wide[HALO - 3 + j : HALO - 3 + j + tokens, lanes], axis=0, keepdims=True
            )
        total = dconv[3 : 3 + HALO + tokens, lanes] * taps[0:1, lanes]
        for j in range(1, 4):
            total = total + dconv[3 - j : 3 - j + HALO + tokens, lanes] * taps[j : j + 1, lanes]
        small = total.astype(HALF)
        dproj_out[:, lanes] = small
        halo_out[:, lanes] = small[:HALO]
        rowsum[...] += jnp.sum(small.astype(FLOAT) * wide[:, lanes], axis=-1, keepdims=True)
    sums_out[HALO:, :] += rowsum[HALO:, :]
    sums_out[:HALO, :] = rowsum[:HALO, :]


def out(shape, dtype):
    return jax.ShapeDtypeStruct(shape, dtype)


def cost(micros):
    return pl.CostEstimate(flops=int(micros * 1.1e7), bytes_accessed=0, transcendentals=0)


def run(kernel, shapes, args, scratch=(), scalars=0, after=(), micros=1.0, megs=12, kept=()):
    vmem = pl.BlockSpec(memory_space=pltpu.VMEM)
    smem = pl.BlockSpec(memory_space=pltpu.SMEM)
    count = len(args)

    def body(*refs):
        kernel(*refs[:count], *refs[count + len(after) :])

    return pl.pallas_call(
        body,
        out_shape=tuple(pltpu.HBM(a.shape, a.dtype) if i in kept else a for i, a in enumerate(shapes)),
        in_specs=[smem] * scalars + [vmem] * (count - scalars) + [pl.BlockSpec(memory_space=pl.ANY)] * len(after),
        out_specs=[pl.BlockSpec() if i in kept else vmem for i in range(len(shapes))],
        scratch_shapes=list(scratch),
        compiler_params=pltpu.CompilerParams(vmem_limit_bytes=megs * 2**20),
        cost_estimate=cost(micros),
    )(*args, *after)


def passed(arrays, after):
    count = len(arrays)
    anywhere = pl.BlockSpec(memory_space=pl.ANY)

    def body(*refs):
        token = refs[-1]
        token[...] = jnp.zeros(token.shape, FLOAT)

    *same, token = pl.pallas_call(
        body,
        out_shape=tuple(out(a.shape, a.dtype) for a in arrays) + (out((8, DK), FLOAT),),
        in_specs=[anywhere] * (count + len(after)),
        out_specs=[anywhere] * count + [pl.BlockSpec(memory_space=pltpu.VMEM)],
        input_output_aliases={i: i for i in range(count)},
        compiler_params=pltpu.CompilerParams(vmem_limit_bytes=2**20),
        cost_estimate=cost(0.1),
    )(*arrays, *after)
    return same, token


def prepare_shapes(heads, chunks):
    tokens, pairs = chunks * CH, heads * chunks
    return (
        out((tokens, heads * DK), HALF),
        out((tokens, heads * DV), HALF),
        out((pairs, CH, CH), HALF),
        out((pairs, DK, DK), HALF),
        out((pairs, DK, DV), FLOAT),
        out((pairs, CH, DK), HALF),
        out((pairs, CH, DV), HALF),
        out((heads, DK + 16, DK + DV), HALF),
    )


def mix_shapes(heads, chunks):
    tokens, pairs = chunks * CH, heads * chunks
    return (
        out((pairs, DK, DV), HALF),
        out((pairs, CH, DV), HALF),
        out((tokens, heads * DV), FLOAT),
        out((tokens, heads * DV), HALF),
        out((4, heads, DK + 16, DK + DV), HALF),
    )


def gate_back_shapes(heads, chunks):
    tokens, pairs = chunks * CH, heads * chunks
    return (
        out((tokens, heads * DV), HALF),
        out((pairs, CH, DV), FLOAT),
        out((pairs, DK, DV), FLOAT),
        out((tokens, heads * DV), HALF),
        out((1, heads * DV), FLOAT),
        out((tokens, 1), FLOAT),
        out((heads, DK, DV), HALF),
    )


def back_shapes(heads, chunks):
    tokens = chunks * CH
    width = heads * (2 * DK + DV)
    return (
        out((HALO + tokens, width), HALF),
        out((HALO, width), HALF),
        out((tokens, heads), FLOAT),
        out((HALO, HALO + tokens), FLOAT),
        out((8, width), FLOAT),
        out((HALO + tokens, 1), FLOAT),
    )


def back_scratch(heads, chunks):
    tokens = chunks * CH
    width = heads * (2 * DK + DV)
    return (pltpu.VMEM((HALO + tokens, width), FLOAT), pltpu.VMEM((HALO + tokens + 8, width), FLOAT), pltpu.VMEM((4, heads, DK, DV), HALF), pltpu.VMEM((HALO + tokens, 1), FLOAT))


def group_shapes(heads):
    pay = (heads, DK + 16, DK + DV)
    return (out((heads, DK, DK + DV), FLOAT), out(pay, HALF), out((4, *pay), HALF))


def group_back_shapes(heads):
    return (
        out((heads, DK, DK + DV), FLOAT),
        out((heads, DK, DV), HALF),
        out((4, heads, DK, DV), HALF),
    )


HEAD = ("x", "c")
SEQ = ("y", "z")
PLANE = ("y", "z", "c")
HALO = 16
EXTRA = 64
TURNS = (0, 1, -1, 2)


def rotated(array, axis, distance):
    size = lax.axis_size(axis)
    return lax.ppermute(array, axis, [(i, (i + distance) % size) for i in range(size)])


def ring_pieces(array, axis):
    return [array] + [rotated(array, axis, -d) for d in TURNS[1:]]


def join_kernel(mine, *refs):
    for k in range(4):
        refs[4][ring_place(mine[0], k)] = refs[k][...]


def head_gather(array, mine, after=()):
    shapes = (out((4, *array.shape), array.dtype),)
    own = run(join_kernel, shapes, (mine, *ring_pieces(array, "x")), scalars=1, after=after)[0]
    return own, rotated(own, "c", 1)


def head_tiles(mine, own, other):
    core = mine[1]
    return [(2 * x + which, ref, x) for which, ref in ((core, own), (1 - core, other)) for x in range(4)]


def copy_kernel(source, target):
    target[...] = source[...]


def turned(array, first, distance):
    pairs = []
    for y in range(4):
        for z in range(4):
            for core in range(2):
                along_z = (core == 0) == first
                to = (y, (z + distance) % 4) if along_z else ((y + distance) % 4, z)
                pairs.append(((y * 4 + z) * 2 + core, (to[0] * 4 + to[1]) * 2 + core))
    return lax.ppermute(array, PLANE, pairs)


def ring_place(mine, k):
    return lax.rem(mine + TURNS[k] + 4, 4)


def lane_block(at, width):
    return pl.ds(pl.multiple_of(at * width, width), width)


def setup_kernel(query, key, value, gate, decay, in_out, gate_out, gcol, grow, token):
    at = 0
    for weight in (query, key, value):
        count = weight.shape[1]
        in_out[at : at + count, :] = weight[...].T
        at += count
    gate_out[...] = gate[...].T
    rows, cols = square_masks()
    heads, tokens = decay.shape
    chunks = tokens // CH
    for h in range(heads):
        for c in range(chunks):
            span = slice(c * CH, (c + 1) * CH)
            flat = jnp.broadcast_to(decay[h : h + 1, span], (CH, CH))
            grow[h * chunks + c : h * chunks + c + 1, :] = jnp.sum(
                jnp.where(rows <= cols, flat.T, 0.0), axis=0, keepdims=True
            )
            gcol[span, h : h + 1] = jnp.sum(jnp.where(cols <= rows, flat, 0.0), axis=1, keepdims=True)
    token[...] = jnp.zeros(token.shape, FLOAT)


def first_norm_kernel(mine, gain, beta_rows, own, other, normed, factor, rows_out, logits, halo_out):
    width = own.shape[2]
    rows = rows_out.shape[0]
    own_rows = lane_block(mine[0] * 2 + mine[1], rows)
    square = 0.0
    for _, ref, x in head_tiles(mine, own, other):
        wide = ref[x].astype(FLOAT)
        square = square + jnp.sum(wide * wide, axis=-1, keepdims=True)
    scale = lax.rsqrt(square / (8 * width) + EPS_NORM)
    factor[...] = scale
    total = 0.0
    for head, ref, x in head_tiles(mine, own, other):
        lanes = lane_block(head, width)
        small = (ref[x].astype(FLOAT) * scale * gain[:, lanes]).astype(HALF)
        normed[:, lanes] = small
        total = total + mm(small, beta_rows[:, lanes], NT)
        rows_out[:, lanes] = ref[x, own_rows, :].astype(FLOAT)
    logits[...] = total
    halo_out[...] = normed[normed.shape[0] - HALO :, :]


def product_grad_kernel(mine, own, other, weight, whole, rows_out, grad, token):
    width = own.shape[2]
    rows = rows_out.shape[0]
    own_rows = lane_block(mine[0] * 2 + mine[1], rows)
    for head, ref, x in head_tiles(mine, own, other):
        lanes = lane_block(head, width)
        whole[:, lanes] = ref[x]
        rows_out[:, lanes] = ref[x, own_rows, :]
    grad[...] = mm(weight[...], whole[...], NT)
    token[...] = jnp.zeros(token.shape, FLOAT)


def hidden_kernel(rows_in, gain, first, second, third, fourth, hidden, unit, factor, normed):
    total = rows_in[...] + first[...] + second[...].astype(FLOAT) + third[...].astype(FLOAT) + fourth[...].astype(FLOAT)
    hidden[...] = total
    scale = lax.rsqrt(jnp.mean(total * total, axis=-1, keepdims=True) + EPS_NORM)
    factor[...] = scale
    unit[...] = total * scale
    normed[...] = (total * scale * gain[...]).astype(HALF)


def second_back_kernel(unit, factor, gain, cot_rows, first, second, third, fourth, d_hidden, gain_part, token):
    token[...] = jnp.zeros(token.shape, FLOAT)
    total = first[...] + second[...].astype(FLOAT) + third[...].astype(FLOAT) + fourth[...].astype(FLOAT)
    n = unit[...]
    gain_part[...] = jnp.sum(total * n, axis=0, keepdims=True)
    e = total * gain[...]
    mean = jnp.mean(e * n, axis=-1, keepdims=True)
    d_hidden[...] = (cot_rows[...].astype(FLOAT) + factor[...] * (e - n * mean)).astype(HALF)


def ffn_kernel(mine, own_in, other_in, gate_rows, up_rows, d_product, normed, product, d_gate, d_up, other, own, token, total):
    rows = own_in.shape[1]
    for head, ref, x in head_tiles(mine, own_in, other_in):
        normed[lane_block(head, rows), :] = ref[x]
    cols = gate_rows.shape[0]
    step = cols // 2
    for at in range(0, cols, step):
        span = slice(at, at + step)
        gate = mm(gate_rows[span, :], normed[...], NT)
        up = mm(up_rows[span, :], normed[...], NT)
        sig = sigmoid(gate)
        act = gate * sig
        product[span, :] = (act * up).astype(HALF)
        grad = d_product[span, :]
        dg = (grad * up * (sig * (1.0 + gate * (1.0 - sig)))).astype(HALF)
        du = (grad * act).astype(HALF)
        d_gate[span, :] = dg
        d_up[span, :] = du
    token[...] = jnp.zeros(token.shape, FLOAT)
    gate_turned = d_gate[...].T
    up_turned = d_up[...].T
    width = normed.shape[1]
    tile = width // 4
    core = mine[1]
    for at in range(0, width, tile):
        lanes = slice(at, at + tile)
        total[...] = mm(gate_turned, gate_rows[:, lanes]) + mm(up_turned, up_rows[:, lanes])
        spread_rows(core, total, own, other, rows, lanes)


def join_rows_kernel(mine, own, other, whole, own_cols):
    rows = own.shape[1]
    lanes = lane_block(mine[0] * 2 + mine[1], own_cols.shape[1])
    for head, ref, x in head_tiles(mine, own, other):
        whole[lane_block(head, rows), :] = ref[x]
        own_cols[lane_block(head, rows), :] = ref[x, :, lanes]


def split_sum_kernel(mine, own, arrived, *outs):
    for k in range(4):
        at = ring_place(mine[0], k)
        outs[k][...] = (own[at].astype(FLOAT) + arrived[at].astype(FLOAT)).astype(outs[k].dtype)
    outs[4][...] = jnp.zeros(outs[4].shape, FLOAT)


def head_scatter(own, other, mine, with_token=False, after=()):
    arrived = rotated(other, "c", 1)
    shape = own.shape[1:]
    shapes = (out(shape, FLOAT),) + (out(shape, HALF),) * 3 + (out((8, DK), FLOAT),)
    total, *sent, token = run(split_sum_kernel, shapes, (mine, own, arrived), scalars=1, after=after)
    parts = [total] + [rotated(part, "x", d) for d, part in zip(TURNS[1:], sent)]
    return (parts, token) if with_token else parts


def swapped(array, mask):
    return lax.ppermute(array, "x", [(i, i ^ mask) for i in range(4)])


def first_half_kernel(mine, own, arrived, keep, send, token):
    token[...] = jnp.zeros(token.shape, FLOAT)
    base = jnp.where(mine[0] < 2, 0, 2)
    for target, at in ((keep, base), (send, 2 - base)):
        for i in range(2):
            target[i] = (own[at + i].astype(FLOAT) + arrived[at + i].astype(FLOAT)).astype(target.dtype)


def second_half_kernel(mine, keep, arrived, own, send, token):
    token[...] = jnp.zeros(token.shape, FLOAT)
    at = lax.rem(mine[0], 2)
    own[...] = keep[at].astype(FLOAT) + arrived[at].astype(FLOAT)
    send[...] = (keep[1 - at].astype(FLOAT) + arrived[1 - at].astype(FLOAT)).astype(HALF)


def first_halves(own, other, mine, after):
    pair = out((2, *own.shape[1:]), HALF)
    return run(
        first_half_kernel,
        (pair, pair, out((8, DK), FLOAT)),
        (mine, own, rotated(other, "c", 1)),
        scalars=1,
        after=after,
    )


def second_halves(keep, arrived, mine, after):
    shape = keep.shape[1:]
    return run(
        second_half_kernel,
        (out(shape, FLOAT), out(shape, HALF), out((8, DK), FLOAT)),
        (mine, keep, arrived),
        scalars=1,
        after=after,
    )


def added(parts):
    total = parts[0]
    for part in parts[1:]:
        total = total + part.astype(FLOAT)
    return total


def dest_block(mine, k, o):
    core = mine[1]
    place = ring_place(jnp.where(core == 0, mine[3], mine[2]), k)
    return jnp.where(core == 0, o * 4 + place, place * 4 + o)


def store_tile(outs, k, o, early, value):
    count = early.shape[0]
    if k < 3:
        outs[k][o, :count, :] = early
        outs[k][o, count:, :] = value
    else:
        spare = outs[3].shape[1] - count
        outs[3][o, :count, :] = early
        outs[3][o, count:, :] = value[:spare]
        outs[4][o] = value[spare:]


def mixer_grad_kernel(mine, d_branch, gated, normed, d_pre, gate_rows, *refs):
    outs, (gain_out, gated_turned, pre_turned) = refs[:4], refs[4:]
    gated_turned[...] = gated[...].T
    pre_turned[...] = d_pre[...].T
    for k in range(4):
        for o in (0, 2):
            blocks = [lane_block(dest_block(mine, k, o + i), DK) for i in range(2)]
            mixer = mm(gated_turned[...], jnp.concatenate([d_branch[:, at] for at in blocks], axis=1))
            gate = mm(pre_turned[...], jnp.concatenate([normed[:, at] for at in blocks], axis=1))
            for i, at in enumerate(blocks):
                half = slice(i * DK, (i + 1) * DK)
                outs[k][o + i] = jnp.concatenate([mixer[:, half], gate[:, half]], axis=0).astype(HALF)
                gain_out[:, at] = jnp.sum(gate[:, half] * gate_rows[:, at].astype(FLOAT), axis=0, keepdims=True)


def in_grad_kernel(mine, normed, halo, dproj, d_logit, taps, mixer_gain, gate_gain, second_gain, first_gain, in_rows, beta_rows, *refs):
    early, outs, (token, gains, turned_refs, extra) = refs[:4], refs[4:9], refs[9:]
    token[...] = jnp.zeros(token.shape, FLOAT)
    cols = dproj.shape[1]
    heads = 2
    turned_refs[:cols, :] = dproj[...].T
    turned_refs[cols:, :] = d_logit[...].astype(HALF)
    extra[...] = jnp.zeros(extra.shape, FLOAT)
    per_tap = cols // DK
    for j in range(4):
        for i in range(per_tap):
            extra[j * per_tap + i : j * per_tap + i + 1, :] = taps[j : j + 1, i * DK : (i + 1) * DK]
    for i in range(mixer_gain.shape[1] // DK):
        extra[32 + i : 33 + i, :] = mixer_gain[:, i * DK : (i + 1) * DK]
    for k in range(4):
        for o in (0, 2):
            blocks = [lane_block(dest_block(mine, k, o + i), DK) for i in range(2)]
            left = jnp.concatenate(
                [jnp.concatenate([halo[:, at], normed[:, at]], axis=0) for at in blocks], axis=1
            )
            grads = mm(turned_refs[...], left)
            for i, at in enumerate(blocks):
                half = slice(i * DK, (i + 1) * DK)
                beta = grads[cols : cols + heads, half]
                gain = (
                    jnp.sum(grads[:cols, half] * in_rows[:, at].astype(FLOAT), axis=0, keepdims=True)
                    + jnp.sum(beta * beta_rows[:heads, at].astype(FLOAT), axis=0, keepdims=True)
                    + gate_gain[:, at]
                )
                extra[36 : 36 + heads, :] = beta
                gains[0:1, at] = gain / first_gain[:, at]
                gains[1:2, at] = second_gain[:, at]
                store_tile(
                    outs, k, o + i, early[k][o + i], jnp.concatenate([grads[:cols, half], extra[...]], axis=0).astype(HALF)
                )


def ffn_grad_kernel(turns, mine, cot, normed, d_gate, d_up, product, *refs):
    outs, token = refs[:-1], refs[-1]
    token[...] = jnp.zeros(token.shape, FLOAT)
    cols = d_gate.shape[0]
    half_rows = 3 * cols // 2
    for k in turns:
        for o in (0, 2):
            blocks = [lane_block(dest_block(mine, k, o + i), DK) for i in range(2)]
            lefts = [jnp.concatenate([ref[:, at] for at in blocks], axis=1) for ref in (normed, cot)]
            for n, (right, left) in enumerate(((d_gate, lefts[0]), (d_up, lefts[0]), (product, lefts[1]))):
                both = mm(right[...], left).astype(HALF)
                for i in range(2):
                    tile = both[:, i * DK : (i + 1) * DK]
                    first = n * cols
                    if k < 3:
                        outs[turns.index(k)][o + i, first : first + cols, :] = tile
                    elif first + cols <= half_rows:
                        outs[0][o + i, first : first + cols, :] = tile
                    elif first >= half_rows:
                        outs[1][o + i, first - half_rows : first - half_rows + cols, :] = tile
                    else:
                        outs[0][o + i, first:, :] = tile[: half_rows - first]
                        outs[1][o + i, : first + cols - half_rows, :] = tile[half_rows - first :]


def ffn_grads(turns, mine, cot, normed, d_gate, d_up, product, after):
    rows = 3 * d_gate.shape[0]
    if turns == (3,):
        shapes = (out((4, rows // 2, DK), HALF),) * 2
    else:
        shapes = (out((4, rows, DK), HALF),) * len(turns)
    return run(
        partial(ffn_grad_kernel, turns),
        shapes + (out((8, DK), FLOAT),),
        (mine, cot, normed, d_gate, d_up, product),
        scalars=1,
        after=(after,),
    )


def put_gains_kernel(mine, gains, arrived, *refs):
    outs, token = refs[-6:-1], refs[-1]
    token[...] = jnp.zeros(token.shape, FLOAT)
    count = outs[0].shape[1] - EXTRA + 32
    for k in range(4):
        target, rows = (outs[k], count) if k < 3 else (outs[4], count - outs[3].shape[1])
        here = slice(rows, rows + 16)
        for o in range(4):
            old = target[o, here, :].astype(FLOAT)
            lanes = lane_block(dest_block(mine, k, o), DK)
            new = gains[:, lanes] + arrived[:, lanes]
            target[o, here, :] = jnp.concatenate([old[:8], new, old[10:]], axis=0).astype(HALF)


def with_gains(mine, parts, gains, arrived, after):
    vmem = pl.BlockSpec(memory_space=pltpu.VMEM)
    *parts, token = pl.pallas_call(
        put_gains_kernel,
        out_shape=tuple(out(a.shape, a.dtype) for a in parts) + (out((8, DK), FLOAT),),
        in_specs=[pl.BlockSpec(memory_space=pltpu.SMEM)]
        + [vmem] * 7
        + [pl.BlockSpec(memory_space=pl.ANY)] * len(after),
        out_specs=[vmem] * 6,
        input_output_aliases={3 + i: i for i in range(5)},
        compiler_params=pltpu.CompilerParams(vmem_limit_bytes=4 * 2**20),
        cost_estimate=cost(0.3),
    )(mine, gains, arrived, *parts, *after)
    return parts, token


def gain_rows(ref):
    first = ref.shape[1] - EXTRA + 40
    return ref[:, first : first + 8, :].astype(FLOAT)


def last_relay_kernel(own, plus, minus, first, second, plus_out, minus_out, token, rows):
    relay_kernel(plus, minus, first, second, plus_out, minus_out, token)
    for i, ref in enumerate((own, plus_out, minus_out)):
        rows[i] = gain_rows(ref)


def quad_sum_kernel(first, second, third, fourth, own, plus, minus, token):
    token[...] = jnp.zeros(token.shape, FLOAT)
    for i, target in enumerate((own, plus, minus)):
        target[...] = (first[i] + second[i]) + (third[i] + fourth[i])


def relay_kernel(plus, minus, first, second, plus_out, minus_out, token):
    half = first.shape[1]
    plus_out[:, :half, :] = (plus[:, :half, :].astype(FLOAT) + first[...].astype(FLOAT)).astype(HALF)
    plus_out[:, half:, :] = plus[:, half:, :]
    minus_out[:, :half, :] = minus[:, :half, :]
    minus_out[:, half:, :] = (minus[:, half:, :].astype(FLOAT) + second[...].astype(FLOAT)).astype(HALF)
    token[...] = jnp.zeros(token.shape, FLOAT)


def relayed(parts, after, micros):
    shape = out(parts[1].shape, HALF)
    first, second = turned(parts[3], True, 1), turned(parts[4], True, -1)
    plus, minus, token = run(
        relay_kernel,
        (shape, shape, out((8, DK), FLOAT)),
        (parts[1], parts[2], first, second),
        after=after,
        micros=micros,
    )
    return (parts[0], turned(plus, True, 1), turned(minus, True, -1)), token


def last_sum_kernel(mine, own, plus, minus, own_rows, plus_rows, minus_rows, *outs):
    seq_sum_kernel(0, mine, own, plus, minus, *outs)
    rank = jnp.where(mine[1] == 0, mine[2], mine[3])
    first = outs[0].shape[0] - EXTRA + 32
    for k in range(4):
        place = ring_place(rank, k)
        old = own[place, first : first + 16, :].astype(FLOAT)
        old = old + plus[place, first : first + 16, :].astype(FLOAT) + minus[place, first : first + 16, :].astype(FLOAT)
        new = own_rows[place] + plus_rows[place] + minus_rows[place]
        outs[k][first : first + 16, :] = jnp.concatenate([old[:8], new], axis=0).astype(outs[k].dtype)


def seq_sum_kernel(early, mine, *refs):
    rank = jnp.where(mine[1] == 0, mine[2], mine[3])
    group, before = refs[:3], refs[3 : 3 + 4 * early]
    outs = refs[3 + 4 * early : 7 + 4 * early]
    refs[-1][...] = jnp.zeros(refs[-1].shape, FLOAT)
    for k in range(4):
        place = ring_place(rank, k)
        at = 0
        for i in range(early):
            source = before[4 * i + k]
            outs[k][at : at + source.shape[0], :] = source[...]
            at += source.shape[0]
        total = group[0][place].astype(FLOAT) + group[1][place].astype(FLOAT) + group[2][place].astype(FLOAT)
        outs[k][at:, :] = total.astype(outs[k].dtype)


def seq_sums(group, before, mine, after, micros):
    count = group[0].shape[1] + sum(sums[0].shape[0] for sums in before)
    shapes = (out((count, DK), FLOAT),) + (out((count, DK), HALF),) * 3
    shapes += (out((8, DK), FLOAT),)
    flat = [piece for sums in before for piece in sums]
    return run(
        partial(seq_sum_kernel, len(before)), shapes, (mine, *group, *flat), scalars=1, after=after, micros=micros
    )


def second_round(sums):
    return [sums[0]] + [turned(sums[i], False, TURNS[i]) for i in range(1, 4)]


def unpack_kernel(own, first, second, third, *outs):
    total = own[...] + first[...].astype(FLOAT) + second[...].astype(FLOAT) + third[...].astype(FLOAT)
    at = 0
    for target in outs[:5]:
        count = target.shape[1]
        target[...] = total[at : at + count, :].T
        at += count
    extra = total[at:, :]
    per_tap = 8
    first = 0
    for target in outs[5:8]:
        blocks = target.shape[1] // DK
        for j in range(4):
            for i in range(blocks):
                row = j * per_tap + first + i
                target[j : j + 1, i * DK : (i + 1) * DK] = extra[row : row + 1, :]
        first += blocks
    for i in range(outs[8].shape[1] // DK):
        outs[8][:, i * DK : (i + 1) * DK] = extra[32 + i : 33 + i, :]
    outs[9][...] = extra[36:38, :]
    outs[10][...] = extra[40:48, :]


def ffn_unpack_kernel(own, first, second, third, gate, up, down, token):
    cols = gate.shape[0]
    token[...] = jnp.zeros(token.shape, FLOAT)
    for n, target in enumerate((gate, up, down)):
        span = slice(n * cols, (n + 1) * cols)
        target[...] = (
            own[span, :]
            + first[span, :].astype(FLOAT)
            + second[span, :].astype(FLOAT)
            + third[span, :].astype(FLOAT)
        )


def output_kernel(own, arrived, total, token):
    token[...] = jnp.zeros(token.shape, FLOAT)
    total[...] = (own[...] + arrived[...].astype(FLOAT)).astype(HALF)


def tile_of(i, mine):
    return (i % 4) * 2 + jnp.where(i < 4, 1 - mine[1], mine[1])


def whole_block(shape):
    return pl.BlockSpec(shape, lambda i, mine: (0,) * len(shape))


def tile_outs(rows, width):
    return [
        pl.BlockSpec((1, rows, width), lambda i, mine: (jnp.minimum(i, 3), 0, 0)),
        pl.BlockSpec((1, rows, width), lambda i, mine: (jnp.maximum(i - 4, 0), 0, 0)),
    ]


def down_kernel(mine, product, weight, hidden, other, own, token, scratch):
    step = pl.program_id(0)
    rows = hidden.shape[0]

    @pl.when(step == 0)
    def _():
        scratch[...] = product[...].T

    part = mm(scratch[...], weight[...])
    here = lane_block(mine[0] * 2 + mine[1], rows)
    for target, wanted in ((other, step < 4), (own, step >= 4)):

        @pl.when(wanted)
        def _():
            target[0] = part.astype(HALF)
            target[0, here, :] = (target[0, here, :].astype(FLOAT) + hidden[...]).astype(HALF)

    token[...] = jnp.zeros(token.shape, FLOAT)


def down_tiles(mine, product, weight, hidden):
    cols, tokens = product.shape
    width = weight.shape[1] // 8
    spec = pltpu.PrefetchScalarGridSpec(
        num_scalar_prefetch=1,
        grid=(8,),
        in_specs=[
            whole_block(product.shape),
            pl.BlockSpec((cols, width), lambda i, mine: (0, tile_of(i, mine))),
            pl.BlockSpec((hidden.shape[0], width), lambda i, mine: (0, tile_of(i, mine))),
        ],
        out_specs=tile_outs(tokens, width) + [whole_block((8, DK))],
        scratch_shapes=[pltpu.VMEM((tokens, cols), HALF)],
    )
    tiles = out((4, tokens, width), HALF)
    return pl.pallas_call(
        down_kernel,
        grid_spec=spec,
        out_shape=(tiles, tiles, out((8, DK), FLOAT)),
        compiler_params=pltpu.CompilerParams(vmem_limit_bytes=16 * 2**20),
        cost_estimate=cost(4.0),
    )(mine, product, weight, hidden)


def d_first_kernel(mine, dproj, arrived, proj, d_pre, d_logit, sums, in_rows, gate_rows, beta_rows, after, other, own, token, scratch, sum_rows):
    step = pl.program_id(0)
    tokens = d_pre.shape[0]
    width = own.shape[2]

    @pl.when(step == 0)
    def _():
        scratch[: tokens - HALO, :] = dproj[HALO:tokens, :]
        extra = arrived[...].astype(FLOAT)
        scratch[tokens - HALO :, :] = (dproj[tokens:, :].astype(FLOAT) + extra).astype(HALF)
        late = jnp.sum(extra * proj[tokens - HALO :, :].astype(FLOAT), axis=-1, keepdims=True)
        column = jnp.concatenate([sums[HALO:tokens, :], sums[tokens:, :] + late], axis=0)
        row = jnp.broadcast_to(column, (tokens, DK)).T
        sum_rows[...] = jnp.zeros(sum_rows.shape, FLOAT)
        for i in range(tokens // width):
            sum_rows[i : i + 1, :] = row[0:1, i * width : (i + 1) * width]

    part = mm(scratch[...], in_rows[...]) + mm(d_pre[...], gate_rows[...])
    for h in range(2):
        part = part + d_logit[:, h : h + 1] * beta_rows[h : h + 1, :].astype(FLOAT)
    for target, wanted in ((other, step < 4), (own, step >= 4)):

        @pl.when(wanted)
        def _():
            target[0, :tokens, :] = part.astype(HALF)
            target[0, tokens:, :] = sum_rows[...].astype(HALF)

    token[...] = jnp.zeros(token.shape, FLOAT)


def d_first_tiles(mine, dproj, arrived, proj, d_pre, d_logit, sums, in_rows, gate_rows, beta_rows, after):
    tokens = d_pre.shape[0]
    width = in_rows.shape[1] // 8
    count = tokens + HALO

    def tile(rows):
        return pl.BlockSpec((rows, width), lambda i, mine: (0, tile_of(i, mine)))

    spec = pltpu.PrefetchScalarGridSpec(
        num_scalar_prefetch=1,
        grid=(8,),
        in_specs=[whole_block(a.shape) for a in (dproj, arrived, proj, d_pre, d_logit, sums)]
        + [tile(in_rows.shape[0]), tile(gate_rows.shape[0]), tile(beta_rows.shape[0])]
        + [pl.BlockSpec(memory_space=pl.ANY)],
        out_specs=tile_outs(count, width) + [whole_block((8, DK))],
        scratch_shapes=[pltpu.VMEM((tokens, dproj.shape[1]), HALF), pltpu.VMEM((HALO, width), FLOAT)],
    )
    tiles = out((4, count, width), HALF)
    return pl.pallas_call(
        d_first_kernel,
        grid_spec=spec,
        out_shape=(tiles, tiles, out((8, DK), FLOAT)),
        compiler_params=pltpu.CompilerParams(vmem_limit_bytes=16 * 2**20),
        cost_estimate=cost(6.0),
    )(mine, dproj, arrived, proj, d_pre, d_logit, sums, in_rows, gate_rows, beta_rows, after)


def input_grad_kernel(mine, own, arrived, block_input, factor, gain, d_branch, grad):
    total = own[...] + arrived[...].astype(FLOAT)
    tokens, width = block_input.shape
    columns = []
    for i in range(tokens // width):
        row = total[tokens + i : tokens + i + 1, :]
        columns.append(jnp.broadcast_to(row, (DK, width)).T[:, 0:1])
    mean = jnp.concatenate(columns, axis=0) / (8 * width)
    scale = factor[...]
    unit = block_input[...].astype(FLOAT) * scale
    gain_own = gain[:, lane_block(mine[0] * 2 + mine[1], width)]
    grad[...] = d_branch[...].astype(FLOAT) + scale * (total[:tokens, :] * gain_own - unit * mean)


def next_block(array, distance):
    size = 16
    route = [(i, i + distance) for i in range(size) if 0 <= i + distance < size]
    return lax.ppermute(array, SEQ, route)


def dot_nt(a, b):
    return lax.dot_general(a, b, NT, preferred_element_type=FLOAT)


def shards(
    block_input,
    log_decay,
    first_gain,
    query_weight,
    key_weight,
    value_weight,
    gate_weight,
    beta_weight,
    query_conv,
    key_conv,
    value_conv,
    mixer_gain,
    mixer_weight,
    second_gain,
    swiglu_gate,
    swiglu_up,
    swiglu_down,
    cotangent,
):
    heads = log_decay.shape[1]
    tokens, width = block_input.shape
    model = 8 * width
    chunks = tokens // CH
    rows = tokens // 8
    kq, vd = heads * DK, heads * DV
    cols = 2 * kq + vd
    hidden_cols = swiglu_gate.shape[1]
    mine = jnp.stack([lax.axis_index(name) for name in ("x", "c", "y", "z")]).astype(jnp.int32)

    token_out = out((8, DK), FLOAT)
    in_rows, gate_rows, gcol, grow, token = run(
        setup_kernel,
        (
            out((cols, model), HALF),
            out((vd, model), HALF),
            out((tokens, heads), FLOAT),
            out((heads * chunks, CH), FLOAT),
            token_out,
        ),
        (query_weight, key_weight, value_weight, gate_weight, log_decay.T),
        micros=3.0,
    )
    beta_rows = jnp.pad(beta_weight.T, ((0, HALO - heads), (0, 0)))
    taps = jnp.concatenate([query_conv.T, key_conv.T, value_conv.T], axis=1)
    gain_row = mixer_gain.reshape(1, -1)
    first_row = first_gain.reshape(1, -1)

    first_normed, first_factor, my_rows, logits, halo_rows = run(
        first_norm_kernel,
        (
            out((tokens, model), HALF),
            out((tokens, 1), FLOAT),
            out((rows, model), FLOAT),
            out((tokens, HALO), FLOAT),
            out((HALO, model), HALF),
        ),
        (mine, first_row, beta_rows, *head_gather(block_input, mine, (token,))),
        scalars=1,
        micros=3.0,
    )
    halo_normed = next_block(halo_rows, 1)
    proj = dot_nt(first_normed, in_rows).astype(HALF)
    halo_proj = dot_nt(halo_normed, in_rows).astype(HALF)
    gate_pre = dot_nt(first_normed, gate_rows)
    k, v, tri, n, b, w, u, pay, pay_token = run(
        partial(prepare_kernel, heads, chunks),
        prepare_shapes(heads, chunks) + (token_out,),
        (proj, halo_proj, taps, logits, gcol, grow),
        [pltpu.VMEM((HALO + tokens, cols), FLOAT)],
        micros=8.0,
        kept=range(7),
        megs=20,
    )
    near_pieces = ring_pieces(pay, "z")
    q, p, query_token = run(
        partial(query_kernel, heads, chunks),
        (out((tokens, kq), HALF), out((heads * chunks, CH, CH), HALF), token_out),
        (proj, halo_proj, taps, k, gcol, grow),
        [pltpu.VMEM((HALO + tokens, kq), FLOAT)],
        after=(pay_token,),
    )
    before, group, near, group_token = run(
        partial(group_kernel, heads), group_shapes(heads) + (token_out,), (mine, *near_pieces), scalars=1, after=(gate_pre[:8, :DK], query_token), micros=2.0
    )
    half_tiles = out((4, rows, model), HALF)
    states, vns, mixed, gated, branch_other, branch_own, far, mix_token = run(
        partial(mix_kernel, heads, chunks),
        mix_shapes(heads, chunks)[:4] + (half_tiles, half_tiles) + mix_shapes(heads, chunks)[4:] + (token_out,),
        (mine, *ring_pieces(group, "y"), before, q, k, w, u, p, n, b, gcol, gate_pre, gain_row, mixer_weight),
        [pltpu.VMEM((tokens, model // 4), FLOAT)],
        scalars=1,
        kept=(0, 1, 2, 6),
        megs=16,
        micros=4.0,
    )
    branch = head_scatter(branch_own, branch_other, mine)
    cot = run(copy_kernel, (out((tokens, width), HALF),), (cotangent,), after=(group_token,))[0]
    cot_tiles = head_gather(cot, mine, (mix_token,))
    whole_cot, cot_rows, d_product, token = run(
        product_grad_kernel,
        (out((tokens, model), HALF), out((rows, model), HALF), out((hidden_cols, tokens), FLOAT), token_out),
        (mine, *cot_tiles, swiglu_down.T),
        scalars=1,
        micros=4.0,
    )
    wide_rows = out((rows, model), FLOAT)
    second_row = second_gain.reshape(1, -1)
    hidden, second_unit, second_factor, own_normed = run(
        hidden_kernel,
        (wide_rows, wide_rows, out((rows, 1), FLOAT), out((rows, model), HALF)),
        (my_rows, second_row, *branch),
        after=(token,),
    )
    turned_out = out((hidden_cols, tokens), HALF)
    second_normed, product, d_gate, d_up, second_other, second_own, ffn_token = run(
        ffn_kernel,
        (out((tokens, model), HALF), turned_out, turned_out, turned_out, half_tiles, half_tiles, token_out),
        (
            mine,
            *head_gather(own_normed, mine),
            swiglu_gate.T,
            swiglu_up.T,
            d_product,
        ),
        [pltpu.VMEM((tokens, model // 4), FLOAT)],
        scalars=1,
        micros=9.0,
        megs=20,
    )
    second_parts, token = head_scatter(second_own, second_other, mine, True)
    grad_args = (mine, whole_cot, second_normed, d_gate, d_up, product)
    *ffn_ends, token = ffn_grads((3,), *grad_args, token)
    ffn_plus, ffn_minus, token = ffn_grads((1, 2), *grad_args, token)
    d_hidden, second_gain_part, back_token = run(
        second_back_kernel,
        (out((rows, model), HALF), out((1, model), FLOAT), token_out),
        (second_unit, second_factor, second_row, cot_rows, *second_parts),
        after=(token,),
    )
    ffn_group, ffn_token = relayed([None, ffn_plus, ffn_minus, *ffn_ends], (back_token,), 3.0)
    down_other, down_own, down_token = down_tiles(mine, product, swiglu_down.T, hidden)
    d_branch, d_branch_own = run(
        join_rows_kernel,
        (out((tokens, model), HALF), out((tokens, width), HALF)),
        (mine, *head_gather(d_hidden, mine, (down_token, ffn_token))),
        scalars=1,
    )
    d_gated = jnp.dot(d_branch, mixer_weight, preferred_element_type=FLOAT)
    dos, dvns, es, d_gate_pre, gain_part, gate_sums, ends = run(
        partial(gate_back_kernel, heads, chunks),
        gate_back_shapes(heads, chunks),
        (d_gated, mixed, gate_pre, gain_row, q, w, p, n, gcol),
        micros=4.0,
    )
    ffn_own, token = ffn_grads((0,), *grad_args, gate_sums[:8])
    *ffn_sums, ffn_token = seq_sums((ffn_own, *ffn_group[1:]), (), mine, (), 3.0)
    tile = out((4, 2 * vd, DK), HALF)
    *mixer_parts, gate_gain = run(
        mixer_grad_kernel,
        (tile,) * 4 + (out((1, model), FLOAT),),
        (mine, d_branch, gated, first_normed, d_gate_pre, gate_rows),
        [pltpu.VMEM((vd, tokens), HALF), pltpu.VMEM((vd, tokens), HALF)],
        scalars=1,
        micros=5.0,
    )
    after, group_end, _, group_token = run(
        partial(group_back_kernel, heads),
        group_back_shapes(heads) + (token_out,),
        (mine, near, *ring_pieces(ends, "z")),
        scalars=1,
        after=(gate_gain, ffn_token),
        micros=2.0,
    )
    end_pieces = ring_pieces(group_end, "y")
    out_keep, out_send, out_token = first_halves(down_own, down_other, mine, (group_token,))
    square = out((heads * chunks, CH, CH), FLOAT)
    *slopes, slope_token = run(
        partial(slopes_kernel, heads, chunks),
        (out((tokens, cols), FLOAT), square, square, out((tokens, vd), FLOAT), token_out),
        (k, v, states, gcol, grow, proj, halo_proj, taps),
        [pltpu.VMEM((HALO + tokens, cols), FLOAT)],
        after=(group_token,),
    )
    passed_sums, ffn_token = passed(ffn_sums, (*end_pieces[1:], slope_token, out_token))
    dproj, halo_grad, d_logit, logit_rows, taps_part, sums = run(
        partial(back_kernel, heads, chunks),
        back_shapes(heads, chunks),
        (mine, far, *end_pieces, after, q, k, logits, gate_sums, gcol, tri, states, vns, dos, dvns, es, n, proj, halo_proj, taps, *slopes),
        back_scratch(heads, chunks),
        scalars=1,
        after=(ffn_token,),
        micros=11.0,
        megs=30,
    )
    packed = 2 * vd + cols + EXTRA
    tile, half_tile = out((4, packed, DK), HALF), out((4, packed // 2, DK), HALF)
    *in_parts, in_token, gains_part = run(
        in_grad_kernel,
        (tile,) * 3 + (half_tile,) * 2 + (token_out, out((2, model), FLOAT)),
        (mine, first_normed, halo_normed, dproj, logit_rows, taps_part, gain_part, gate_gain, second_gain_part, first_row, in_rows, beta_rows, *mixer_parts),
        [pltpu.VMEM((cols + HALO, HALO + tokens), HALF), pltpu.VMEM((EXTRA, DK), FLOAT)],
        scalars=1,
        micros=6.0,
        megs=16,
    )
    out_mine, out_send, out_token = second_halves(out_keep, swapped(out_send, 2), mine, (in_token,))
    ffn_grad_out = out((hidden_cols, DK), FLOAT)
    grad_gate, grad_up, grad_down, ffn_token = run(
        ffn_unpack_kernel, (ffn_grad_out,) * 3 + (token_out,), second_round(passed_sums), after=(out_token,)
    )
    arrived = next_block(halo_grad, -1)
    in_parts, in_token = with_gains(
        mine, in_parts, gains_part, rotated(gains_part, "c", 1), (ffn_token, arrived)
    )
    first_other, first_own, first_token = d_first_tiles(
        mine, dproj, arrived, proj, d_gate_pre, d_logit, sums, in_rows, gate_rows, beta_rows, in_token
    )
    output, out_token = run(
        output_kernel, (out((tokens, width), HALF), token_out), (out_mine, swapped(out_send, 1))
    )
    tile = out((4, packed, DK), HALF)
    plus, minus, in_token, rows_left = run(
        last_relay_kernel,
        (tile, tile, token_out, out((3, 4, 8, DK), FLOAT)),
        (*in_parts[:3], turned(in_parts[3], True, 1), turned(in_parts[4], True, -1)),
        after=(first_token, out_token),
    )
    in_group = (in_parts[0], turned(plus, True, 1), turned(minus, True, -1))
    own_rows, plus_rows, minus_rows, gain_token = run(
        quad_sum_kernel, (out((4, 8, DK), FLOAT),) * 3 + (token_out,), ring_pieces(rows_left, "x"), after=(in_token,)
    )
    first_keep, first_send, _ = first_halves(first_own, first_other, mine, (gain_token,))
    first_mine, first_send, _ = second_halves(first_keep, swapped(first_send, 2), mine, ())
    *sums_out, sum_token = run(
        last_sum_kernel,
        (out((packed, DK), FLOAT),) + (out((packed, DK), HALF),) * 3 + (token_out,),
        (mine, *in_group, own_rows, turned(plus_rows, True, 1), turned(minus_rows, True, -1)),
        scalars=1,
    )
    totals = [sums_out[0]] + [turned(sums_out[i], False, TURNS[i]) for i in range(1, 4)]
    grad_mixer_weight, grad_gate_weight, grad_query, grad_key, grad_value, *taps_grad, gain_grad, beta_grad, both = run(
        unpack_kernel,
        tuple(out((DK, count), FLOAT) for count in (vd, vd, kq, kq, vd)) + tuple(out((rows_, count), FLOAT) for rows_, count in ((4, kq), (4, kq), (4, vd), (1, vd), (heads, DK), (8, DK))),
        totals,
    )
    grad_input = run(
        input_grad_kernel,
        (out((tokens, width), FLOAT),),
        (mine, first_mine, swapped(first_send, 1), block_input, first_factor, first_row, d_branch_own),
        scalars=1,
    )[0]
    return (
        output,
        grad_input,
        both[0],
        grad_query,
        grad_key,
        grad_value,
        grad_gate_weight,
        beta_grad.T,
        taps_grad[0].T,
        taps_grad[1].T,
        taps_grad[2].T,
        gain_grad.reshape(-1),
        grad_mixer_weight,
        both[1],
        grad_gate.T,
        grad_up.T,
        grad_down.T,
    )


def solution(mesh):
    torus = Mesh(mesh.devices.reshape(4, 4, 4, 2), SEQ + HEAD)
    in_specs = (
        P(SEQ, HEAD),
        P(SEQ, HEAD),
        P(),
        P(None, HEAD),
        P(None, HEAD),
        P(None, HEAD),
        P(None, HEAD),
        P(None, HEAD),
        P(HEAD, None),
        P(HEAD, None),
        P(HEAD, None),
        P(HEAD),
        P(None, HEAD),
        P(),
        P(None, HEAD),
        P(None, HEAD),
        P(None, HEAD),
        P(SEQ, HEAD),
    )
    out_specs = (
        P(SEQ, HEAD),
        P(SEQ, HEAD),
        P(SEQ),
        P(SEQ, HEAD),
        P(SEQ, HEAD),
        P(SEQ, HEAD),
        P(SEQ, HEAD),
        P(SEQ, HEAD),
        P(HEAD, None),
        P(HEAD, None),
        P(HEAD, None),
        P(HEAD),
        P(SEQ, HEAD),
        P(SEQ),
        P(SEQ, HEAD),
        P(SEQ, HEAD),
        P(SEQ, HEAD),
    )
    return jax.shard_map(
        shards, mesh=torus, in_specs=in_specs, out_specs=out_specs, check_vma=False
    )
```

```python
from functools import partial

import jax
import jax.numpy as jnp
from jax import lax
from jax.experimental import pallas as pl
from jax.experimental.pallas import tpu as pltpu
from jax.sharding import Mesh
from jax.sharding import PartitionSpec as P

DK = 128
DV = 256
CH = 128
EPS_NORM = 1e-06
EPS_GATE = 1e-05
FLOAT = jnp.float32
HALF = jnp.bfloat16
NN = (((1,), (0,)), ((), ()))
NT = (((1,), (1,)), ((), ()))
TN = (((0,), (0,)), ((), ()))


def mm(a, b, dims=NN):
    return lax.dot_general(a.astype(HALF), b.astype(HALF), dims, preferred_element_type=FLOAT)


def halves(a):
    high = a.astype(HALF)
    return high, (a - high.astype(FLOAT)).astype(HALF)


def mm2(a, b, dims=NN):
    high, low = halves(b)
    return mm(a, high, dims) + mm(a, low, dims)


def mm3(a, b, dims=NN):
    a_high, a_low = halves(a)
    b_high, b_low = halves(b)
    return mm(a_high, b_high, dims) + (mm(a_high, b_low, dims) + mm(a_low, b_high, dims))


def sigmoid(v):
    return 1.0 / (1.0 + jnp.exp(-v))


def square_masks():
    rows = lax.broadcasted_iota(jnp.int32, (CH, CH), 0)
    cols = lax.broadcasted_iota(jnp.int32, (CH, CH), 1)
    return rows, cols


def decay_matrix(gcol, grow):
    rows, cols = square_masks()
    return jnp.where(rows >= cols, jnp.exp(jnp.minimum(gcol - grow, 0.0)), 0.0)


def conv_of(wide, taps, start, count, lanes):
    total = wide[HALO - 3 + start : HALO - 3 + start + count, lanes] * taps[0:1, lanes]
    for j in range(1, 4):
        total = total + wide[HALO - 3 + j + start : HALO - 3 + j + start + count, lanes] * taps[j : j + 1, lanes]
    return total


def query_kernel(heads, chunks, proj, halo, taps, k, gcol, grow, q_out, p_out, token, wide):
    token[...] = jnp.zeros(token.shape, FLOAT)
    kq = heads * DK
    wide[:HALO, :] = halo[:, :kq].astype(FLOAT)
    wide[HALO:, :] = proj[:, :kq].astype(FLOAT)
    for h in range(heads):
        for c in range(chunks):
            span = slice(c * CH, (c + 1) * CH)
            lanes = slice(h * DK, (h + 1) * DK)
            at = h * chunks + c
            cq = conv_of(wide, taps, c * CH, CH, lanes)
            query = (cq * sigmoid(cq)).astype(HALF)
            q_out[span, lanes] = query
            spread = decay_matrix(gcol[span, h : h + 1], grow[at : at + 1, :])
            p_out[at] = (spread * mm(query, k[span, lanes], NT)).astype(HALF)


def prepare_kernel(heads, chunks, proj, halo, taps, logits, gcol, grow, k_out, v_out, t_out, n_out, b_out, w_out, u_out, pay, token, wide):
    token[...] = jnp.zeros(token.shape, FLOAT)
    rows, cols = square_masks()
    differ = rows ^ cols
    eye = jnp.where(rows == cols, 1.0, 0.0)
    wide[:HALO, :] = halo[...].astype(FLOAT)
    wide[HALO:, :] = proj[...].astype(FLOAT)
    kq = heads * DK
    work = [(h, c) for h in range(heads) for c in range(chunks)]
    low, keys, sides = {}, {}, {}
    for h, c in work:
        span = slice(c * CH, (c + 1) * CH)
        ql, kl, vl = (
            slice(h * DK, (h + 1) * DK),
            slice(kq + h * DK, kq + (h + 1) * DK),
            slice(2 * kq + h * DV, 2 * kq + (h + 1) * DV),
        )
        ck = conv_of(wide, taps, c * CH, CH, kl)
        act = ck * sigmoid(ck)
        key = (act * lax.rsqrt(jnp.sum(act * act, axis=-1, keepdims=True) + EPS_NORM)).astype(HALF)
        cv = conv_of(wide, taps, c * CH, CH, vl)
        value = (cv * sigmoid(cv)).astype(HALF)
        k_out[span, ql] = key
        v_out[span, h * DV : (h + 1) * DV] = value
        beta = sigmoid(logits[span, h : h + 1])
        g = gcol[span, h : h + 1]
        spread = decay_matrix(g, grow[h * chunks + c : h * chunks + c + 1, :])
        inner = mm(key, key, NT)
        low[h, c] = jnp.where(rows > cols, beta * spread * inner, 0.0)
        keys[h, c] = key
        sides[h, c] = jnp.concatenate([(beta * jnp.exp(g)) * key.astype(FLOAT), beta * value.astype(FLOAT)], axis=1)
    tri = {at: eye - jnp.where(differ < 2, low[at], 0.0) for at in work}
    size = 2
    while size < CH:
        part = {at: mm3(jnp.where((differ >= size) & (differ < 2 * size), low[at], 0.0), tri[at]) for at in work}
        tri = {at: tri[at] - mm3(tri[at], part[at]) for at in work}
        size *= 2
    steps = {}
    for h, c in work:
        at = h * chunks + c
        t_out[at] = tri[h, c].astype(HALF)
        solved = mm3(tri[h, c], sides[h, c])
        w_out[at] = solved[:, :DK].astype(HALF)
        u_out[at] = solved[:, DK:].astype(HALF)
        g = gcol[c * CH : (c + 1) * CH, h : h + 1]
        last = gcol[(c + 1) * CH - 1 : (c + 1) * CH, h : h + 1]
        step = mm2(keys[h, c], jnp.exp(last - g) * solved, TN)
        n_out[at] = step[:, :DK].astype(HALF)
        b_out[at] = step[:, DK:]
        steps[h, c] = (jnp.exp(last), step)
    zero = jnp.zeros((DK, DK), FLOAT)
    for h in range(heads):
        decay, step = steps[h, 0]
        total = jnp.concatenate([decay * eye - step[:, :DK], step[:, DK:]], axis=1)
        whole = decay
        for c in range(1, chunks):
            decay, step = steps[h, c]
            total = decay * total - mm3(step[:, :DK], total) + jnp.concatenate([zero, step[:, DK:]], axis=1)
            whole = whole * decay
        pack_map(pay, h, total, whole, eye)


def whole_decay(pay, j, h):
    return pay[j, h, DK : DK + 1, 0:1].astype(FLOAT) + pay[j, h, DK + 8 : DK + 9, 0:1].astype(FLOAT)


def apply_whole(pay, j, h, state, dims):
    return whole_decay(pay, j, h) * state + mm(pay[j, h, :DK, :DK], state, dims)


def pack_map(pay, h, total, whole, eye):
    pay[h, :DK, :] = jnp.concatenate([total[:, :DK] - whole * eye, total[:, DK:]], axis=1).astype(HALF)
    rest = jnp.broadcast_to(whole, (8, DK + DV))
    first = rest.astype(HALF).astype(FLOAT)
    pay[h, DK:, :] = jnp.concatenate([first, rest - first], axis=0).astype(HALF)


def group_kernel(heads, mine, p0, p1, p2, p3, before, group, near, token):
    token[...] = jnp.zeros(token.shape, FLOAT)
    me = mine[3]
    for k, piece in enumerate((p0, p1, p2, p3)):
        near[ring_place(me, k)] = piece[...]
    rows, cols = square_masks()
    eye = jnp.where(rows == cols, 1.0, 0.0)
    zero = jnp.zeros((DK, DK), FLOAT)
    start = jnp.concatenate([eye, jnp.zeros((DK, DV), FLOAT)], axis=1)
    totals, keeps, wholes = [start] * heads, [start] * heads, [jnp.ones((1, 1), FLOAT)] * heads
    for j in range(near.shape[0]):
        for h in range(heads):
            added = jnp.concatenate([zero, near[j, h, :DK, DK:].astype(FLOAT)], axis=1)
            if j == 0:
                moved = jnp.concatenate([whole_decay(near, j, h) * eye + near[j, h, :DK, :DK].astype(FLOAT), added[:, DK:]], axis=1)
            else:
                moved = apply_whole(near, j, h, totals[h], NN) + added
            totals[h] = moved
            wholes[h] = wholes[h] * whole_decay(near, j, h)
            keeps[h] = jnp.where(me == j + 1, moved, keeps[h])
    for h in range(heads):
        before[h] = keeps[h]
        pack_map(group, h, totals[h], wholes[h], eye)


def group_back_kernel(heads, mine, near, p0, p1, p2, p3, after, group, ends, token):
    token[...] = jnp.zeros(token.shape, FLOAT)
    me = mine[3]
    for k, piece in enumerate((p0, p1, p2, p3)):
        ends[ring_place(me, k)] = piece[...]
    rows, cols = square_masks()
    eye = jnp.where(rows == cols, 1.0, 0.0)
    zero = jnp.zeros((DK, DK), FLOAT)
    start = jnp.concatenate([eye, jnp.zeros((DK, DV), FLOAT)], axis=1)
    totals, keeps = [start] * heads, [start] * heads
    for j in reversed(range(near.shape[0])):
        for h in range(heads):
            keeps[h] = jnp.where(me == j, totals[h], keeps[h])
            added = jnp.concatenate([zero, ends[j, h].astype(FLOAT)], axis=1)
            totals[h] = apply_whole(near, j, h, totals[h], TN) + added
    for h in range(heads):
        after[h] = keeps[h]
        group[h] = totals[h][:, DK:].astype(HALF)


def spread_rows(core, total, own, other, rows, lanes):
    for x in range(4):
        mine = pl.ds(pl.multiple_of((2 * x + core) * rows, rows), rows)
        away = pl.ds(pl.multiple_of((2 * x + 1 - core) * rows, rows), rows)
        own[x, :, lanes] = total[mine, :].astype(HALF)
        other[x, :, lanes] = total[away, :].astype(HALF)


def mix_kernel(heads, chunks, mine, p0, p1, p2, p3, before, q, k, w, u, p, n, b, gcol, gate, gain, weight, s_out, vn_out, o_out, gated, other, own, pay, token, total):
    token[...] = jnp.zeros(token.shape, FLOAT)
    ranks = pay.shape[0]
    me = mine[2]
    for at, piece in enumerate((p0, p1, p2, p3)):
        pay[ring_place(me, at)] = piece[...]
    states = [jnp.zeros((DK, DV), FLOAT) for h in range(heads)]
    for j in range(ranks - 1):
        passed = j < me
        for h in range(heads):
            moved = apply_whole(pay, j, h, states[h], NN) + pay[j, h, :DK, DK:].astype(FLOAT)
            states[h] = jnp.where(passed, moved, states[h])
    for h in range(heads):
        states[h] = mm3(before[h, :, :DK], states[h]) + before[h, :, DK:]
    for c in range(chunks):
        span = slice(c * CH, (c + 1) * CH)
        for h in range(heads):
            at = h * chunks + c
            state = states[h].astype(HALF)
            s_out[at] = state
            g = gcol[span, h : h + 1]
            last = gcol[(c + 1) * CH - 1 : (c + 1) * CH, h : h + 1]
            vn = (u[at].astype(FLOAT) - mm(w[at], state)).astype(HALF)
            vn_out[at] = vn
            out = jnp.exp(g) * mm(q[span, h * DK : (h + 1) * DK], state) + mm(p[at], vn)
            vl = slice(h * DV, (h + 1) * DV)
            o_out[span, vl] = out
            factor = lax.rsqrt(jnp.mean(out * out, axis=-1, keepdims=True) + EPS_GATE)
            pre = gate[span, vl]
            gated[span, vl] = (out * factor * gain[:, vl] * (pre * sigmoid(pre))).astype(HALF)
            if c + 1 < chunks:
                states[h] = jnp.exp(last) * states[h] - mm(n[at], state) + b[at]
    width = weight.shape[0]
    tile = total.shape[1]
    rows = own.shape[1]
    for at in range(0, width, tile):
        lanes = slice(at, at + tile)
        total[...] = mm(gated[...], weight[lanes, :], NT)
        spread_rows(mine[1], total, own, other, rows, lanes)


def gate_back_kernel(heads, chunks, d_gated, out, gate, gain, q, w, p, n, gcol, do_out, dvn_out, e_out, dpre_out, dgain_out, sums_out, pay):
    dgain = [jnp.zeros((1, DV), FLOAT) for h in range(heads)]
    ends = [None] * heads
    for c in reversed(range(chunks)):
        span = slice(c * CH, (c + 1) * CH)
        for h in range(heads):
            at = h * chunks + c
            vl = slice(h * DV, (h + 1) * DV)
            dg, o, pre, gn = d_gated[span, vl], out[span, vl], gate[span, vl], gain[:, vl]
            sig = sigmoid(pre)
            factor = lax.rsqrt(jnp.mean(o * o, axis=-1, keepdims=True) + EPS_GATE)
            m = o * factor
            s = pre * sig
            dgm = dg * m
            dgain[h] = dgain[h] + jnp.sum(dgm * s, axis=0, keepdims=True)
            dpre = dgm * gn * (sig * (1.0 + pre * (1.0 - sig)))
            dpre_out[span, vl] = dpre.astype(HALF)
            row_sum = jnp.sum(dpre * pre, axis=-1, keepdims=True)
            sums_out[span, :] = row_sum if h == 0 else sums_out[span, :] + row_sum
            e = dg * gn * s
            dout = factor * (e - m * jnp.mean(e * m, axis=-1, keepdims=True))
            do_out[span, vl] = dout.astype(HALF)
            g = gcol[span, h : h + 1]
            last = gcol[(c + 1) * CH - 1 : (c + 1) * CH, h : h + 1]
            dvn = mm(p[at], dout, TN)
            dvn_out[at] = dvn
            source = mm(q[span, h * DK : (h + 1) * DK], jnp.exp(g) * dout, TN) - mm(w[at], dvn, TN)
            e_out[at] = source
            if ends[h] is None:
                ends[h] = source
            else:
                ends[h] = jnp.exp(last) * ends[h] - mm(n[at], ends[h], TN) + source
    for h in range(heads):
        pay[h] = ends[h].astype(HALF)
        dgain_out[0:1, h * DV : (h + 1) * DV] = dgain[h]


def slopes_kernel(heads, chunks, k, v, states, gcol, grow, proj, halo, taps, slopes, inner_out, spread_out, rest, token, wide):
    token[...] = jnp.zeros(token.shape, FLOAT)
    kq = heads * DK
    wide[:HALO, :] = halo[...].astype(FLOAT)
    wide[HALO:, :] = proj[...].astype(FLOAT)
    for h in range(heads):
        for c in range(chunks):
            span = slice(c * CH, (c + 1) * CH)
            at = h * chunks + c
            kl = slice(kq + h * DK, kq + (h + 1) * DK)
            for lanes in (slice(h * DK, (h + 1) * DK), slice(2 * kq + h * DV, 2 * kq + (h + 1) * DV)):
                pre = conv_of(wide, taps, c * CH, CH, lanes)
                sig = sigmoid(pre)
                slopes[span, lanes] = sig * (1.0 + pre * (1.0 - sig))
            pre = conv_of(wide, taps, c * CH, CH, kl)
            sig = sigmoid(pre)
            act = pre * sig
            unit = lax.rsqrt(jnp.sum(act * act, axis=-1, keepdims=True) + EPS_NORM)
            slopes[span, kl] = unit * (sig * (1.0 + pre * (1.0 - sig)))
            key = k[span, h * DK : (h + 1) * DK]
            g = gcol[span, h : h + 1]
            inner_out[at] = mm(key, key, NT)
            spread_out[at] = decay_matrix(g, grow[at : at + 1, :])
            vl = slice(h * DV, (h + 1) * DV)
            rest[span, vl] = v[span, vl].astype(FLOAT) - jnp.exp(g) * mm(key, states[at])


def back_kernel(heads, chunks, mine, pay, p0, p1, p2, p3, after, q, k, logits, gate_sums, gcol, tri, states, vns, dos, dvns, es, ns, proj, halo, taps, slopes, inner_in, spread_in, rest, dproj_out, halo_out, dlogit_out, logit_rows, dtaps_out, sums_out, wide, dconv, late, rowsum):
    ranks = pay.shape[0]
    tokens = chunks * CH
    me = mine[2]
    for at, piece in enumerate((p0, p1, p2, p3)):
        late[ring_place(me, at)] = piece[...]
    kq = heads * DK
    width = 2 * kq + heads * DV
    rows, cols = square_masks()
    grads = [jnp.zeros((DK, DV), FLOAT) for h in range(heads)]
    for j in reversed(range(1, ranks)):
        passed = j > me
        for h in range(heads):
            moved = apply_whole(pay, j, h, grads[h], TN) + late[j, h].astype(FLOAT)
            grads[h] = jnp.where(passed, moved, grads[h])
    for h in range(heads):
        grads[h] = mm3(after[h, :, :DK], grads[h]) + after[h, :, DK:]
    wide[:HALO, :] = halo[...].astype(FLOAT)
    wide[HALO:, :] = proj[...].astype(FLOAT)
    logit_rows[...] = jnp.zeros(logit_rows.shape, FLOAT)
    dconv[0:HALO, :] = jnp.zeros((HALO, width), FLOAT)
    dconv[HALO + tokens :, :] = jnp.zeros((8, width), FLOAT)
    for c in reversed(range(chunks)):
        span = slice(c * CH, (c + 1) * CH)
        for h in range(heads):
            at = h * chunks + c
            ql, kl, vl, ol = (
                slice(h * DK, (h + 1) * DK),
                slice(kq + h * DK, kq + (h + 1) * DK),
                slice(2 * kq + h * DV, 2 * kq + (h + 1) * DV),
                slice(h * DV, (h + 1) * DV),
            )
            grad = grads[h].astype(HALF)
            query, key = q[span, ql], k[span, ql]
            state, vn, dout = states[at], vns[at], dos[span, ol]
            logit = logits[span, h : h + 1]
            beta = sigmoid(logit)
            g = gcol[span, h : h + 1]
            last = gcol[(c + 1) * CH - 1 : (c + 1) * CH, h : h + 1]
            eg, ed = jnp.exp(g), jnp.exp(last - g)
            spread = spread_in[at]
            strict = jnp.where(rows > cols, spread, 0.0)
            inner = inner_in[at]
            dvn = dvns[at] + ed * mm(key, grad)
            dr = mm(tri[at], dvn, TN)
            drh = dr.astype(HALF)
            dval = beta * dr
            both = mm(jnp.concatenate([dout, drh], axis=0), state, NT)
            dkeep = mm(vn, grad, NT)
            pair = mm(jnp.concatenate([dout, drh], axis=0), vn, NT)
            dqk = spread * pair[:CH]
            da = -(strict * pair[CH:])
            dkk = beta * da
            dbeta = jnp.sum(dr * rest[span, ol], axis=-1, keepdims=True) + jnp.sum(
                da * inner, axis=-1, keepdims=True
            )
            dqkh = dqk.astype(HALF)
            dkkh = dkk.astype(HALF)
            dquery = eg * both[:CH] + mm(dqkh, key)
            dkey = (
                ed * dkeep
                - (beta * eg) * both[CH:]
                + mm(dqkh, query, TN)
                + mm(dkkh, key)
                + mm(dkkh, key, TN)
            )
            if c > 0:
                grads[h] = jnp.exp(last) * grads[h] - mm(ns[at], grad, TN) + es[at]
            dlogit = dbeta * beta * (1.0 - beta)
            dlogit_out[span, h : h + 1] = dlogit
            logit_rows[h : h + 1, HALO + c * CH : HALO + (c + 1) * CH] = jnp.broadcast_to(dlogit, (CH, DK)).T[0:1]
            extra_sum = dlogit * logit
            far_span = slice(HALO + c * CH, HALO + (c + 1) * CH)
            sums_out[far_span, :] = (gate_sums[span, :] if h == 0 else sums_out[far_span, :]) + extra_sum
            there = slice(HALO + c * CH, HALO + (c + 1) * CH)
            dconv[there, ql] = dquery * slopes[span, ql]
            dconv[there, vl] = dval * slopes[span, vl]
            unit = key.astype(FLOAT)
            dconv[there, kl] = (dkey - unit * jnp.sum(dkey * unit, axis=-1, keepdims=True)) * slopes[span, kl]
    dtaps_out[4:8, :] = jnp.zeros((4, width), FLOAT)
    rowsum[...] = jnp.zeros((HALO + tokens, 1), FLOAT)
    for at in range(0, width, DK):
        lanes = slice(at, at + DK)
        for j in range(4):
            dtaps_out[j : j + 1, lanes] = jnp.sum(
                dconv[HALO : HALO + tokens, lanes] * wide[HALO - 3 + j : HALO - 3 + j + tokens, lanes], axis=0, keepdims=True
            )
        total = dconv[3 : 3 + HALO + tokens, lanes] * taps[0:1, lanes]
        for j in range(1, 4):
            total = total + dconv[3 - j : 3 - j + HALO + tokens, lanes] * taps[j : j + 1, lanes]
        small = total.astype(HALF)
        dproj_out[:, lanes] = small
        halo_out[:, lanes] = small[:HALO]
        rowsum[...] += jnp.sum(small.astype(FLOAT) * wide[:, lanes], axis=-1, keepdims=True)
    sums_out[HALO:, :] += rowsum[HALO:, :]
    sums_out[:HALO, :] = rowsum[:HALO, :]


def out(shape, dtype):
    return jax.ShapeDtypeStruct(shape, dtype)


def cost(micros):
    return pl.CostEstimate(flops=int(micros * 1.1e7), bytes_accessed=0, transcendentals=0)


def run(kernel, shapes, args, scratch=(), scalars=0, after=(), micros=1.0, megs=12, kept=()):
    vmem = pl.BlockSpec(memory_space=pltpu.VMEM)
    smem = pl.BlockSpec(memory_space=pltpu.SMEM)
    count = len(args)

    def body(*refs):
        kernel(*refs[:count], *refs[count + len(after) :])

    return pl.pallas_call(
        body,
        out_shape=tuple(pltpu.HBM(a.shape, a.dtype) if i in kept else a for i, a in enumerate(shapes)),
        in_specs=[smem] * scalars + [vmem] * (count - scalars) + [pl.BlockSpec(memory_space=pl.ANY)] * len(after),
        out_specs=[pl.BlockSpec() if i in kept else vmem for i in range(len(shapes))],
        scratch_shapes=list(scratch),
        compiler_params=pltpu.CompilerParams(vmem_limit_bytes=megs * 2**20),
        cost_estimate=cost(micros),
    )(*args, *after)


def passed(arrays, after):
    count = len(arrays)
    anywhere = pl.BlockSpec(memory_space=pl.ANY)

    def body(*refs):
        token = refs[-1]
        token[...] = jnp.zeros(token.shape, FLOAT)

    *same, token = pl.pallas_call(
        body,
        out_shape=tuple(out(a.shape, a.dtype) for a in arrays) + (out((8, DK), FLOAT),),
        in_specs=[anywhere] * (count + len(after)),
        out_specs=[anywhere] * count + [pl.BlockSpec(memory_space=pltpu.VMEM)],
        input_output_aliases={i: i for i in range(count)},
        compiler_params=pltpu.CompilerParams(vmem_limit_bytes=2**20),
        cost_estimate=cost(0.1),
    )(*arrays, *after)
    return same, token


def prepare_shapes(heads, chunks):
    tokens, pairs = chunks * CH, heads * chunks
    return (
        out((tokens, heads * DK), HALF),
        out((tokens, heads * DV), HALF),
        out((pairs, CH, CH), HALF),
        out((pairs, DK, DK), HALF),
        out((pairs, DK, DV), FLOAT),
        out((pairs, CH, DK), HALF),
        out((pairs, CH, DV), HALF),
        out((heads, DK + 16, DK + DV), HALF),
    )


def mix_shapes(heads, chunks):
    tokens, pairs = chunks * CH, heads * chunks
    return (
        out((pairs, DK, DV), HALF),
        out((pairs, CH, DV), HALF),
        out((tokens, heads * DV), FLOAT),
        out((tokens, heads * DV), HALF),
        out((4, heads, DK + 16, DK + DV), HALF),
    )


def gate_back_shapes(heads, chunks):
    tokens, pairs = chunks * CH, heads * chunks
    return (
        out((tokens, heads * DV), HALF),
        out((pairs, CH, DV), FLOAT),
        out((pairs, DK, DV), FLOAT),
        out((tokens, heads * DV), HALF),
        out((1, heads * DV), FLOAT),
        out((tokens, 1), FLOAT),
        out((heads, DK, DV), HALF),
    )


def back_shapes(heads, chunks):
    tokens = chunks * CH
    width = heads * (2 * DK + DV)
    return (
        out((HALO + tokens, width), HALF),
        out((HALO, width), HALF),
        out((tokens, heads), FLOAT),
        out((HALO, HALO + tokens), FLOAT),
        out((8, width), FLOAT),
        out((HALO + tokens, 1), FLOAT),
    )


def back_scratch(heads, chunks):
    tokens = chunks * CH
    width = heads * (2 * DK + DV)
    return (pltpu.VMEM((HALO + tokens, width), FLOAT), pltpu.VMEM((HALO + tokens + 8, width), FLOAT), pltpu.VMEM((4, heads, DK, DV), HALF), pltpu.VMEM((HALO + tokens, 1), FLOAT))


def group_shapes(heads):
    pay = (heads, DK + 16, DK + DV)
    return (out((heads, DK, DK + DV), FLOAT), out(pay, HALF), out((4, *pay), HALF))


def group_back_shapes(heads):
    return (
        out((heads, DK, DK + DV), FLOAT),
        out((heads, DK, DV), HALF),
        out((4, heads, DK, DV), HALF),
    )


HEAD = ("x", "c")
SEQ = ("y", "z")
PLANE = ("y", "z", "c")
HALO = 16
EXTRA = 64
TURNS = (0, 1, -1, 2)


def rotated(array, axis, distance):
    size = lax.axis_size(axis)
    return lax.ppermute(array, axis, [(i, (i + distance) % size) for i in range(size)])


def ring_pieces(array, axis):
    return [array] + [rotated(array, axis, -d) for d in TURNS[1:]]


def join_kernel(mine, *refs):
    for k in range(4):
        refs[4][ring_place(mine[0], k)] = refs[k][...]


def head_gather(array, mine, after=()):
    shapes = (out((4, *array.shape), array.dtype),)
    own = run(join_kernel, shapes, (mine, *ring_pieces(array, "x")), scalars=1, after=after)[0]
    return own, rotated(own, "c", 1)


def head_tiles(mine, own, other):
    core = mine[1]
    return [(2 * x + which, ref, x) for which, ref in ((core, own), (1 - core, other)) for x in range(4)]


def copy_kernel(source, target):
    target[...] = source[...]


def turned(array, first, distance):
    pairs = []
    for y in range(4):
        for z in range(4):
            for core in range(2):
                along_z = (core == 0) == first
                to = (y, (z + distance) % 4) if along_z else ((y + distance) % 4, z)
                pairs.append(((y * 4 + z) * 2 + core, (to[0] * 4 + to[1]) * 2 + core))
    return lax.ppermute(array, PLANE, pairs)


def ring_place(mine, k):
    return lax.rem(mine + TURNS[k] + 4, 4)


def lane_block(at, width):
    return pl.ds(pl.multiple_of(at * width, width), width)


def setup_kernel(query, key, value, gate, decay, in_out, gate_out, gcol, grow, token):
    at = 0
    for weight in (query, key, value):
        count = weight.shape[1]
        in_out[at : at + count, :] = weight[...].T
        at += count
    gate_out[...] = gate[...].T
    rows, cols = square_masks()
    heads, tokens = decay.shape
    chunks = tokens // CH
    for h in range(heads):
        for c in range(chunks):
            span = slice(c * CH, (c + 1) * CH)
            flat = jnp.broadcast_to(decay[h : h + 1, span], (CH, CH))
            grow[h * chunks + c : h * chunks + c + 1, :] = jnp.sum(
                jnp.where(rows <= cols, flat.T, 0.0), axis=0, keepdims=True
            )
            gcol[span, h : h + 1] = jnp.sum(jnp.where(cols <= rows, flat, 0.0), axis=1, keepdims=True)
    token[...] = jnp.zeros(token.shape, FLOAT)


def first_norm_kernel(mine, gain, beta_rows, own, other, normed, factor, rows_out, logits, halo_out):
    width = own.shape[2]
    rows = rows_out.shape[0]
    own_rows = lane_block(mine[0] * 2 + mine[1], rows)
    square = 0.0
    for _, ref, x in head_tiles(mine, own, other):
        wide = ref[x].astype(FLOAT)
        square = square + jnp.sum(wide * wide, axis=-1, keepdims=True)
    scale = lax.rsqrt(square / (8 * width) + EPS_NORM)
    factor[...] = scale
    total = 0.0
    for head, ref, x in head_tiles(mine, own, other):
        lanes = lane_block(head, width)
        small = (ref[x].astype(FLOAT) * scale * gain[:, lanes]).astype(HALF)
        normed[:, lanes] = small
        total = total + mm(small, beta_rows[:, lanes], NT)
        rows_out[:, lanes] = ref[x, own_rows, :].astype(FLOAT)
    logits[...] = total
    halo_out[...] = normed[normed.shape[0] - HALO :, :]


def product_grad_kernel(mine, own, other, weight, whole, rows_out, grad, token):
    width = own.shape[2]
    rows = rows_out.shape[0]
    own_rows = lane_block(mine[0] * 2 + mine[1], rows)
    for head, ref, x in head_tiles(mine, own, other):
        lanes = lane_block(head, width)
        whole[:, lanes] = ref[x]
        rows_out[:, lanes] = ref[x, own_rows, :]
    grad[...] = mm(weight[...], whole[...], NT)
    token[...] = jnp.zeros(token.shape, FLOAT)


def hidden_kernel(rows_in, gain, first, second, third, fourth, hidden, unit, factor, normed):
    total = rows_in[...] + first[...] + second[...].astype(FLOAT) + third[...].astype(FLOAT) + fourth[...].astype(FLOAT)
    hidden[...] = total
    scale = lax.rsqrt(jnp.mean(total * total, axis=-1, keepdims=True) + EPS_NORM)
    factor[...] = scale
    unit[...] = total * scale
    normed[...] = (total * scale * gain[...]).astype(HALF)


def second_back_kernel(unit, factor, gain, cot_rows, first, second, third, fourth, d_hidden, gain_part, token):
    token[...] = jnp.zeros(token.shape, FLOAT)
    total = first[...] + second[...].astype(FLOAT) + third[...].astype(FLOAT) + fourth[...].astype(FLOAT)
    n = unit[...]
    gain_part[...] = jnp.sum(total * n, axis=0, keepdims=True)
    e = total * gain[...]
    mean = jnp.mean(e * n, axis=-1, keepdims=True)
    d_hidden[...] = (cot_rows[...].astype(FLOAT) + factor[...] * (e - n * mean)).astype(HALF)


def ffn_kernel(mine, own_in, other_in, gate_rows, up_rows, d_product, normed, product, d_gate, d_up, other, own, token, total):
    rows = own_in.shape[1]
    for head, ref, x in head_tiles(mine, own_in, other_in):
        normed[lane_block(head, rows), :] = ref[x]
    cols = gate_rows.shape[0]
    step = cols // 2
    for at in range(0, cols, step):
        span = slice(at, at + step)
        gate = mm(gate_rows[span, :], normed[...], NT)
        up = mm(up_rows[span, :], normed[...], NT)
        sig = sigmoid(gate)
        act = gate * sig
        product[span, :] = (act * up).astype(HALF)
        grad = d_product[span, :]
        dg = (grad * up * (sig * (1.0 + gate * (1.0 - sig)))).astype(HALF)
        du = (grad * act).astype(HALF)
        d_gate[span, :] = dg
        d_up[span, :] = du
    token[...] = jnp.zeros(token.shape, FLOAT)
    gate_turned = d_gate[...].T
    up_turned = d_up[...].T
    width = normed.shape[1]
    tile = width // 4
    core = mine[1]
    for at in range(0, width, tile):
        lanes = slice(at, at + tile)
        total[...] = mm(gate_turned, gate_rows[:, lanes]) + mm(up_turned, up_rows[:, lanes])
        spread_rows(core, total, own, other, rows, lanes)


def join_rows_kernel(mine, own, other, whole, own_cols):
    rows = own.shape[1]
    lanes = lane_block(mine[0] * 2 + mine[1], own_cols.shape[1])
    for head, ref, x in head_tiles(mine, own, other):
        whole[lane_block(head, rows), :] = ref[x]
        own_cols[lane_block(head, rows), :] = ref[x, :, lanes]


def split_sum_kernel(mine, own, arrived, *outs):
    for k in range(4):
        at = ring_place(mine[0], k)
        outs[k][...] = (own[at].astype(FLOAT) + arrived[at].astype(FLOAT)).astype(outs[k].dtype)
    outs[4][...] = jnp.zeros(outs[4].shape, FLOAT)


def head_scatter(own, other, mine, with_token=False, after=()):
    arrived = rotated(other, "c", 1)
    shape = own.shape[1:]
    shapes = (out(shape, FLOAT),) + (out(shape, HALF),) * 3 + (out((8, DK), FLOAT),)
    total, *sent, token = run(split_sum_kernel, shapes, (mine, own, arrived), scalars=1, after=after)
    parts = [total] + [rotated(part, "x", d) for d, part in zip(TURNS[1:], sent)]
    return (parts, token) if with_token else parts


def swapped(array, mask):
    return lax.ppermute(array, "x", [(i, i ^ mask) for i in range(4)])


def first_half_kernel(mine, own, arrived, keep, send, token):
    token[...] = jnp.zeros(token.shape, FLOAT)
    base = jnp.where(mine[0] < 2, 0, 2)
    for target, at in ((keep, base), (send, 2 - base)):
        for i in range(2):
            target[i] = (own[at + i].astype(FLOAT) + arrived[at + i].astype(FLOAT)).astype(target.dtype)


def second_half_kernel(mine, keep, arrived, own, send, token):
    token[...] = jnp.zeros(token.shape, FLOAT)
    at = lax.rem(mine[0], 2)
    own[...] = keep[at].astype(FLOAT) + arrived[at].astype(FLOAT)
    send[...] = (keep[1 - at].astype(FLOAT) + arrived[1 - at].astype(FLOAT)).astype(HALF)


def first_halves(own, other, mine, after):
    pair = out((2, *own.shape[1:]), HALF)
    return run(
        first_half_kernel,
        (pair, pair, out((8, DK), FLOAT)),
        (mine, own, rotated(other, "c", 1)),
        scalars=1,
        after=after,
    )


def second_halves(keep, arrived, mine, after):
    shape = keep.shape[1:]
    return run(
        second_half_kernel,
        (out(shape, FLOAT), out(shape, HALF), out((8, DK), FLOAT)),
        (mine, keep, arrived),
        scalars=1,
        after=after,
    )


def added(parts):
    total = parts[0]
    for part in parts[1:]:
        total = total + part.astype(FLOAT)
    return total


def dest_block(mine, k, o):
    core = mine[1]
    place = ring_place(jnp.where(core == 0, mine[3], mine[2]), k)
    return jnp.where(core == 0, o * 4 + place, place * 4 + o)


def store_tile(outs, k, o, early, value):
    count = early.shape[0]
    if k < 3:
        outs[k][o, :count, :] = early
        outs[k][o, count:, :] = value
    else:
        spare = outs[3].shape[1] - count
        outs[3][o, :count, :] = early
        outs[3][o, count:, :] = value[:spare]
        outs[4][o] = value[spare:]


def mixer_grad_kernel(mine, d_branch, gated, normed, d_pre, gate_rows, *refs):
    outs, (gain_out, gated_turned, pre_turned) = refs[:4], refs[4:]
    gated_turned[...] = gated[...].T
    pre_turned[...] = d_pre[...].T
    for k in range(4):
        for o in (0, 2):
            blocks = [lane_block(dest_block(mine, k, o + i), DK) for i in range(2)]
            mixer = mm(gated_turned[...], jnp.concatenate([d_branch[:, at] for at in blocks], axis=1))
            gate = mm(pre_turned[...], jnp.concatenate([normed[:, at] for at in blocks], axis=1))
            for i, at in enumerate(blocks):
                half = slice(i * DK, (i + 1) * DK)
                outs[k][o + i] = jnp.concatenate([mixer[:, half], gate[:, half]], axis=0).astype(HALF)
                gain_out[:, at] = jnp.sum(gate[:, half] * gate_rows[:, at].astype(FLOAT), axis=0, keepdims=True)


def in_grad_kernel(mine, normed, halo, dproj, d_logit, taps, mixer_gain, gate_gain, second_gain, first_gain, in_rows, beta_rows, *refs):
    early, outs, (token, gains, turned_refs, extra) = refs[:4], refs[4:9], refs[9:]
    token[...] = jnp.zeros(token.shape, FLOAT)
    cols = dproj.shape[1]
    heads = 2
    turned_refs[:cols, :] = dproj[...].T
    turned_refs[cols:, :] = d_logit[...].astype(HALF)
    extra[...] = jnp.zeros(extra.shape, FLOAT)
    per_tap = cols // DK
    for j in range(4):
        for i in range(per_tap):
            extra[j * per_tap + i : j * per_tap + i + 1, :] = taps[j : j + 1, i * DK : (i + 1) * DK]
    for i in range(mixer_gain.shape[1] // DK):
        extra[32 + i : 33 + i, :] = mixer_gain[:, i * DK : (i + 1) * DK]
    for k in range(4):
        for o in (0, 2):
            blocks = [lane_block(dest_block(mine, k, o + i), DK) for i in range(2)]
            left = jnp.concatenate(
                [jnp.concatenate([halo[:, at], normed[:, at]], axis=0) for at in blocks], axis=1
            )
            grads = mm(turned_refs[...], left)
            for i, at in enumerate(blocks):
                half = slice(i * DK, (i + 1) * DK)
                beta = grads[cols : cols + heads, half]
                gain = (
                    jnp.sum(grads[:cols, half] * in_rows[:, at].astype(FLOAT), axis=0, keepdims=True)
                    + jnp.sum(beta * beta_rows[:heads, at].astype(FLOAT), axis=0, keepdims=True)
                    + gate_gain[:, at]
                )
                extra[36 : 36 + heads, :] = beta
                gains[0:1, at] = gain / first_gain[:, at]
                gains[1:2, at] = second_gain[:, at]
                store_tile(
                    outs, k, o + i, early[k][o + i], jnp.concatenate([grads[:cols, half], extra[...]], axis=0).astype(HALF)
                )


def ffn_grad_kernel(turns, mine, cot, normed, d_gate, d_up, product, *refs):
    outs, token = refs[:-1], refs[-1]
    token[...] = jnp.zeros(token.shape, FLOAT)
    cols = d_gate.shape[0]
    half_rows = 3 * cols // 2
    for k in turns:
        for o in (0, 2):
            blocks = [lane_block(dest_block(mine, k, o + i), DK) for i in range(2)]
            lefts = [jnp.concatenate([ref[:, at] for at in blocks], axis=1) for ref in (normed, cot)]
            for n, (right, left) in enumerate(((d_gate, lefts[0]), (d_up, lefts[0]), (product, lefts[1]))):
                both = mm(right[...], left).astype(HALF)
                for i in range(2):
                    tile = both[:, i * DK : (i + 1) * DK]
                    first = n * cols
                    if k < 3:
                        outs[turns.index(k)][o + i, first : first + cols, :] = tile
                    elif first + cols <= half_rows:
                        outs[0][o + i, first : first + cols, :] = tile
                    elif first >= half_rows:
                        outs[1][o + i, first - half_rows : first - half_rows + cols, :] = tile
                    else:
                        outs[0][o + i, first:, :] = tile[: half_rows - first]
                        outs[1][o + i, : first + cols - half_rows, :] = tile[half_rows - first :]


def ffn_grads(turns, mine, cot, normed, d_gate, d_up, product, after):
    rows = 3 * d_gate.shape[0]
    if turns == (3,):
        shapes = (out((4, rows // 2, DK), HALF),) * 2
    else:
        shapes = (out((4, rows, DK), HALF),) * len(turns)
    return run(
        partial(ffn_grad_kernel, turns),
        shapes + (out((8, DK), FLOAT),),
        (mine, cot, normed, d_gate, d_up, product),
        scalars=1,
        after=(after,),
    )


def put_gains_kernel(mine, gains, arrived, *refs):
    outs, token = refs[-6:-1], refs[-1]
    token[...] = jnp.zeros(token.shape, FLOAT)
    count = outs[0].shape[1] - EXTRA + 32
    for k in range(4):
        target, rows = (outs[k], count) if k < 3 else (outs[4], count - outs[3].shape[1])
        here = slice(rows, rows + 16)
        for o in range(4):
            old = target[o, here, :].astype(FLOAT)
            lanes = lane_block(dest_block(mine, k, o), DK)
            new = gains[:, lanes] + arrived[:, lanes]
            target[o, here, :] = jnp.concatenate([old[:8], new, old[10:]], axis=0).astype(HALF)


def with_gains(mine, parts, gains, arrived, after):
    vmem = pl.BlockSpec(memory_space=pltpu.VMEM)
    *parts, token = pl.pallas_call(
        put_gains_kernel,
        out_shape=tuple(out(a.shape, a.dtype) for a in parts) + (out((8, DK), FLOAT),),
        in_specs=[pl.BlockSpec(memory_space=pltpu.SMEM)]
        + [vmem] * 7
        + [pl.BlockSpec(memory_space=pl.ANY)] * len(after),
        out_specs=[vmem] * 6,
        input_output_aliases={3 + i: i for i in range(5)},
        compiler_params=pltpu.CompilerParams(vmem_limit_bytes=4 * 2**20),
        cost_estimate=cost(0.3),
    )(mine, gains, arrived, *parts, *after)
    return parts, token


def gain_rows(ref):
    first = ref.shape[1] - EXTRA + 40
    return ref[:, first : first + 8, :].astype(FLOAT)


def last_relay_kernel(own, plus, minus, first, second, plus_out, minus_out, token, rows):
    relay_kernel(plus, minus, first, second, plus_out, minus_out, token)
    for i, ref in enumerate((own, plus_out, minus_out)):
        rows[i] = gain_rows(ref)


def quad_sum_kernel(first, second, third, fourth, own, plus, minus, token):
    token[...] = jnp.zeros(token.shape, FLOAT)
    for i, target in enumerate((own, plus, minus)):
        target[...] = (first[i] + second[i]) + (third[i] + fourth[i])


def relay_kernel(plus, minus, first, second, plus_out, minus_out, token):
    half = first.shape[1]
    plus_out[:, :half, :] = (plus[:, :half, :].astype(FLOAT) + first[...].astype(FLOAT)).astype(HALF)
    plus_out[:, half:, :] = plus[:, half:, :]
    minus_out[:, :half, :] = minus[:, :half, :]
    minus_out[:, half:, :] = (minus[:, half:, :].astype(FLOAT) + second[...].astype(FLOAT)).astype(HALF)
    token[...] = jnp.zeros(token.shape, FLOAT)


def relayed(parts, after, micros):
    shape = out(parts[1].shape, HALF)
    first, second = turned(parts[3], True, 1), turned(parts[4], True, -1)
    plus, minus, token = run(
        relay_kernel,
        (shape, shape, out((8, DK), FLOAT)),
        (parts[1], parts[2], first, second),
        after=after,
        micros=micros,
    )
    return (parts[0], turned(plus, True, 1), turned(minus, True, -1)), token


def last_sum_kernel(mine, own, plus, minus, own_rows, plus_rows, minus_rows, *outs):
    seq_sum_kernel(0, mine, own, plus, minus, *outs)
    rank = jnp.where(mine[1] == 0, mine[2], mine[3])
    first = outs[0].shape[0] - EXTRA + 32
    for k in range(4):
        place = ring_place(rank, k)
        old = own[place, first : first + 16, :].astype(FLOAT)
        old = old + plus[place, first : first + 16, :].astype(FLOAT) + minus[place, first : first + 16, :].astype(FLOAT)
        new = own_rows[place] + plus_rows[place] + minus_rows[place]
        outs[k][first : first + 16, :] = jnp.concatenate([old[:8], new], axis=0).astype(outs[k].dtype)


def seq_sum_kernel(early, mine, *refs):
    rank = jnp.where(mine[1] == 0, mine[2], mine[3])
    group, before = refs[:3], refs[3 : 3 + 4 * early]
    outs = refs[3 + 4 * early : 7 + 4 * early]
    refs[-1][...] = jnp.zeros(refs[-1].shape, FLOAT)
    for k in range(4):
        place = ring_place(rank, k)
        at = 0
        for i in range(early):
            source = before[4 * i + k]
            outs[k][at : at + source.shape[0], :] = source[...]
            at += source.shape[0]
        total = group[0][place].astype(FLOAT) + group[1][place].astype(FLOAT) + group[2][place].astype(FLOAT)
        outs[k][at:, :] = total.astype(outs[k].dtype)


def seq_sums(group, before, mine, after, micros):
    count = group[0].shape[1] + sum(sums[0].shape[0] for sums in before)
    shapes = (out((count, DK), FLOAT),) + (out((count, DK), HALF),) * 3
    shapes += (out((8, DK), FLOAT),)
    flat = [piece for sums in before for piece in sums]
    return run(
        partial(seq_sum_kernel, len(before)), shapes, (mine, *group, *flat), scalars=1, after=after, micros=micros
    )


def second_round(sums):
    return [sums[0]] + [turned(sums[i], False, TURNS[i]) for i in range(1, 4)]


def unpack_kernel(own, first, second, third, *outs):
    total = own[...] + first[...].astype(FLOAT) + second[...].astype(FLOAT) + third[...].astype(FLOAT)
    at = 0
    for target in outs[:5]:
        count = target.shape[1]
        target[...] = total[at : at + count, :].T
        at += count
    extra = total[at:, :]
    per_tap = 8
    first = 0
    for target in outs[5:8]:
        blocks = target.shape[1] // DK
        for j in range(4):
            for i in range(blocks):
                row = j * per_tap + first + i
                target[j : j + 1, i * DK : (i + 1) * DK] = extra[row : row + 1, :]
        first += blocks
    for i in range(outs[8].shape[1] // DK):
        outs[8][:, i * DK : (i + 1) * DK] = extra[32 + i : 33 + i, :]
    outs[9][...] = extra[36:38, :]
    outs[10][...] = extra[40:48, :]


def ffn_unpack_kernel(own, first, second, third, gate, up, down, token):
    cols = gate.shape[0]
    token[...] = jnp.zeros(token.shape, FLOAT)
    for n, target in enumerate((gate, up, down)):
        span = slice(n * cols, (n + 1) * cols)
        target[...] = (
            own[span, :]
            + first[span, :].astype(FLOAT)
            + second[span, :].astype(FLOAT)
            + third[span, :].astype(FLOAT)
        )


def output_kernel(own, arrived, total, token):
    token[...] = jnp.zeros(token.shape, FLOAT)
    total[...] = (own[...] + arrived[...].astype(FLOAT)).astype(HALF)


def tile_of(i, mine):
    return (i % 4) * 2 + jnp.where(i < 4, 1 - mine[1], mine[1])


def whole_block(shape):
    return pl.BlockSpec(shape, lambda i, mine: (0,) * len(shape))


def tile_outs(rows, width):
    return [
        pl.BlockSpec((1, rows, width), lambda i, mine: (jnp.minimum(i, 3), 0, 0)),
        pl.BlockSpec((1, rows, width), lambda i, mine: (jnp.maximum(i - 4, 0), 0, 0)),
    ]


def down_kernel(mine, product, weight, hidden, other, own, token, scratch):
    step = pl.program_id(0)
    rows = hidden.shape[0]

    @pl.when(step == 0)
    def _():
        scratch[...] = product[...].T

    part = mm(scratch[...], weight[...])
    here = lane_block(mine[0] * 2 + mine[1], rows)
    for target, wanted in ((other, step < 4), (own, step >= 4)):

        @pl.when(wanted)
        def _():
            target[0] = part.astype(HALF)
            target[0, here, :] = (target[0, here, :].astype(FLOAT) + hidden[...]).astype(HALF)

    token[...] = jnp.zeros(token.shape, FLOAT)


def down_tiles(mine, product, weight, hidden):
    cols, tokens = product.shape
    width = weight.shape[1] // 8
    spec = pltpu.PrefetchScalarGridSpec(
        num_scalar_prefetch=1,
        grid=(8,),
        in_specs=[
            whole_block(product.shape),
            pl.BlockSpec((cols, width), lambda i, mine: (0, tile_of(i, mine))),
            pl.BlockSpec((hidden.shape[0], width), lambda i, mine: (0, tile_of(i, mine))),
        ],
        out_specs=tile_outs(tokens, width) + [whole_block((8, DK))],
        scratch_shapes=[pltpu.VMEM((tokens, cols), HALF)],
    )
    tiles = out((4, tokens, width), HALF)
    return pl.pallas_call(
        down_kernel,
        grid_spec=spec,
        out_shape=(tiles, tiles, out((8, DK), FLOAT)),
        compiler_params=pltpu.CompilerParams(vmem_limit_bytes=16 * 2**20),
        cost_estimate=cost(4.0),
    )(mine, product, weight, hidden)


def d_first_kernel(mine, dproj, arrived, proj, d_pre, d_logit, sums, in_rows, gate_rows, beta_rows, after, other, own, token, scratch, sum_rows):
    step = pl.program_id(0)
    tokens = d_pre.shape[0]
    width = own.shape[2]

    @pl.when(step == 0)
    def _():
        scratch[: tokens - HALO, :] = dproj[HALO:tokens, :]
        extra = arrived[...].astype(FLOAT)
        scratch[tokens - HALO :, :] = (dproj[tokens:, :].astype(FLOAT) + extra).astype(HALF)
        late = jnp.sum(extra * proj[tokens - HALO :, :].astype(FLOAT), axis=-1, keepdims=True)
        column = jnp.concatenate([sums[HALO:tokens, :], sums[tokens:, :] + late], axis=0)
        row = jnp.broadcast_to(column, (tokens, DK)).T
        sum_rows[...] = jnp.zeros(sum_rows.shape, FLOAT)
        for i in range(tokens // width):
            sum_rows[i : i + 1, :] = row[0:1, i * width : (i + 1) * width]

    part = mm(scratch[...], in_rows[...]) + mm(d_pre[...], gate_rows[...])
    for h in range(2):
        part = part + d_logit[:, h : h + 1] * beta_rows[h : h + 1, :].astype(FLOAT)
    for target, wanted in ((other, step < 4), (own, step >= 4)):

        @pl.when(wanted)
        def _():
            target[0, :tokens, :] = part.astype(HALF)
            target[0, tokens:, :] = sum_rows[...].astype(HALF)

    token[...] = jnp.zeros(token.shape, FLOAT)


def d_first_tiles(mine, dproj, arrived, proj, d_pre, d_logit, sums, in_rows, gate_rows, beta_rows, after):
    tokens = d_pre.shape[0]
    width = in_rows.shape[1] // 8
    count = tokens + HALO

    def tile(rows):
        return pl.BlockSpec((rows, width), lambda i, mine: (0, tile_of(i, mine)))

    spec = pltpu.PrefetchScalarGridSpec(
        num_scalar_prefetch=1,
        grid=(8,),
        in_specs=[whole_block(a.shape) for a in (dproj, arrived, proj, d_pre, d_logit, sums)]
        + [tile(in_rows.shape[0]), tile(gate_rows.shape[0]), tile(beta_rows.shape[0])]
        + [pl.BlockSpec(memory_space=pl.ANY)],
        out_specs=tile_outs(count, width) + [whole_block((8, DK))],
        scratch_shapes=[pltpu.VMEM((tokens, dproj.shape[1]), HALF), pltpu.VMEM((HALO, width), FLOAT)],
    )
    tiles = out((4, count, width), HALF)
    return pl.pallas_call(
        d_first_kernel,
        grid_spec=spec,
        out_shape=(tiles, tiles, out((8, DK), FLOAT)),
        compiler_params=pltpu.CompilerParams(vmem_limit_bytes=16 * 2**20),
        cost_estimate=cost(6.0),
    )(mine, dproj, arrived, proj, d_pre, d_logit, sums, in_rows, gate_rows, beta_rows, after)


def input_grad_kernel(mine, own, arrived, block_input, factor, gain, d_branch, grad):
    total = own[...] + arrived[...].astype(FLOAT)
    tokens, width = block_input.shape
    columns = []
    for i in range(tokens // width):
        row = total[tokens + i : tokens + i + 1, :]
        columns.append(jnp.broadcast_to(row, (DK, width)).T[:, 0:1])
    mean = jnp.concatenate(columns, axis=0) / (8 * width)
    scale = factor[...]
    unit = block_input[...].astype(FLOAT) * scale
    gain_own = gain[:, lane_block(mine[0] * 2 + mine[1], width)]
    grad[...] = d_branch[...].astype(FLOAT) + scale * (total[:tokens, :] * gain_own - unit * mean)


def next_block(array, distance):
    size = 16
    route = [(i, i + distance) for i in range(size) if 0 <= i + distance < size]
    return lax.ppermute(array, SEQ, route)


def dot_nt(a, b):
    return lax.dot_general(a, b, NT, preferred_element_type=FLOAT)


def shards(
    block_input,
    log_decay,
    first_gain,
    query_weight,
    key_weight,
    value_weight,
    gate_weight,
    beta_weight,
    query_conv,
    key_conv,
    value_conv,
    mixer_gain,
    mixer_weight,
    second_gain,
    swiglu_gate,
    swiglu_up,
    swiglu_down,
    cotangent,
):
    heads = log_decay.shape[1]
    tokens, width = block_input.shape
    model = 8 * width
    chunks = tokens // CH
    rows = tokens // 8
    kq, vd = heads * DK, heads * DV
    cols = 2 * kq + vd
    hidden_cols = swiglu_gate.shape[1]
    mine = jnp.stack([lax.axis_index(name) for name in ("x", "c", "y", "z")]).astype(jnp.int32)

    token_out = out((8, DK), FLOAT)
    in_rows, gate_rows, gcol, grow, token = run(
        setup_kernel,
        (
            out((cols, model), HALF),
            out((vd, model), HALF),
            out((tokens, heads), FLOAT),
            out((heads * chunks, CH), FLOAT),
            token_out,
        ),
        (query_weight, key_weight, value_weight, gate_weight, log_decay.T),
        micros=3.0,
    )
    beta_rows = jnp.pad(beta_weight.T, ((0, HALO - heads), (0, 0)))
    taps = jnp.concatenate([query_conv.T, key_conv.T, value_conv.T], axis=1)
    gain_row = mixer_gain.reshape(1, -1)
    first_row = first_gain.reshape(1, -1)

    first_normed, first_factor, my_rows, logits, halo_rows = run(
        first_norm_kernel,
        (
            out((tokens, model), HALF),
            out((tokens, 1), FLOAT),
            out((rows, model), FLOAT),
            out((tokens, HALO), FLOAT),
            out((HALO, model), HALF),
        ),
        (mine, first_row, beta_rows, *head_gather(block_input, mine, (token,))),
        scalars=1,
        micros=3.0,
    )
    halo_normed = next_block(halo_rows, 1)
    proj = dot_nt(first_normed, in_rows).astype(HALF)
    halo_proj = dot_nt(halo_normed, in_rows).astype(HALF)
    gate_pre = dot_nt(first_normed, gate_rows)
    k, v, tri, n, b, w, u, pay, pay_token = run(
        partial(prepare_kernel, heads, chunks),
        prepare_shapes(heads, chunks) + (token_out,),
        (proj, halo_proj, taps, logits, gcol, grow),
        [pltpu.VMEM((HALO + tokens, cols), FLOAT)],
        micros=8.0,
        kept=range(7),
        megs=20,
    )
    near_pieces = ring_pieces(pay, "z")
    q, p, query_token = run(
        partial(query_kernel, heads, chunks),
        (out((tokens, kq), HALF), out((heads * chunks, CH, CH), HALF), token_out),
        (proj, halo_proj, taps, k, gcol, grow),
        [pltpu.VMEM((HALO + tokens, kq), FLOAT)],
        after=(pay_token,),
    )
    before, group, near, group_token = run(
        partial(group_kernel, heads), group_shapes(heads) + (token_out,), (mine, *near_pieces), scalars=1, after=(gate_pre[:8, :DK], query_token), micros=2.0
    )
    half_tiles = out((4, rows, model), HALF)
    states, vns, mixed, gated, branch_other, branch_own, far, mix_token = run(
        partial(mix_kernel, heads, chunks),
        mix_shapes(heads, chunks)[:4] + (half_tiles, half_tiles) + mix_shapes(heads, chunks)[4:] + (token_out,),
        (mine, *ring_pieces(group, "y"), before, q, k, w, u, p, n, b, gcol, gate_pre, gain_row, mixer_weight),
        [pltpu.VMEM((tokens, model // 4), FLOAT)],
        scalars=1,
        kept=(0, 1, 2, 6),
        megs=16,
        micros=4.0,
    )
    branch = head_scatter(branch_own, branch_other, mine)
    cot = run(copy_kernel, (out((tokens, width), HALF),), (cotangent,), after=(group_token,))[0]
    cot_tiles = head_gather(cot, mine, (mix_token,))
    whole_cot, cot_rows, d_product, token = run(
        product_grad_kernel,
        (out((tokens, model), HALF), out((rows, model), HALF), out((hidden_cols, tokens), FLOAT), token_out),
        (mine, *cot_tiles, swiglu_down.T),
        scalars=1,
        micros=4.0,
    )
    wide_rows = out((rows, model), FLOAT)
    second_row = second_gain.reshape(1, -1)
    hidden, second_unit, second_factor, own_normed = run(
        hidden_kernel,
        (wide_rows, wide_rows, out((rows, 1), FLOAT), out((rows, model), HALF)),
        (my_rows, second_row, *branch),
        after=(token,),
    )
    turned_out = out((hidden_cols, tokens), HALF)
    second_normed, product, d_gate, d_up, second_other, second_own, ffn_token = run(
        ffn_kernel,
        (out((tokens, model), HALF), turned_out, turned_out, turned_out, half_tiles, half_tiles, token_out),
        (
            mine,
            *head_gather(own_normed, mine),
            swiglu_gate.T,
            swiglu_up.T,
            d_product,
        ),
        [pltpu.VMEM((tokens, model // 4), FLOAT)],
        scalars=1,
        micros=9.0,
        megs=20,
    )
    grad_args = (mine, whole_cot, second_normed, d_gate, d_up, product)
    *ffn_ends, token = ffn_grads((3,), *grad_args, ffn_token)
    second_parts, token = head_scatter(second_own, second_other, mine, True, (token,))
    ffn_plus, ffn_minus, token = ffn_grads((1, 2), *grad_args, token)
    d_hidden, second_gain_part, back_token = run(
        second_back_kernel,
        (out((rows, model), HALF), out((1, model), FLOAT), token_out),
        (second_unit, second_factor, second_row, cot_rows, *second_parts),
        after=(token,),
    )
    ffn_group, ffn_token = relayed([None, ffn_plus, ffn_minus, *ffn_ends], (back_token,), 3.0)
    down_other, down_own, down_token = down_tiles(mine, product, swiglu_down.T, hidden)
    ffn_own, own_token = ffn_grads((0,), *grad_args, back_token)
    d_branch, d_branch_own = run(
        join_rows_kernel,
        (out((tokens, model), HALF), out((tokens, width), HALF)),
        (mine, *head_gather(d_hidden, mine, (down_token, ffn_token, own_token))),
        scalars=1,
    )
    d_gated = jnp.dot(d_branch, mixer_weight, preferred_element_type=FLOAT)
    dos, dvns, es, d_gate_pre, gain_part, gate_sums, ends = run(
        partial(gate_back_kernel, heads, chunks),
        gate_back_shapes(heads, chunks),
        (d_gated, mixed, gate_pre, gain_row, q, w, p, n, gcol),
        micros=4.0,
    )
    *ffn_sums, ffn_token = seq_sums((ffn_own, *ffn_group[1:]), (), mine, (), 3.0)
    tile = out((4, 2 * vd, DK), HALF)
    *mixer_parts, gate_gain = run(
        mixer_grad_kernel,
        (tile,) * 4 + (out((1, model), FLOAT),),
        (mine, d_branch, gated, first_normed, d_gate_pre, gate_rows),
        [pltpu.VMEM((vd, tokens), HALF), pltpu.VMEM((vd, tokens), HALF)],
        scalars=1,
        micros=5.0,
    )
    after, group_end, _, group_token = run(
        partial(group_back_kernel, heads),
        group_back_shapes(heads) + (token_out,),
        (mine, near, *ring_pieces(ends, "z")),
        scalars=1,
        after=(gate_gain, ffn_token),
        micros=2.0,
    )
    end_pieces = ring_pieces(group_end, "y")
    out_keep, out_send, out_token = first_halves(down_own, down_other, mine, (group_token,))
    square = out((heads * chunks, CH, CH), FLOAT)
    *slopes, slope_token = run(
        partial(slopes_kernel, heads, chunks),
        (out((tokens, cols), FLOAT), square, square, out((tokens, vd), FLOAT), token_out),
        (k, v, states, gcol, grow, proj, halo_proj, taps),
        [pltpu.VMEM((HALO + tokens, cols), FLOAT)],
        after=(group_token,),
    )
    passed_sums, ffn_token = passed(ffn_sums, (*end_pieces[1:], slope_token, out_token))
    dproj, halo_grad, d_logit, logit_rows, taps_part, sums = run(
        partial(back_kernel, heads, chunks),
        back_shapes(heads, chunks),
        (mine, far, *end_pieces, after, q, k, logits, gate_sums, gcol, tri, states, vns, dos, dvns, es, n, proj, halo_proj, taps, *slopes),
        back_scratch(heads, chunks),
        scalars=1,
        after=(ffn_token,),
        micros=11.0,
        megs=30,
    )
    packed = 2 * vd + cols + EXTRA
    tile, half_tile = out((4, packed, DK), HALF), out((4, packed // 2, DK), HALF)
    *in_parts, in_token, gains_part = run(
        in_grad_kernel,
        (tile,) * 3 + (half_tile,) * 2 + (token_out, out((2, model), FLOAT)),
        (mine, first_normed, halo_normed, dproj, logit_rows, taps_part, gain_part, gate_gain, second_gain_part, first_row, in_rows, beta_rows, *mixer_parts),
        [pltpu.VMEM((cols + HALO, HALO + tokens), HALF), pltpu.VMEM((EXTRA, DK), FLOAT)],
        scalars=1,
        micros=6.0,
        megs=16,
    )
    out_mine, out_send, out_token = second_halves(out_keep, swapped(out_send, 2), mine, (in_token,))
    ffn_grad_out = out((hidden_cols, DK), FLOAT)
    grad_gate, grad_up, grad_down, ffn_token = run(
        ffn_unpack_kernel, (ffn_grad_out,) * 3 + (token_out,), second_round(passed_sums), after=(out_token,)
    )
    arrived = next_block(halo_grad, -1)
    in_parts, in_token = with_gains(
        mine, in_parts, gains_part, rotated(gains_part, "c", 1), (ffn_token, arrived)
    )
    first_other, first_own, first_token = d_first_tiles(
        mine, dproj, arrived, proj, d_gate_pre, d_logit, sums, in_rows, gate_rows, beta_rows, in_token
    )
    output, out_token = run(
        output_kernel, (out((tokens, width), HALF), token_out), (out_mine, swapped(out_send, 1))
    )
    tile = out((4, packed, DK), HALF)
    plus, minus, in_token, rows_left = run(
        last_relay_kernel,
        (tile, tile, token_out, out((3, 4, 8, DK), FLOAT)),
        (*in_parts[:3], turned(in_parts[3], True, 1), turned(in_parts[4], True, -1)),
        after=(first_token, out_token),
    )
    in_group = (in_parts[0], turned(plus, True, 1), turned(minus, True, -1))
    own_rows, plus_rows, minus_rows, gain_token = run(
        quad_sum_kernel, (out((4, 8, DK), FLOAT),) * 3 + (token_out,), ring_pieces(rows_left, "x"), after=(in_token,)
    )
    first_keep, first_send, _ = first_halves(first_own, first_other, mine, (gain_token,))
    first_mine, first_send, _ = second_halves(first_keep, swapped(first_send, 2), mine, ())
    *sums_out, sum_token = run(
        last_sum_kernel,
        (out((packed, DK), FLOAT),) + (out((packed, DK), HALF),) * 3 + (token_out,),
        (mine, *in_group, own_rows, turned(plus_rows, True, 1), turned(minus_rows, True, -1)),
        scalars=1,
    )
    totals = [sums_out[0]] + [turned(sums_out[i], False, TURNS[i]) for i in range(1, 4)]
    grad_mixer_weight, grad_gate_weight, grad_query, grad_key, grad_value, *taps_grad, gain_grad, beta_grad, both = run(
        unpack_kernel,
        tuple(out((DK, count), FLOAT) for count in (vd, vd, kq, kq, vd)) + tuple(out((rows_, count), FLOAT) for rows_, count in ((4, kq), (4, kq), (4, vd), (1, vd), (heads, DK), (8, DK))),
        totals,
    )
    grad_input = run(
        input_grad_kernel,
        (out((tokens, width), FLOAT),),
        (mine, first_mine, swapped(first_send, 1), block_input, first_factor, first_row, d_branch_own),
        scalars=1,
    )[0]
    return (
        output,
        grad_input,
        both[0],
        grad_query,
        grad_key,
        grad_value,
        grad_gate_weight,
        beta_grad.T,
        taps_grad[0].T,
        taps_grad[1].T,
        taps_grad[2].T,
        gain_grad.reshape(-1),
        grad_mixer_weight,
        both[1],
        grad_gate.T,
        grad_up.T,
        grad_down.T,
    )


def solution(mesh):
    torus = Mesh(mesh.devices.reshape(4, 4, 4, 2), SEQ + HEAD)
    in_specs = (
        P(SEQ, HEAD),
        P(SEQ, HEAD),
        P(),
        P(None, HEAD),
        P(None, HEAD),
        P(None, HEAD),
        P(None, HEAD),
        P(None, HEAD),
        P(HEAD, None),
        P(HEAD, None),
        P(HEAD, None),
        P(HEAD),
        P(None, HEAD),
        P(),
        P(None, HEAD),
        P(None, HEAD),
        P(None, HEAD),
        P(SEQ, HEAD),
    )
    out_specs = (
        P(SEQ, HEAD),
        P(SEQ, HEAD),
        P(SEQ),
        P(SEQ, HEAD),
        P(SEQ, HEAD),
        P(SEQ, HEAD),
        P(SEQ, HEAD),
        P(SEQ, HEAD),
        P(HEAD, None),
        P(HEAD, None),
        P(HEAD, None),
        P(HEAD),
        P(SEQ, HEAD),
        P(SEQ),
        P(SEQ, HEAD),
        P(SEQ, HEAD),
        P(SEQ, HEAD),
    )
    return jax.shard_map(
        shards, mesh=torus, in_specs=in_specs, out_specs=out_specs, check_vma=False
    )
```

```python
from functools import partial

import jax
import jax.numpy as jnp
from jax import lax
from jax.experimental import pallas as pl
from jax.experimental.pallas import tpu as pltpu
from jax.sharding import Mesh
from jax.sharding import PartitionSpec as P

DK = 128
DV = 256
CH = 128
EPS_NORM = 1e-06
EPS_GATE = 1e-05
FLOAT = jnp.float32
HALF = jnp.bfloat16
NN = (((1,), (0,)), ((), ()))
NT = (((1,), (1,)), ((), ()))
TN = (((0,), (0,)), ((), ()))


def mm(a, b, dims=NN):
    return lax.dot_general(a.astype(HALF), b.astype(HALF), dims, preferred_element_type=FLOAT)


def halves(a):
    high = a.astype(HALF)
    return high, (a - high.astype(FLOAT)).astype(HALF)


def mm2(a, b, dims=NN):
    high, low = halves(b)
    return mm(a, high, dims) + mm(a, low, dims)


def mm3(a, b, dims=NN):
    a_high, a_low = halves(a)
    b_high, b_low = halves(b)
    return mm(a_high, b_high, dims) + (mm(a_high, b_low, dims) + mm(a_low, b_high, dims))


def sigmoid(v):
    return 1.0 / (1.0 + jnp.exp(-v))


def square_masks():
    rows = lax.broadcasted_iota(jnp.int32, (CH, CH), 0)
    cols = lax.broadcasted_iota(jnp.int32, (CH, CH), 1)
    return rows, cols


def decay_matrix(gcol, grow):
    rows, cols = square_masks()
    return jnp.where(rows >= cols, jnp.exp(jnp.minimum(gcol - grow, 0.0)), 0.0)


def conv_of(wide, taps, start, count, lanes):
    total = wide[HALO - 3 + start : HALO - 3 + start + count, lanes] * taps[0:1, lanes]
    for j in range(1, 4):
        total = total + wide[HALO - 3 + j + start : HALO - 3 + j + start + count, lanes] * taps[j : j + 1, lanes]
    return total


def query_kernel(heads, chunks, proj, halo, taps, k, gcol, grow, q_out, p_out, token, wide):
    token[...] = jnp.zeros(token.shape, FLOAT)
    kq = heads * DK
    wide[:HALO, :] = halo[:, :kq].astype(FLOAT)
    wide[HALO:, :] = proj[:, :kq].astype(FLOAT)
    for h in range(heads):
        for c in range(chunks):
            span = slice(c * CH, (c + 1) * CH)
            lanes = slice(h * DK, (h + 1) * DK)
            at = h * chunks + c
            cq = conv_of(wide, taps, c * CH, CH, lanes)
            query = (cq * sigmoid(cq)).astype(HALF)
            q_out[span, lanes] = query
            spread = decay_matrix(gcol[span, h : h + 1], grow[at : at + 1, :])
            p_out[at] = (spread * mm(query, k[span, lanes], NT)).astype(HALF)


def prepare_kernel(heads, chunks, proj, halo, taps, logits, gcol, grow, k_out, v_out, t_out, n_out, b_out, w_out, u_out, pay, token, wide):
    token[...] = jnp.zeros(token.shape, FLOAT)
    rows, cols = square_masks()
    differ = rows ^ cols
    eye = jnp.where(rows == cols, 1.0, 0.0)
    wide[:HALO, :] = halo[...].astype(FLOAT)
    wide[HALO:, :] = proj[...].astype(FLOAT)
    kq = heads * DK
    work = [(h, c) for h in range(heads) for c in range(chunks)]
    low, keys, sides = {}, {}, {}
    for h, c in work:
        span = slice(c * CH, (c + 1) * CH)
        ql, kl, vl = (
            slice(h * DK, (h + 1) * DK),
            slice(kq + h * DK, kq + (h + 1) * DK),
            slice(2 * kq + h * DV, 2 * kq + (h + 1) * DV),
        )
        ck = conv_of(wide, taps, c * CH, CH, kl)
        act = ck * sigmoid(ck)
        key = (act * lax.rsqrt(jnp.sum(act * act, axis=-1, keepdims=True) + EPS_NORM)).astype(HALF)
        cv = conv_of(wide, taps, c * CH, CH, vl)
        value = (cv * sigmoid(cv)).astype(HALF)
        k_out[span, ql] = key
        v_out[span, h * DV : (h + 1) * DV] = value
        beta = sigmoid(logits[span, h : h + 1])
        g = gcol[span, h : h + 1]
        spread = decay_matrix(g, grow[h * chunks + c : h * chunks + c + 1, :])
        inner = mm(key, key, NT)
        low[h, c] = jnp.where(rows > cols, beta * spread * inner, 0.0)
        keys[h, c] = key
        sides[h, c] = jnp.concatenate([(beta * jnp.exp(g)) * key.astype(FLOAT), beta * value.astype(FLOAT)], axis=1)
    tri = {at: eye - jnp.where(differ < 2, low[at], 0.0) for at in work}
    size = 2
    while size < CH:
        part = {at: mm3(jnp.where((differ >= size) & (differ < 2 * size), low[at], 0.0), tri[at]) for at in work}
        tri = {at: tri[at] - mm3(tri[at], part[at]) for at in work}
        size *= 2
    steps = {}
    for h, c in work:
        at = h * chunks + c
        t_out[at] = tri[h, c].astype(HALF)
        solved = mm3(tri[h, c], sides[h, c])
        w_out[at] = solved[:, :DK].astype(HALF)
        u_out[at] = solved[:, DK:].astype(HALF)
        g = gcol[c * CH : (c + 1) * CH, h : h + 1]
        last = gcol[(c + 1) * CH - 1 : (c + 1) * CH, h : h + 1]
        step = mm2(keys[h, c], jnp.exp(last - g) * solved, TN)
        n_out[at] = step[:, :DK].astype(HALF)
        b_out[at] = step[:, DK:]
        steps[h, c] = (jnp.exp(last), step)
    zero = jnp.zeros((DK, DK), FLOAT)
    for h in range(heads):
        decay, step = steps[h, 0]
        total = jnp.concatenate([decay * eye - step[:, :DK], step[:, DK:]], axis=1)
        whole = decay
        for c in range(1, chunks):
            decay, step = steps[h, c]
            total = decay * total - mm3(step[:, :DK], total) + jnp.concatenate([zero, step[:, DK:]], axis=1)
            whole = whole * decay
        pack_map(pay, h, total, whole, eye)


def whole_decay(pay, j, h):
    return pay[j, h, DK : DK + 1, 0:1].astype(FLOAT) + pay[j, h, DK + 8 : DK + 9, 0:1].astype(FLOAT)


def apply_whole(pay, j, h, state, dims):
    return whole_decay(pay, j, h) * state + mm(pay[j, h, :DK, :DK], state, dims)


def pack_map(pay, h, total, whole, eye):
    pay[h, :DK, :] = jnp.concatenate([total[:, :DK] - whole * eye, total[:, DK:]], axis=1).astype(HALF)
    rest = jnp.broadcast_to(whole, (8, DK + DV))
    first = rest.astype(HALF).astype(FLOAT)
    pay[h, DK:, :] = jnp.concatenate([first, rest - first], axis=0).astype(HALF)


def group_kernel(heads, mine, p0, p1, p2, p3, before, group, near, token):
    token[...] = jnp.zeros(token.shape, FLOAT)
    me = mine[3]
    for k, piece in enumerate((p0, p1, p2, p3)):
        near[ring_place(me, k)] = piece[...]
    rows, cols = square_masks()
    eye = jnp.where(rows == cols, 1.0, 0.0)
    zero = jnp.zeros((DK, DK), FLOAT)
    start = jnp.concatenate([eye, jnp.zeros((DK, DV), FLOAT)], axis=1)
    totals, keeps, wholes = [start] * heads, [start] * heads, [jnp.ones((1, 1), FLOAT)] * heads
    for j in range(near.shape[0]):
        for h in range(heads):
            added = jnp.concatenate([zero, near[j, h, :DK, DK:].astype(FLOAT)], axis=1)
            if j == 0:
                moved = jnp.concatenate([whole_decay(near, j, h) * eye + near[j, h, :DK, :DK].astype(FLOAT), added[:, DK:]], axis=1)
            else:
                moved = apply_whole(near, j, h, totals[h], NN) + added
            totals[h] = moved
            wholes[h] = wholes[h] * whole_decay(near, j, h)
            keeps[h] = jnp.where(me == j + 1, moved, keeps[h])
    for h in range(heads):
        before[h] = keeps[h]
        pack_map(group, h, totals[h], wholes[h], eye)


def group_back_kernel(heads, mine, near, p0, p1, p2, p3, after, group, ends, token):
    token[...] = jnp.zeros(token.shape, FLOAT)
    me = mine[3]
    for k, piece in enumerate((p0, p1, p2, p3)):
        ends[ring_place(me, k)] = piece[...]
    rows, cols = square_masks()
    eye = jnp.where(rows == cols, 1.0, 0.0)
    zero = jnp.zeros((DK, DK), FLOAT)
    start = jnp.concatenate([eye, jnp.zeros((DK, DV), FLOAT)], axis=1)
    totals, keeps = [start] * heads, [start] * heads
    for j in reversed(range(near.shape[0])):
        for h in range(heads):
            keeps[h] = jnp.where(me == j, totals[h], keeps[h])
            added = jnp.concatenate([zero, ends[j, h].astype(FLOAT)], axis=1)
            totals[h] = apply_whole(near, j, h, totals[h], TN) + added
    for h in range(heads):
        after[h] = keeps[h]
        group[h] = totals[h][:, DK:].astype(HALF)


def spread_rows(core, total, own, other, rows, lanes):
    for x in range(4):
        mine = pl.ds(pl.multiple_of((2 * x + core) * rows, rows), rows)
        away = pl.ds(pl.multiple_of((2 * x + 1 - core) * rows, rows), rows)
        own[x, :, lanes] = total[mine, :].astype(HALF)
        other[x, :, lanes] = total[away, :].astype(HALF)


def mix_kernel(heads, chunks, mine, p0, p1, p2, p3, before, q, k, w, u, p, n, b, gcol, gate, gain, weight, s_out, vn_out, o_out, gated, other, own, pay, token, total):
    token[...] = jnp.zeros(token.shape, FLOAT)
    ranks = pay.shape[0]
    me = mine[2]
    for at, piece in enumerate((p0, p1, p2, p3)):
        pay[ring_place(me, at)] = piece[...]
    states = [jnp.zeros((DK, DV), FLOAT) for h in range(heads)]
    for j in range(ranks - 1):
        passed = j < me
        for h in range(heads):
            moved = apply_whole(pay, j, h, states[h], NN) + pay[j, h, :DK, DK:].astype(FLOAT)
            states[h] = jnp.where(passed, moved, states[h])
    for h in range(heads):
        states[h] = mm3(before[h, :, :DK], states[h]) + before[h, :, DK:]
    for c in range(chunks):
        span = slice(c * CH, (c + 1) * CH)
        for h in range(heads):
            at = h * chunks + c
            state = states[h].astype(HALF)
            s_out[at] = state
            g = gcol[span, h : h + 1]
            last = gcol[(c + 1) * CH - 1 : (c + 1) * CH, h : h + 1]
            vn = (u[at].astype(FLOAT) - mm(w[at], state)).astype(HALF)
            vn_out[at] = vn
            out = jnp.exp(g) * mm(q[span, h * DK : (h + 1) * DK], state) + mm(p[at], vn)
            vl = slice(h * DV, (h + 1) * DV)
            o_out[span, vl] = out
            factor = lax.rsqrt(jnp.mean(out * out, axis=-1, keepdims=True) + EPS_GATE)
            pre = gate[span, vl]
            gated[span, vl] = (out * factor * gain[:, vl] * (pre * sigmoid(pre))).astype(HALF)
            if c + 1 < chunks:
                states[h] = jnp.exp(last) * states[h] - mm(n[at], state) + b[at]
    width = weight.shape[0]
    tile = total.shape[1]
    rows = own.shape[1]
    for at in range(0, width, tile):
        lanes = slice(at, at + tile)
        total[...] = mm(gated[...], weight[lanes, :], NT)
        spread_rows(mine[1], total, own, other, rows, lanes)


def gate_back_kernel(heads, chunks, d_gated, out, gate, gain, q, w, p, n, gcol, do_out, dvn_out, e_out, dpre_out, dgain_out, sums_out, pay):
    dgain = [jnp.zeros((1, DV), FLOAT) for h in range(heads)]
    ends = [None] * heads
    for c in reversed(range(chunks)):
        span = slice(c * CH, (c + 1) * CH)
        for h in range(heads):
            at = h * chunks + c
            vl = slice(h * DV, (h + 1) * DV)
            dg, o, pre, gn = d_gated[span, vl], out[span, vl], gate[span, vl], gain[:, vl]
            sig = sigmoid(pre)
            factor = lax.rsqrt(jnp.mean(o * o, axis=-1, keepdims=True) + EPS_GATE)
            m = o * factor
            s = pre * sig
            dgm = dg * m
            dgain[h] = dgain[h] + jnp.sum(dgm * s, axis=0, keepdims=True)
            dpre = dgm * gn * (sig * (1.0 + pre * (1.0 - sig)))
            dpre_out[span, vl] = dpre.astype(HALF)
            row_sum = jnp.sum(dpre * pre, axis=-1, keepdims=True)
            sums_out[span, :] = row_sum if h == 0 else sums_out[span, :] + row_sum
            e = dg * gn * s
            dout = factor * (e - m * jnp.mean(e * m, axis=-1, keepdims=True))
            do_out[span, vl] = dout.astype(HALF)
            g = gcol[span, h : h + 1]
            last = gcol[(c + 1) * CH - 1 : (c + 1) * CH, h : h + 1]
            dvn = mm(p[at], dout, TN)
            dvn_out[at] = dvn
            source = mm(q[span, h * DK : (h + 1) * DK], jnp.exp(g) * dout, TN) - mm(w[at], dvn, TN)
            e_out[at] = source
            if ends[h] is None:
                ends[h] = source
            else:
                ends[h] = jnp.exp(last) * ends[h] - mm(n[at], ends[h], TN) + source
    for h in range(heads):
        pay[h] = ends[h].astype(HALF)
        dgain_out[0:1, h * DV : (h + 1) * DV] = dgain[h]


def slopes_kernel(heads, chunks, k, v, states, gcol, grow, proj, halo, taps, slopes, inner_out, spread_out, rest, token, wide):
    token[...] = jnp.zeros(token.shape, FLOAT)
    kq = heads * DK
    wide[:HALO, :] = halo[...].astype(FLOAT)
    wide[HALO:, :] = proj[...].astype(FLOAT)
    for h in range(heads):
        for c in range(chunks):
            span = slice(c * CH, (c + 1) * CH)
            at = h * chunks + c
            kl = slice(kq + h * DK, kq + (h + 1) * DK)
            for lanes in (slice(h * DK, (h + 1) * DK), slice(2 * kq + h * DV, 2 * kq + (h + 1) * DV)):
                pre = conv_of(wide, taps, c * CH, CH, lanes)
                sig = sigmoid(pre)
                slopes[span, lanes] = sig * (1.0 + pre * (1.0 - sig))
            pre = conv_of(wide, taps, c * CH, CH, kl)
            sig = sigmoid(pre)
            act = pre * sig
            unit = lax.rsqrt(jnp.sum(act * act, axis=-1, keepdims=True) + EPS_NORM)
            slopes[span, kl] = unit * (sig * (1.0 + pre * (1.0 - sig)))
            key = k[span, h * DK : (h + 1) * DK]
            g = gcol[span, h : h + 1]
            inner_out[at] = mm(key, key, NT)
            spread_out[at] = decay_matrix(g, grow[at : at + 1, :])
            vl = slice(h * DV, (h + 1) * DV)
            rest[span, vl] = v[span, vl].astype(FLOAT) - jnp.exp(g) * mm(key, states[at])


def back_kernel(heads, chunks, mine, pay, p0, p1, p2, p3, after, q, k, logits, gate_sums, gcol, tri, states, vns, dos, dvns, es, ns, proj, halo, taps, slopes, inner_in, spread_in, rest, dproj_out, halo_out, dlogit_out, logit_rows, dtaps_out, sums_out, wide, dconv, late, rowsum):
    ranks = pay.shape[0]
    tokens = chunks * CH
    me = mine[2]
    for at, piece in enumerate((p0, p1, p2, p3)):
        late[ring_place(me, at)] = piece[...]
    kq = heads * DK
    width = 2 * kq + heads * DV
    rows, cols = square_masks()
    grads = [jnp.zeros((DK, DV), FLOAT) for h in range(heads)]
    for j in reversed(range(1, ranks)):
        passed = j > me
        for h in range(heads):
            moved = apply_whole(pay, j, h, grads[h], TN) + late[j, h].astype(FLOAT)
            grads[h] = jnp.where(passed, moved, grads[h])
    for h in range(heads):
        grads[h] = mm3(after[h, :, :DK], grads[h]) + after[h, :, DK:]
    wide[:HALO, :] = halo[...].astype(FLOAT)
    wide[HALO:, :] = proj[...].astype(FLOAT)
    logit_rows[...] = jnp.zeros(logit_rows.shape, FLOAT)
    dconv[0:HALO, :] = jnp.zeros((HALO, width), FLOAT)
    dconv[HALO + tokens :, :] = jnp.zeros((8, width), FLOAT)
    for c in reversed(range(chunks)):
        span = slice(c * CH, (c + 1) * CH)
        for h in range(heads):
            at = h * chunks + c
            ql, kl, vl, ol = (
                slice(h * DK, (h + 1) * DK),
                slice(kq + h * DK, kq + (h + 1) * DK),
                slice(2 * kq + h * DV, 2 * kq + (h + 1) * DV),
                slice(h * DV, (h + 1) * DV),
            )
            grad = grads[h].astype(HALF)
            query, key = q[span, ql], k[span, ql]
            state, vn, dout = states[at], vns[at], dos[span, ol]
            logit = logits[span, h : h + 1]
            beta = sigmoid(logit)
            g = gcol[span, h : h + 1]
            last = gcol[(c + 1) * CH - 1 : (c + 1) * CH, h : h + 1]
            eg, ed = jnp.exp(g), jnp.exp(last - g)
            spread = spread_in[at]
            strict = jnp.where(rows > cols, spread, 0.0)
            inner = inner_in[at]
            dvn = dvns[at] + ed * mm(key, grad)
            dr = mm(tri[at], dvn, TN)
            drh = dr.astype(HALF)
            dval = beta * dr
            both = mm(jnp.concatenate([dout, drh], axis=0), state, NT)
            dkeep = mm(vn, grad, NT)
            pair = mm(jnp.concatenate([dout, drh], axis=0), vn, NT)
            dqk = spread * pair[:CH]
            da = -(strict * pair[CH:])
            dkk = beta * da
            dbeta = jnp.sum(dr * rest[span, ol], axis=-1, keepdims=True) + jnp.sum(
                da * inner, axis=-1, keepdims=True
            )
            dqkh = dqk.astype(HALF)
            dkkh = dkk.astype(HALF)
            dquery = eg * both[:CH] + mm(dqkh, key)
            dkey = (
                ed * dkeep
                - (beta * eg) * both[CH:]
                + mm(dqkh, query, TN)
                + mm(dkkh, key)
                + mm(dkkh, key, TN)
            )
            if c > 0:
                grads[h] = jnp.exp(last) * grads[h] - mm(ns[at], grad, TN) + es[at]
            dlogit = dbeta * beta * (1.0 - beta)
            dlogit_out[span, h : h + 1] = dlogit
            logit_rows[h : h + 1, HALO + c * CH : HALO + (c + 1) * CH] = jnp.broadcast_to(dlogit, (CH, DK)).T[0:1]
            extra_sum = dlogit * logit
            far_span = slice(HALO + c * CH, HALO + (c + 1) * CH)
            sums_out[far_span, :] = (gate_sums[span, :] if h == 0 else sums_out[far_span, :]) + extra_sum
            there = slice(HALO + c * CH, HALO + (c + 1) * CH)
            dconv[there, ql] = dquery * slopes[span, ql]
            dconv[there, vl] = dval * slopes[span, vl]
            unit = key.astype(FLOAT)
            dconv[there, kl] = (dkey - unit * jnp.sum(dkey * unit, axis=-1, keepdims=True)) * slopes[span, kl]
    dtaps_out[4:8, :] = jnp.zeros((4, width), FLOAT)
    rowsum[...] = jnp.zeros((HALO + tokens, 1), FLOAT)
    for at in range(0, width, DK):
        lanes = slice(at, at + DK)
        for j in range(4):
            dtaps_out[j : j + 1, lanes] = jnp.sum(
                dconv[HALO : HALO + tokens, lanes] * wide[HALO - 3 + j : HALO - 3 + j + tokens, lanes], axis=0, keepdims=True
            )
        total = dconv[3 : 3 + HALO + tokens, lanes] * taps[0:1, lanes]
        for j in range(1, 4):
            total = total + dconv[3 - j : 3 - j + HALO + tokens, lanes] * taps[j : j + 1, lanes]
        small = total.astype(HALF)
        dproj_out[:, lanes] = small
        halo_out[:, lanes] = small[:HALO]
        rowsum[...] += jnp.sum(small.astype(FLOAT) * wide[:, lanes], axis=-1, keepdims=True)
    sums_out[HALO:, :] += rowsum[HALO:, :]
    sums_out[:HALO, :] = rowsum[:HALO, :]


def out(shape, dtype):
    return jax.ShapeDtypeStruct(shape, dtype)


def cost(micros):
    return pl.CostEstimate(flops=int(micros * 1.1e7), bytes_accessed=0, transcendentals=0)


def run(kernel, shapes, args, scratch=(), scalars=0, after=(), micros=1.0, megs=12, kept=()):
    vmem = pl.BlockSpec(memory_space=pltpu.VMEM)
    smem = pl.BlockSpec(memory_space=pltpu.SMEM)
    count = len(args)

    def body(*refs):
        kernel(*refs[:count], *refs[count + len(after) :])

    return pl.pallas_call(
        body,
        out_shape=tuple(pltpu.HBM(a.shape, a.dtype) if i in kept else a for i, a in enumerate(shapes)),
        in_specs=[smem] * scalars + [vmem] * (count - scalars) + [pl.BlockSpec(memory_space=pl.ANY)] * len(after),
        out_specs=[pl.BlockSpec() if i in kept else vmem for i in range(len(shapes))],
        scratch_shapes=list(scratch),
        compiler_params=pltpu.CompilerParams(vmem_limit_bytes=megs * 2**20),
        cost_estimate=cost(micros),
    )(*args, *after)


def passed(arrays, after):
    count = len(arrays)
    anywhere = pl.BlockSpec(memory_space=pl.ANY)

    def body(*refs):
        token = refs[-1]
        token[...] = jnp.zeros(token.shape, FLOAT)

    *same, token = pl.pallas_call(
        body,
        out_shape=tuple(out(a.shape, a.dtype) for a in arrays) + (out((8, DK), FLOAT),),
        in_specs=[anywhere] * (count + len(after)),
        out_specs=[anywhere] * count + [pl.BlockSpec(memory_space=pltpu.VMEM)],
        input_output_aliases={i: i for i in range(count)},
        compiler_params=pltpu.CompilerParams(vmem_limit_bytes=2**20),
        cost_estimate=cost(0.1),
    )(*arrays, *after)
    return same, token


def prepare_shapes(heads, chunks):
    tokens, pairs = chunks * CH, heads * chunks
    return (
        out((tokens, heads * DK), HALF),
        out((tokens, heads * DV), HALF),
        out((pairs, CH, CH), HALF),
        out((pairs, DK, DK), HALF),
        out((pairs, DK, DV), FLOAT),
        out((pairs, CH, DK), HALF),
        out((pairs, CH, DV), HALF),
        out((heads, DK + 16, DK + DV), HALF),
    )


def mix_shapes(heads, chunks):
    tokens, pairs = chunks * CH, heads * chunks
    return (
        out((pairs, DK, DV), HALF),
        out((pairs, CH, DV), HALF),
        out((tokens, heads * DV), FLOAT),
        out((tokens, heads * DV), HALF),
        out((4, heads, DK + 16, DK + DV), HALF),
    )


def gate_back_shapes(heads, chunks):
    tokens, pairs = chunks * CH, heads * chunks
    return (
        out((tokens, heads * DV), HALF),
        out((pairs, CH, DV), FLOAT),
        out((pairs, DK, DV), FLOAT),
        out((tokens, heads * DV), HALF),
        out((1, heads * DV), FLOAT),
        out((tokens, 1), FLOAT),
        out((heads, DK, DV), HALF),
    )


def back_shapes(heads, chunks):
    tokens = chunks * CH
    width = heads * (2 * DK + DV)
    return (
        out((HALO + tokens, width), HALF),
        out((HALO, width), HALF),
        out((tokens, heads), FLOAT),
        out((HALO, HALO + tokens), FLOAT),
        out((8, width), FLOAT),
        out((HALO + tokens, 1), FLOAT),
    )


def back_scratch(heads, chunks):
    tokens = chunks * CH
    width = heads * (2 * DK + DV)
    return (pltpu.VMEM((HALO + tokens, width), FLOAT), pltpu.VMEM((HALO + tokens + 8, width), FLOAT), pltpu.VMEM((4, heads, DK, DV), HALF), pltpu.VMEM((HALO + tokens, 1), FLOAT))


def group_shapes(heads):
    pay = (heads, DK + 16, DK + DV)
    return (out((heads, DK, DK + DV), FLOAT), out(pay, HALF), out((4, *pay), HALF))


def group_back_shapes(heads):
    return (
        out((heads, DK, DK + DV), FLOAT),
        out((heads, DK, DV), HALF),
        out((4, heads, DK, DV), HALF),
    )


HEAD = ("x", "c")
SEQ = ("y", "z")
PLANE = ("y", "z", "c")
HALO = 16
EXTRA = 64
TURNS = (0, 1, -1, 2)


def rotated(array, axis, distance):
    size = lax.axis_size(axis)
    return lax.ppermute(array, axis, [(i, (i + distance) % size) for i in range(size)])


def ring_pieces(array, axis):
    return [array] + [rotated(array, axis, -d) for d in TURNS[1:]]


def join_kernel(mine, *refs):
    for k in range(4):
        refs[4][ring_place(mine[0], k)] = refs[k][...]


def head_gather(array, mine, after=()):
    shapes = (out((4, *array.shape), array.dtype),)
    own = run(join_kernel, shapes, (mine, *ring_pieces(array, "x")), scalars=1, after=after)[0]
    return own, rotated(own, "c", 1)


def head_tiles(mine, own, other):
    core = mine[1]
    return [(2 * x + which, ref, x) for which, ref in ((core, own), (1 - core, other)) for x in range(4)]


def copy_kernel(source, target):
    target[...] = source[...]


def turned(array, first, distance):
    pairs = []
    for y in range(4):
        for z in range(4):
            for core in range(2):
                along_z = (core == 0) == first
                to = (y, (z + distance) % 4) if along_z else ((y + distance) % 4, z)
                pairs.append(((y * 4 + z) * 2 + core, (to[0] * 4 + to[1]) * 2 + core))
    return lax.ppermute(array, PLANE, pairs)


def ring_place(mine, k):
    return lax.rem(mine + TURNS[k] + 4, 4)


def lane_block(at, width):
    return pl.ds(pl.multiple_of(at * width, width), width)


def setup_kernel(query, key, value, gate, decay, in_out, gate_out, gcol, grow, token):
    at = 0
    for weight in (query, key, value):
        count = weight.shape[1]
        in_out[at : at + count, :] = weight[...].T
        at += count
    gate_out[...] = gate[...].T
    rows, cols = square_masks()
    heads, tokens = decay.shape
    chunks = tokens // CH
    for h in range(heads):
        for c in range(chunks):
            span = slice(c * CH, (c + 1) * CH)
            flat = jnp.broadcast_to(decay[h : h + 1, span], (CH, CH))
            grow[h * chunks + c : h * chunks + c + 1, :] = jnp.sum(
                jnp.where(rows <= cols, flat.T, 0.0), axis=0, keepdims=True
            )
            gcol[span, h : h + 1] = jnp.sum(jnp.where(cols <= rows, flat, 0.0), axis=1, keepdims=True)
    token[...] = jnp.zeros(token.shape, FLOAT)


def first_norm_kernel(mine, gain, beta_rows, own, other, normed, factor, rows_out, logits, halo_out):
    width = own.shape[2]
    rows = rows_out.shape[0]
    own_rows = lane_block(mine[0] * 2 + mine[1], rows)
    square = 0.0
    for _, ref, x in head_tiles(mine, own, other):
        wide = ref[x].astype(FLOAT)
        square = square + jnp.sum(wide * wide, axis=-1, keepdims=True)
    scale = lax.rsqrt(square / (8 * width) + EPS_NORM)
    factor[...] = scale
    total = 0.0
    for head, ref, x in head_tiles(mine, own, other):
        lanes = lane_block(head, width)
        small = (ref[x].astype(FLOAT) * scale * gain[:, lanes]).astype(HALF)
        normed[:, lanes] = small
        total = total + mm(small, beta_rows[:, lanes], NT)
        rows_out[:, lanes] = ref[x, own_rows, :].astype(FLOAT)
    logits[...] = total
    halo_out[...] = normed[normed.shape[0] - HALO :, :]


def product_grad_kernel(mine, own, other, weight, whole, rows_out, grad, token):
    width = own.shape[2]
    rows = rows_out.shape[0]
    own_rows = lane_block(mine[0] * 2 + mine[1], rows)
    for head, ref, x in head_tiles(mine, own, other):
        lanes = lane_block(head, width)
        whole[:, lanes] = ref[x]
        rows_out[:, lanes] = ref[x, own_rows, :]
    grad[...] = mm(weight[...], whole[...], NT)
    token[...] = jnp.zeros(token.shape, FLOAT)


def hidden_kernel(rows_in, gain, first, second, third, fourth, hidden, unit, factor, normed):
    total = rows_in[...] + first[...] + second[...].astype(FLOAT) + third[...].astype(FLOAT) + fourth[...].astype(FLOAT)
    hidden[...] = total
    scale = lax.rsqrt(jnp.mean(total * total, axis=-1, keepdims=True) + EPS_NORM)
    factor[...] = scale
    unit[...] = total * scale
    normed[...] = (total * scale * gain[...]).astype(HALF)


def second_back_kernel(unit, factor, gain, cot_rows, first, second, third, fourth, d_hidden, gain_part, token):
    token[...] = jnp.zeros(token.shape, FLOAT)
    total = first[...] + second[...].astype(FLOAT) + third[...].astype(FLOAT) + fourth[...].astype(FLOAT)
    n = unit[...]
    gain_part[...] = jnp.sum(total * n, axis=0, keepdims=True)
    e = total * gain[...]
    mean = jnp.mean(e * n, axis=-1, keepdims=True)
    d_hidden[...] = (cot_rows[...].astype(FLOAT) + factor[...] * (e - n * mean)).astype(HALF)


def ffn_kernel(mine, own_in, other_in, gate_rows, up_rows, d_product, normed, product, d_gate, d_up, other, own, token, total):
    rows = own_in.shape[1]
    for head, ref, x in head_tiles(mine, own_in, other_in):
        normed[lane_block(head, rows), :] = ref[x]
    cols = gate_rows.shape[0]
    step = cols // 2
    for at in range(0, cols, step):
        span = slice(at, at + step)
        gate = mm(gate_rows[span, :], normed[...], NT)
        up = mm(up_rows[span, :], normed[...], NT)
        sig = sigmoid(gate)
        act = gate * sig
        product[span, :] = (act * up).astype(HALF)
        grad = d_product[span, :]
        dg = (grad * up * (sig * (1.0 + gate * (1.0 - sig)))).astype(HALF)
        du = (grad * act).astype(HALF)
        d_gate[span, :] = dg
        d_up[span, :] = du
    token[...] = jnp.zeros(token.shape, FLOAT)
    gate_turned = d_gate[...].T
    up_turned = d_up[...].T
    width = normed.shape[1]
    tile = width // 4
    core = mine[1]
    for at in range(0, width, tile):
        lanes = slice(at, at + tile)
        total[...] = mm(gate_turned, gate_rows[:, lanes]) + mm(up_turned, up_rows[:, lanes])
        spread_rows(core, total, own, other, rows, lanes)


def join_rows_kernel(mine, own, other, whole, own_cols):
    rows = own.shape[1]
    lanes = lane_block(mine[0] * 2 + mine[1], own_cols.shape[1])
    for head, ref, x in head_tiles(mine, own, other):
        whole[lane_block(head, rows), :] = ref[x]
        own_cols[lane_block(head, rows), :] = ref[x, :, lanes]


def split_sum_kernel(mine, own, arrived, *outs):
    for k in range(4):
        at = ring_place(mine[0], k)
        outs[k][...] = (own[at].astype(FLOAT) + arrived[at].astype(FLOAT)).astype(outs[k].dtype)
    outs[4][...] = jnp.zeros(outs[4].shape, FLOAT)


def head_scatter(own, other, mine, with_token=False, after=()):
    arrived = rotated(other, "c", 1)
    shape = own.shape[1:]
    shapes = (out(shape, FLOAT),) + (out(shape, HALF),) * 3 + (out((8, DK), FLOAT),)
    total, *sent, token = run(split_sum_kernel, shapes, (mine, own, arrived), scalars=1, after=after)
    parts = [total] + [rotated(part, "x", d) for d, part in zip(TURNS[1:], sent)]
    return (parts, token) if with_token else parts


def swapped(array, mask):
    return lax.ppermute(array, "x", [(i, i ^ mask) for i in range(4)])


def first_half_kernel(mine, own, arrived, keep, send, token):
    token[...] = jnp.zeros(token.shape, FLOAT)
    base = jnp.where(mine[0] < 2, 0, 2)
    for target, at in ((keep, base), (send, 2 - base)):
        for i in range(2):
            target[i] = (own[at + i].astype(FLOAT) + arrived[at + i].astype(FLOAT)).astype(target.dtype)


def second_half_kernel(mine, keep, arrived, own, send, token):
    token[...] = jnp.zeros(token.shape, FLOAT)
    at = lax.rem(mine[0], 2)
    own[...] = keep[at].astype(FLOAT) + arrived[at].astype(FLOAT)
    send[...] = (keep[1 - at].astype(FLOAT) + arrived[1 - at].astype(FLOAT)).astype(HALF)


def first_halves(own, arrived, mine, after):
    pair = out((2, *own.shape[1:]), HALF)
    return run(
        first_half_kernel,
        (pair, pair, out((8, DK), FLOAT)),
        (mine, own, arrived),
        scalars=1,
        after=after,
    )


def second_halves(keep, arrived, mine, after):
    shape = keep.shape[1:]
    return run(
        second_half_kernel,
        (out(shape, FLOAT), out(shape, HALF), out((8, DK), FLOAT)),
        (mine, keep, arrived),
        scalars=1,
        after=after,
    )


def added(parts):
    total = parts[0]
    for part in parts[1:]:
        total = total + part.astype(FLOAT)
    return total


def dest_block(mine, k, o):
    core = mine[1]
    place = ring_place(jnp.where(core == 0, mine[3], mine[2]), k)
    return jnp.where(core == 0, o * 4 + place, place * 4 + o)


def store_tile(outs, k, o, early, value):
    count = early.shape[0]
    if k < 3:
        outs[k][o, :count, :] = early
        outs[k][o, count:, :] = value
    else:
        spare = outs[3].shape[1] - count
        outs[3][o, :count, :] = early
        outs[3][o, count:, :] = value[:spare]
        outs[4][o] = value[spare:]


def mixer_grad_kernel(mine, d_branch, gated, normed, d_pre, gate_rows, *refs):
    outs, (gain_out, gated_turned, pre_turned) = refs[:4], refs[4:]
    gated_turned[...] = gated[...].T
    pre_turned[...] = d_pre[...].T
    for k in range(4):
        for o in (0, 2):
            blocks = [lane_block(dest_block(mine, k, o + i), DK) for i in range(2)]
            mixer = mm(gated_turned[...], jnp.concatenate([d_branch[:, at] for at in blocks], axis=1))
            gate = mm(pre_turned[...], jnp.concatenate([normed[:, at] for at in blocks], axis=1))
            for i, at in enumerate(blocks):
                half = slice(i * DK, (i + 1) * DK)
                outs[k][o + i] = jnp.concatenate([mixer[:, half], gate[:, half]], axis=0).astype(HALF)
                gain_out[:, at] = jnp.sum(gate[:, half] * gate_rows[:, at].astype(FLOAT), axis=0, keepdims=True)


def in_grad_kernel(mine, normed, halo, dproj, d_logit, taps, mixer_gain, gate_gain, second_gain, first_gain, in_rows, beta_rows, *refs):
    early, outs, (token, gains, turned_refs, extra) = refs[:4], refs[4:9], refs[9:]
    token[...] = jnp.zeros(token.shape, FLOAT)
    cols = dproj.shape[1]
    heads = 2
    turned_refs[:cols, :] = dproj[...].T
    turned_refs[cols:, :] = d_logit[...].astype(HALF)
    extra[...] = jnp.zeros(extra.shape, FLOAT)
    per_tap = cols // DK
    for j in range(4):
        for i in range(per_tap):
            extra[j * per_tap + i : j * per_tap + i + 1, :] = taps[j : j + 1, i * DK : (i + 1) * DK]
    for i in range(mixer_gain.shape[1] // DK):
        extra[32 + i : 33 + i, :] = mixer_gain[:, i * DK : (i + 1) * DK]
    for k in range(4):
        for o in (0, 2):
            blocks = [lane_block(dest_block(mine, k, o + i), DK) for i in range(2)]
            left = jnp.concatenate(
                [jnp.concatenate([halo[:, at], normed[:, at]], axis=0) for at in blocks], axis=1
            )
            grads = mm(turned_refs[...], left)
            for i, at in enumerate(blocks):
                half = slice(i * DK, (i + 1) * DK)
                beta = grads[cols : cols + heads, half]
                gain = (
                    jnp.sum(grads[:cols, half] * in_rows[:, at].astype(FLOAT), axis=0, keepdims=True)
                    + jnp.sum(beta * beta_rows[:heads, at].astype(FLOAT), axis=0, keepdims=True)
                    + gate_gain[:, at]
                )
                extra[36 : 36 + heads, :] = beta
                gains[0:1, at] = gain / first_gain[:, at]
                gains[1:2, at] = second_gain[:, at]
                store_tile(
                    outs, k, o + i, early[k][o + i], jnp.concatenate([grads[:cols, half], extra[...]], axis=0).astype(HALF)
                )


def ffn_grad_kernel(turns, mine, cot, normed, d_gate, d_up, product, *refs):
    outs, token = refs[:-1], refs[-1]
    token[...] = jnp.zeros(token.shape, FLOAT)
    cols = d_gate.shape[0]
    half_rows = 3 * cols // 2
    for k in turns:
        for o in (0, 2):
            blocks = [lane_block(dest_block(mine, k, o + i), DK) for i in range(2)]
            lefts = [jnp.concatenate([ref[:, at] for at in blocks], axis=1) for ref in (normed, cot)]
            for n, (right, left) in enumerate(((d_gate, lefts[0]), (d_up, lefts[0]), (product, lefts[1]))):
                both = mm(right[...], left).astype(HALF)
                for i in range(2):
                    tile = both[:, i * DK : (i + 1) * DK]
                    first = n * cols
                    if k < 3:
                        outs[turns.index(k)][o + i, first : first + cols, :] = tile
                    elif first + cols <= half_rows:
                        outs[0][o + i, first : first + cols, :] = tile
                    elif first >= half_rows:
                        outs[1][o + i, first - half_rows : first - half_rows + cols, :] = tile
                    else:
                        outs[0][o + i, first:, :] = tile[: half_rows - first]
                        outs[1][o + i, : first + cols - half_rows, :] = tile[half_rows - first :]


def ffn_grads(turns, mine, cot, normed, d_gate, d_up, product, after):
    rows = 3 * d_gate.shape[0]
    if turns == (3,):
        shapes = (out((4, rows // 2, DK), HALF),) * 2
    else:
        shapes = (out((4, rows, DK), HALF),) * len(turns)
    return run(
        partial(ffn_grad_kernel, turns),
        shapes + (out((8, DK), FLOAT),),
        (mine, cot, normed, d_gate, d_up, product),
        scalars=1,
        after=(after,),
    )


def put_gains_kernel(mine, gains, arrived, *refs):
    outs, token = refs[-6:-1], refs[-1]
    token[...] = jnp.zeros(token.shape, FLOAT)
    count = outs[0].shape[1] - EXTRA + 32
    for k in range(4):
        target, rows = (outs[k], count) if k < 3 else (outs[4], count - outs[3].shape[1])
        here = slice(rows, rows + 16)
        for o in range(4):
            old = target[o, here, :].astype(FLOAT)
            lanes = lane_block(dest_block(mine, k, o), DK)
            new = gains[:, lanes] + arrived[:, lanes]
            target[o, here, :] = jnp.concatenate([old[:8], new, old[10:]], axis=0).astype(HALF)


def with_gains(mine, parts, gains, arrived, after):
    vmem = pl.BlockSpec(memory_space=pltpu.VMEM)
    *parts, token = pl.pallas_call(
        put_gains_kernel,
        out_shape=tuple(out(a.shape, a.dtype) for a in parts) + (out((8, DK), FLOAT),),
        in_specs=[pl.BlockSpec(memory_space=pltpu.SMEM)]
        + [vmem] * 7
        + [pl.BlockSpec(memory_space=pl.ANY)] * len(after),
        out_specs=[vmem] * 6,
        input_output_aliases={3 + i: i for i in range(5)},
        compiler_params=pltpu.CompilerParams(vmem_limit_bytes=4 * 2**20),
        cost_estimate=cost(0.3),
    )(mine, gains, arrived, *parts, *after)
    return parts, token


def gain_rows(ref):
    first = ref.shape[1] - EXTRA + 40
    return ref[:, first : first + 8, :].astype(FLOAT)


def last_relay_kernel(own, plus, minus, first, second, plus_out, minus_out, token, rows):
    relay_kernel(plus, minus, first, second, plus_out, minus_out, token)
    for i, ref in enumerate((own, plus_out, minus_out)):
        rows[i] = gain_rows(ref)


def quad_sum_kernel(first, second, third, fourth, own, plus, minus, token):
    token[...] = jnp.zeros(token.shape, FLOAT)
    for i, target in enumerate((own, plus, minus)):
        target[...] = (first[i] + second[i]) + (third[i] + fourth[i])


def relay_kernel(plus, minus, first, second, plus_out, minus_out, token):
    half = first.shape[1]
    plus_out[:, :half, :] = (plus[:, :half, :].astype(FLOAT) + first[...].astype(FLOAT)).astype(HALF)
    plus_out[:, half:, :] = plus[:, half:, :]
    minus_out[:, :half, :] = minus[:, :half, :]
    minus_out[:, half:, :] = (minus[:, half:, :].astype(FLOAT) + second[...].astype(FLOAT)).astype(HALF)
    token[...] = jnp.zeros(token.shape, FLOAT)


def relayed(parts, after, micros):
    shape = out(parts[1].shape, HALF)
    first, second = turned(parts[3], True, 1), turned(parts[4], True, -1)
    plus, minus, token = run(
        relay_kernel,
        (shape, shape, out((8, DK), FLOAT)),
        (parts[1], parts[2], first, second),
        after=after,
        micros=micros,
    )
    return (parts[0], turned(plus, True, 1), turned(minus, True, -1)), token


def last_sum_kernel(mine, own, plus, minus, own_rows, plus_rows, minus_rows, *outs):
    seq_sum_kernel(0, mine, own, plus, minus, *outs)
    rank = jnp.where(mine[1] == 0, mine[2], mine[3])
    first = outs[0].shape[0] - EXTRA + 32
    for k in range(4):
        place = ring_place(rank, k)
        old = own[place, first : first + 16, :].astype(FLOAT)
        old = old + plus[place, first : first + 16, :].astype(FLOAT) + minus[place, first : first + 16, :].astype(FLOAT)
        new = own_rows[place] + plus_rows[place] + minus_rows[place]
        outs[k][first : first + 16, :] = jnp.concatenate([old[:8], new], axis=0).astype(outs[k].dtype)


def seq_sum_kernel(early, mine, *refs):
    rank = jnp.where(mine[1] == 0, mine[2], mine[3])
    group, before = refs[:3], refs[3 : 3 + 4 * early]
    outs = refs[3 + 4 * early : 7 + 4 * early]
    refs[-1][...] = jnp.zeros(refs[-1].shape, FLOAT)
    for k in range(4):
        place = ring_place(rank, k)
        at = 0
        for i in range(early):
            source = before[4 * i + k]
            outs[k][at : at + source.shape[0], :] = source[...]
            at += source.shape[0]
        total = group[0][place].astype(FLOAT) + group[1][place].astype(FLOAT) + group[2][place].astype(FLOAT)
        outs[k][at:, :] = total.astype(outs[k].dtype)


def seq_sums(group, before, mine, after, micros):
    count = group[0].shape[1] + sum(sums[0].shape[0] for sums in before)
    shapes = (out((count, DK), FLOAT),) + (out((count, DK), HALF),) * 3
    shapes += (out((8, DK), FLOAT),)
    flat = [piece for sums in before for piece in sums]
    return run(
        partial(seq_sum_kernel, len(before)), shapes, (mine, *group, *flat), scalars=1, after=after, micros=micros
    )


def second_round(sums):
    return [sums[0]] + [turned(sums[i], False, TURNS[i]) for i in range(1, 4)]


def unpack_kernel(own, first, second, third, *outs):
    total = own[...] + first[...].astype(FLOAT) + second[...].astype(FLOAT) + third[...].astype(FLOAT)
    at = 0
    for target in outs[:5]:
        count = target.shape[1]
        target[...] = total[at : at + count, :].T
        at += count
    extra = total[at:, :]
    per_tap = 8
    first = 0
    for target in outs[5:8]:
        blocks = target.shape[1] // DK
        for j in range(4):
            for i in range(blocks):
                row = j * per_tap + first + i
                target[j : j + 1, i * DK : (i + 1) * DK] = extra[row : row + 1, :]
        first += blocks
    for i in range(outs[8].shape[1] // DK):
        outs[8][:, i * DK : (i + 1) * DK] = extra[32 + i : 33 + i, :]
    outs[9][...] = extra[36:38, :]
    outs[10][...] = extra[40:48, :]


def ffn_unpack_kernel(own, first, second, third, gate, up, down, token):
    cols = gate.shape[0]
    token[...] = jnp.zeros(token.shape, FLOAT)
    for n, target in enumerate((gate, up, down)):
        span = slice(n * cols, (n + 1) * cols)
        target[...] = (
            own[span, :]
            + first[span, :].astype(FLOAT)
            + second[span, :].astype(FLOAT)
            + third[span, :].astype(FLOAT)
        )


def output_kernel(own, arrived, total, token):
    token[...] = jnp.zeros(token.shape, FLOAT)
    total[...] = (own[...] + arrived[...].astype(FLOAT)).astype(HALF)


def tile_of(i, mine):
    return (i % 4) * 2 + jnp.where(i < 4, 1 - mine[1], mine[1])


def whole_block(shape):
    return pl.BlockSpec(shape, lambda i, mine: (0,) * len(shape))


def tile_outs(rows, width):
    return [
        pl.BlockSpec((1, rows, width), lambda i, mine: (jnp.minimum(i, 3), 0, 0)),
        pl.BlockSpec((1, rows, width), lambda i, mine: (jnp.maximum(i - 4, 0), 0, 0)),
    ]


def down_kernel(mine, product, weight, hidden, other, own, token, scratch):
    step = pl.program_id(0)
    rows = hidden.shape[0]

    @pl.when(step == 0)
    def _():
        scratch[...] = product[...].T

    part = mm(scratch[...], weight[...])
    here = lane_block(mine[0] * 2 + mine[1], rows)
    for target, wanted in ((other, step < 4), (own, step >= 4)):

        @pl.when(wanted)
        def _():
            target[0] = part.astype(HALF)
            target[0, here, :] = (target[0, here, :].astype(FLOAT) + hidden[...]).astype(HALF)

    token[...] = jnp.zeros(token.shape, FLOAT)


def down_tiles(mine, product, weight, hidden):
    cols, tokens = product.shape
    width = weight.shape[1] // 8
    spec = pltpu.PrefetchScalarGridSpec(
        num_scalar_prefetch=1,
        grid=(8,),
        in_specs=[
            whole_block(product.shape),
            pl.BlockSpec((cols, width), lambda i, mine: (0, tile_of(i, mine))),
            pl.BlockSpec((hidden.shape[0], width), lambda i, mine: (0, tile_of(i, mine))),
        ],
        out_specs=tile_outs(tokens, width) + [whole_block((8, DK))],
        scratch_shapes=[pltpu.VMEM((tokens, cols), HALF)],
    )
    tiles = out((4, tokens, width), HALF)
    return pl.pallas_call(
        down_kernel,
        grid_spec=spec,
        out_shape=(tiles, tiles, out((8, DK), FLOAT)),
        compiler_params=pltpu.CompilerParams(vmem_limit_bytes=16 * 2**20),
        cost_estimate=cost(4.0),
    )(mine, product, weight, hidden)


def d_first_kernel(mine, dproj, arrived, proj, d_pre, d_logit, sums, in_rows, gate_rows, beta_rows, after, other, own, token, scratch, sum_rows):
    step = pl.program_id(0)
    tokens = d_pre.shape[0]
    width = own.shape[2]

    @pl.when(step == 0)
    def _():
        scratch[: tokens - HALO, :] = dproj[HALO:tokens, :]
        extra = arrived[...].astype(FLOAT)
        scratch[tokens - HALO :, :] = (dproj[tokens:, :].astype(FLOAT) + extra).astype(HALF)
        late = jnp.sum(extra * proj[tokens - HALO :, :].astype(FLOAT), axis=-1, keepdims=True)
        column = jnp.concatenate([sums[HALO:tokens, :], sums[tokens:, :] + late], axis=0)
        row = jnp.broadcast_to(column, (tokens, DK)).T
        sum_rows[...] = jnp.zeros(sum_rows.shape, FLOAT)
        for i in range(tokens // width):
            sum_rows[i : i + 1, :] = row[0:1, i * width : (i + 1) * width]

    part = mm(scratch[...], in_rows[...]) + mm(d_pre[...], gate_rows[...])
    for h in range(2):
        part = part + d_logit[:, h : h + 1] * beta_rows[h : h + 1, :].astype(FLOAT)
    for target, wanted in ((other, step < 4), (own, step >= 4)):

        @pl.when(wanted)
        def _():
            target[0, :tokens, :] = part.astype(HALF)
            target[0, tokens:, :] = sum_rows[...].astype(HALF)

    token[...] = jnp.zeros(token.shape, FLOAT)


def d_first_tiles(mine, dproj, arrived, proj, d_pre, d_logit, sums, in_rows, gate_rows, beta_rows, after):
    tokens = d_pre.shape[0]
    width = in_rows.shape[1] // 8
    count = tokens + HALO

    def tile(rows):
        return pl.BlockSpec((rows, width), lambda i, mine: (0, tile_of(i, mine)))

    spec = pltpu.PrefetchScalarGridSpec(
        num_scalar_prefetch=1,
        grid=(8,),
        in_specs=[whole_block(a.shape) for a in (dproj, arrived, proj, d_pre, d_logit, sums)]
        + [tile(in_rows.shape[0]), tile(gate_rows.shape[0]), tile(beta_rows.shape[0])]
        + [pl.BlockSpec(memory_space=pl.ANY)],
        out_specs=tile_outs(count, width) + [whole_block((8, DK))],
        scratch_shapes=[pltpu.VMEM((tokens, dproj.shape[1]), HALF), pltpu.VMEM((HALO, width), FLOAT)],
    )
    tiles = out((4, count, width), HALF)
    return pl.pallas_call(
        d_first_kernel,
        grid_spec=spec,
        out_shape=(tiles, tiles, out((8, DK), FLOAT)),
        compiler_params=pltpu.CompilerParams(vmem_limit_bytes=16 * 2**20),
        cost_estimate=cost(6.0),
    )(mine, dproj, arrived, proj, d_pre, d_logit, sums, in_rows, gate_rows, beta_rows, after)


def input_grad_kernel(mine, own, arrived, block_input, factor, gain, d_branch, grad):
    total = own[...] + arrived[...].astype(FLOAT)
    tokens, width = block_input.shape
    columns = []
    for i in range(tokens // width):
        row = total[tokens + i : tokens + i + 1, :]
        columns.append(jnp.broadcast_to(row, (DK, width)).T[:, 0:1])
    mean = jnp.concatenate(columns, axis=0) / (8 * width)
    scale = factor[...]
    unit = block_input[...].astype(FLOAT) * scale
    gain_own = gain[:, lane_block(mine[0] * 2 + mine[1], width)]
    grad[...] = d_branch[...].astype(FLOAT) + scale * (total[:tokens, :] * gain_own - unit * mean)


def next_block(array, distance):
    size = 16
    route = [(i, i + distance) for i in range(size) if 0 <= i + distance < size]
    return lax.ppermute(array, SEQ, route)


def dot_nt(a, b):
    return lax.dot_general(a, b, NT, preferred_element_type=FLOAT)


def shards(
    block_input,
    log_decay,
    first_gain,
    query_weight,
    key_weight,
    value_weight,
    gate_weight,
    beta_weight,
    query_conv,
    key_conv,
    value_conv,
    mixer_gain,
    mixer_weight,
    second_gain,
    swiglu_gate,
    swiglu_up,
    swiglu_down,
    cotangent,
):
    heads = log_decay.shape[1]
    tokens, width = block_input.shape
    model = 8 * width
    chunks = tokens // CH
    rows = tokens // 8
    kq, vd = heads * DK, heads * DV
    cols = 2 * kq + vd
    hidden_cols = swiglu_gate.shape[1]
    mine = jnp.stack([lax.axis_index(name) for name in ("x", "c", "y", "z")]).astype(jnp.int32)

    token_out = out((8, DK), FLOAT)
    in_rows, gate_rows, gcol, grow, token = run(
        setup_kernel,
        (
            out((cols, model), HALF),
            out((vd, model), HALF),
            out((tokens, heads), FLOAT),
            out((heads * chunks, CH), FLOAT),
            token_out,
        ),
        (query_weight, key_weight, value_weight, gate_weight, log_decay.T),
        micros=3.0,
    )
    beta_rows = jnp.pad(beta_weight.T, ((0, HALO - heads), (0, 0)))
    taps = jnp.concatenate([query_conv.T, key_conv.T, value_conv.T], axis=1)
    gain_row = mixer_gain.reshape(1, -1)
    first_row = first_gain.reshape(1, -1)

    first_normed, first_factor, my_rows, logits, halo_rows = run(
        first_norm_kernel,
        (
            out((tokens, model), HALF),
            out((tokens, 1), FLOAT),
            out((rows, model), FLOAT),
            out((tokens, HALO), FLOAT),
            out((HALO, model), HALF),
        ),
        (mine, first_row, beta_rows, *head_gather(block_input, mine, (token,))),
        scalars=1,
        micros=3.0,
    )
    halo_normed = next_block(halo_rows, 1)
    proj = dot_nt(first_normed, in_rows).astype(HALF)
    halo_proj = dot_nt(halo_normed, in_rows).astype(HALF)
    gate_pre = dot_nt(first_normed, gate_rows)
    k, v, tri, n, b, w, u, pay, pay_token = run(
        partial(prepare_kernel, heads, chunks),
        prepare_shapes(heads, chunks) + (token_out,),
        (proj, halo_proj, taps, logits, gcol, grow),
        [pltpu.VMEM((HALO + tokens, cols), FLOAT)],
        micros=8.0,
        kept=range(7),
        megs=20,
    )
    near_pieces = ring_pieces(pay, "z")
    q, p, query_token = run(
        partial(query_kernel, heads, chunks),
        (out((tokens, kq), HALF), out((heads * chunks, CH, CH), HALF), token_out),
        (proj, halo_proj, taps, k, gcol, grow),
        [pltpu.VMEM((HALO + tokens, kq), FLOAT)],
        after=(pay_token,),
    )
    before, group, near, group_token = run(
        partial(group_kernel, heads), group_shapes(heads) + (token_out,), (mine, *near_pieces), scalars=1, after=(gate_pre[:8, :DK], query_token), micros=2.0
    )
    half_tiles = out((4, rows, model), HALF)
    states, vns, mixed, gated, branch_other, branch_own, far, mix_token = run(
        partial(mix_kernel, heads, chunks),
        mix_shapes(heads, chunks)[:4] + (half_tiles, half_tiles) + mix_shapes(heads, chunks)[4:] + (token_out,),
        (mine, *ring_pieces(group, "y"), before, q, k, w, u, p, n, b, gcol, gate_pre, gain_row, mixer_weight),
        [pltpu.VMEM((tokens, model // 4), FLOAT)],
        scalars=1,
        kept=(0, 1, 2, 6),
        megs=16,
        micros=4.0,
    )
    branch = head_scatter(branch_own, branch_other, mine)
    cot = run(copy_kernel, (out((tokens, width), HALF),), (cotangent,), after=(group_token,))[0]
    cot_tiles = head_gather(cot, mine, (mix_token,))
    whole_cot, cot_rows, d_product, token = run(
        product_grad_kernel,
        (out((tokens, model), HALF), out((rows, model), HALF), out((hidden_cols, tokens), FLOAT), token_out),
        (mine, *cot_tiles, swiglu_down.T),
        scalars=1,
        micros=4.0,
    )
    wide_rows = out((rows, model), FLOAT)
    second_row = second_gain.reshape(1, -1)
    hidden, second_unit, second_factor, own_normed = run(
        hidden_kernel,
        (wide_rows, wide_rows, out((rows, 1), FLOAT), out((rows, model), HALF)),
        (my_rows, second_row, *branch),
        after=(token,),
    )
    turned_out = out((hidden_cols, tokens), HALF)
    second_normed, product, d_gate, d_up, second_other, second_own, ffn_token = run(
        ffn_kernel,
        (out((tokens, model), HALF), turned_out, turned_out, turned_out, half_tiles, half_tiles, token_out),
        (
            mine,
            *head_gather(own_normed, mine),
            swiglu_gate.T,
            swiglu_up.T,
            d_product,
        ),
        [pltpu.VMEM((tokens, model // 4), FLOAT)],
        scalars=1,
        micros=9.0,
        megs=20,
    )
    grad_args = (mine, whole_cot, second_normed, d_gate, d_up, product)
    *ffn_ends, token = ffn_grads((3,), *grad_args, ffn_token)
    second_parts, token = head_scatter(second_own, second_other, mine, True, (token,))
    ffn_plus, ffn_minus, token = ffn_grads((1, 2), *grad_args, token)
    d_hidden, second_gain_part, back_token = run(
        second_back_kernel,
        (out((rows, model), HALF), out((1, model), FLOAT), token_out),
        (second_unit, second_factor, second_row, cot_rows, *second_parts),
        after=(token,),
    )
    ffn_group, ffn_token = relayed([None, ffn_plus, ffn_minus, *ffn_ends], (back_token,), 3.0)
    down_other, down_own, down_token = down_tiles(mine, product, swiglu_down.T, hidden)
    ffn_own, own_token = ffn_grads((0,), *grad_args, back_token)
    d_branch, d_branch_own = run(
        join_rows_kernel,
        (out((tokens, model), HALF), out((tokens, width), HALF)),
        (mine, *head_gather(d_hidden, mine, (down_token, ffn_token, own_token))),
        scalars=1,
    )
    down_arrived = rotated(down_other, "c", 1)
    d_gated = jnp.dot(d_branch, mixer_weight, preferred_element_type=FLOAT)
    dos, dvns, es, d_gate_pre, gain_part, gate_sums, ends = run(
        partial(gate_back_kernel, heads, chunks),
        gate_back_shapes(heads, chunks),
        (d_gated, mixed, gate_pre, gain_row, q, w, p, n, gcol),
        after=(down_arrived,),
        micros=4.0,
    )
    *ffn_sums, ffn_token = seq_sums((ffn_own, *ffn_group[1:]), (), mine, (), 3.0)
    tile = out((4, 2 * vd, DK), HALF)
    *mixer_parts, gate_gain = run(
        mixer_grad_kernel,
        (tile,) * 4 + (out((1, model), FLOAT),),
        (mine, d_branch, gated, first_normed, d_gate_pre, gate_rows),
        [pltpu.VMEM((vd, tokens), HALF), pltpu.VMEM((vd, tokens), HALF)],
        scalars=1,
        micros=5.0,
    )
    after, group_end, _, group_token = run(
        partial(group_back_kernel, heads),
        group_back_shapes(heads) + (token_out,),
        (mine, near, *ring_pieces(ends, "z")),
        scalars=1,
        after=(gate_gain, ffn_token),
        micros=2.0,
    )
    end_pieces = ring_pieces(group_end, "y")
    out_keep, out_send, out_token = first_halves(down_own, down_arrived, mine, (group_token,))
    square = out((heads * chunks, CH, CH), FLOAT)
    *slopes, slope_token = run(
        partial(slopes_kernel, heads, chunks),
        (out((tokens, cols), FLOAT), square, square, out((tokens, vd), FLOAT), token_out),
        (k, v, states, gcol, grow, proj, halo_proj, taps),
        [pltpu.VMEM((HALO + tokens, cols), FLOAT)],
        after=(group_token,),
    )
    passed_sums, ffn_token = passed(ffn_sums, (*end_pieces[1:], slope_token, out_token))
    dproj, halo_grad, d_logit, logit_rows, taps_part, sums = run(
        partial(back_kernel, heads, chunks),
        back_shapes(heads, chunks),
        (mine, far, *end_pieces, after, q, k, logits, gate_sums, gcol, tri, states, vns, dos, dvns, es, n, proj, halo_proj, taps, *slopes),
        back_scratch(heads, chunks),
        scalars=1,
        after=(ffn_token,),
        micros=11.0,
        megs=30,
    )
    packed = 2 * vd + cols + EXTRA
    tile, half_tile = out((4, packed, DK), HALF), out((4, packed // 2, DK), HALF)
    *in_parts, in_token, gains_part = run(
        in_grad_kernel,
        (tile,) * 3 + (half_tile,) * 2 + (token_out, out((2, model), FLOAT)),
        (mine, first_normed, halo_normed, dproj, logit_rows, taps_part, gain_part, gate_gain, second_gain_part, first_row, in_rows, beta_rows, *mixer_parts),
        [pltpu.VMEM((cols + HALO, HALO + tokens), HALF), pltpu.VMEM((EXTRA, DK), FLOAT)],
        scalars=1,
        micros=6.0,
        megs=16,
    )
    out_mine, out_send, out_token = second_halves(out_keep, swapped(out_send, 2), mine, (in_token,))
    ffn_grad_out = out((hidden_cols, DK), FLOAT)
    grad_gate, grad_up, grad_down, ffn_token = run(
        ffn_unpack_kernel, (ffn_grad_out,) * 3 + (token_out,), second_round(passed_sums), after=(out_token,)
    )
    arrived = next_block(halo_grad, -1)
    in_parts, in_token = with_gains(
        mine, in_parts, gains_part, rotated(gains_part, "c", 1), (ffn_token, arrived)
    )
    first_other, first_own, first_token = d_first_tiles(
        mine, dproj, arrived, proj, d_gate_pre, d_logit, sums, in_rows, gate_rows, beta_rows, in_token
    )
    output, out_token = run(
        output_kernel, (out((tokens, width), HALF), token_out), (out_mine, swapped(out_send, 1))
    )
    tile = out((4, packed, DK), HALF)
    plus, minus, in_token, rows_left = run(
        last_relay_kernel,
        (tile, tile, token_out, out((3, 4, 8, DK), FLOAT)),
        (*in_parts[:3], turned(in_parts[3], True, 1), turned(in_parts[4], True, -1)),
        after=(first_token, out_token),
    )
    in_group = (in_parts[0], turned(plus, True, 1), turned(minus, True, -1))
    own_rows, plus_rows, minus_rows, gain_token = run(
        quad_sum_kernel, (out((4, 8, DK), FLOAT),) * 3 + (token_out,), ring_pieces(rows_left, "x"), after=(in_token,)
    )
    first_keep, first_send, _ = first_halves(first_own, rotated(first_other, "c", 1), mine, (gain_token,))
    first_mine, first_send, _ = second_halves(first_keep, swapped(first_send, 2), mine, ())
    *sums_out, sum_token = run(
        last_sum_kernel,
        (out((packed, DK), FLOAT),) + (out((packed, DK), HALF),) * 3 + (token_out,),
        (mine, *in_group, own_rows, turned(plus_rows, True, 1), turned(minus_rows, True, -1)),
        scalars=1,
    )
    totals = [sums_out[0]] + [turned(sums_out[i], False, TURNS[i]) for i in range(1, 4)]
    grad_mixer_weight, grad_gate_weight, grad_query, grad_key, grad_value, *taps_grad, gain_grad, beta_grad, both = run(
        unpack_kernel,
        tuple(out((DK, count), FLOAT) for count in (vd, vd, kq, kq, vd)) + tuple(out((rows_, count), FLOAT) for rows_, count in ((4, kq), (4, kq), (4, vd), (1, vd), (heads, DK), (8, DK))),
        totals,
    )
    grad_input = run(
        input_grad_kernel,
        (out((tokens, width), FLOAT),),
        (mine, first_mine, swapped(first_send, 1), block_input, first_factor, first_row, d_branch_own),
        scalars=1,
    )[0]
    return (
        output,
        grad_input,
        both[0],
        grad_query,
        grad_key,
        grad_value,
        grad_gate_weight,
        beta_grad.T,
        taps_grad[0].T,
        taps_grad[1].T,
        taps_grad[2].T,
        gain_grad.reshape(-1),
        grad_mixer_weight,
        both[1],
        grad_gate.T,
        grad_up.T,
        grad_down.T,
    )


def solution(mesh):
    torus = Mesh(mesh.devices.reshape(4, 4, 4, 2), SEQ + HEAD)
    in_specs = (
        P(SEQ, HEAD),
        P(SEQ, HEAD),
        P(),
        P(None, HEAD),
        P(None, HEAD),
        P(None, HEAD),
        P(None, HEAD),
        P(None, HEAD),
        P(HEAD, None),
        P(HEAD, None),
        P(HEAD, None),
        P(HEAD),
        P(None, HEAD),
        P(),
        P(None, HEAD),
        P(None, HEAD),
        P(None, HEAD),
        P(SEQ, HEAD),
    )
    out_specs = (
        P(SEQ, HEAD),
        P(SEQ, HEAD),
        P(SEQ),
        P(SEQ, HEAD),
        P(SEQ, HEAD),
        P(SEQ, HEAD),
        P(SEQ, HEAD),
        P(SEQ, HEAD),
        P(HEAD, None),
        P(HEAD, None),
        P(HEAD, None),
        P(HEAD),
        P(SEQ, HEAD),
        P(SEQ),
        P(SEQ, HEAD),
        P(SEQ, HEAD),
        P(SEQ, HEAD),
    )
    return jax.shard_map(
        shards, mesh=torus, in_specs=in_specs, out_specs=out_specs, check_vma=False
    )
```
